32 devices in a mesh: group: 2 (over x), ccd: 16 (over z, y, core).
Axes of the slice: x: 2, y: 2, z: 4, core: 2. Of those that a mesh axis runs over, the one named last changes fastest.
Arguments:
- images: float32 [4, 4096, 512], P(None, ('group', 'ccd')), parts along dimension 1, may hold values from -6 to 6
- basis_taps: float32 [2, 9, 11], replicated, may hold values from -1.75 to 1.75
- psf_coef: float32 [4, 10, 9, 3], P(None, 'group'), parts along dimension 1, may hold values from -3 to 3
- affine: float32 [4, 10, 2, 2], P(None, 'group'), parts along dimension 1, may hold values from -0.5 to 0.5
- visit_weight: bfloat16 [4, 10], P(None, 'group'), parts along dimension 1, may hold values from 0.25 to 4
- block_patch: int32 [32, 16, 1], P(('group', 'ccd')), parts along dimension 0, may hold values from 0 to 15; in each aligned block of 16 rows (0 to 15, 16 to 31, ..., all dimensions but the last counted through in order) at most 2 rows name the same one
- block_slot: int32 [32, 16], P(('group', 'ccd')), parts along dimension 0, may hold values from 0 to 15
- patch_owner: int32 [32], P('group'), parts along dimension 0, may hold values from 0 to 15, each once
Outputs:
- coadd: float32 [32, 512, 512], P(('group', 'ccd')), parts along dimension 0
The draws below stay inside these ranges and needn't reach their ends.
There are 2 independent parts, one for each index of `group`. The reference program is written for one: setup_inputs(seed, part) draws one part's arguments, and reference() takes and returns one part's arrays. A program takes and returns all parts, laid end to end along the dimension named above; an argument that names none is the same for every part. Nothing has to cross between parts.
Inputs may be any that keep to these rules, and one draw needn't show every extreme that they name: `block_patch`: among the 16 blocks of one band no patch is named more than 2 times, and in every draw some band names some patch exactly 2 times. `patch_owner`: each device index along ccd owns exactly one patch.
All inputs are finite; a program needn't handle non-finite values.
Results may differ from the reference program's by a relative error of at most 0.0029.
Values may be sent and summed in bfloat16 or wider, within the bound.
No kernel may reach another device: no remote copies, remote signals or barrier semaphores. Data moves between devices by JAX's collectives and lax.ppermute only.
A program may use at most 64 MiB of HBM per device.

```python
import math
import jax
import jax.numpy as jnp
import numpy as np
from jax import lax

V = 4
BLOCK = 128
BLKC = 4
SPLIT = 4
TAPS = 11
NBASIS = 9
PSIDE = 4
BANDS = 16
NCCD = 5
NPATCH = 16
BLK_DEV = 16
CAP = 2


def touch_ends(result, own_key, low, high):
    place = [jax.random.randint(jax.random.fold_in(own_key, axis), (), 0, length) for axis, length in enumerate(result.shape)]
    longest = result.shape.index(max(result.shape))
    beside = place[:longest] + [(place[longest] + 1) % result.shape[longest]] + place[longest + 1:]
    return result.at[tuple(place)].set(low).at[tuple(beside)].set(high)


def level_of(own_key, extent, pieces, low, largest):
    def one(axis_at, parts):
        draws = jax.random.uniform(jax.random.fold_in(jax.random.fold_in(own_key, 6), axis_at), (parts,), jnp.float32, low / len(pieces), largest / len(pieces))
        return jnp.repeat(jnp.exp(draws), extent[axis_at] // parts).reshape((-1,) + (1,) * (len(extent) - axis_at - 1))

    level = one(*pieces[0])
    for cut in pieces[1:]:
        level = level * one(*cut)
    return level


def shared_out(rng, own, number, rows, amount, top, limit, lean):
    ranking = jax.random.permutation(rng, amount)
    crowded, usual = shares(amount, rows * top, limit, lean, True), shares(amount, rows * top, limit, lean, False)
    places = jnp.arange(amount)

    def named(lengths, offset_by):
        used = int((lengths > 0).sum())
        fixed = max(1, used // 4)
        passed = fixed + (places - fixed + offset_by * (used - fixed)) % max(1, amount - fixed)
        return jnp.zeros((amount,), jnp.int32).at[ranking[jnp.where(places < fixed, places, passed)]].set(jnp.asarray(lengths, jnp.int32))

    lengths = jnp.where(number % 4 == 0, named(crowded, number // 4), named(usual, number - number // 4 - 1))
    mixed = jax.random.permutation(jax.random.fold_in(own, 3), amount)
    source_of, taker = mixed[0:amount // 2 * 2:2], mixed[1:amount // 2 * 2:2]
    margin = jnp.minimum(lengths[source_of] - 1, limit - lengths[taker]) // 2
    margin = jnp.where((source_of == ranking[0]) | (taker == ranking[0]) | (lengths[taker] == 0), 0, jnp.maximum(margin, 0))
    passed = jax.random.randint(jax.random.fold_in(own, 4), (amount // 2,), 0, 1 << 20) % (margin + 1)
    lengths = lengths.at[source_of].add(-passed).at[taker].add(passed)
    labels = jnp.searchsorted(jnp.cumsum(lengths), jnp.arange(rows * top), side="right").astype(jnp.int32)
    listing = labels.reshape(top, rows).T
    listing = listing[jax.random.permutation(jax.random.fold_in(own, 1), rows)]
    offset_by = jax.random.randint(jax.random.fold_in(own, 2), (rows, 1), 0, top)
    return jnp.take_along_axis(listing, (jnp.arange(top)[None, :] + offset_by) % top, axis=1)


def shares(count, total, most, slope, full):
    weights = [(1 << 20) // math.isqrt(grade ** slope) + 1 for grade in range(1, count + 1)]
    largest = most if full else min(most, max(-(-total // count), total * weights[0] // sum(weights)))
    least = 1 if total - largest >= count - 1 else 0
    given, surplus = [largest] + [least] * (count - 1), total - largest - least * (count - 1)
    while surplus > 0:
        candidates = [i for i in range(1, count) if given[i] < largest] or [i for i in range(1, count) if given[i] < most]
        pool, left = sum([weights[i] for i in candidates]), surplus
        for i in candidates:
            more = min(most - given[i], max(1, left * weights[i] // pool), surplus)
            given[i] = given[i] + more
            surplus = surplus - more
    return np.array(given)


def bell_draw(rng, shape, spread, most, cuts=(), kind=jnp.bfloat16):
    values = spread * jax.random.normal(rng, shape, jnp.float32)
    if cuts:
        values = values * level_of(rng, shape, cuts, -0.22, 0.18)
    return jnp.clip(values, -most, most).astype(kind)


def setup_inputs(seed: int = 0, part: int = 0) -> dict:
    splits = jax.random.split(jax.random.key(seed), 9)
    part_splits = jax.random.split(jax.random.fold_in(splits[8], part), 9)
    images = bell_draw(part_splits[0], (V, BANDS * BLOCK, BLKC * BLOCK), 1.0, 6.0, ((1, 16),), jnp.float32)
    basis_taps = bell_draw(splits[1], (2, NBASIS, TAPS), TAPS ** -0.5, 1.75, (), jnp.float32)
    psf_coef = bell_draw(part_splits[2], (V, NCCD, NBASIS, 3), 0.35, 3.0, (), jnp.float32)
    affine = jnp.clip(jax.random.uniform(part_splits[3], (V, NCCD, 2, 2), jnp.float32, -0.5, 0.5), -0.5, 0.5)
    visit_weight = jnp.clip(jnp.exp(jax.random.uniform(part_splits[4], (V, NCCD), jnp.float32, math.log(0.25), math.log(4.0))), 0.25, 4.0).astype(jnp.bfloat16)
    block_patch_keys = jax.random.split(jax.random.fold_in(part_splits[5], 1), BANDS * BLK_DEV // BLK_DEV)
    block_patch_turns = jax.random.permutation(jax.random.fold_in(part_splits[5], 3), BANDS * BLK_DEV // BLK_DEV)
    block_patch = jax.vmap(lambda own, number: shared_out(jax.random.fold_in(part_splits[5], 2), own, number, BLK_DEV, NPATCH, 1, CAP, 2))(block_patch_keys, block_patch_turns).reshape((BANDS, BLK_DEV, 1))
    block_slot = touch_ends(jax.random.randint(part_splits[6], (BANDS, BLK_DEV), 0, PSIDE * PSIDE), jax.random.fold_in(part_splits[6], 1), 0, (PSIDE * PSIDE) - 1).astype(jnp.int32)
    patch_owner = jax.random.permutation(part_splits[7], NPATCH).astype(jnp.int32)
    return {"images": images, "basis_taps": basis_taps, "psf_coef": psf_coef, "affine": affine, "visit_weight": visit_weight, "block_patch": block_patch, "block_slot": block_slot, "patch_owner": patch_owner}


def lanczos(offset):
    inside = jnp.abs(offset) < 3.0
    return jnp.where(inside, jnp.sinc(offset) * jnp.sinc(offset / 3.0), 0.0)


def match_warp(inputs, basis_taps):
    ccd_image, psf_terms, affine_map, ccd_number = inputs
    height = SPLIT * BLOCK
    ccd_width = BLKC * BLOCK
    half_taps = TAPS // 2
    offset_rows = (SPLIT // 2) * BLOCK
    row_pos = (2.0 * jnp.arange(height, dtype=jnp.float32) + 1.0) / height - 1.0
    col_pos = (2.0 * jnp.arange(ccd_width, dtype=jnp.float32) + 1.0) / ccd_width - 1.0
    padded = jnp.pad(ccd_image, ((0, 0), (half_taps, half_taps)))
    matched = jnp.zeros((height, ccd_width), jnp.float32)
    for basis_index in range(NBASIS):
        column_pass = jnp.zeros((height, ccd_width), jnp.float32)
        for tap_index in range(TAPS):
            column_pass = column_pass + basis_taps[1, basis_index, tap_index] * padded[:, tap_index:tap_index + ccd_width]
        row_padded = jnp.pad(column_pass, ((half_taps, half_taps), (0, 0)))
        row_pass = jnp.zeros((height, ccd_width), jnp.float32)
        for tap_index in range(TAPS):
            row_pass = row_pass + basis_taps[0, basis_index, tap_index] * row_padded[tap_index:tap_index + height]
        spatial = psf_terms[basis_index, 0] + psf_terms[basis_index, 1] * row_pos[:, None] + psf_terms[basis_index, 2] * col_pos[None, :]
        matched = matched + spatial * row_pass
    region_row = ccd_number * height + jnp.arange(height, dtype=jnp.int32) - offset_rows
    keep = ((region_row >= 0) & (region_row < BANDS * BLOCK)).astype(jnp.float32)
    matched = matched * keep[:, None]
    rows_global = jnp.arange(height, dtype=jnp.float32)
    row_shift = affine_map[0, 0] + affine_map[0, 1] * (rows_global - (height - 1) / 2.0) / height
    framed = jnp.pad(matched, ((3, 3), (0, 0)))
    row_warped = jnp.zeros((height, ccd_width), jnp.float32)
    for step_index in range(-3, 4):
        row_warped = row_warped + lanczos(row_shift - step_index)[:, None] * framed[3 + step_index:3 + step_index + height]
    cols_global = jnp.arange(ccd_width, dtype=jnp.float32)
    col_shift = affine_map[1, 0] + affine_map[1, 1] * (cols_global - (ccd_width - 1) / 2.0) / ccd_width
    framed_cols = jnp.pad(row_warped, ((0, 0), (3, 3)))
    warped = jnp.zeros((height, ccd_width), jnp.float32)
    for step_index in range(-3, 4):
        warped = warped + lanczos(col_shift - step_index)[None, :] * framed_cols[:, 3 + step_index:3 + step_index + ccd_width]
    return warped.astype(jnp.bfloat16)


def reference(images, basis_taps, psf_coef, affine, visit_weight, block_patch, block_slot, patch_owner):
    height = SPLIT * BLOCK
    ccd_width = BLKC * BLOCK
    offset_rows = (SPLIT // 2) * BLOCK
    tail_rows = NCCD * height - BANDS * BLOCK - offset_rows
    padded_images = jnp.pad(images, ((0, 0), (offset_rows, tail_rows), (0, 0)))
    stacked = padded_images.reshape(V * NCCD, height, ccd_width)
    psf_terms = psf_coef.reshape(V * NCCD, NBASIS, 3)
    affine_maps = affine.reshape(V * NCCD, 2, 2)
    ccd_numbers = jnp.tile(jnp.arange(NCCD, dtype=jnp.int32), V)

    def one_ccd(inputs):
        return match_warp(inputs, basis_taps)

    warped = lax.map(one_ccd, (stacked, psf_terms, affine_maps, ccd_numbers))
    warped = warped.reshape(V, NCCD * height, ccd_width)[:, offset_rows:offset_rows + BANDS * BLOCK]
    blocks = warped.reshape(V, BANDS, BLOCK, BLKC, BLOCK).transpose(1, 0, 3, 2, 4)
    blocks = blocks.reshape(BANDS * V * BLKC, BLOCK * BLOCK)
    band_ccd = (jnp.arange(BANDS, dtype=jnp.int32) + SPLIT // 2) // SPLIT
    weights = visit_weight.astype(jnp.float32).T[band_ccd]
    weights = jnp.repeat(weights, BLKC, axis=1).reshape(-1)
    cells = PSIDE * PSIDE
    segment_ids = (block_patch[:, :, 0] * cells + block_slot).reshape(-1).astype(jnp.int32)
    contrib = weights[:, None] * blocks.astype(jnp.float32)
    numerator = jax.ops.segment_sum(contrib, segment_ids, num_segments=NPATCH * cells)
    denominator = jax.ops.segment_sum(weights, segment_ids, num_segments=NPATCH * cells)
    patches = numerator / jnp.maximum(denominator, 1.0)[:, None]
    patches = patches.reshape(NPATCH, PSIDE, PSIDE, BLOCK, BLOCK).transpose(0, 1, 3, 2, 4)
    patches = patches.reshape(NPATCH, PSIDE * BLOCK, PSIDE * BLOCK)
    coadd = jnp.zeros_like(patches).at[patch_owner].set(patches)
    return coadd
```

```python
import functools

import jax
import jax.numpy as jnp
from jax import lax
from jax.experimental import pallas as pl
from jax.experimental.pallas import tpu as pltpu
from jax.sharding import PartitionSpec as P

V = 4
BLOCK = 128
BLKC = 4
SPLIT = 4
TAPS = 11
NBASIS = 9
PSIDE = 4
CELLS = PSIDE * PSIDE
CAP = 2

HALF = TAPS // 2
WARP = 3
RIM = HALF + WARP
HEIGHT = SPLIT * BLOCK
WIDTH = BLKC * BLOCK
PARTS = 2
ROWS = BLOCK // PARTS
RAW = ROWS + 2 * RIM
MATCH = ROWS + 8
DEPTH = -(-TAPS * RAW // 128) * 128
MARGIN = 128
F32 = jnp.float32
BF16 = jnp.bfloat16


def sin_pi(t):
    whole = jnp.round(t)
    f = t - whole
    odd = whole - 2.0 * jnp.floor(0.5 * whole)
    f2 = f * f
    out = 0.0
    for c in (
        0.00046630280576761, -0.0073704309457144, 0.0821458866111282,
        -0.599264529320792, 2.55016403987734, -5.16771278004997, 3.14159265358979,
    ):
        out = out * f2 + c
    return f * out * (1.0 - 2.0 * odd)


def lanczos(t):
    zero = t == 0.0
    safe = jnp.where(zero, 1.0, t)
    pt = jnp.pi * safe
    value = 3.0 * sin_pi(safe) * sin_pi(safe / 3.0) / (pt * pt)
    return jnp.where(jnp.abs(t) < 3.0, jnp.where(zero, 1.0, value), 0.0)


def split(x):
    high = x.astype(BF16)
    return high, (x - high.astype(F32)).astype(BF16)


def iota(shape, dim):
    return lax.broadcasted_iota(jnp.int32, shape, dim)


def warp_kernel(
    part,
    place, patch, owner, taps, psf, affine, image, rim, out,
    basis, padded, shifted, framed, ready, seen, sem,
):
    visit = pl.program_id(0)
    visits = pl.num_programs(0)
    top_row = place[1] + part * ROWS
    inside = place[2 + part]

    @pl.when(visit == 0)
    def _():
        lane = iota((TAPS, DEPTH), 1)
        tap = iota((TAPS, DEPTH), 0)
        seg = lane // RAW
        rows = jnp.dot(taps[0], (lane - seg * RAW == tap).astype(F32),
                       precision=lax.Precision.HIGHEST, preferred_element_type=F32)
        cols = jnp.dot(taps[1], (seg == tap).astype(F32),
                       precision=lax.Precision.HIGHEST, preferred_element_type=F32)
        basis[...] = rows * cols
        padded[...] = jnp.zeros_like(padded)
        framed[...] = jnp.zeros_like(framed)
        shifted[:, TAPS * RAW:, :] = jnp.zeros((2, DEPTH - TAPS * RAW, WIDTH), BF16)

    edge = jnp.where(inside > 0, rim[0], 0.0)
    if part == 0:
        raw = jnp.concatenate([edge, image[0, : ROWS + RIM]], axis=0)
    else:
        raw = jnp.concatenate([image[0, BLOCK - ROWS - RIM :], edge], axis=0)
    for term, value in enumerate(split(raw)):
        padded[term, :, MARGIN : MARGIN + WIDTH] = value
    for term in range(2):
        for u in range(TAPS):
            start = MARGIN + u - HALF
            shifted[term, u * RAW : (u + 1) * RAW, :] = padded[term, :, start : start + WIDTH]

    kernels = lax.dot_general(
        psf[0, 0], basis[...], (((0,), (0,)), ((), ())),
        precision=lax.Precision.HIGHEST, preferred_element_type=F32,
    )
    bands = []
    for c in range(3):
        first = jnp.broadcast_to(kernels[c : c + 1], (8, DEPTH))
        first = pltpu.roll(first, 0, 1, stride=1, stride_axis=0)
        bands.append(
            jnp.concatenate(
                [first] + [pltpu.roll(first, 8 * a, 1) for a in range(1, MATCH // 8)], axis=0
            )
        )
    match_row = (top_row - WARP + iota((MATCH, 1), 0)).astype(F32)
    row_pos = (2.0 * match_row + 1.0) / HEIGHT - 1.0
    level = bands[0] + row_pos * bands[1]
    level_hi, level_lo = split(level)
    slope_hi, slope_lo = split(bands[2])
    both_hi = jnp.concatenate([level_hi, slope_hi], axis=0)
    both_lo = jnp.concatenate([level_lo, slope_lo], axis=0)
    high, low = shifted[0], shifted[1]
    terms = jnp.dot(both_hi, high, preferred_element_type=F32)
    terms = terms + jnp.dot(both_lo, high, preferred_element_type=F32)
    terms = terms + jnp.dot(both_hi, low, preferred_element_type=F32)
    col_pos = (2.0 * iota((1, WIDTH), 1).astype(F32) + 1.0) / WIDTH - 1.0
    matched = terms[:MATCH] + col_pos * terms[MATCH:]

    a = affine[0, 0]
    out_row = iota((ROWS, MATCH), 0)
    in_row = iota((ROWS, MATCH), 1)
    row = (top_row + out_row).astype(F32)
    shift = a[0:1, 0:1] + a[0:1, 1:2] * (row - (HEIGHT - 1) / 2.0) / HEIGHT
    step = in_row - out_row - WARP
    keep = jnp.abs(step) <= WARP
    outer = in_row < WARP if part == 0 else in_row >= ROWS + WARP
    keep = keep & (jnp.logical_not(outer) | (inside > 0))
    weights = jnp.where(keep, lanczos(shift - step.astype(F32)), 0.0)
    weights_hi, weights_lo = split(weights)
    matched_hi, matched_lo = split(matched)
    warped = jnp.dot(weights_hi, matched_hi, preferred_element_type=F32)
    warped = warped + jnp.dot(weights_lo, matched_hi, preferred_element_type=F32)
    warped = warped + jnp.dot(weights_hi, matched_lo, preferred_element_type=F32)

    framed[:, MARGIN : MARGIN + WIDTH] = warped
    col = iota((8, WIDTH), 1).astype(F32)
    col_shift = a[1:2, 0:1] + a[1:2, 1:2] * (col - (WIDTH - 1) / 2.0) / WIDTH
    col_weights = lanczos(col_shift - (iota((8, WIDTH), 0) - WARP).astype(F32))
    total = jnp.zeros((ROWS, WIDTH), F32)
    for s in range(2 * WARP + 1):
        start = MARGIN + s - WARP
        total = total + col_weights[s : s + 1] * framed[:, start : start + WIDTH]
    result = total.astype(BF16)

    @pl.when(visit == 0)
    def _():
        def clear(p, _):
            seen[p] = 0
            return 0

        lax.fori_loop(0, owner.shape[0], clear, 0)

    for j in range(BLKC):
        block = visit * BLKC + j
        ready[block] = result[:, j * BLOCK : (j + 1) * BLOCK]
        p = patch[0, block]
        rank = seen[p]
        seen[p] = rank + 1
        pltpu.make_async_copy(ready.at[block], out.at[owner[p], rank], sem.at[block]).start()

    @pl.when(visit == visits - 1)
    def _():
        for block in range(V * BLKC):
            pltpu.make_async_copy(ready.at[block], out.at[0, 0], sem.at[block]).wait()


def warp(part, place, patch, owner, taps, psf, affine, images, rim, devices):
    smem = pl.BlockSpec(memory_space=pltpu.SMEM)
    return pl.pallas_call(
        functools.partial(warp_kernel, part),
        grid_spec=pltpu.PrefetchScalarGridSpec(
            num_scalar_prefetch=1,
            grid=(V,),
            in_specs=[
                smem,
                smem,
                pl.BlockSpec((2, NBASIS, TAPS), lambda v, place: (0, 0, 0)),
                pl.BlockSpec((1, 1, NBASIS, 3), lambda v, place: (v, place[0], 0, 0)),
                pl.BlockSpec((1, 1, 2, 2), lambda v, place: (v, place[0], 0, 0)),
                pl.BlockSpec((1, BLOCK, WIDTH), lambda v, place: (v, 0, 0)),
                pl.BlockSpec((1, RIM, WIDTH), lambda v, place: (v, 0, 0)),
            ],
            out_specs=pl.BlockSpec(memory_space=pl.ANY),
            scratch_shapes=[
                pltpu.VMEM((NBASIS, DEPTH), F32),
                pltpu.VMEM((2, RAW, WIDTH + 2 * MARGIN), BF16),
                pltpu.VMEM((2, DEPTH, WIDTH), BF16),
                pltpu.VMEM((ROWS, WIDTH + 2 * MARGIN), F32),
                pltpu.VMEM((V * BLKC, ROWS, BLOCK), BF16),
                pltpu.SMEM((owner.shape[0],), jnp.int32),
                pltpu.SemaphoreType.DMA((V * BLKC,)),
            ],
        ),
        out_shape=jax.ShapeDtypeStruct((devices, CAP, ROWS, BLOCK), BF16),
        compiler_params=pltpu.CompilerParams(vmem_limit_bytes=32 << 20),
        cost_estimate=pl.CostEstimate(
            flops=V * 2 * 3 * 2 * MATCH * DEPTH * WIDTH,
            bytes_accessed=V * (BLOCK * WIDTH * 4 + ROWS * WIDTH * 2),
            transcendentals=0,
        ),
        name="match_warp_" + str(part),
    )(place, patch, owner, taps, psf, affine, images, rim)


def table_kernel(place, names, weights, owner, cell_out, weight_out, sum_out):
    devices = names.shape[0]
    me = place[4]

    def find(p, mine):
        return jnp.where(owner[p] == me, p, mine)

    mine = lax.fori_loop(0, owner.shape[0], find, 0)
    for c in range(CELLS):
        sum_out[c] = 0.0

    def source(s, _):
        cell_out[s * CAP] = -1
        cell_out[s * CAP + 1] = -1
        ccd = (s + SPLIT // 2) // SPLIT
        rank = 0
        for e in range(V * BLKC):
            name = names[s, e]
            hit = name // CELLS == mine

            @pl.when(hit)
            def _(rank=rank, name=name, e=e):
                cell = name % CELLS
                weight = weights[e // BLKC, ccd]
                cell_out[s * CAP + rank] = cell
                weight_out[s * CAP + rank] = weight
                sum_out[cell] += weight

            rank = rank + hit.astype(jnp.int32)
        return 0

    lax.fori_loop(0, devices, source, 0)


def table(place, names, weights, owner):
    smem = pl.BlockSpec(memory_space=pltpu.SMEM)
    devices = names.shape[0]
    return pl.pallas_call(
        table_kernel,
        in_specs=[smem] * 4,
        out_specs=[smem] * 3,
        out_shape=[
            jax.ShapeDtypeStruct((devices * CAP,), jnp.int32),
            jax.ShapeDtypeStruct((devices * CAP,), F32),
            jax.ShapeDtypeStruct((CELLS,), F32),
        ],
        name="contents",
    )(place, names, weights, owner)


def coadd_kernel(cell, weight, sums, got, *refs):
    out = refs[-1]
    out[...] = jnp.zeros_like(out)

    def add(k, _):
        c = cell[k]

        @pl.when(c >= 0)
        def _():
            r = c // PSIDE
            lanes = pl.ds(pl.multiple_of(c % PSIDE * BLOCK, BLOCK), BLOCK)
            out[r, 0, :, lanes] += weight[k] * got[k].astype(F32)

        return 0

    lax.fori_loop(0, got.shape[0], add, 0)
    for c in range(CELLS):
        lanes = slice(c % PSIDE * BLOCK, (c % PSIDE + 1) * BLOCK)
        total = jnp.maximum(jnp.full((1, BLOCK), sums[c], F32), 1.0)
        out[c // PSIDE, 0, :, lanes] = out[c // PSIDE, 0, :, lanes] / total


def coadd(part, cell, weight, sums, got, before):
    smem = pl.BlockSpec(memory_space=pltpu.SMEM)
    got = got.reshape(-1, ROWS, BLOCK)
    args = [cell, weight, sums, got]
    specs = [smem] * 3 + [pl.BlockSpec(got.shape, lambda i: (0, 0, 0))]
    alias = {}
    if before is not None:
        alias = {len(args): 0}
        args.append(before)
        specs.append(pl.BlockSpec(memory_space=pl.ANY))
    return pl.pallas_call(
        coadd_kernel,
        grid=(1,),
        in_specs=specs,
        out_specs=pl.BlockSpec((PSIDE, 1, ROWS, WIDTH), lambda i: (0, part, 0, 0)),
        out_shape=jax.ShapeDtypeStruct((PSIDE, PARTS, ROWS, PSIDE * BLOCK), F32),
        input_output_aliases=alias,
        compiler_params=pltpu.CompilerParams(vmem_limit_bytes=32 << 20),
        name="coadd_" + str(part),
    )(*args)


def shards(
    images, basis_taps, psf_coef, affine, visit_weight, block_patch, block_slot, patch_owner
):
    band = lax.axis_index("ccd")
    devices = lax.axis_size("ccd")
    shifted = band + SPLIT // 2
    quarter = shifted % SPLIT
    place = jnp.stack(
        [
            shifted // SPLIT,
            quarter * BLOCK,
            ((quarter > 0) & (band > 0)).astype(jnp.int32),
            ((quarter < SPLIT - 1) & (band < devices - 1)).astype(jnp.int32),
            band,
        ]
    ).astype(jnp.int32)
    down = [(i, i + 1) for i in range(devices - 1)]
    up = [(i + 1, i) for i in range(devices - 1)]
    above = lax.ppermute(images[:, BLOCK - RIM :], "ccd", down)
    below = lax.ppermute(images[:, :RIM], "ccd", up)
    patch = block_patch[:, :, 0]
    names = lax.all_gather(patch * CELLS + block_slot, "ccd", axis=0, tiled=True)
    cell, weight, sums = table(place, names, visit_weight.astype(F32), patch_owner)
    result = None
    sent = [
        warp(part, place, patch, patch_owner, basis_taps, psf_coef, affine, images, rim, devices)
        for part, rim in enumerate((above, below))
    ]
    for part, blocks in enumerate(sent):
        got = lax.all_to_all(blocks, "ccd", split_axis=0, concat_axis=0, tiled=True)
        result = coadd(part, cell, weight, sums, got, result)
    return result.reshape(1, PSIDE * BLOCK, PSIDE * BLOCK)


def solution(mesh):
    placed = (
        P(None, ("group", "ccd"), None),
        P(),
        P(None, "group", None, None),
        P(None, "group", None, None),
        P(None, "group"),
        P(("group", "ccd"), None, None),
        P(("group", "ccd"), None),
        P("group"),
    )
    return jax.shard_map(
        shards,
        mesh=mesh,
        in_specs=placed,
        out_specs=P(("group", "ccd"), None, None),
        check_vma=False,
    )
```

```python
import functools

import jax
import jax.numpy as jnp
from jax import lax
from jax.experimental import pallas as pl
from jax.experimental.pallas import tpu as pltpu
from jax.sharding import PartitionSpec as P

V = 4
BLOCK = 128
BLKC = 4
SPLIT = 4
TAPS = 11
NBASIS = 9
PSIDE = 4
CELLS = PSIDE * PSIDE
CAP = 2

HALF = TAPS // 2
WARP = 3
RIM = HALF + WARP
HEIGHT = SPLIT * BLOCK
WIDTH = BLKC * BLOCK
PARTS = 2
ROWS = BLOCK // PARTS
RAW = ROWS + 2 * RIM
MATCH = ROWS + 8
STRIP = 24
STEP = -(-(STRIP + TAPS - 1) // 8) * 8
BAND = -(-9 * STEP // 128) * 128
TALL = MATCH - STRIP + STEP
LABEL = 16
F32 = jnp.float32
BF16 = jnp.bfloat16


def sin_pi(t):
    whole = jnp.round(t)
    f = t - whole
    odd = whole - 2.0 * jnp.floor(0.5 * whole)
    f2 = f * f
    out = 0.0
    for c in (
        0.00046630280576761, -0.0073704309457144, 0.0821458866111282,
        -0.599264529320792, 2.55016403987734, -5.16771278004997, 3.14159265358979,
    ):
        out = out * f2 + c
    return f * out * (1.0 - 2.0 * odd)


def lanczos(t):
    zero = t == 0.0
    safe = jnp.where(zero, 1.0, t)
    pt = jnp.pi * safe
    value = 3.0 * sin_pi(safe) * sin_pi(safe / 3.0) / (pt * pt)
    return jnp.where(jnp.abs(t) < 3.0, jnp.where(zero, 1.0, value), 0.0)


def iota(shape, dim):
    return lax.broadcasted_iota(jnp.int32, shape, dim)


def rolled(x, shift):
    return x if shift == 0 else pltpu.roll(x, -shift % x.shape[1], 1)


def prepare_kernel(place, taps, psf, affine, bands_out, rows_out, cols_out, row_taps):
    visit = pl.program_id(0)
    lane = iota((1, BAND), 1)
    seg = lane // STEP
    tap = lane - seg * STEP

    @pl.when(visit == 0)
    def _():
        onehot = (tap == iota((TAPS, BAND), 0)) & (seg < 9)
        row_taps[...] = jnp.dot(
            taps[0], onehot.astype(F32),
            precision=lax.Precision.HIGHEST, preferred_element_type=F32,
        )

    p = psf[0, 0]
    r = row_taps[...]
    first = seg < 3
    term = jnp.where(first, p[:, 0:1], jnp.where(seg < 6, p[:, 1:2], p[:, 2:3]))
    row_move = jnp.where(first, (tap - HALF).astype(F32) * (2.0 / HEIGHT), 0.0)
    plain = r * (term - row_move * p[:, 1:2])
    moved = r * jnp.where(first, p[:, 2:3], 0.0)

    def over_bases(x):
        return lax.dot_general(
            taps[1], x, (((0,), (0,)), ((), ())),
            precision=lax.Precision.HIGHEST, preferred_element_type=F32,
        )

    col_move = (iota((TAPS, 1), 0) - HALF).astype(F32) * (2.0 / WIDTH)
    kernels = over_bases(plain) - col_move * over_bases(moved)
    low_lanes = seg % 3 == 2
    parts = []
    for u in range(TAPS):
        x = jnp.broadcast_to(kernels[u : u + 1], (8, BAND))
        x = pltpu.roll(x, 0, 1, stride=1, stride_axis=0)
        x = jnp.concatenate([x] + [pltpu.roll(x, 8 * k, 1) for k in range(1, STRIP // 8)], axis=0)
        high = x.astype(BF16).astype(F32)
        parts.append(jnp.where(low_lanes, x - high, high))
    bands_out[0] = jnp.concatenate(parts, axis=0).astype(BF16)

    a = affine[0, 0]
    out_row = iota((BLOCK, 128), 0)
    local = out_row % ROWS
    in_row = iota((BLOCK, 128), 1)
    row = (place[1] + out_row).astype(F32)
    shift = a[0:1, 0:1] + a[0:1, 1:2] * (row - (HEIGHT - 1) / 2.0) / HEIGHT
    step = in_row - local - WARP
    band_row = out_row + step
    keep = jnp.abs(step) <= WARP
    keep = keep & ((band_row >= 0) | (place[2] > 0)) & ((band_row < BLOCK) | (place[3] > 0))
    weights = jnp.where(keep, lanczos(shift - step.astype(F32)), 0.0)
    high = weights.astype(BF16).astype(F32)
    zero = jnp.zeros_like(weights)
    wide = jnp.concatenate([high, zero], axis=1)
    low = jnp.concatenate([weights - high, zero], axis=1)
    wide = wide + pltpu.roll(wide, MATCH, 1) + pltpu.roll(low, 2 * MATCH, 1)
    rows_out[0] = wide.astype(BF16)

    col = iota((8, WIDTH), 1)
    offset = iota((8, WIDTH), 0) - WARP
    col_shift = a[1:2, 0:1] + a[1:2, 1:2] * (col.astype(F32) - (WIDTH - 1) / 2.0) / WIDTH
    within = (col + offset >= 0) & (col + offset < WIDTH)
    cols_out[0] = jnp.where(within, lanczos(col_shift - offset.astype(F32)), 0.0)


def prepare(place, taps, psf, affine):
    return pl.pallas_call(
        prepare_kernel,
        grid_spec=pltpu.PrefetchScalarGridSpec(
            num_scalar_prefetch=1,
            grid=(V,),
            in_specs=[
                pl.BlockSpec((2, NBASIS, TAPS), lambda v, place: (0, 0, 0)),
                pl.BlockSpec((1, 1, NBASIS, 3), lambda v, place: (v, place[0], 0, 0)),
                pl.BlockSpec((1, 1, 2, 2), lambda v, place: (v, place[0], 0, 0)),
            ],
            out_specs=[
                pl.BlockSpec((1, TAPS * STRIP, BAND), lambda v, place: (v, 0, 0)),
                pl.BlockSpec((1, BLOCK, 256), lambda v, place: (v, 0, 0)),
                pl.BlockSpec((1, 8, WIDTH), lambda v, place: (v, 0, 0)),
            ],
            scratch_shapes=[pltpu.VMEM((NBASIS, BAND), F32)],
        ),
        out_shape=[
            jax.ShapeDtypeStruct((V, TAPS * STRIP, BAND), BF16),
            jax.ShapeDtypeStruct((V, BLOCK, 256), BF16),
            jax.ShapeDtypeStruct((V, 8, WIDTH), F32),
        ],
        compiler_params=pltpu.CompilerParams(vmem_limit_bytes=32 << 20),
        cost_estimate=pl.CostEstimate(flops=1 << 30, bytes_accessed=1 << 20, transcendentals=0),
        name="prepare",
    )(place, taps, psf, affine)


def warp_kernel(
    part,
    place, patch, slot, owner, weight, bands, row_weights, col_weights, image, rim, out,
    terms, ready, seen, sem, *extra,
):
    visit = pl.program_id(0)
    visits = pl.num_programs(0)
    top_row = place[1] + part * ROWS
    inside = place[2 + part]

    edge = jnp.where(inside > 0, rim[0], 0.0)
    empty = jnp.zeros((TALL - RAW, WIDTH), F32)
    if part == 0:
        raw = jnp.concatenate([edge, image[0, : ROWS + RIM], empty], axis=0)
    else:
        raw = jnp.concatenate([image[0, BLOCK - ROWS - RIM :], edge, empty], axis=0)
    raw_row = (top_row - RIM + iota((TALL, 1), 0)).astype(F32)
    row_pos = (2.0 * raw_row + 1.0) / HEIGHT - 1.0
    col_pos = (2.0 * iota((1, WIDTH), 1).astype(F32) + 1.0) / WIDTH - 1.0
    for c, value in enumerate((raw, raw * row_pos, raw * col_pos)):
        high = value.astype(BF16).astype(F32)
        terms[c, 0] = high
        terms[c, 1] = value - high

    lane = iota((1, 128), 1)
    strips = []
    for k in range(MATCH // STRIP):
        rows = slice(k * STRIP, k * STRIP + STEP)
        stack = [terms[c, h, rows] for c in range(3) for h in (0, 1, 0)]
        stack.append(jnp.zeros((BAND - 9 * STEP, WIDTH), F32))
        columns = jnp.concatenate(stack, axis=0).astype(BF16)
        taps = jnp.dot(bands[0], columns, preferred_element_type=F32)
        total = None
        for u in range(TAPS):
            move = u - HALF
            value = rolled(taps[u * STRIP : (u + 1) * STRIP], move)
            if move < 0:
                head = jnp.where(lane >= -move, value[:, :128], 0.0)
                value = jnp.concatenate([head, value[:, 128:]], axis=1)
            if move > 0:
                tail = jnp.where(lane < 128 - move, value[:, WIDTH - 128 :], 0.0)
                value = jnp.concatenate([value[:, : WIDTH - 128], tail], axis=1)
            total = value if total is None else total + value
        strips.append(total)
    matched = jnp.concatenate(strips, axis=0)

    high = matched.astype(BF16).astype(F32)
    columns = jnp.concatenate(
        [high, matched - high, high, jnp.zeros((256 - 3 * MATCH, WIDTH), F32)], axis=0
    ).astype(BF16)
    warped = jnp.dot(row_weights[0], columns, preferred_element_type=F32)

    col = col_weights[0]
    total = None
    for s in range(2 * WARP + 1):
        value = col[s : s + 1] * rolled(warped, s - WARP)
        total = value if total is None else total + value
    result = total.astype(BF16)

    @pl.when(visit == 0)
    def _():
        def clear(p, _):
            seen[p] = 0
            return 0

        lax.fori_loop(0, owner.shape[0], clear, 0)
        if extra:
            extra[0][...] = jnp.zeros_like(extra[0])

    for j in range(BLKC):
        block = visit * BLKC + j
        ready[block] = result[:, j * BLOCK : (j + 1) * BLOCK]
        p = patch[0, block]
        rank = seen[p]
        seen[p] = rank + 1
        to = out.at[owner[p], pl.ds(pl.multiple_of(rank * ROWS, ROWS), ROWS)]
        pltpu.make_async_copy(ready.at[block], to, sem.at[block]).start()
        if extra:
            label = extra[0]
            at = rank * 2
            label[owner[p], pl.ds(at, 1), :] = jnp.full((1, BLOCK), weight[visit, place[0]], F32)
            label[owner[p], pl.ds(at + 1, 1), :] = jnp.full((1, BLOCK), slot[0, block].astype(F32), F32)

    @pl.when(visit == visits - 1)
    def _():
        if extra:
            label, label_ready, label_sem = extra
            label_ready[...] = label[...].astype(BF16)
            copy = pltpu.make_async_copy(
                label_ready, out.at[:, pl.ds(CAP * ROWS, LABEL)], label_sem
            )
            copy.start()
            copy.wait()
        for block in range(V * BLKC):
            pltpu.make_async_copy(ready.at[block], out.at[0, pl.ds(0, ROWS)], sem.at[block]).wait()


def warp(part, place, patch, slot, owner, weight, ready, images, rim, devices):
    smem = pl.BlockSpec(memory_space=pltpu.SMEM)
    rows = CAP * ROWS
    scratch = [
        pltpu.VMEM((3, 2, TALL, WIDTH), F32),
        pltpu.VMEM((V * BLKC, ROWS, BLOCK), BF16),
        pltpu.SMEM((owner.shape[0],), jnp.int32),
        pltpu.SemaphoreType.DMA((V * BLKC,)),
    ]
    if part == 0:
        rows += LABEL
        scratch += [
            pltpu.VMEM((devices, LABEL, BLOCK), F32),
            pltpu.VMEM((devices, LABEL, BLOCK), BF16),
            pltpu.SemaphoreType.DMA(()),
        ]
    return pl.pallas_call(
        functools.partial(warp_kernel, part),
        grid_spec=pltpu.PrefetchScalarGridSpec(
            num_scalar_prefetch=1,
            grid=(V,),
            in_specs=[
                smem,
                smem,
                smem,
                smem,
                pl.BlockSpec((1, TAPS * STRIP, BAND), lambda v, place: (v, 0, 0)),
                pl.BlockSpec((1, ROWS, 256), lambda v, place: (v, part, 0)),
                pl.BlockSpec((1, 8, WIDTH), lambda v, place: (v, 0, 0)),
                pl.BlockSpec((1, BLOCK, WIDTH), lambda v, place: (v, 0, 0)),
                pl.BlockSpec((1, RIM, WIDTH), lambda v, place: (v, 0, 0)),
            ],
            out_specs=pl.BlockSpec(memory_space=pl.ANY),
            scratch_shapes=scratch,
        ),
        out_shape=jax.ShapeDtypeStruct((devices, rows, BLOCK), BF16),
        compiler_params=pltpu.CompilerParams(vmem_limit_bytes=32 << 20),
        cost_estimate=pl.CostEstimate(
            flops=V * 2 * 2 * MATCH * TAPS * BAND * WIDTH,
            bytes_accessed=V * (BLOCK * WIDTH * 4 + ROWS * WIDTH * 2),
            transcendentals=0,
        ),
        name="match_warp_" + str(part),
    )(place, patch, slot, owner, weight, *ready, images, rim)


def coadd_kernel(labels, got, *refs):
    out, sums = refs[-2:]
    out[...] = jnp.zeros_like(out)
    for c in range(CELLS):
        sums[c] = 0.0

    def add(k, _):
        source, rank = k // CAP, k % CAP
        weight = labels[source, rank * 2]

        @pl.when(weight > 0.0)
        def _():
            c = labels[source, rank * 2 + 1].astype(jnp.int32)
            sums[c] += weight
            lanes = pl.ds(pl.multiple_of(c % PSIDE * BLOCK, BLOCK), BLOCK)
            rows = pl.ds(pl.multiple_of(rank * ROWS, ROWS), ROWS)
            out[c // PSIDE, 0, :, lanes] += weight * got[source, rows].astype(F32)

        return 0

    lax.fori_loop(0, got.shape[0] * CAP, add, 0)
    for c in range(CELLS):
        lanes = slice(c % PSIDE * BLOCK, (c % PSIDE + 1) * BLOCK)
        total = jnp.maximum(jnp.full((1, BLOCK), sums[c], F32), 1.0)
        out[c // PSIDE, 0, :, lanes] = out[c // PSIDE, 0, :, lanes] / total


def coadd(part, labels, got, before):
    smem = pl.BlockSpec(memory_space=pltpu.SMEM)
    args = [labels, got]
    specs = [smem, pl.BlockSpec((got.shape[0], CAP * ROWS, BLOCK), lambda i: (0, 0, 0))]
    alias = {}
    if before is not None:
        alias = {len(args): 0}
        args.append(before)
        specs.append(pl.BlockSpec(memory_space=pl.ANY))
    return pl.pallas_call(
        coadd_kernel,
        grid=(1,),
        in_specs=specs,
        out_specs=pl.BlockSpec((PSIDE, 1, ROWS, WIDTH), lambda i: (0, part, 0, 0)),
        out_shape=jax.ShapeDtypeStruct((PSIDE, PARTS, ROWS, PSIDE * BLOCK), F32),
        scratch_shapes=[pltpu.SMEM((CELLS,), F32)],
        input_output_aliases=alias,
        compiler_params=pltpu.CompilerParams(vmem_limit_bytes=32 << 20),
        name="coadd_" + str(part),
    )(*args)


def shards(
    images, basis_taps, psf_coef, affine, visit_weight, block_patch, block_slot, patch_owner
):
    band = lax.axis_index("ccd")
    devices = lax.axis_size("ccd")
    shifted = band + SPLIT // 2
    quarter = shifted % SPLIT
    place = jnp.stack(
        [
            shifted // SPLIT,
            quarter * BLOCK,
            ((quarter > 0) & (band > 0)).astype(jnp.int32),
            ((quarter < SPLIT - 1) & (band < devices - 1)).astype(jnp.int32),
            band,
        ]
    ).astype(jnp.int32)
    down = [(i, i + 1) for i in range(devices - 1)]
    up = [(i + 1, i) for i in range(devices - 1)]
    above = lax.ppermute(images[:, BLOCK - RIM :], "ccd", down)
    below = lax.ppermute(images[:, :RIM], "ccd", up)
    patch = block_patch[:, :, 0]
    weight = visit_weight.astype(F32)
    ready = prepare(place, basis_taps, psf_coef, affine)
    sent = [
        warp(part, place, patch, block_slot, patch_owner, weight, ready, images, rim, devices)
        for part, rim in enumerate((above, below))
    ]
    result = labels = None
    for part, blocks in enumerate(sent):
        got = lax.all_to_all(blocks, "ccd", split_axis=0, concat_axis=0, tiled=True)
        if part == 0:
            labels = got[:, CAP * ROWS : CAP * ROWS + 2 * CAP, 0].astype(F32)
        result = coadd(part, labels, got, result)
    return result.reshape(1, PSIDE * BLOCK, PSIDE * BLOCK)


def solution(mesh):
    placed = (
        P(None, ("group", "ccd"), None),
        P(),
        P(None, "group", None, None),
        P(None, "group", None, None),
        P(None, "group"),
        P(("group", "ccd"), None, None),
        P(("group", "ccd"), None),
        P("group"),
    )
    return jax.shard_map(
        shards,
        mesh=mesh,
        in_specs=placed,
        out_specs=P(("group", "ccd"), None, None),
        check_vma=False,
    )
```

```python
import jax
import jax.numpy as jnp
import numpy as np
from jax import lax
from jax.experimental import pallas as pl
from jax.experimental.pallas import tpu as pltpu
from jax.sharding import PartitionSpec as P

V = 4
BLOCK = 128
BLKC = 4
SPLIT = 4
TAPS = 11
NBASIS = 9
PSIDE = 4
CELLS = PSIDE * PSIDE
CAP = 2

HALF = TAPS // 2
WARP = 3
RIM = HALF + WARP
HEIGHT = SPLIT * BLOCK
WIDTH = BLKC * BLOCK
LANES = 128
LANE_BLOCKS = WIDTH // LANES
STRIP = 16
STEP = 32
STRIPS = -(-(BLOCK + 2 * WARP) // STRIP)
GROUPS = 6
BAND = 256
TALL = (STRIPS - 1) * STRIP + STEP
HALVES = 2
ROWS = BLOCK // HALVES
MATCH = ROWS + 8
LABEL = 16
F32 = jnp.float32
BF16 = jnp.bfloat16


def sin_pi(t):
    whole = jnp.round(t)
    f = t - whole
    odd = whole - 2.0 * jnp.floor(0.5 * whole)
    f2 = f * f
    out = 0.0
    for c in (
        0.00046630280576761, -0.0073704309457144, 0.0821458866111282,
        -0.599264529320792, 2.55016403987734, -5.16771278004997, 3.14159265358979,
    ):
        out = out * f2 + c
    return f * out * (1.0 - 2.0 * odd)


def lanczos(t):
    zero = t == 0.0
    safe = jnp.where(zero, 1.0, t)
    pt = jnp.pi * safe
    value = 3.0 * sin_pi(safe) * sin_pi(safe / 3.0) / (pt * pt)
    return jnp.where(jnp.abs(t) < 3.0, jnp.where(zero, 1.0, value), 0.0)


def iota(shape, dim):
    return lax.broadcasted_iota(jnp.int32, shape, dim)


def deinterleave():
    order = np.arange(WIDTH).reshape(LANES, LANE_BLOCKS).T.reshape(-1)
    return (np.arange(WIDTH)[:, None] == order[None, :]).astype(np.float32)


def column_at(lane):
    return lane % LANES * LANE_BLOCKS + lane // LANES


def prepare_kernel(place, taps, psf, affine, level_out, slope_out, rows_out, cols_out):
    lane = iota((1, BAND), 1)
    seg = lane // STEP
    tap = lane - seg * STEP
    row_taps, col_taps = taps[:, 0], taps[:, 1]
    onehot = (tap == iota((TAPS, BAND), 0)) & (seg < GROUPS)
    r = jnp.dot(
        row_taps, onehot.astype(F32),
        precision=lax.Precision.HIGHEST, preferred_element_type=F32,
    )
    is_level = seg < 3
    low_lanes = seg % 3 == 2
    ccd_lane = iota((1, 1, affine.shape[3]), 2) == place[0]

    turned = lax.dot_general(
        (iota((TAPS, STRIP), 0) == iota((TAPS, STRIP), 1)).astype(F32), col_taps,
        (((0,), (1,)), ((), ())),
        precision=lax.Precision.HIGHEST, preferred_element_type=F32,
    )
    kernels = jnp.dot(
        jnp.concatenate(
            [turned * psf[0, c, v : v + 1, :] for v in range(V) for c in range(3)], axis=0
        ),
        r, precision=lax.Precision.HIGHEST, preferred_element_type=F32,
    )

    col_move = (iota((STRIP, 1), 0) - HALF).astype(F32) * (2.0 / WIDTH)
    for visit in range(V):
        const, by_row, by_col = (
            kernels[(visit * 3 + c) * STRIP : (visit * 3 + c + 1) * STRIP] for c in range(3)
        )
        const = jnp.where(is_level, const - col_move * by_col, by_col)
        by_row = jnp.where(is_level, by_row, 0.0)
        for u in range(TAPS):
            x = jnp.broadcast_to(const[u : u + 1], (8, BAND))
            x = pltpu.roll(x, 0, 1, stride=1, stride_axis=0)
            x = jnp.concatenate([x, pltpu.roll(x, 8, 1)], axis=0)
            y = jnp.broadcast_to(by_row[u : u + 1, :LANES], (8, LANES))
            y = pltpu.roll(y, 0, 1, stride=1, stride_axis=0)
            y = jnp.concatenate([y, pltpu.roll(y, 8, 1)], axis=0)
            at = slice(u * STRIP, (u + 1) * STRIP)
            level_out[visit, 0, at] = x[:, :LANES]
            level_out[visit, 1, at] = y
            high = x.astype(BF16).astype(F32)
            slope_out[visit, at] = jnp.where(low_lanes, x - high, high)[:, LANES:].astype(BF16)

        a = jnp.sum(jnp.where(ccd_lane, affine[visit], 0.0), axis=2, keepdims=True)
        out_row = iota((BLOCK, LANES), 0)
        local = out_row % ROWS
        in_row = iota((BLOCK, LANES), 1)
        row = (place[1] + out_row).astype(F32)
        shift = a[0, 0:1] + a[0, 1:2] * (row - (HEIGHT - 1) / 2.0) / HEIGHT
        step = in_row - local - WARP
        band_row = out_row + step
        keep = jnp.abs(step) <= WARP
        keep = keep & ((band_row >= 0) | (place[2] > 0)) & ((band_row < BLOCK) | (place[3] > 0))
        weights = jnp.where(keep, lanczos(shift - step.astype(F32)), 0.0)
        high = weights.astype(BF16).astype(F32)
        zero = jnp.zeros_like(weights)
        wide = jnp.concatenate([high, zero], axis=1)
        low = jnp.concatenate([weights - high, zero], axis=1)
        wide = wide + pltpu.roll(wide, MATCH, 1) + pltpu.roll(low, 2 * MATCH, 1)
        rows_out[visit] = wide.astype(BF16)

        lanes = iota((8, WIDTH), 1)
        offset = iota((8, WIDTH), 0) - WARP
        block = lanes // LANES
        carry = (block + offset + LANE_BLOCKS) // LANE_BLOCKS - 1
        from_lane = lanes % LANES - carry
        col = (from_lane * LANE_BLOCKS + block).astype(F32)
        col_shift = a[1, 0:1] + a[1, 1:2] * (col - (WIDTH - 1) / 2.0) / WIDTH
        within = (from_lane >= 0) & (from_lane < LANES) & (offset <= WARP)
        cols_out[visit] = jnp.where(within, lanczos(col_shift - offset.astype(F32)), 0.0)


def prepare(place, taps, psf, affine):
    ccds = affine.shape[1]
    return pl.pallas_call(
        prepare_kernel,
        grid_spec=pltpu.PrefetchScalarGridSpec(
            num_scalar_prefetch=1,
            grid=(1,),
            in_specs=[
                pl.BlockSpec((NBASIS, 2, TAPS), lambda i, place: (0, 0, 0)),
                pl.BlockSpec((1, 3, V, NBASIS), lambda i, place: (place[0], 0, 0, 0)),
                pl.BlockSpec((V, 2, 2, ccds), lambda i, place: (0, 0, 0, 0)),
            ],
            out_specs=[
                pl.BlockSpec((V, 2, TAPS * STRIP, LANES), lambda i, place: (0, 0, 0, 0)),
                pl.BlockSpec((V, TAPS * STRIP, BAND - LANES), lambda i, place: (0, 0, 0)),
                pl.BlockSpec((V, BLOCK, 256), lambda i, place: (0, 0, 0)),
                pl.BlockSpec((V, 8, WIDTH), lambda i, place: (0, 0, 0)),
            ],
        ),
        out_shape=[
            jax.ShapeDtypeStruct((V, 2, TAPS * STRIP, LANES), F32),
            jax.ShapeDtypeStruct((V, TAPS * STRIP, BAND - LANES), BF16),
            jax.ShapeDtypeStruct((V, BLOCK, 256), BF16),
            jax.ShapeDtypeStruct((V, 8, WIDTH), F32),
        ],
        compiler_params=pltpu.CompilerParams(vmem_limit_bytes=32 << 20),
        cost_estimate=pl.CostEstimate(flops=1 << 30, bytes_accessed=1 << 20, transcendentals=0),
        name="prepare",
    )(place, taps.transpose(1, 0, 2), psf.transpose(1, 3, 0, 2), affine.transpose(0, 2, 3, 1))


def lane_block(x, v):
    return x[:, v * LANES : (v + 1) * LANES]


def warp_kernel(
    place, patch, slot, owner, weight, level, slope, row_weights, col_weights, sort, unsort,
    image, above, below, out,
    terms, ready, seen, label, label_ready, sem, label_sem,
):
    visit = pl.program_id(0)
    visits = pl.num_programs(0)
    top_row = place[1]

    @pl.when(visit == 0)
    def _():
        terms[:, BLOCK + 2 * RIM :] = jnp.zeros((4, TALL - BLOCK - 2 * RIM, WIDTH), BF16)

    raw = jnp.concatenate(
        [jnp.where(place[2] > 0, above[0], 0.0), image[0], jnp.where(place[3] > 0, below[0], 0.0)],
        axis=0,
    )
    raw_high = raw.astype(BF16)
    raw_low = (raw - raw_high.astype(F32)).astype(BF16)
    tall = BLOCK + 2 * RIM
    sorted_terms = jnp.dot(
        jnp.concatenate([raw_high, raw_low], axis=0), sort[...], preferred_element_type=F32
    )
    high, low = sorted_terms[:tall], sorted_terms[tall:]
    col_pos = (2.0 * column_at(iota((1, WIDTH), 1)).astype(F32) + 1.0) / WIDTH - 1.0
    tilted = (high + low) * col_pos
    tilted_high = tilted.astype(BF16)
    terms[0, :tall] = high.astype(BF16)
    terms[1, :tall] = low.astype(BF16)
    terms[2, :tall] = tilted_high
    terms[3, :tall] = (tilted - tilted_high.astype(F32)).astype(BF16)

    lane = iota((1, LANES), 1)
    low_lanes = (lane // STEP) % 3 == 2
    level_lanes = lane < 3 * STEP
    strip_row = (iota((TAPS * STRIP, 1), 0) % STRIP).astype(F32)
    filler = jnp.zeros((BAND - GROUPS * STEP, WIDTH), BF16)
    strips = []
    for k in range(STRIPS):
        match_row = (top_row + (k * STRIP - WARP)).astype(F32) + strip_row
        row_pos = (2.0 * match_row + 1.0) / HEIGHT - 1.0
        x = level[0, 0] + row_pos * level[0, 1]
        x = jnp.where(low_lanes, x - x.astype(BF16).astype(F32), x)
        matrix = jnp.concatenate([x.astype(BF16), slope[0]], axis=1)
        rows = slice(k * STRIP, k * STRIP + STEP)
        columns = jnp.concatenate(
            [terms[h, rows] for h in (0, 1, 0, 2, 3, 2)] + [filler], axis=0
        )
        taps = jnp.dot(matrix, columns, preferred_element_type=F32)
        out_blocks = []
        for v in range(LANE_BLOCKS):
            total = None
            for q in range(-(HALF // LANE_BLOCKS) - 1, HALF // LANE_BLOCKS + 2):
                part = None
                for u in range(TAPS):
                    if (v + u - HALF) // LANE_BLOCKS != q:
                        continue
                    w = (v + u - HALF) % LANE_BLOCKS
                    piece = lane_block(taps[u * STRIP : (u + 1) * STRIP], w)
                    part = piece if part is None else part + piece
                if part is None:
                    continue
                if q:
                    part = pltpu.roll(part, -q % LANES, 1)
                    part = jnp.where((lane + q >= 0) & (lane + q < LANES), part, 0.0)
                total = part if total is None else total + part
            out_blocks.append(total)
        strips.append(jnp.concatenate(out_blocks, axis=1))
    matched = jnp.concatenate(strips, axis=0)

    high = matched.astype(BF16).astype(F32)
    low = matched - high
    empty = jnp.zeros((256 - 3 * MATCH, WIDTH), F32)
    halves = []
    for h in range(HALVES):
        rows = slice(h * ROWS, h * ROWS + MATCH)
        columns = jnp.concatenate([high[rows], low[rows], high[rows], empty], axis=0).astype(BF16)
        halves.append(
            jnp.dot(
                row_weights[0, h * ROWS : (h + 1) * ROWS], columns, preferred_element_type=F32
            )
        )
    warped = jnp.concatenate(halves, axis=0)
    col = col_weights[0]
    out_blocks = []
    for v in range(LANE_BLOCKS):
        total = None
        for q in (-1, 0, 1):
            part = None
            for s in range(2 * WARP + 1):
                if (v + s - WARP) // LANE_BLOCKS != q:
                    continue
                w = (v + s - WARP) % LANE_BLOCKS
                piece = lane_block(col[s : s + 1], v) * lane_block(warped, w)
                part = piece if part is None else part + piece
            if part is None:
                continue
            if q:
                part = pltpu.roll(part, -q % LANES, 1)
            total = part if total is None else total + part
        out_blocks.append(total.astype(BF16))
    result = jnp.dot(
        jnp.concatenate(out_blocks, axis=1), unsort[...], preferred_element_type=F32
    ).astype(BF16)

    @pl.when(visit == 0)
    def _():
        def clear(p, _):
            seen[p] = 0
            return 0

        lax.fori_loop(0, owner.shape[0], clear, 0)
        label[...] = jnp.zeros_like(label)

    for j in range(BLKC):
        block = visit * BLKC + j
        ready[block] = result[:, j * BLOCK : (j + 1) * BLOCK]
        p = patch[0, block]
        rank = seen[p]
        seen[p] = rank + 1
        to = out.at[owner[p], pl.ds(pl.multiple_of(rank * BLOCK, BLOCK), BLOCK)]
        pltpu.make_async_copy(ready.at[block], to, sem.at[block]).start()
        at = rank * 2
        label[owner[p], pl.ds(at, 1), :] = jnp.full((1, BLOCK), weight[visit, place[0]], F32)
        label[owner[p], pl.ds(at + 1, 1), :] = jnp.full((1, BLOCK), slot[0, block].astype(F32), F32)

    @pl.when(visit == visits - 1)
    def _():
        label_ready[...] = label[...].astype(BF16)
        copy = pltpu.make_async_copy(label_ready, out.at[:, pl.ds(CAP * BLOCK, LABEL)], label_sem)
        copy.start()
        copy.wait()
        for block in range(V * BLKC):
            pltpu.make_async_copy(ready.at[block], out.at[0, pl.ds(0, BLOCK)], sem.at[block]).wait()


def warp(place, patch, slot, owner, weight, ready, images, above, below, devices):
    smem = pl.BlockSpec(memory_space=pltpu.SMEM)
    sort = deinterleave()
    whole = pl.BlockSpec((WIDTH, WIDTH), lambda v, place: (0, 0))
    return pl.pallas_call(
        warp_kernel,
        grid_spec=pltpu.PrefetchScalarGridSpec(
            num_scalar_prefetch=1,
            grid=(V,),
            in_specs=[
                smem,
                smem,
                smem,
                smem,
                pl.BlockSpec((1, 2, TAPS * STRIP, LANES), lambda v, place: (v, 0, 0, 0)),
                pl.BlockSpec((1, TAPS * STRIP, BAND - LANES), lambda v, place: (v, 0, 0)),
                pl.BlockSpec((1, BLOCK, 256), lambda v, place: (v, 0, 0)),
                pl.BlockSpec((1, 8, WIDTH), lambda v, place: (v, 0, 0)),
                whole,
                whole,
                pl.BlockSpec((1, BLOCK, WIDTH), lambda v, place: (v, 0, 0)),
                pl.BlockSpec((1, RIM, WIDTH), lambda v, place: (v, 0, 0)),
                pl.BlockSpec((1, RIM, WIDTH), lambda v, place: (v, 0, 0)),
            ],
            out_specs=pl.BlockSpec(memory_space=pl.ANY),
            scratch_shapes=[
                pltpu.VMEM((4, TALL, WIDTH), BF16),
                pltpu.VMEM((V * BLKC, BLOCK, BLOCK), BF16),
                pltpu.SMEM((owner.shape[0],), jnp.int32),
                pltpu.VMEM((devices, LABEL, BLOCK), F32),
                pltpu.VMEM((devices, LABEL, BLOCK), BF16),
                pltpu.SemaphoreType.DMA((V * BLKC,)),
                pltpu.SemaphoreType.DMA(()),
            ],
        ),
        out_shape=jax.ShapeDtypeStruct((devices, CAP * BLOCK + LABEL, BLOCK), BF16),
        compiler_params=pltpu.CompilerParams(vmem_limit_bytes=32 << 20),
        cost_estimate=pl.CostEstimate(
            flops=V * 2 * STRIPS * TAPS * STRIP * BAND * WIDTH,
            bytes_accessed=V * (BLOCK * WIDTH * 6),
            transcendentals=0,
        ),
        name="match_warp",
    )(
        place, patch, slot, owner, weight, *ready,
        jnp.asarray(sort, BF16), jnp.asarray(sort.T, BF16), images, above, below,
    )


def coadd_kernel(labels, got, out, sums):
    out[...] = jnp.zeros_like(out)
    for c in range(CELLS):
        sums[c] = 0.0

    def add(k, _):
        source, rank = k // CAP, k % CAP
        weight = labels[source, rank * 2]

        @pl.when(weight > 0.0)
        def _():
            c = labels[source, rank * 2 + 1].astype(jnp.int32)
            sums[c] += weight
            lanes = pl.ds(pl.multiple_of(c % PSIDE * BLOCK, BLOCK), BLOCK)
            rows = pl.ds(pl.multiple_of(rank * BLOCK, BLOCK), BLOCK)
            out[c // PSIDE, :, lanes] += weight * got[source, rows].astype(F32)

        return 0

    lax.fori_loop(0, got.shape[0] * CAP, add, 0)
    for c in range(CELLS):
        lanes = slice(c % PSIDE * BLOCK, (c % PSIDE + 1) * BLOCK)
        inverse = 1.0 / jnp.maximum(jnp.full((1, BLOCK), sums[c], F32), 1.0)
        out[c // PSIDE, :, lanes] = out[c // PSIDE, :, lanes] * inverse


def coadd(labels, got):
    smem = pl.BlockSpec(memory_space=pltpu.SMEM)
    return pl.pallas_call(
        coadd_kernel,
        grid=(1,),
        in_specs=[smem, pl.BlockSpec((got.shape[0], CAP * BLOCK, BLOCK), lambda i: (0, 0, 0))],
        out_specs=pl.BlockSpec((PSIDE, BLOCK, WIDTH), lambda i: (0, 0, 0)),
        out_shape=jax.ShapeDtypeStruct((PSIDE, BLOCK, PSIDE * BLOCK), F32),
        scratch_shapes=[pltpu.SMEM((CELLS,), F32)],
        compiler_params=pltpu.CompilerParams(vmem_limit_bytes=32 << 20),
        name="coadd",
    )(labels, got)


def shards(
    images, basis_taps, psf_coef, affine, visit_weight, block_patch, block_slot, patch_owner
):
    band = lax.axis_index("ccd")
    devices = lax.axis_size("ccd")
    shifted = band + SPLIT // 2
    quarter = shifted % SPLIT
    place = jnp.stack(
        [
            shifted // SPLIT,
            quarter * BLOCK,
            ((quarter > 0) & (band > 0)).astype(jnp.int32),
            ((quarter < SPLIT - 1) & (band < devices - 1)).astype(jnp.int32),
            band,
        ]
    ).astype(jnp.int32)
    down = [(i, i + 1) for i in range(devices - 1)]
    up = [(i + 1, i) for i in range(devices - 1)]
    above = lax.ppermute(images[:, BLOCK - RIM :], "ccd", down)
    below = lax.ppermute(images[:, :RIM], "ccd", up)
    patch = block_patch[:, :, 0]
    weight = visit_weight.astype(F32)
    ready = prepare(place, basis_taps, psf_coef, affine)
    sent = warp(
        place, patch, block_slot, patch_owner, weight, ready, images, above, below, devices
    )
    got = lax.all_to_all(sent, "ccd", split_axis=0, concat_axis=0, tiled=True)
    labels = got[:, CAP * BLOCK : CAP * BLOCK + 2 * CAP, 0].astype(F32)
    result = coadd(labels, got)
    return result.reshape(1, PSIDE * BLOCK, PSIDE * BLOCK)


def solution(mesh):
    placed = (
        P(None, ("group", "ccd"), None),
        P(),
        P(None, "group", None, None),
        P(None, "group", None, None),
        P(None, "group"),
        P(("group", "ccd"), None, None),
        P(("group", "ccd"), None),
        P("group"),
    )
    return jax.shard_map(
        shards,
        mesh=mesh,
        in_specs=placed,
        out_specs=P(("group", "ccd"), None, None),
        check_vma=False,
    )
```

```python
import jax
import jax.numpy as jnp
import numpy as np
from jax import lax
from jax.experimental import pallas as pl
from jax.experimental.pallas import tpu as pltpu
from jax.sharding import PartitionSpec as P

V = 4
BLOCK = 128
BLKC = 4
SPLIT = 4
TAPS = 11
NBASIS = 9
PSIDE = 4
CELLS = PSIDE * PSIDE

HALF = TAPS // 2
WARP = 3
RIM = HALF + WARP
HEIGHT = SPLIT * BLOCK
WIDTH = BLKC * BLOCK
LANES = 128
LANE_BLOCKS = WIDTH // LANES
STRIP = 16
STEP = 32
STRIPS = -(-(BLOCK + 2 * WARP) // STRIP)
GROUPS = 6
BAND = 256
TALL = (STRIPS - 1) * STRIP + STEP
HALVES = 2
ROWS = BLOCK // HALVES
MATCH = ROWS + 8
SHARED = 2
LABEL = 16
F32 = jnp.float32
BF16 = jnp.bfloat16


def sin_pi(t):
    whole = jnp.round(t)
    f = t - whole
    odd = whole - 2.0 * jnp.floor(0.5 * whole)
    f2 = f * f
    out = 0.0
    for c in (
        0.00046630280576761, -0.0073704309457144, 0.0821458866111282,
        -0.599264529320792, 2.55016403987734, -5.16771278004997, 3.14159265358979,
    ):
        out = out * f2 + c
    return f * out * (1.0 - 2.0 * odd)


def lanczos(t):
    zero = t == 0.0
    safe = jnp.where(zero, 1.0, t)
    pt = jnp.pi * safe
    value = 3.0 * sin_pi(safe) * sin_pi(safe / 3.0) / (pt * pt)
    return jnp.where(jnp.abs(t) < 3.0, jnp.where(zero, 1.0, value), 0.0)


def iota(shape, dim):
    return lax.broadcasted_iota(jnp.int32, shape, dim)


def deinterleave():
    order = np.arange(WIDTH).reshape(LANES, LANE_BLOCKS).T.reshape(-1)
    return (np.arange(WIDTH)[:, None] == order[None, :]).astype(np.float32)


def column_at(lane):
    return lane % LANES * LANE_BLOCKS + lane // LANES


def prepare_kernel(
    place, taps_in, psf_in, affine_in, level_out, slope_out, rows_out, cols_out,
    taps, psf, affine, sems,
):
    copies = [
        pltpu.make_async_copy(taps_in, taps, sems.at[0]),
        pltpu.make_async_copy(psf_in.at[pl.ds(place[0], 1)], psf, sems.at[1]),
        pltpu.make_async_copy(affine_in, affine, sems.at[2]),
    ]
    for copy in copies:
        copy.start()
    for copy in copies:
        copy.wait()
    lane = iota((1, BAND), 1)
    seg = lane // STEP
    tap = lane - seg * STEP
    row_taps, col_taps = taps[:, 0], taps[:, 1]
    onehot = (tap == iota((TAPS, BAND), 0)) & (seg < GROUPS)
    r = jnp.dot(
        row_taps, onehot.astype(F32),
        precision=lax.Precision.HIGHEST, preferred_element_type=F32,
    )
    is_level = seg < 3
    low_lanes = seg % 3 == 2
    ccd_lane = iota((1, 1, affine.shape[3]), 2) == place[0]

    turned = lax.dot_general(
        (iota((TAPS, STRIP), 0) == iota((TAPS, STRIP), 1)).astype(F32), col_taps,
        (((0,), (1,)), ((), ())),
        precision=lax.Precision.HIGHEST, preferred_element_type=F32,
    )
    kernels = jnp.dot(
        jnp.concatenate(
            [turned * psf[0, c, v : v + 1, :] for v in range(V) for c in range(3)], axis=0
        ),
        r, precision=lax.Precision.HIGHEST, preferred_element_type=F32,
    )

    col_move = (iota((STRIP, 1), 0) - HALF).astype(F32) * (2.0 / WIDTH)
    for visit in range(V):
        const, by_row, by_col = (
            kernels[(visit * 3 + c) * STRIP : (visit * 3 + c + 1) * STRIP] for c in range(3)
        )
        const = jnp.where(is_level, const - col_move * by_col, by_col)
        by_row = jnp.where(is_level, by_row, 0.0)
        for u in range(TAPS):
            x = jnp.broadcast_to(const[u : u + 1], (8, BAND))
            x = pltpu.roll(x, 0, 1, stride=1, stride_axis=0)
            x = jnp.concatenate([x, pltpu.roll(x, 8, 1)], axis=0)
            y = jnp.broadcast_to(by_row[u : u + 1, :LANES], (8, LANES))
            y = pltpu.roll(y, 0, 1, stride=1, stride_axis=0)
            y = jnp.concatenate([y, pltpu.roll(y, 8, 1)], axis=0)
            at = slice(u * STRIP, (u + 1) * STRIP)
            level_out[visit, 0, at] = x[:, :LANES]
            level_out[visit, 1, at] = y
            high = x.astype(BF16).astype(F32)
            slope_out[visit, at] = jnp.where(low_lanes, x - high, high)[:, LANES:].astype(BF16)

        a = jnp.sum(jnp.where(ccd_lane, affine[visit], 0.0), axis=2, keepdims=True)
        out_row = iota((BLOCK, LANES), 0)
        local = out_row % ROWS
        in_row = iota((BLOCK, LANES), 1)
        row = (place[1] + out_row).astype(F32)
        shift = a[0, 0:1] + a[0, 1:2] * (row - (HEIGHT - 1) / 2.0) / HEIGHT
        step = in_row - local - WARP
        band_row = out_row + step
        keep = jnp.abs(step) <= WARP
        keep = keep & ((band_row >= 0) | (place[2] > 0)) & ((band_row < BLOCK) | (place[3] > 0))
        weights = jnp.where(keep, lanczos(shift - step.astype(F32)), 0.0)
        high = weights.astype(BF16).astype(F32)
        zero = jnp.zeros_like(weights)
        wide = jnp.concatenate([high, zero], axis=1)
        low = jnp.concatenate([weights - high, zero], axis=1)
        wide = wide + pltpu.roll(wide, MATCH, 1) + pltpu.roll(low, 2 * MATCH, 1)
        rows_out[visit] = wide.astype(BF16)

        lanes = iota((8, WIDTH), 1)
        offset = iota((8, WIDTH), 0) - WARP
        block = lanes // LANES
        carry = (block + offset + LANE_BLOCKS) // LANE_BLOCKS - 1
        from_lane = lanes % LANES - carry
        col = (from_lane * LANE_BLOCKS + block).astype(F32)
        col_shift = a[1, 0:1] + a[1, 1:2] * (col - (WIDTH - 1) / 2.0) / WIDTH
        within = (from_lane >= 0) & (from_lane < LANES) & (offset <= WARP)
        cols_out[visit] = jnp.where(within, lanczos(col_shift - offset.astype(F32)), 0.0)


def prepare(place, taps, psf, affine):
    ccds = affine.shape[1]
    return pl.pallas_call(
        prepare_kernel,
        grid_spec=pltpu.PrefetchScalarGridSpec(
            num_scalar_prefetch=1,
            grid=(1,),
            in_specs=[pl.BlockSpec(memory_space=pltpu.HBM)] * 3,
            out_specs=[
                pl.BlockSpec((V, 2, TAPS * STRIP, LANES), lambda i, place: (0, 0, 0, 0)),
                pl.BlockSpec((V, TAPS * STRIP, BAND - LANES), lambda i, place: (0, 0, 0)),
                pl.BlockSpec((V, BLOCK, 256), lambda i, place: (0, 0, 0)),
                pl.BlockSpec((V, 8, WIDTH), lambda i, place: (0, 0, 0)),
            ],
            scratch_shapes=[
                pltpu.VMEM((NBASIS, 2, TAPS), F32),
                pltpu.VMEM((1, 3, V, NBASIS), F32),
                pltpu.VMEM((V, 2, 2, ccds), F32),
                pltpu.SemaphoreType.DMA((3,)),
            ],
        ),
        out_shape=[
            jax.ShapeDtypeStruct((V, 2, TAPS * STRIP, LANES), F32),
            jax.ShapeDtypeStruct((V, TAPS * STRIP, BAND - LANES), BF16),
            jax.ShapeDtypeStruct((V, BLOCK, 256), BF16),
            jax.ShapeDtypeStruct((V, 8, WIDTH), F32),
        ],
        compiler_params=pltpu.CompilerParams(vmem_limit_bytes=32 << 20),
        cost_estimate=pl.CostEstimate(flops=1 << 30, bytes_accessed=1 << 20, transcendentals=0),
        name="prepare",
    )(place, taps.transpose(1, 0, 2), psf.transpose(1, 3, 0, 2), affine.transpose(0, 2, 3, 1))


def lane_block(x, v):
    return x[:, v * LANES : (v + 1) * LANES]


def warp_kernel(
    place, patch, slot, owner, weight, level, slope, row_weights, col_weights, sort, unsort,
    image, above, below, first_out, shared_out, rest_out,
    terms, ready, seen, order, label, sem, label_sem,
):
    visit = pl.program_id(0)
    visits = pl.num_programs(0)
    top_row = place[1]

    @pl.when(visit == 0)
    def _():
        terms[:, BLOCK + 2 * RIM :] = jnp.zeros((4, TALL - BLOCK - 2 * RIM, WIDTH), BF16)

    raw = jnp.concatenate(
        [jnp.where(place[2] > 0, above[0], 0.0), image[0], jnp.where(place[3] > 0, below[0], 0.0)],
        axis=0,
    )
    raw_high = raw.astype(BF16)
    raw_low = (raw - raw_high.astype(F32)).astype(BF16)
    tall = BLOCK + 2 * RIM
    sorted_terms = jnp.dot(
        jnp.concatenate([raw_high, raw_low], axis=0), sort[...], preferred_element_type=F32
    )
    high, low = sorted_terms[:tall], sorted_terms[tall:]
    col_pos = (2.0 * column_at(iota((1, WIDTH), 1)).astype(F32) + 1.0) / WIDTH - 1.0
    tilted = (high + low) * col_pos
    tilted_high = tilted.astype(BF16)
    terms[0, :tall] = high.astype(BF16)
    terms[1, :tall] = low.astype(BF16)
    terms[2, :tall] = tilted_high
    terms[3, :tall] = (tilted - tilted_high.astype(F32)).astype(BF16)

    lane = iota((1, LANES), 1)
    low_lanes = (lane // STEP) % 3 == 2
    level_lanes = lane < 3 * STEP
    strip_row = (iota((TAPS * STRIP, 1), 0) % STRIP).astype(F32)
    filler = jnp.zeros((BAND - GROUPS * STEP, WIDTH), BF16)
    strips = []
    for k in range(STRIPS):
        match_row = (top_row + (k * STRIP - WARP)).astype(F32) + strip_row
        row_pos = (2.0 * match_row + 1.0) / HEIGHT - 1.0
        x = level[0, 0] + row_pos * level[0, 1]
        x = jnp.where(low_lanes, x - x.astype(BF16).astype(F32), x)
        matrix = jnp.concatenate([x.astype(BF16), slope[0]], axis=1)
        rows = slice(k * STRIP, k * STRIP + STEP)
        columns = jnp.concatenate(
            [terms[h, rows] for h in (0, 1, 0, 2, 3, 2)] + [filler], axis=0
        )
        taps = jnp.dot(matrix, columns, preferred_element_type=F32)
        out_blocks = []
        for v in range(LANE_BLOCKS):
            total = None
            for q in range(-(HALF // LANE_BLOCKS) - 1, HALF // LANE_BLOCKS + 2):
                part = None
                for u in range(TAPS):
                    if (v + u - HALF) // LANE_BLOCKS != q:
                        continue
                    w = (v + u - HALF) % LANE_BLOCKS
                    piece = lane_block(taps[u * STRIP : (u + 1) * STRIP], w)
                    part = piece if part is None else part + piece
                if part is None:
                    continue
                if q:
                    part = pltpu.roll(part, -q % LANES, 1)
                    part = jnp.where((lane + q >= 0) & (lane + q < LANES), part, 0.0)
                total = part if total is None else total + part
            out_blocks.append(total)
        strips.append(jnp.concatenate(out_blocks, axis=1))
    matched = jnp.concatenate(strips, axis=0)

    high = matched.astype(BF16).astype(F32)
    low = matched - high
    empty = jnp.zeros((256 - 3 * MATCH, WIDTH), F32)
    halves = []
    for h in range(HALVES):
        rows = slice(h * ROWS, h * ROWS + MATCH)
        columns = jnp.concatenate([high[rows], low[rows], high[rows], empty], axis=0).astype(BF16)
        halves.append(
            jnp.dot(
                row_weights[0, h * ROWS : (h + 1) * ROWS], columns, preferred_element_type=F32
            )
        )
    warped = jnp.concatenate(halves, axis=0)
    col = col_weights[0]
    out_blocks = []
    for v in range(LANE_BLOCKS):
        total = None
        for q in (-1, 0, 1):
            part = None
            for s in range(2 * WARP + 1):
                if (v + s - WARP) // LANE_BLOCKS != q:
                    continue
                w = (v + s - WARP) % LANE_BLOCKS
                piece = lane_block(col[s : s + 1], v) * lane_block(warped, w)
                part = piece if part is None else part + piece
            if part is None:
                continue
            if q:
                part = pltpu.roll(part, -q % LANES, 1)
            total = part if total is None else total + part
        out_blocks.append(total.astype(BF16))
    result = jnp.dot(
        jnp.concatenate(out_blocks, axis=1), unsort[...], preferred_element_type=F32
    ).astype(BF16)

    @pl.when(visit == 0)
    def _():
        def clear(p, _):
            seen[p] = 0
            return 0

        lax.fori_loop(0, owner.shape[0], clear, 0)
        order[V * BLKC] = 0

    for j in range(BLKC):
        block = visit * BLKC + j
        ready[block] = result[:, j * BLOCK : (j + 1) * BLOCK]
        p = patch[0, block]
        again = seen[p] > 0
        place_in_rest = order[V * BLKC]
        seen[p] = 1
        order[block] = jnp.where(again, place_in_rest + 1, 0)
        order[V * BLKC] = place_in_rest + again.astype(jnp.int32)
        share = again & (place_in_rest < SHARED)

        def send(to):
            pltpu.make_async_copy(ready.at[block], to, sem.at[block]).start()

        @pl.when(jnp.logical_not(again))
        def _():
            send(first_out.at[owner[p]])

        @pl.when(share)
        def _():
            send(shared_out.at[0, pl.ds(pl.multiple_of(place_in_rest * BLOCK, BLOCK), BLOCK)])

        @pl.when(again & jnp.logical_not(share))
        def _():
            send(rest_out.at[owner[p]])

    @pl.when(visit == visits - 1)
    def _():
        lane = iota((1, LANES), 1)
        blocks = V * BLKC
        row = jnp.zeros((1, LANES), F32)
        ccd = iota(weight.shape, 1) == place[0]
        own = jnp.sum(jnp.where(ccd, weight[...].astype(F32), 0.0), axis=1, keepdims=True)
        for e in range(blocks):
            row = jnp.where(lane == e, patch[0, e].astype(F32), row)
            row = jnp.where(lane == blocks + e, slot[0, e].astype(F32), row)
            row = jnp.where(lane == 2 * blocks + e, own[e // BLKC : e // BLKC + 1], row)
            row = jnp.where(lane == 3 * blocks + e, order[e].astype(F32), row)
        row = jnp.where(lane == 4 * blocks, order[blocks].astype(F32), row)
        label[...] = jnp.broadcast_to(row, (LABEL, LANES)).astype(BF16)
        copy = pltpu.make_async_copy(
            label, shared_out.at[0, pl.ds(SHARED * BLOCK, LABEL)], label_sem
        )
        copy.start()
        copy.wait()
        for block in range(blocks):
            pltpu.make_async_copy(ready.at[block], first_out.at[0], sem.at[block]).wait()


def warp(place, patch, slot, owner, weight, ready, images, above, below, devices):
    smem = pl.BlockSpec(memory_space=pltpu.SMEM)
    sort = deinterleave()
    whole = pl.BlockSpec((WIDTH, WIDTH), lambda v, place: (0, 0))
    return pl.pallas_call(
        warp_kernel,
        grid_spec=pltpu.PrefetchScalarGridSpec(
            num_scalar_prefetch=1,
            grid=(V,),
            in_specs=[
                smem,
                smem,
                smem,
                pl.BlockSpec(weight.shape, lambda v, place: (0, 0)),
                pl.BlockSpec((1, 2, TAPS * STRIP, LANES), lambda v, place: (v, 0, 0, 0)),
                pl.BlockSpec((1, TAPS * STRIP, BAND - LANES), lambda v, place: (v, 0, 0)),
                pl.BlockSpec((1, BLOCK, 256), lambda v, place: (v, 0, 0)),
                pl.BlockSpec((1, 8, WIDTH), lambda v, place: (v, 0, 0)),
                whole,
                whole,
                pl.BlockSpec((1, BLOCK, WIDTH), lambda v, place: (v, 0, 0)),
                pl.BlockSpec((1, RIM, WIDTH), lambda v, place: (v, 0, 0)),
                pl.BlockSpec((1, RIM, WIDTH), lambda v, place: (v, 0, 0)),
            ],
            out_specs=[pl.BlockSpec(memory_space=pl.ANY)] * 3,
            scratch_shapes=[
                pltpu.VMEM((4, TALL, WIDTH), BF16),
                pltpu.VMEM((V * BLKC, BLOCK, BLOCK), BF16),
                pltpu.SMEM((owner.shape[0],), jnp.int32),
                pltpu.SMEM((V * BLKC + 1,), jnp.int32),
                pltpu.VMEM((LABEL, LANES), BF16),
                pltpu.SemaphoreType.DMA((V * BLKC,)),
                pltpu.SemaphoreType.DMA(()),
            ],
        ),
        out_shape=[
            jax.ShapeDtypeStruct((devices, BLOCK, BLOCK), BF16),
            jax.ShapeDtypeStruct((1, SHARED * BLOCK + LABEL, BLOCK), BF16),
            jax.ShapeDtypeStruct((devices, BLOCK, BLOCK), BF16),
        ],
        compiler_params=pltpu.CompilerParams(vmem_limit_bytes=32 << 20),
        cost_estimate=pl.CostEstimate(
            flops=V * 2 * STRIPS * TAPS * STRIP * BAND * WIDTH,
            bytes_accessed=V * (BLOCK * WIDTH * 6),
            transcendentals=0,
        ),
        name="match_warp",
    )(
        place, patch, slot, owner, weight, *ready,
        jnp.asarray(sort, BF16), jnp.asarray(sort.T, BF16), images, above, below,
    )


def coadd_kernel(place, owner, first, shared, *refs):
    rest = refs[0] if len(refs) == 6 else None
    out, table, numbers, sums, sem = refs[-5:]
    devices = first.shape[0]
    me = place[4]

    def find(p, mine):
        return jnp.where(owner[p] == me, p, mine)

    mine = lax.fori_loop(0, owner.shape[0], find, 0)

    blocks = V * BLKC
    label = shared[:, SHARED * BLOCK : SHARED * BLOCK + LABEL].astype(F32)[:, 0]
    lane = iota(label.shape, 1)
    slots, weights, orders = (pltpu.roll(label, LANES - k * blocks, 1) for k in (1, 2, 3))
    match = (lane < blocks) & (label == mine.astype(F32))
    one = match & (orders == 0.0)
    two = match & (orders > 0.0)
    found = jnp.zeros_like(label)
    for k, (which, value) in enumerate(
        ((one, weights), (one, slots), (two, weights), (two, slots), (two, orders))
    ):
        column = jnp.sum(jnp.where(which, value, 0.0), axis=1, keepdims=True)
        found = jnp.where(lane == k, column, found)
    table[...] = found
    copy = pltpu.make_async_copy(table, numbers, sem)
    copy.start()
    out[...] = jnp.zeros_like(out)
    for c in range(CELLS):
        sums[c] = 0.0
    copy.wait()

    def add(weight, cell, block):
        c = cell.astype(jnp.int32)
        sums[c] += weight
        lanes = pl.ds(pl.multiple_of(c % PSIDE * BLOCK, BLOCK), BLOCK)
        out[c // PSIDE, :, lanes] += weight * block.astype(F32)

    def source(s, _):
        @pl.when(numbers[s, 0] > 0.0)
        def _():
            add(numbers[s, 0], numbers[s, 1], first[s])

        second = numbers[s, 4].astype(jnp.int32) - 1

        @pl.when((second >= 0) & (second < SHARED))
        def _():
            rows = pl.ds(pl.multiple_of(second * BLOCK, BLOCK), BLOCK)
            add(numbers[s, 2], numbers[s, 3], shared[s, rows])

        if rest is not None:

            @pl.when(second >= SHARED)
            def _():
                add(numbers[s, 2], numbers[s, 3], rest[s])

        return 0

    lax.fori_loop(0, devices, source, 0)
    for c in range(CELLS):
        lanes = slice(c % PSIDE * BLOCK, (c % PSIDE + 1) * BLOCK)
        inverse = 1.0 / jnp.maximum(jnp.full((1, BLOCK), sums[c], F32), 1.0)
        out[c // PSIDE, :, lanes] = out[c // PSIDE, :, lanes] * inverse


def coadd(place, owner, *got):
    smem = pl.BlockSpec(memory_space=pltpu.SMEM)
    devices = got[0].shape[0]
    return pl.pallas_call(
        coadd_kernel,
        grid=(1,),
        in_specs=[smem, smem] + [pl.BlockSpec(x.shape, lambda i: (0, 0, 0)) for x in got],
        out_specs=pl.BlockSpec((PSIDE, BLOCK, WIDTH), lambda i: (0, 0, 0)),
        out_shape=jax.ShapeDtypeStruct((PSIDE, BLOCK, PSIDE * BLOCK), F32),
        scratch_shapes=[
            pltpu.VMEM((devices, LANES), F32),
            pltpu.SMEM((devices, LANES), F32),
            pltpu.SMEM((CELLS,), F32),
            pltpu.SemaphoreType.DMA(()),
        ],
        compiler_params=pltpu.CompilerParams(vmem_limit_bytes=32 << 20),
        name="coadd_" + str(len(got)),
    )(place, owner, *got)


def shards(
    images, basis_taps, psf_coef, affine, visit_weight, block_patch, block_slot, patch_owner
):
    band = lax.axis_index("ccd")
    devices = lax.axis_size("ccd")
    shifted = band + SPLIT // 2
    quarter = shifted % SPLIT
    place = jnp.stack(
        [
            shifted // SPLIT,
            quarter * BLOCK,
            ((quarter > 0) & (band > 0)).astype(jnp.int32),
            ((quarter < SPLIT - 1) & (band < devices - 1)).astype(jnp.int32),
            band,
        ]
    ).astype(jnp.int32)
    down = [(i, i + 1) for i in range(devices - 1)]
    up = [(i + 1, i) for i in range(devices - 1)]
    above = lax.ppermute(images[:, BLOCK - RIM :], "ccd", down)
    below = lax.ppermute(images[:, :RIM], "ccd", up)
    patch = block_patch[:, :, 0]
    ready = prepare(place, basis_taps, psf_coef, affine)
    first, shared, rest = warp(
        place, patch, block_slot, patch_owner, visit_weight, ready, images, above, below, devices
    )
    shared = lax.all_gather(shared, "ccd", axis=0, tiled=True)
    first = lax.all_to_all(first, "ccd", split_axis=0, concat_axis=0, tiled=True)
    seconds = jnp.max(shared[:, SHARED * BLOCK, 4 * V * BLKC])

    def more(first, shared, rest):
        rest = lax.all_to_all(rest, "ccd", split_axis=0, concat_axis=0, tiled=True)
        return coadd(place, patch_owner, first, shared, rest)

    def all_here(first, shared, rest):
        return coadd(place, patch_owner, first, shared)

    result = lax.cond(seconds > SHARED, more, all_here, first, shared, rest)
    return result.reshape(1, PSIDE * BLOCK, PSIDE * BLOCK)


def solution(mesh):
    placed = (
        P(None, ("group", "ccd"), None),
        P(),
        P(None, "group", None, None),
        P(None, "group", None, None),
        P(None, "group"),
        P(("group", "ccd"), None, None),
        P(("group", "ccd"), None),
        P("group"),
    )
    return jax.shard_map(
        shards,
        mesh=mesh,
        in_specs=placed,
        out_specs=P(("group", "ccd"), None, None),
        check_vma=False,
    )
```

```python
import jax
import jax.numpy as jnp
import numpy as np
from jax import lax
from jax.experimental import pallas as pl
from jax.experimental.pallas import tpu as pltpu
from jax.sharding import PartitionSpec as P

V = 4
BLOCK = 128
BLKC = 4
SPLIT = 4
TAPS = 11
NBASIS = 9
PSIDE = 4
CELLS = PSIDE * PSIDE
CAP = 2

HALF = TAPS // 2
WARP = 3
RIM = HALF + WARP
HEIGHT = SPLIT * BLOCK
WIDTH = BLKC * BLOCK
LANES = 128
LANE_BLOCKS = WIDTH // LANES
STRIP = 16
STEP = 32
STRIPS = -(-(BLOCK + 2 * WARP) // STRIP)
GROUPS = 6
BAND = 256
TALL = (STRIPS - 1) * STRIP + STEP
HALVES = 2
TOGETHER = 2
ROWS = BLOCK // HALVES
MATCH = ROWS + 8
LABEL = 16
F32 = jnp.float32
BF16 = jnp.bfloat16


def sin_pi(t):
    whole = jnp.round(t)
    f = t - whole
    odd = whole - 2.0 * jnp.floor(0.5 * whole)
    f2 = f * f
    out = 0.0
    for c in (
        0.00046630280576761, -0.0073704309457144, 0.0821458866111282,
        -0.599264529320792, 2.55016403987734, -5.16771278004997, 3.14159265358979,
    ):
        out = out * f2 + c
    return f * out * (1.0 - 2.0 * odd)


def lanczos(t):
    zero = t == 0.0
    safe = jnp.where(zero, 1.0, t)
    pt = jnp.pi * safe
    value = 3.0 * sin_pi(safe) * sin_pi(safe / 3.0) / (pt * pt)
    return jnp.where(jnp.abs(t) < 3.0, jnp.where(zero, 1.0, value), 0.0)


def iota(shape, dim):
    return lax.broadcasted_iota(jnp.int32, shape, dim)


def deinterleave():
    order = np.arange(WIDTH).reshape(LANES, LANE_BLOCKS).T.reshape(-1)
    return (np.arange(WIDTH)[:, None] == order[None, :]).astype(np.float32)


def column_at(lane):
    return lane % LANES * LANE_BLOCKS + lane // LANES


def prepare_kernel(
    place, taps_in, psf_in, affine_in, level_out, slope_out, rows_out, cols_out,
    taps, psf, affine, sems,
):
    copies = [
        pltpu.make_async_copy(taps_in, taps, sems.at[0]),
        pltpu.make_async_copy(psf_in.at[pl.ds(place[0], 1)], psf, sems.at[1]),
        pltpu.make_async_copy(affine_in, affine, sems.at[2]),
    ]
    for copy in copies:
        copy.start()
    for copy in copies:
        copy.wait()
    lane = iota((1, BAND), 1)
    seg = lane // STEP
    tap = lane - seg * STEP
    row_taps, col_taps = taps[:, 0], taps[:, 1]
    onehot = (tap == iota((TAPS, BAND), 0)) & (seg < GROUPS)
    r = jnp.dot(
        row_taps, onehot.astype(F32),
        precision=lax.Precision.HIGHEST, preferred_element_type=F32,
    )
    is_level = seg < 3
    low_lanes = seg % 3 == 2
    ccd_lane = iota((1, 1, affine.shape[3]), 2) == place[0]

    turned = lax.dot_general(
        (iota((TAPS, STRIP), 0) == iota((TAPS, STRIP), 1)).astype(F32), col_taps,
        (((0,), (1,)), ((), ())),
        precision=lax.Precision.HIGHEST, preferred_element_type=F32,
    )
    kernels = jnp.dot(
        jnp.concatenate(
            [turned * psf[0, c, v : v + 1, :] for v in range(V) for c in range(3)], axis=0
        ),
        r, precision=lax.Precision.HIGHEST, preferred_element_type=F32,
    )

    col_move = (iota((STRIP, 1), 0) - HALF).astype(F32) * (2.0 / WIDTH)
    for visit in range(V):
        const, by_row, by_col = (
            kernels[(visit * 3 + c) * STRIP : (visit * 3 + c + 1) * STRIP] for c in range(3)
        )
        const = jnp.where(is_level, const - col_move * by_col, by_col)
        by_row = jnp.where(is_level, by_row, 0.0)
        for u in range(TAPS):
            x = jnp.broadcast_to(const[u : u + 1], (8, BAND))
            x = pltpu.roll(x, 0, 1, stride=1, stride_axis=0)
            x = jnp.concatenate([x, pltpu.roll(x, 8, 1)], axis=0)
            y = jnp.broadcast_to(by_row[u : u + 1, :LANES], (8, LANES))
            y = pltpu.roll(y, 0, 1, stride=1, stride_axis=0)
            y = jnp.concatenate([y, pltpu.roll(y, 8, 1)], axis=0)
            at = slice(u * STRIP, (u + 1) * STRIP)
            level_out[visit, 0, at] = x[:, :LANES]
            level_out[visit, 1, at] = y
            high = x.astype(BF16).astype(F32)
            slope_out[visit, at] = jnp.where(low_lanes, x - high, high)[:, LANES:].astype(BF16)

        a = jnp.sum(jnp.where(ccd_lane, affine[visit], 0.0), axis=2, keepdims=True)
        out_row = iota((BLOCK, LANES), 0)
        local = out_row % ROWS
        in_row = iota((BLOCK, LANES), 1)
        row = (place[1] + out_row).astype(F32)
        shift = a[0, 0:1] + a[0, 1:2] * (row - (HEIGHT - 1) / 2.0) / HEIGHT
        step = in_row - local - WARP
        band_row = out_row + step
        keep = jnp.abs(step) <= WARP
        keep = keep & ((band_row >= 0) | (place[2] > 0)) & ((band_row < BLOCK) | (place[3] > 0))
        weights = jnp.where(keep, lanczos(shift - step.astype(F32)), 0.0)
        high = weights.astype(BF16).astype(F32)
        zero = jnp.zeros_like(weights)
        wide = jnp.concatenate([high, zero], axis=1)
        low = jnp.concatenate([weights - high, zero], axis=1)
        wide = wide + pltpu.roll(wide, MATCH, 1) + pltpu.roll(low, 2 * MATCH, 1)
        rows_out[visit] = wide.astype(BF16)

        lanes = iota((8, WIDTH), 1)
        offset = iota((8, WIDTH), 0) - WARP
        block = lanes // LANES
        carry = (block + offset + LANE_BLOCKS) // LANE_BLOCKS - 1
        from_lane = lanes % LANES - carry
        col = (from_lane * LANE_BLOCKS + block).astype(F32)
        col_shift = a[1, 0:1] + a[1, 1:2] * (col - (WIDTH - 1) / 2.0) / WIDTH
        within = (from_lane >= 0) & (from_lane < LANES) & (offset <= WARP)
        cols_out[visit] = jnp.where(within, lanczos(col_shift - offset.astype(F32)), 0.0)


def prepare(place, taps, psf, affine):
    ccds = affine.shape[1]
    return pl.pallas_call(
        prepare_kernel,
        grid_spec=pltpu.PrefetchScalarGridSpec(
            num_scalar_prefetch=1,
            grid=(1,),
            in_specs=[pl.BlockSpec(memory_space=pl.ANY)] * 3,
            out_specs=[
                pl.BlockSpec((V, 2, TAPS * STRIP, LANES), lambda i, place: (0, 0, 0, 0)),
                pl.BlockSpec((V, TAPS * STRIP, BAND - LANES), lambda i, place: (0, 0, 0)),
                pl.BlockSpec((V, BLOCK, 256), lambda i, place: (0, 0, 0)),
                pl.BlockSpec((V, 8, WIDTH), lambda i, place: (0, 0, 0)),
            ],
            scratch_shapes=[
                pltpu.VMEM((NBASIS, 2, TAPS), F32),
                pltpu.VMEM((1, 3, V, NBASIS), F32),
                pltpu.VMEM((V, 2, 2, ccds), F32),
                pltpu.SemaphoreType.DMA((3,)),
            ],
        ),
        out_shape=[
            jax.ShapeDtypeStruct((V, 2, TAPS * STRIP, LANES), F32),
            jax.ShapeDtypeStruct((V, TAPS * STRIP, BAND - LANES), BF16),
            jax.ShapeDtypeStruct((V, BLOCK, 256), BF16),
            jax.ShapeDtypeStruct((V, 8, WIDTH), F32),
        ],
        cost_estimate=pl.CostEstimate(flops=1 << 30, bytes_accessed=1 << 20, transcendentals=0),
        name="prepare",
    )(place, taps.transpose(1, 0, 2), psf.transpose(1, 3, 0, 2), affine.transpose(0, 2, 3, 1))


def lane_block(x, v):
    return x[:, v * LANES : (v + 1) * LANES]


def match(columns_of, level, slope, top_row):
    lane = iota((1, LANES), 1)
    low_lanes = (lane // STEP) % 3 == 2
    strip_row = (iota((TAPS * STRIP, 1), 0) % STRIP).astype(F32)

    def strip(k):
        match_row = (top_row + (k * STRIP - WARP)).astype(F32) + strip_row
        row_pos = (2.0 * match_row + 1.0) / HEIGHT - 1.0
        x = level[0] + row_pos * level[1]
        x = jnp.where(low_lanes, x - x.astype(BF16).astype(F32), x)
        matrix = jnp.concatenate([x.astype(BF16), slope], axis=1)
        taps = jnp.dot(matrix, columns_of(k), preferred_element_type=F32)
        out_blocks = []
        for v in range(LANE_BLOCKS):
            total = None
            for q in range(-(HALF // LANE_BLOCKS) - 1, HALF // LANE_BLOCKS + 2):
                part = None
                for u in range(TAPS):
                    if (v + u - HALF) // LANE_BLOCKS != q:
                        continue
                    w = (v + u - HALF) % LANE_BLOCKS
                    piece = lane_block(taps[u * STRIP : (u + 1) * STRIP], w)
                    part = piece if part is None else part + piece
                if part is None:
                    continue
                if q:
                    part = pltpu.roll(part, -q % LANES, 1)
                    part = jnp.where((lane + q >= 0) & (lane + q < LANES), part, 0.0)
                total = part if total is None else total + part
            out_blocks.append(total)
        return jnp.concatenate(out_blocks, axis=1)

    return strip


def warp_kernel(
    place, patch, slot, owner, weight, level, slope, row_weights, col_weights, sort_in, unsort_in,
    image, above, below, out,
    terms, ready, seen, label, label_ready, sort, unsort, sem, label_sem, sort_sem,
):
    step = pl.program_id(0)
    steps = pl.num_programs(0)
    top_row = place[1]
    tall = BLOCK + 2 * RIM
    sort_copy = pltpu.make_async_copy(sort_in, sort, sort_sem.at[0])
    unsort_copy = pltpu.make_async_copy(unsort_in, unsort, sort_sem.at[1])

    @pl.when(step == 0)
    def _():
        sort_copy.start()
        unsort_copy.start()
        terms[:, :, tall:] = jnp.zeros((TOGETHER, 4, TALL - tall, WIDTH), BF16)
        label[...] = jnp.zeros_like(label)

        def clear(p, _):
            seen[p] = 0
            return 0

        lax.fori_loop(0, owner.shape[0], clear, 0)
        sort_copy.wait()

    col_pos = (2.0 * column_at(iota((1, WIDTH), 1)).astype(F32) + 1.0) / WIDTH - 1.0
    for i in range(TOGETHER):
        raw = jnp.concatenate(
            [
                jnp.where(place[2] > 0, above[i], 0.0),
                image[i],
                jnp.where(place[3] > 0, below[i], 0.0),
            ],
            axis=0,
        )
        raw_high = raw.astype(BF16)
        raw_low = (raw - raw_high.astype(F32)).astype(BF16)
        sorted_terms = jnp.dot(
            jnp.concatenate([raw_high, raw_low], axis=0), sort[...], preferred_element_type=F32
        )
        high, low = sorted_terms[:tall], sorted_terms[tall:]
        tilted = (high + low) * col_pos
        tilted_high = tilted.astype(BF16)
        terms[i, 0, :tall] = high.astype(BF16)
        terms[i, 1, :tall] = low.astype(BF16)
        terms[i, 2, :tall] = tilted_high
        terms[i, 3, :tall] = (tilted - tilted_high.astype(F32)).astype(BF16)

    filler = jnp.zeros((BAND - GROUPS * STEP, WIDTH), BF16)

    def columns_of(i):
        def at(k):
            rows = slice(k * STRIP, k * STRIP + STEP)
            return jnp.concatenate([terms[i, h, rows] for h in (0, 1, 0, 2, 3, 2)] + [filler], axis=0)

        return at

    makers = [match(columns_of(i), level[i], slope[i], top_row) for i in range(TOGETHER)]
    strips = [[] for _ in makers]
    for k in range(STRIPS):
        for i, maker in enumerate(makers):
            strips[i].append(maker(k))

    empty = jnp.zeros((256 - 3 * MATCH, WIDTH), F32)
    warped = []
    for i in range(TOGETHER):
        matched = jnp.concatenate(strips[i], axis=0)
        high = matched.astype(BF16).astype(F32)
        low = matched - high
        halves = []
        for h in range(HALVES):
            rows = slice(h * ROWS, h * ROWS + MATCH)
            columns = jnp.concatenate([high[rows], low[rows], high[rows], empty], axis=0)
            halves.append(
                jnp.dot(
                    row_weights[i, h * ROWS : (h + 1) * ROWS], columns.astype(BF16),
                    preferred_element_type=F32,
                )
            )
        warped.append(jnp.concatenate(halves, axis=0))

    @pl.when(step == 0)
    def _():
        unsort_copy.wait()

    results = []
    for i in range(TOGETHER):
        col = col_weights[i]
        out_blocks = []
        for v in range(LANE_BLOCKS):
            total = None
            for q in (-1, 0, 1):
                part = None
                for s in range(2 * WARP + 1):
                    if (v + s - WARP) // LANE_BLOCKS != q:
                        continue
                    w = (v + s - WARP) % LANE_BLOCKS
                    piece = lane_block(col[s : s + 1], v) * lane_block(warped[i], w)
                    part = piece if part is None else part + piece
                if part is None:
                    continue
                if q:
                    part = pltpu.roll(part, -q % LANES, 1)
                total = part if total is None else total + part
            out_blocks.append(total.astype(BF16))
        results.append(
            jnp.dot(
                jnp.concatenate(out_blocks, axis=1), unsort[...], preferred_element_type=F32
            ).astype(BF16)
        )

    lane = iota((1, LANES), 1)
    ccd = iota(weight.shape, 1) == place[0]
    weights = jnp.sum(jnp.where(ccd, weight[...].astype(F32), 0.0), axis=1, keepdims=True)
    visits = iota((V, 1), 0)
    for i in range(TOGETHER):
        visit = step * TOGETHER + i
        own = jnp.sum(jnp.where(visits == visit, weights, 0.0), axis=0, keepdims=True)
        for j in range(BLKC):
            block = visit * BLKC + j
            ready[block] = results[i][:, j * BLOCK : (j + 1) * BLOCK]
            p = patch[0, block]
            rank = seen[p]
            seen[p] = rank + 1
            to = out.at[owner[p], pl.ds(pl.multiple_of(rank * BLOCK, BLOCK), BLOCK)]
            pltpu.make_async_copy(ready.at[block], to, sem.at[block]).start()
            row = label[pl.ds(owner[p], 1), :]
            row = jnp.where(lane == rank * 2, own, row)
            label[pl.ds(owner[p], 1), :] = jnp.where(
                lane == rank * 2 + 1, slot[0, block].astype(F32), row
            )

    @pl.when(step == steps - 1)
    def _():
        devices = label.shape[0]
        label_ready[...] = jnp.broadcast_to(
            label[...].reshape(devices, 1, LANES), (devices, LABEL, LANES)
        ).astype(BF16)
        copy = pltpu.make_async_copy(label_ready, out.at[:, pl.ds(CAP * BLOCK, LABEL)], label_sem)
        copy.start()
        copy.wait()
        for block in range(V * BLKC):
            pltpu.make_async_copy(ready.at[block], out.at[0, pl.ds(0, BLOCK)], sem.at[block]).wait()


def warp(place, patch, slot, owner, weight, ready, images, above, below, devices):
    smem = pl.BlockSpec(memory_space=pltpu.SMEM)
    hbm = pl.BlockSpec(memory_space=pl.ANY)
    sort = deinterleave()
    n = TOGETHER
    return pl.pallas_call(
        warp_kernel,
        grid_spec=pltpu.PrefetchScalarGridSpec(
            num_scalar_prefetch=1,
            grid=(V // n,),
            in_specs=[
                smem,
                smem,
                smem,
                pl.BlockSpec(weight.shape, lambda v, place: (0, 0)),
                pl.BlockSpec((n, 2, TAPS * STRIP, LANES), lambda v, place: (v, 0, 0, 0)),
                pl.BlockSpec((n, TAPS * STRIP, BAND - LANES), lambda v, place: (v, 0, 0)),
                pl.BlockSpec((n, BLOCK, 256), lambda v, place: (v, 0, 0)),
                pl.BlockSpec((n, 8, WIDTH), lambda v, place: (v, 0, 0)),
                hbm,
                hbm,
                pl.BlockSpec((n, BLOCK, WIDTH), lambda v, place: (v, 0, 0)),
                pl.BlockSpec((n, RIM, WIDTH), lambda v, place: (v, 0, 0)),
                pl.BlockSpec((n, RIM, WIDTH), lambda v, place: (v, 0, 0)),
            ],
            out_specs=hbm,
            scratch_shapes=[
                pltpu.VMEM((n, 4, TALL, WIDTH), BF16),
                pltpu.VMEM((V * BLKC, BLOCK, BLOCK), BF16),
                pltpu.SMEM((owner.shape[0],), jnp.int32),
                pltpu.VMEM((devices, LANES), F32),
                pltpu.VMEM((devices, LABEL, LANES), BF16),
                pltpu.VMEM((WIDTH, WIDTH), BF16),
                pltpu.VMEM((WIDTH, WIDTH), BF16),
                pltpu.SemaphoreType.DMA((V * BLKC,)),
                pltpu.SemaphoreType.DMA(()),
                pltpu.SemaphoreType.DMA((2,)),
            ],
        ),
        out_shape=jax.ShapeDtypeStruct((devices, CAP * BLOCK + LABEL, BLOCK), BF16),
        compiler_params=pltpu.CompilerParams(vmem_limit_bytes=60 << 20),
        cost_estimate=pl.CostEstimate(
            flops=V * 2 * STRIPS * TAPS * STRIP * BAND * WIDTH,
            bytes_accessed=V * (BLOCK * WIDTH * 6),
            transcendentals=0,
        ),
        name="match_warp",
    )(
        place, patch, slot, owner, weight, *ready,
        jnp.asarray(sort, BF16), jnp.asarray(sort.T, BF16), images, above, below,
    )


def coadd_kernel(got, out, total, table, numbers, sums, sem, out_sem):
    devices = got.shape[0]
    table[...] = got[:, CAP * BLOCK : CAP * BLOCK + LABEL].astype(F32)[:, 0]
    copy = pltpu.make_async_copy(table, numbers, sem)
    copy.start()
    total[...] = jnp.zeros_like(total)
    for c in range(CELLS):
        sums[c] = 0.0
    copy.wait()

    def add(source, _):
        for rank in range(CAP):
            weight = numbers[source, rank * 2]

            @pl.when(weight > 0.0)
            def _(rank=rank, weight=weight):
                c = numbers[source, rank * 2 + 1].astype(jnp.int32)
                sums[c] += weight
                rows = slice(rank * BLOCK, (rank + 1) * BLOCK)
                total[c] += weight * got[source, rows].astype(F32)

        return 0

    lax.fori_loop(0, devices, add, 0, unroll=4)
    copies = []
    for c in range(CELLS):
        inverse = 1.0 / jnp.maximum(jnp.full((1, BLOCK), sums[c], F32), 1.0)
        total[c] = total[c] * inverse
        rows = slice(c // PSIDE * BLOCK, (c // PSIDE + 1) * BLOCK)
        lanes = slice(c % PSIDE * BLOCK, (c % PSIDE + 1) * BLOCK)
        copies.append(pltpu.make_async_copy(total.at[c], out.at[0, rows, lanes], out_sem.at[c]))
        copies[-1].start()
    for copy in copies:
        copy.wait()


def coadd(got):
    devices = got.shape[0]
    return pl.pallas_call(
        coadd_kernel,
        in_specs=[pl.BlockSpec(memory_space=pltpu.VMEM)],
        out_specs=pl.BlockSpec(memory_space=pl.ANY),
        out_shape=jax.ShapeDtypeStruct((1, PSIDE * BLOCK, PSIDE * BLOCK), F32),
        scratch_shapes=[
            pltpu.VMEM((CELLS, BLOCK, BLOCK), F32),
            pltpu.VMEM((devices, LANES), F32),
            pltpu.SMEM((devices, LANES), F32),
            pltpu.SMEM((CELLS,), F32),
            pltpu.SemaphoreType.DMA(()),
            pltpu.SemaphoreType.DMA((CELLS,)),
        ],
        compiler_params=pltpu.CompilerParams(vmem_limit_bytes=32 << 20),
        name="coadd",
    )(got)


def shards(
    images, basis_taps, psf_coef, affine, visit_weight, block_patch, block_slot, patch_owner
):
    band = lax.axis_index("ccd")
    devices = lax.axis_size("ccd")
    shifted = band + SPLIT // 2
    quarter = shifted % SPLIT
    place = jnp.stack(
        [
            shifted // SPLIT,
            quarter * BLOCK,
            ((quarter > 0) & (band > 0)).astype(jnp.int32),
            ((quarter < SPLIT - 1) & (band < devices - 1)).astype(jnp.int32),
            band,
        ]
    ).astype(jnp.int32)
    down = [(i, i + 1) for i in range(devices - 1)]
    up = [(i + 1, i) for i in range(devices - 1)]
    above = lax.ppermute(images[:, BLOCK - RIM :], "ccd", down)
    below = lax.ppermute(images[:, :RIM], "ccd", up)
    patch = block_patch[:, :, 0]
    ready = prepare(place, basis_taps, psf_coef, affine)
    sent = warp(
        place, patch, block_slot, patch_owner, visit_weight, ready, images, above, below, devices
    )
    got = lax.all_to_all(sent, "ccd", split_axis=0, concat_axis=0, tiled=True)
    return coadd(got)


def solution(mesh):
    placed = (
        P(None, ("group", "ccd"), None),
        P(),
        P(None, "group", None, None),
        P(None, "group", None, None),
        P(None, "group"),
        P(("group", "ccd"), None, None),
        P(("group", "ccd"), None),
        P("group"),
    )
    return jax.shard_map(
        shards,
        mesh=mesh,
        in_specs=placed,
        out_specs=P(("group", "ccd"), None, None),
        check_vma=False,
    )
```

```python
import jax
import jax.numpy as jnp
import numpy as np
from jax import lax
from jax.experimental import pallas as pl
from jax.experimental.pallas import tpu as pltpu
from jax.sharding import PartitionSpec as P

V = 4
BLOCK = 128
BLKC = 4
SPLIT = 4
TAPS = 11
NBASIS = 9
PSIDE = 4
CELLS = PSIDE * PSIDE
CAP = 2

HALF = TAPS // 2
WARP = 3
RIM = HALF + WARP
HEIGHT = SPLIT * BLOCK
WIDTH = BLKC * BLOCK
LANES = 128
LANE_BLOCKS = WIDTH // LANES
STRIP = 16
STEP = 32
STRIPS = -(-(BLOCK + 2 * WARP) // STRIP)
GROUPS = 6
BAND = 256
TALL = (STRIPS - 1) * STRIP + STEP
HALVES = 2
ROWS = BLOCK // HALVES
WINDOW = ROWS + STRIP
LABEL = 16
F32 = jnp.float32
BF16 = jnp.bfloat16


def sin_pi(t):
    whole = jnp.round(t)
    f = t - whole
    odd = whole - 2.0 * jnp.floor(0.5 * whole)
    f2 = f * f
    out = 0.0
    for c in (
        0.00046630280576761, -0.0073704309457144, 0.0821458866111282,
        -0.599264529320792, 2.55016403987734, -5.16771278004997, 3.14159265358979,
    ):
        out = out * f2 + c
    return f * out * (1.0 - 2.0 * odd)


def lanczos(t):
    zero = t == 0.0
    safe = jnp.where(zero, 1.0, t)
    pt = jnp.pi * safe
    value = 3.0 * sin_pi(safe) * sin_pi(safe / 3.0) / (pt * pt)
    return jnp.where(jnp.abs(t) < 3.0, jnp.where(zero, 1.0, value), 0.0)


def iota(shape, dim):
    return lax.broadcasted_iota(jnp.int32, shape, dim)


def deinterleave():
    order = np.arange(WIDTH).reshape(LANES, LANE_BLOCKS).T.reshape(-1)
    return (np.arange(WIDTH)[:, None] == order[None, :]).astype(np.float32)


def column_at(lane):
    return lane % LANES * LANE_BLOCKS + lane // LANES


def lane_block(x, v):
    return x[:, v * LANES : (v + 1) * LANES]


def dot_exact(a, b, dims):
    return lax.dot_general(
        a, b, (dims, ((), ())), precision=lax.Precision.HIGHEST, preferred_element_type=F32
    )


def staircase(x, first):
    return jnp.concatenate(
        [
            pltpu.roll(x[g : g + 8], first + g, 1, stride=1, stride_axis=0)
            for g in range(0, x.shape[0], 8)
        ],
        axis=0,
    )


def lane_sum(terms_of, lane, count, weigh):
    blocks = []
    for v in range(LANE_BLOCKS):
        total = None
        half = count // 2
        for q in range(-(-half // LANE_BLOCKS) * -1, (half + LANE_BLOCKS - 1) // LANE_BLOCKS + 1):
            part = None
            for u in range(count):
                if (v + u - half) // LANE_BLOCKS != q:
                    continue
                piece = terms_of(u, v, (v + u - half) % LANE_BLOCKS)
                part = piece if part is None else part + piece
            if part is None:
                continue
            if q:
                part = pltpu.roll(part, -q % LANES, 1)
                if not weigh:
                    part = jnp.where((lane + q >= 0) & (lane + q < LANES), part, 0.0)
            total = part if total is None else total + part
        blocks.append(total)
    return blocks


def warp_kernel(
    patch, slot, owner, weight, taps, psf, affine, sort_in, unsort_in, image, above, below, out,
    row_taps, turned_taps, high_level, step_level, slope, terms, matched_terms,
    ready, seen, label, label_ready, sort, unsort, sem, label_sem, sort_sem,
):
    visit = pl.program_id(0)
    visits = pl.num_programs(0)
    band = lax.axis_index("ccd")
    devices = label.shape[0]
    ccd = (band + SPLIT // 2) // SPLIT
    quarter = (band + SPLIT // 2) % SPLIT
    top_row = quarter * BLOCK
    has_above = (quarter > 0) & (band > 0)
    has_below = (quarter < SPLIT - 1) & (band < devices - 1)
    tall = BLOCK + 2 * RIM
    sort_copy = pltpu.make_async_copy(sort_in, sort, sort_sem.at[0])
    unsort_copy = pltpu.make_async_copy(unsort_in, unsort, sort_sem.at[1])
    band_lane = iota((1, BAND), 1)
    seg = band_lane // STEP
    lane = iota((1, LANES), 1)

    @pl.when(visit == 0)
    def _():
        sort_copy.start()
        unsort_copy.start()
        tap = band_lane - seg * STEP
        onehot = (tap == iota((TAPS, BAND), 0)) & (seg < GROUPS)
        row_taps[...] = dot_exact(taps[:, 0], onehot.astype(F32), ((1,), (0,)))
        eye = (iota((TAPS, STRIP), 0) == iota((TAPS, STRIP), 1)).astype(F32)
        turned_taps[...] = dot_exact(eye, taps[:, 1], ((0,), (1,)))
        terms[:, tall:] = jnp.zeros((4, TALL - tall, WIDTH), BF16)
        label[...] = jnp.zeros_like(label)

        def clear(p, _):
            seen[p] = 0
            return 0

        lax.fori_loop(0, owner.shape[0], clear, 0)
        sort_copy.wait()

    col_pos = (2.0 * column_at(iota((1, WIDTH), 1)).astype(F32) + 1.0) / WIDTH - 1.0
    raw = jnp.concatenate(
        [jnp.where(has_above, above[0], 0.0), image[0], jnp.where(has_below, below[0], 0.0)],
        axis=0,
    )
    raw_high = raw.astype(BF16)
    raw_low = (raw - raw_high.astype(F32)).astype(BF16)
    sorted_terms = jnp.dot(
        jnp.concatenate([raw_high, raw_low], axis=0), sort[...], preferred_element_type=F32
    )
    high, low = sorted_terms[:tall], sorted_terms[tall:]
    tilted = (high + low) * col_pos
    tilted_high = tilted.astype(BF16)
    terms[0, :tall] = high.astype(BF16)
    terms[1, :tall] = low.astype(BF16)
    terms[2, :tall] = tilted_high
    terms[3, :tall] = (tilted - tilted_high.astype(F32)).astype(BF16)

    lhs = jnp.concatenate(
        [turned_taps[...] * psf[ccd, c, pl.ds(visit, 1), :] for c in range(3)], axis=0
    )
    kernels = dot_exact(lhs, row_taps[...], ((1,), (0,)))
    const, by_row, by_col = (kernels[c * STRIP : (c + 1) * STRIP] for c in range(3))
    is_level = seg < 3
    middle = STRIPS // 2
    per_strip = 2.0 * STRIP / HEIGHT
    middle_row = (top_row + (middle * STRIP - WARP)).astype(F32)
    middle_pos = (2.0 * middle_row + 1.0) / HEIGHT - 1.0
    col_move = (iota((STRIP, 1), 0) - HALF).astype(F32) * (2.0 / WIDTH)
    by_row = jnp.where(is_level, by_row, 0.0)
    const = jnp.where(is_level, const + middle_pos * by_row - col_move * by_col, by_col)
    reach = per_strip * (STRIPS - middle)
    largest = jnp.max(jnp.abs(const) + reach * jnp.abs(by_row), axis=(0, 1), keepdims=True)
    unit = jnp.maximum(largest, 1e-30) * (1.0 / 200.0)
    const = const / unit
    by_row = (by_row * per_strip) / unit
    low_lanes = (lane // STEP) % 3 == 2
    low_band = seg % 3 == 2
    row_part = iota((STRIP, 1), 0).astype(F32) * (1.0 / STRIP)
    for u in range(TAPS):
        at = slice(u * STRIP, (u + 1) * STRIP)
        x = staircase(jnp.broadcast_to(const[u : u + 1], (STRIP, BAND)), 0)
        y = staircase(jnp.broadcast_to(by_row[u : u + 1, :LANES], (STRIP, LANES)), 0)
        tail = x[:, LANES:]
        high = tail.astype(BF16).astype(F32)
        slope[at] = jnp.where(low_band[:, LANES:], tail - high, high).astype(BF16)
        x = x[:, :LANES] + row_part * y
        high = jnp.where(lane < 3 * STEP, jnp.round(x), x.astype(BF16).astype(F32))
        high_level[at] = jnp.where(low_lanes, x - high, high)
        high = jnp.round(y)
        step_level[at] = jnp.where(low_lanes, y - high, high)

    filler = jnp.zeros((BAND - GROUPS * STEP, WIDTH), BF16)
    for k in range(STRIPS):
        level = high_level[...]
        if k != middle:
            level = level + float(k - middle) * step_level[...]
        matrix = jnp.concatenate([level.astype(BF16), slope[...]], axis=1)
        rows = slice(k * STRIP, k * STRIP + STEP)
        columns = jnp.concatenate([terms[h, rows] for h in (0, 1, 0, 2, 3, 2)] + [filler], axis=0)
        results = jnp.dot(matrix, columns, preferred_element_type=F32)
        blocks = lane_sum(
            lambda u, v, w: lane_block(results[u * STRIP : (u + 1) * STRIP], w), lane, TAPS, False
        )
        matched = jnp.concatenate(blocks, axis=1)
        high = matched.astype(BF16)
        at = slice(k * STRIP, (k + 1) * STRIP)
        matched_terms[0, at] = high
        matched_terms[1, at] = (matched - high.astype(F32)).astype(BF16)

    a = jnp.sum(
        jnp.where(iota((1, 1, affine.shape[3]), 2) == ccd, affine[visit], 0.0),
        axis=2, keepdims=True,
    )
    offset = iota((8, LANES), 0) - WARP
    row = (top_row + lane).astype(F32)
    shift = a[0, 0:1] + a[0, 1:2] * (row - (HEIGHT - 1) / 2.0) / HEIGHT
    band_row = lane + offset
    keep = (offset <= WARP) & ((band_row >= 0) | has_above) & ((band_row < BLOCK) | has_below)
    weights = jnp.where(keep, lanczos(shift - offset.astype(F32)), 0.0) * unit
    weights = jnp.concatenate([weights, jnp.zeros((LANES - 8, LANES), F32)], axis=0).T
    empty = jnp.zeros((LANES - WINDOW, WIDTH), BF16)
    halves = []
    for h in range(HALVES):
        matrix = staircase(weights[h * ROWS : (h + 1) * ROWS], 0)
        high = matrix.astype(BF16)
        low = (matrix - high.astype(F32)).astype(BF16)
        rows = slice(h * ROWS, h * ROWS + WINDOW)
        first = jnp.concatenate([matched_terms[0, rows], empty], axis=0)
        second = jnp.concatenate([matched_terms[1, rows], empty], axis=0)
        both = jnp.dot(
            jnp.concatenate([high, high], axis=1), jnp.concatenate([first, second], axis=0),
            preferred_element_type=F32,
        )
        halves.append(both + jnp.dot(low, first, preferred_element_type=F32))
    warped = jnp.concatenate(halves, axis=0)

    lanes = iota((8, WIDTH), 1)
    step = iota((8, WIDTH), 0) - WARP
    block = lanes // LANES
    carry = (block + step + LANE_BLOCKS) // LANE_BLOCKS - 1
    from_lane = lanes % LANES - carry
    col = (from_lane * LANE_BLOCKS + block).astype(F32)
    col_shift = a[1, 0:1] + a[1, 1:2] * (col - (WIDTH - 1) / 2.0) / WIDTH
    within = (from_lane >= 0) & (from_lane < LANES) & (step <= WARP)
    cols = jnp.where(within, lanczos(col_shift - step.astype(F32)), 0.0)
    blocks = lane_sum(
        lambda s, v, w: lane_block(cols[s : s + 1], v) * lane_block(warped, w),
        lane, 2 * WARP + 1, True,
    )

    @pl.when(visit == 0)
    def _():
        unsort_copy.wait()

    result = jnp.dot(
        jnp.concatenate(blocks, axis=1).astype(BF16), unsort[...], preferred_element_type=F32
    ).astype(BF16)

    own = jnp.where(iota(weight.shape, 1) == ccd, weight[...].astype(F32), 0.0)
    own = jnp.where(iota(weight.shape, 0) == visit, own, 0.0)
    own = jnp.sum(own, axis=(0, 1), keepdims=True)
    for j in range(BLKC):
        block = visit * BLKC + j
        ready[block] = result[:, j * BLOCK : (j + 1) * BLOCK]
        p = patch[0, block]
        rank = seen[p]
        seen[p] = rank + 1
        to = out.at[owner[p], pl.ds(pl.multiple_of(rank * BLOCK, BLOCK), BLOCK)]
        pltpu.make_async_copy(ready.at[block], to, sem.at[block]).start()
        line = label[pl.ds(owner[p], 1), :]
        line = jnp.where(lane == rank * 2, own, line)
        label[pl.ds(owner[p], 1), :] = jnp.where(
            lane == rank * 2 + 1, slot[0, block].astype(F32), line
        )

    @pl.when(visit == visits - 1)
    def _():
        label_ready[...] = jnp.broadcast_to(
            label[...].reshape(devices, 1, LANES), (devices, LABEL, LANES)
        ).astype(BF16)
        copy = pltpu.make_async_copy(label_ready, out.at[:, pl.ds(CAP * BLOCK, LABEL)], label_sem)
        copy.start()
        copy.wait()
        for block in range(V * BLKC):
            pltpu.make_async_copy(ready.at[block], out.at[0, pl.ds(0, BLOCK)], sem.at[block]).wait()


def warp(patch, slot, owner, weight, taps, psf, affine, images, above, below, devices):
    smem = pl.BlockSpec(memory_space=pltpu.SMEM)
    hbm = pl.BlockSpec(memory_space=pl.ANY)
    sort = deinterleave()
    taps = taps.transpose(1, 0, 2)
    psf = psf.transpose(1, 3, 0, 2)
    affine = affine.transpose(0, 2, 3, 1)

    def whole(x):
        return pl.BlockSpec(x.shape, lambda v: (0,) * x.ndim)

    def by_visit(x):
        return pl.BlockSpec((1,) + x.shape[1:], lambda v: (v, 0, 0))

    return pl.pallas_call(
        warp_kernel,
        grid=(V,),
        in_specs=[smem, smem, smem, whole(weight), whole(taps), whole(psf), whole(affine)]
        + [hbm, hbm, by_visit(images), by_visit(above), by_visit(below)],
        out_specs=hbm,
        scratch_shapes=[
            pltpu.VMEM((NBASIS, BAND), F32),
            pltpu.VMEM((STRIP, NBASIS), F32),
            pltpu.VMEM((TAPS * STRIP, LANES), F32),
            pltpu.VMEM((TAPS * STRIP, LANES), F32),
            pltpu.VMEM((TAPS * STRIP, BAND - LANES), BF16),
            pltpu.VMEM((4, TALL, WIDTH), BF16),
            pltpu.VMEM((2, STRIPS * STRIP, WIDTH), BF16),
            pltpu.VMEM((V * BLKC, BLOCK, BLOCK), BF16),
            pltpu.SMEM((owner.shape[0],), jnp.int32),
            pltpu.VMEM((devices, LANES), F32),
            pltpu.VMEM((devices, LABEL, LANES), BF16),
            pltpu.VMEM((WIDTH, WIDTH), BF16),
            pltpu.VMEM((WIDTH, WIDTH), BF16),
            pltpu.SemaphoreType.DMA((V * BLKC,)),
            pltpu.SemaphoreType.DMA(()),
            pltpu.SemaphoreType.DMA((2,)),
        ],
        out_shape=jax.ShapeDtypeStruct((devices, CAP * BLOCK + LABEL, BLOCK), BF16),
        compiler_params=pltpu.CompilerParams(vmem_limit_bytes=32 << 20),
        cost_estimate=pl.CostEstimate(
            flops=V * 2 * STRIPS * TAPS * STRIP * BAND * WIDTH,
            bytes_accessed=V * (BLOCK * WIDTH * 6),
            transcendentals=0,
        ),
        name="match_warp",
    )(
        patch, slot, owner, weight, taps, psf, affine,
        jnp.asarray(sort, BF16), jnp.asarray(sort.T, BF16), images, above, below,
    )


def coadd_kernel(got, out, total, table, numbers, sums, sem, out_sem):
    devices = got.shape[0]
    table[...] = got[:, CAP * BLOCK : CAP * BLOCK + LABEL].astype(F32)[:, 0]
    copy = pltpu.make_async_copy(table, numbers, sem)
    copy.start()
    total[...] = jnp.zeros_like(total)
    for c in range(CELLS):
        sums[c] = 0.0
    copy.wait()

    def add(source, _):
        for rank in range(CAP):
            weight = numbers[source, rank * 2]

            @pl.when(weight > 0.0)
            def _(rank=rank, weight=weight):
                c = numbers[source, rank * 2 + 1].astype(jnp.int32)
                sums[c] += weight
                rows = slice(rank * BLOCK, (rank + 1) * BLOCK)
                total[c] += weight * got[source, rows].astype(F32)

        return 0

    lax.fori_loop(0, devices, add, 0, unroll=4)
    copies = []
    for c in range(CELLS):
        inverse = 1.0 / jnp.maximum(jnp.full((1, BLOCK), sums[c], F32), 1.0)
        total[c] = total[c] * inverse
        rows = slice(c // PSIDE * BLOCK, (c // PSIDE + 1) * BLOCK)
        lanes = slice(c % PSIDE * BLOCK, (c % PSIDE + 1) * BLOCK)
        copies.append(pltpu.make_async_copy(total.at[c], out.at[0, rows, lanes], out_sem.at[c]))
        copies[-1].start()
    for copy in copies:
        copy.wait()


def coadd(got):
    devices = got.shape[0]
    return pl.pallas_call(
        coadd_kernel,
        in_specs=[pl.BlockSpec(memory_space=pltpu.VMEM)],
        out_specs=pl.BlockSpec(memory_space=pl.ANY),
        out_shape=jax.ShapeDtypeStruct((1, PSIDE * BLOCK, PSIDE * BLOCK), F32),
        scratch_shapes=[
            pltpu.VMEM((CELLS, BLOCK, BLOCK), F32),
            pltpu.VMEM((devices, LANES), F32),
            pltpu.SMEM((devices, LANES), F32),
            pltpu.SMEM((CELLS,), F32),
            pltpu.SemaphoreType.DMA(()),
            pltpu.SemaphoreType.DMA((CELLS,)),
        ],
        compiler_params=pltpu.CompilerParams(vmem_limit_bytes=32 << 20),
        name="coadd",
    )(got)


def shards(
    images, basis_taps, psf_coef, affine, visit_weight, block_patch, block_slot, patch_owner
):
    devices = lax.axis_size("ccd")
    down = [(i, i + 1) for i in range(devices - 1)]
    up = [(i + 1, i) for i in range(devices - 1)]
    above = lax.ppermute(images[:, BLOCK - RIM :], "ccd", down)
    below = lax.ppermute(images[:, :RIM], "ccd", up)
    patch = block_patch[:, :, 0]
    sent = warp(
        patch, block_slot, patch_owner, visit_weight, basis_taps, psf_coef, affine,
        images, above, below, devices,
    )
    got = lax.all_to_all(sent, "ccd", split_axis=0, concat_axis=0, tiled=True)
    return coadd(got)


def solution(mesh):
    placed = (
        P(None, ("group", "ccd"), None),
        P(),
        P(None, "group", None, None),
        P(None, "group", None, None),
        P(None, "group"),
        P(("group", "ccd"), None, None),
        P(("group", "ccd"), None),
        P("group"),
    )
    return jax.shard_map(
        shards,
        mesh=mesh,
        in_specs=placed,
        out_specs=P(("group", "ccd"), None, None),
        check_vma=False,
    )
```

```python
import functools

import jax
import jax.numpy as jnp
import numpy as np
from jax import lax
from jax.experimental import pallas as pl
from jax.experimental.pallas import tpu as pltpu
from jax.sharding import PartitionSpec as P

V = 4
BLOCK = 128
BLKC = 4
SPLIT = 4
TAPS = 11
NBASIS = 9
PSIDE = 4
CELLS = PSIDE * PSIDE
CAP = 2

HALF = TAPS // 2
WARP = 3
RIM = HALF + WARP
HEIGHT = SPLIT * BLOCK
WIDTH = BLKC * BLOCK
LANES = 128
LANE_BLOCKS = WIDTH // LANES
STRIP = 16
STEP = 32
STRIPS = -(-(BLOCK + 2 * WARP) // STRIP)
MIDDLE = STRIPS // 2
GROUPS = 6
BAND = 256
TALL = (STRIPS - 1) * STRIP + STEP
HALVES = 2
ROWS = BLOCK // HALVES
WINDOW = ROWS + STRIP
LABEL = 16
F32 = jnp.float32
BF16 = jnp.bfloat16


def sin_pi(t):
    whole = jnp.round(t)
    f = t - whole
    odd = whole - 2.0 * jnp.floor(0.5 * whole)
    f2 = f * f
    out = 0.0
    for c in (
        0.00046630280576761, -0.0073704309457144, 0.0821458866111282,
        -0.599264529320792, 2.55016403987734, -5.16771278004997, 3.14159265358979,
    ):
        out = out * f2 + c
    return f * out * (1.0 - 2.0 * odd)


def lanczos(t):
    zero = t == 0.0
    safe = jnp.where(zero, 1.0, t)
    pt = jnp.pi * safe
    value = 3.0 * sin_pi(safe) * sin_pi(safe / 3.0) / (pt * pt)
    return jnp.where(jnp.abs(t) < 3.0, jnp.where(zero, 1.0, value), 0.0)


def iota(shape, dim):
    return lax.broadcasted_iota(jnp.int32, shape, dim)


def deinterleave():
    order = np.arange(WIDTH).reshape(LANES, LANE_BLOCKS).T.reshape(-1)
    return (np.arange(WIDTH)[:, None] == order[None, :]).astype(np.float32)


def column_at(lane):
    return lane % LANES * LANE_BLOCKS + lane // LANES


def lane_block(x, v):
    return x[:, v * LANES : (v + 1) * LANES]


def dot_exact(a, b, dims):
    return lax.dot_general(
        a, b, (dims, ((), ())), precision=lax.Precision.HIGHEST, preferred_element_type=F32
    )


def staircase(x, first):
    return jnp.concatenate(
        [
            pltpu.roll(x[g : g + 8], first + g, 1, stride=1, stride_axis=0)
            for g in range(0, x.shape[0], 8)
        ],
        axis=0,
    )


def lane_sum(terms_of, lane, count, weigh):
    blocks = []
    for v in range(LANE_BLOCKS):
        total = None
        half = count // 2
        for q in range(-(-half // LANE_BLOCKS) * -1, (half + LANE_BLOCKS - 1) // LANE_BLOCKS + 1):
            part = None
            for u in range(count):
                if (v + u - half) // LANE_BLOCKS != q:
                    continue
                piece = terms_of(u, v, (v + u - half) % LANE_BLOCKS)
                part = piece if part is None else part + piece
            if part is None:
                continue
            if q:
                part = pltpu.roll(part, -q % LANES, 1)
                if not weigh:
                    part = jnp.where((lane + q >= 0) & (lane + q < LANES), part, 0.0)
            total = part if total is None else total + part
        blocks.append(total)
    return blocks


def whereabouts(devices):
    band = lax.axis_index("ccd")
    quarter = (band + SPLIT // 2) % SPLIT
    has_above = (quarter > 0) & (band > 0)
    has_below = (quarter < SPLIT - 1) & (band < devices - 1)
    return (band + SPLIT // 2) // SPLIT, quarter * BLOCK, has_above, has_below


def prepare_kernel(devices, taps, psf, affine, high_level, step_level, slope, rows_high, rows_low, cols_out):
    ccd, top_row, has_above, has_below = whereabouts(devices)
    band_lane = iota((1, BAND), 1)
    seg = band_lane // STEP
    lane = iota((1, LANES), 1)
    tap = band_lane - seg * STEP
    onehot = (tap == iota((TAPS, BAND), 0)) & (seg < GROUPS)
    row_taps = dot_exact(taps[:, 0], onehot.astype(F32), ((1,), (0,)))
    eye = (iota((TAPS, STRIP), 0) == iota((TAPS, STRIP), 1)).astype(F32)
    turned_taps = dot_exact(eye, taps[:, 1], ((0,), (1,)))
    for visit in range(V):
        lhs = jnp.concatenate(
            [turned_taps * psf[ccd, c, visit : visit + 1, :] for c in range(3)], axis=0
        )
        kernels = dot_exact(lhs, row_taps, ((1,), (0,)))
        const, by_row, by_col = (kernels[c * STRIP : (c + 1) * STRIP] for c in range(3))
        is_level = seg < 3
        per_strip = 2.0 * STRIP / HEIGHT
        middle_row = (top_row + (MIDDLE * STRIP - WARP)).astype(F32)
        middle_pos = (2.0 * middle_row + 1.0) / HEIGHT - 1.0
        col_move = (iota((STRIP, 1), 0) - HALF).astype(F32) * (2.0 / WIDTH)
        by_row = jnp.where(is_level, by_row, 0.0)
        const = jnp.where(is_level, const + middle_pos * by_row - col_move * by_col, by_col)
        reach = per_strip * (STRIPS - MIDDLE)
        largest = jnp.max(jnp.abs(const) + reach * jnp.abs(by_row), axis=(0, 1), keepdims=True)
        unit = jnp.maximum(largest, 1e-30) * (1.0 / 200.0)
        const = const / unit
        by_row = (by_row * per_strip) / unit
        low_lanes = (lane // STEP) % 3 == 2
        low_band = seg % 3 == 2
        row_part = iota((STRIP, 1), 0).astype(F32) * (1.0 / STRIP)
        for u in range(TAPS):
            at = slice(u * STRIP, (u + 1) * STRIP)
            x = staircase(jnp.broadcast_to(const[u : u + 1], (STRIP, BAND)), 0)
            y = staircase(jnp.broadcast_to(by_row[u : u + 1, :LANES], (STRIP, LANES)), 0)
            tail = x[:, LANES:]
            high = tail.astype(BF16).astype(F32)
            slope[visit, at] = jnp.where(low_band[:, LANES:], tail - high, high).astype(BF16)
            x = x[:, :LANES] + row_part * y
            high = jnp.where(lane < 3 * STEP, jnp.round(x), x.astype(BF16).astype(F32))
            high_level[visit, at] = jnp.where(low_lanes, x - high, high)
            high = jnp.round(y)
            step_level[visit, at] = jnp.where(low_lanes, y - high, high)

        a = jnp.sum(
            jnp.where(iota((1, 1, affine.shape[3]), 2) == ccd, affine[visit], 0.0),
            axis=2, keepdims=True,
        )
        offset = iota((8, LANES), 0) - WARP
        row = (top_row + lane).astype(F32)
        shift = a[0, 0:1] + a[0, 1:2] * (row - (HEIGHT - 1) / 2.0) / HEIGHT
        band_row = lane + offset
        keep = (offset <= WARP) & ((band_row >= 0) | has_above) & ((band_row < BLOCK) | has_below)
        weights = jnp.where(keep, lanczos(shift - offset.astype(F32)), 0.0) * unit
        weights = jnp.concatenate([weights, jnp.zeros((LANES - 8, LANES), F32)], axis=0).T
        for h in range(HALVES):
            at = slice(h * ROWS, (h + 1) * ROWS)
            matrix = staircase(weights[at], 0)
            high = matrix.astype(BF16)
            rows_high[visit, at] = high
            rows_low[visit, at] = (matrix - high.astype(F32)).astype(BF16)

        lanes = iota((8, WIDTH), 1)
        step = iota((8, WIDTH), 0) - WARP
        block = lanes // LANES
        carry = (block + step + LANE_BLOCKS) // LANE_BLOCKS - 1
        from_lane = lanes % LANES - carry
        col = (from_lane * LANE_BLOCKS + block).astype(F32)
        col_shift = a[1, 0:1] + a[1, 1:2] * (col - (WIDTH - 1) / 2.0) / WIDTH
        within = (from_lane >= 0) & (from_lane < LANES) & (step <= WARP)
        cols_out[visit] = jnp.where(within, lanczos(col_shift - step.astype(F32)), 0.0)


def prepare(taps, psf, affine, devices):
    shapes = [
        ((V, TAPS * STRIP, LANES), F32),
        ((V, TAPS * STRIP, LANES), F32),
        ((V, TAPS * STRIP, BAND - LANES), BF16),
        ((V, BLOCK, LANES), BF16),
        ((V, BLOCK, LANES), BF16),
        ((V, 8, WIDTH), F32),
    ]
    args = [taps.transpose(1, 0, 2), psf.transpose(1, 3, 0, 2), affine.transpose(0, 2, 3, 1)]
    return pl.pallas_call(
        functools.partial(prepare_kernel, devices),
        grid=(1,),
        in_specs=[pl.BlockSpec(x.shape, lambda i, n=x.ndim: (0,) * n) for x in args],
        out_specs=[pl.BlockSpec(shape, lambda i: (0, 0, 0)) for shape, _ in shapes],
        out_shape=[jax.ShapeDtypeStruct(shape, kind) for shape, kind in shapes],
        compiler_params=pltpu.CompilerParams(vmem_limit_bytes=32 << 20),
        cost_estimate=pl.CostEstimate(flops=1 << 30, bytes_accessed=1 << 20, transcendentals=0),
        name="prepare",
    )(*args)


def warp_kernel(
    patch, slot, owner, weight, high_level, step_level, slope, rows_high, rows_low, col_weights,
    sort, unsort, image, above, below, out,
    terms, matched_terms, ready, seen, label, label_ready, sem, label_sem,
):
    visit = pl.program_id(0)
    visits = pl.num_programs(0)
    devices = label.shape[0]
    ccd, _, has_above, has_below = whereabouts(devices)
    tall = BLOCK + 2 * RIM
    lane = iota((1, LANES), 1)

    @pl.when(visit == 0)
    def _():
        terms[:, tall:] = jnp.zeros((4, TALL - tall, WIDTH), BF16)
        label[...] = jnp.zeros_like(label)

        def clear(p, _):
            seen[p] = 0
            return 0

        lax.fori_loop(0, owner.shape[0], clear, 0)

    col_pos = (2.0 * column_at(iota((1, WIDTH), 1)).astype(F32) + 1.0) / WIDTH - 1.0
    raw = jnp.concatenate(
        [jnp.where(has_above, above[0], 0.0), image[0], jnp.where(has_below, below[0], 0.0)],
        axis=0,
    )
    raw_high = raw.astype(BF16)
    raw_low = (raw - raw_high.astype(F32)).astype(BF16)
    sorted_terms = jnp.dot(
        jnp.concatenate([raw_high, raw_low], axis=0), sort[...], preferred_element_type=F32
    )
    high, low = sorted_terms[:tall], sorted_terms[tall:]
    tilted = (high + low) * col_pos
    tilted_high = tilted.astype(BF16)
    terms[0, :tall] = high.astype(BF16)
    terms[1, :tall] = low.astype(BF16)
    terms[2, :tall] = tilted_high
    terms[3, :tall] = (tilted - tilted_high.astype(F32)).astype(BF16)

    filler = jnp.zeros((BAND - GROUPS * STEP, WIDTH), BF16)
    for k in range(STRIPS):
        level = high_level[0]
        if k != MIDDLE:
            level = level + float(k - MIDDLE) * step_level[0]
        matrix = jnp.concatenate([level.astype(BF16), slope[0]], axis=1)
        rows = slice(k * STRIP, k * STRIP + STEP)
        columns = jnp.concatenate([terms[h, rows] for h in (0, 1, 0, 2, 3, 2)] + [filler], axis=0)
        results = jnp.dot(matrix, columns, preferred_element_type=F32)
        blocks = lane_sum(
            lambda u, v, w: lane_block(results[u * STRIP : (u + 1) * STRIP], w), lane, TAPS, False
        )
        matched = jnp.concatenate(blocks, axis=1)
        high = matched.astype(BF16)
        at = slice(k * STRIP, (k + 1) * STRIP)
        matched_terms[0, at] = high
        matched_terms[1, at] = (matched - high.astype(F32)).astype(BF16)

    empty = jnp.zeros((LANES - WINDOW, WIDTH), BF16)
    halves = []
    for h in range(HALVES):
        high = rows_high[0, h * ROWS : (h + 1) * ROWS]
        low = rows_low[0, h * ROWS : (h + 1) * ROWS]
        rows = slice(h * ROWS, h * ROWS + WINDOW)
        first = jnp.concatenate([matched_terms[0, rows], empty], axis=0)
        second = jnp.concatenate([matched_terms[1, rows], empty], axis=0)
        both = jnp.dot(
            jnp.concatenate([high, high], axis=1), jnp.concatenate([first, second], axis=0),
            preferred_element_type=F32,
        )
        halves.append(both + jnp.dot(low, first, preferred_element_type=F32))
    warped = jnp.concatenate(halves, axis=0)

    cols = col_weights[0]
    blocks = lane_sum(
        lambda s, v, w: lane_block(cols[s : s + 1], v) * lane_block(warped, w),
        lane, 2 * WARP + 1, True,
    )

    result = jnp.dot(
        jnp.concatenate(blocks, axis=1).astype(BF16), unsort[...], preferred_element_type=F32
    ).astype(BF16)

    own = jnp.where(iota(weight.shape, 1) == ccd, weight[...].astype(F32), 0.0)
    own = jnp.where(iota(weight.shape, 0) == visit, own, 0.0)
    own = jnp.sum(own, axis=(0, 1), keepdims=True)
    for j in range(BLKC):
        block = visit * BLKC + j
        ready[block] = result[:, j * BLOCK : (j + 1) * BLOCK]
        p = patch[0, block]
        rank = seen[p]
        seen[p] = rank + 1
        to = out.at[owner[p], pl.ds(pl.multiple_of(rank * BLOCK, BLOCK), BLOCK)]
        pltpu.make_async_copy(ready.at[block], to, sem.at[block]).start()
        line = label[pl.ds(owner[p], 1), :]
        line = jnp.where(lane == rank * 2, own, line)
        label[pl.ds(owner[p], 1), :] = jnp.where(
            lane == rank * 2 + 1, slot[0, block].astype(F32), line
        )

    @pl.when(visit == visits - 1)
    def _():
        label_ready[...] = jnp.broadcast_to(
            label[...].reshape(devices, 1, LANES), (devices, LABEL, LANES)
        ).astype(BF16)
        copy = pltpu.make_async_copy(label_ready, out.at[:, pl.ds(CAP * BLOCK, LABEL)], label_sem)
        copy.start()
        copy.wait()
        for block in range(V * BLKC):
            pltpu.make_async_copy(ready.at[block], out.at[0, pl.ds(0, BLOCK)], sem.at[block]).wait()


def warp(patch, slot, owner, weight, ready, images, above, below, devices):
    smem = pl.BlockSpec(memory_space=pltpu.SMEM)
    hbm = pl.BlockSpec(memory_space=pl.ANY)
    sort = deinterleave()
    constants = [jnp.asarray(sort, BF16), jnp.asarray(sort.T, BF16)]

    def whole(x):
        return pl.BlockSpec(x.shape, lambda v: (0,) * x.ndim)

    def by_visit(x):
        return pl.BlockSpec((1,) + x.shape[1:], lambda v: (v, 0, 0))

    return pl.pallas_call(
        warp_kernel,
        grid=(V,),
        in_specs=[smem, smem, smem, whole(weight)]
        + [by_visit(x) for x in ready]
        + [whole(x) for x in constants]
        + [by_visit(x) for x in (images, above, below)],
        out_specs=hbm,
        scratch_shapes=[
            pltpu.VMEM((4, TALL, WIDTH), BF16),
            pltpu.VMEM((2, STRIPS * STRIP, WIDTH), BF16),
            pltpu.VMEM((V * BLKC, BLOCK, BLOCK), BF16),
            pltpu.SMEM((owner.shape[0],), jnp.int32),
            pltpu.VMEM((devices, LANES), F32),
            pltpu.VMEM((devices, LABEL, LANES), BF16),
            pltpu.SemaphoreType.DMA((V * BLKC,)),
            pltpu.SemaphoreType.DMA(()),
        ],
        out_shape=jax.ShapeDtypeStruct((devices, CAP * BLOCK + LABEL, BLOCK), BF16),
        compiler_params=pltpu.CompilerParams(vmem_limit_bytes=32 << 20),
        cost_estimate=pl.CostEstimate(
            flops=V * 2 * STRIPS * TAPS * STRIP * BAND * WIDTH,
            bytes_accessed=V * (BLOCK * WIDTH * 6),
            transcendentals=0,
        ),
        name="match_warp",
    )(patch, slot, owner, weight, *ready, *constants, images, above, below)


def coadd_kernel(got, out, total, table, numbers, sums, sem, out_sem):
    devices = got.shape[0]
    table[...] = got[:, CAP * BLOCK : CAP * BLOCK + LABEL].astype(F32)[:, 0]
    copy = pltpu.make_async_copy(table, numbers, sem)
    copy.start()
    total[...] = jnp.zeros_like(total)
    for c in range(CELLS):
        sums[c] = 0.0
    copy.wait()

    def add(source, _):
        for rank in range(CAP):
            weight = numbers[source, rank * 2]

            @pl.when(weight > 0.0)
            def _(rank=rank, weight=weight):
                c = numbers[source, rank * 2 + 1].astype(jnp.int32)
                sums[c] += weight
                rows = slice(rank * BLOCK, (rank + 1) * BLOCK)
                total[c] += weight * got[source, rows].astype(F32)

        return 0

    lax.fori_loop(0, devices, add, 0, unroll=4)
    copies = []
    for c in range(CELLS):
        inverse = 1.0 / jnp.maximum(jnp.full((1, BLOCK), sums[c], F32), 1.0)
        total[c] = total[c] * inverse
        rows = slice(c // PSIDE * BLOCK, (c // PSIDE + 1) * BLOCK)
        lanes = slice(c % PSIDE * BLOCK, (c % PSIDE + 1) * BLOCK)
        copies.append(pltpu.make_async_copy(total.at[c], out.at[0, rows, lanes], out_sem.at[c]))
        copies[-1].start()
    for copy in copies:
        copy.wait()


def coadd(got):
    devices = got.shape[0]
    return pl.pallas_call(
        coadd_kernel,
        in_specs=[pl.BlockSpec(memory_space=pltpu.VMEM)],
        out_specs=pl.BlockSpec(memory_space=pl.ANY),
        out_shape=jax.ShapeDtypeStruct((1, PSIDE * BLOCK, PSIDE * BLOCK), F32),
        scratch_shapes=[
            pltpu.VMEM((CELLS, BLOCK, BLOCK), F32),
            pltpu.VMEM((devices, LANES), F32),
            pltpu.SMEM((devices, LANES), F32),
            pltpu.SMEM((CELLS,), F32),
            pltpu.SemaphoreType.DMA(()),
            pltpu.SemaphoreType.DMA((CELLS,)),
        ],
        compiler_params=pltpu.CompilerParams(vmem_limit_bytes=32 << 20),
        name="coadd",
    )(got)


def shards(
    images, basis_taps, psf_coef, affine, visit_weight, block_patch, block_slot, patch_owner
):
    devices = lax.axis_size("ccd")
    down = [(i, i + 1) for i in range(devices - 1)]
    up = [(i + 1, i) for i in range(devices - 1)]
    above = lax.ppermute(images[:, BLOCK - RIM :], "ccd", down)
    below = lax.ppermute(images[:, :RIM], "ccd", up)
    patch = block_patch[:, :, 0]
    ready = prepare(basis_taps, psf_coef, affine, devices)
    sent = warp(
        patch, block_slot, patch_owner, visit_weight, ready, images, above, below, devices
    )
    got = lax.all_to_all(sent, "ccd", split_axis=0, concat_axis=0, tiled=True)
    return coadd(got)


def solution(mesh):
    placed = (
        P(None, ("group", "ccd"), None),
        P(),
        P(None, "group", None, None),
        P(None, "group", None, None),
        P(None, "group"),
        P(("group", "ccd"), None, None),
        P(("group", "ccd"), None),
        P("group"),
    )
    return jax.shard_map(
        shards,
        mesh=mesh,
        in_specs=placed,
        out_specs=P(("group", "ccd"), None, None),
        check_vma=False,
    )
```

```python
import functools

import jax
import jax.numpy as jnp
import numpy as np
from jax import lax
from jax.experimental import pallas as pl
from jax.experimental.pallas import tpu as pltpu
from jax.sharding import PartitionSpec as P

V = 4
BLOCK = 128
BLKC = 4
SPLIT = 4
TAPS = 11
NBASIS = 9
PSIDE = 4
CELLS = PSIDE * PSIDE
CAP = 2

HALF = TAPS // 2
WARP = 3
RIM = HALF + WARP
HEIGHT = SPLIT * BLOCK
WIDTH = BLKC * BLOCK
LANES = 128
LANE_BLOCKS = WIDTH // LANES
STRIP = 16
STEP = 32
STRIPS = -(-(BLOCK + 2 * WARP) // STRIP)
MIDDLE = STRIPS // 2
GROUPS = 6
BAND = 256
TALL = (STRIPS - 1) * STRIP + STEP
HALVES = 2
TOGETHER = 2
ROWS = BLOCK // HALVES
WINDOW = ROWS + STRIP
LABEL = 16
F32 = jnp.float32
BF16 = jnp.bfloat16


def sin_pi(t):
    whole = jnp.round(t)
    f = t - whole
    odd = whole - 2.0 * jnp.floor(0.5 * whole)
    f2 = f * f
    out = 0.0
    for c in (
        0.00046630280576761, -0.0073704309457144, 0.0821458866111282,
        -0.599264529320792, 2.55016403987734, -5.16771278004997, 3.14159265358979,
    ):
        out = out * f2 + c
    return f * out * (1.0 - 2.0 * odd)


def lanczos(t):
    zero = t == 0.0
    safe = jnp.where(zero, 1.0, t)
    pt = jnp.pi * safe
    value = 3.0 * sin_pi(safe) * sin_pi(safe / 3.0) / (pt * pt)
    return jnp.where(jnp.abs(t) < 3.0, jnp.where(zero, 1.0, value), 0.0)


def iota(shape, dim):
    return lax.broadcasted_iota(jnp.int32, shape, dim)


def deinterleave():
    order = np.arange(WIDTH).reshape(LANES, LANE_BLOCKS).T.reshape(-1)
    return (np.arange(WIDTH)[:, None] == order[None, :]).astype(np.float32)


def column_at(lane):
    return lane % LANES * LANE_BLOCKS + lane // LANES


def lane_block(x, v):
    return x[:, v * LANES : (v + 1) * LANES]


def dot_exact(a, b, dims):
    return lax.dot_general(
        a, b, (dims, ((), ())), precision=lax.Precision.HIGHEST, preferred_element_type=F32
    )


def staircase(x, first):
    return jnp.concatenate(
        [
            pltpu.roll(x[g : g + 8], first + g, 1, stride=1, stride_axis=0)
            for g in range(0, x.shape[0], 8)
        ],
        axis=0,
    )


def lane_sum(terms_of, lane, count, weigh):
    blocks = []
    for v in range(LANE_BLOCKS):
        total = None
        half = count // 2
        for q in range(-(-half // LANE_BLOCKS) * -1, (half + LANE_BLOCKS - 1) // LANE_BLOCKS + 1):
            part = None
            for u in range(count):
                if (v + u - half) // LANE_BLOCKS != q:
                    continue
                piece = terms_of(u, v, (v + u - half) % LANE_BLOCKS)
                part = piece if part is None else part + piece
            if part is None:
                continue
            if q:
                part = pltpu.roll(part, -q % LANES, 1)
                if not weigh:
                    part = jnp.where((lane + q >= 0) & (lane + q < LANES), part, 0.0)
            total = part if total is None else total + part
        blocks.append(total)
    return blocks


def whereabouts(devices):
    band = lax.axis_index("ccd")
    quarter = (band + SPLIT // 2) % SPLIT
    has_above = (quarter > 0) & (band > 0)
    has_below = (quarter < SPLIT - 1) & (band < devices - 1)
    return (band + SPLIT // 2) // SPLIT, quarter * BLOCK, has_above, has_below


def prepare_kernel(devices, taps, psf, affine, high_level, step_level, slope, rows_high, rows_low, cols_out):
    ccd, top_row, has_above, has_below = whereabouts(devices)
    band_lane = iota((1, BAND), 1)
    seg = band_lane // STEP
    lane = iota((1, LANES), 1)
    tap = band_lane - seg * STEP
    onehot = (tap == iota((TAPS, BAND), 0)) & (seg < GROUPS)
    row_taps = dot_exact(taps[:, 0], onehot.astype(F32), ((1,), (0,)))
    eye = (iota((TAPS, STRIP), 0) == iota((TAPS, STRIP), 1)).astype(F32)
    turned_taps = dot_exact(eye, taps[:, 1], ((0,), (1,)))
    for visit in range(V):
        lhs = jnp.concatenate(
            [turned_taps * psf[ccd, c, visit : visit + 1, :] for c in range(3)], axis=0
        )
        kernels = dot_exact(lhs, row_taps, ((1,), (0,)))
        const, by_row, by_col = (kernels[c * STRIP : (c + 1) * STRIP] for c in range(3))
        is_level = seg < 3
        per_strip = 2.0 * STRIP / HEIGHT
        middle_row = (top_row + (MIDDLE * STRIP - WARP)).astype(F32)
        middle_pos = (2.0 * middle_row + 1.0) / HEIGHT - 1.0
        col_move = (iota((STRIP, 1), 0) - HALF).astype(F32) * (2.0 / WIDTH)
        by_row = jnp.where(is_level, by_row, 0.0)
        const = jnp.where(is_level, const + middle_pos * by_row - col_move * by_col, by_col)
        reach = per_strip * (STRIPS - MIDDLE)
        largest = jnp.max(jnp.abs(const) + reach * jnp.abs(by_row), axis=(0, 1), keepdims=True)
        unit = jnp.maximum(largest, 1e-30) * (1.0 / 200.0)
        const = const / unit
        by_row = (by_row * per_strip) / unit
        low_lanes = (lane // STEP) % 3 == 2
        low_band = seg % 3 == 2
        row_part = iota((STRIP, 1), 0).astype(F32) * (1.0 / STRIP)
        for u in range(TAPS):
            at = slice(u * STRIP, (u + 1) * STRIP)
            x = staircase(jnp.broadcast_to(const[u : u + 1], (STRIP, BAND)), 0)
            y = staircase(jnp.broadcast_to(by_row[u : u + 1, :LANES], (STRIP, LANES)), 0)
            tail = x[:, LANES:]
            high = tail.astype(BF16).astype(F32)
            slope[visit, at] = jnp.where(low_band[:, LANES:], tail - high, high).astype(BF16)
            x = x[:, :LANES] + row_part * y
            high = jnp.where(lane < 3 * STEP, jnp.round(x), x.astype(BF16).astype(F32))
            high_level[visit, at] = jnp.where(low_lanes, x - high, high)
            high = jnp.round(y)
            step_level[visit, at] = jnp.where(low_lanes, y - high, high)

        a = jnp.sum(
            jnp.where(iota((1, 1, affine.shape[3]), 2) == ccd, affine[visit], 0.0),
            axis=2, keepdims=True,
        )
        offset = iota((8, LANES), 0) - WARP
        row = (top_row + lane).astype(F32)
        shift = a[0, 0:1] + a[0, 1:2] * (row - (HEIGHT - 1) / 2.0) / HEIGHT
        band_row = lane + offset
        keep = (offset <= WARP) & ((band_row >= 0) | has_above) & ((band_row < BLOCK) | has_below)
        weights = jnp.where(keep, lanczos(shift - offset.astype(F32)), 0.0) * unit
        weights = jnp.concatenate([weights, jnp.zeros((LANES - 8, LANES), F32)], axis=0).T
        for h in range(HALVES):
            at = slice(h * ROWS, (h + 1) * ROWS)
            matrix = staircase(weights[at], 0)
            high = matrix.astype(BF16)
            rows_high[visit, at] = high
            rows_low[visit, at] = (matrix - high.astype(F32)).astype(BF16)

        lanes = iota((8, WIDTH), 1)
        step = iota((8, WIDTH), 0) - WARP
        block = lanes // LANES
        carry = (block + step + LANE_BLOCKS) // LANE_BLOCKS - 1
        from_lane = lanes % LANES - carry
        col = (from_lane * LANE_BLOCKS + block).astype(F32)
        col_shift = a[1, 0:1] + a[1, 1:2] * (col - (WIDTH - 1) / 2.0) / WIDTH
        within = (from_lane >= 0) & (from_lane < LANES) & (step <= WARP)
        cols_out[visit] = jnp.where(within, lanczos(col_shift - step.astype(F32)), 0.0)


def prepare(taps, psf, affine, devices):
    shapes = [
        ((V, TAPS * STRIP, LANES), F32),
        ((V, TAPS * STRIP, LANES), F32),
        ((V, TAPS * STRIP, BAND - LANES), BF16),
        ((V, BLOCK, LANES), BF16),
        ((V, BLOCK, LANES), BF16),
        ((V, 8, WIDTH), F32),
    ]
    args = [taps.transpose(1, 0, 2), psf.transpose(1, 3, 0, 2), affine.transpose(0, 2, 3, 1)]
    return pl.pallas_call(
        functools.partial(prepare_kernel, devices),
        grid=(1,),
        in_specs=[pl.BlockSpec(x.shape, lambda i, n=x.ndim: (0,) * n) for x in args],
        out_specs=[pl.BlockSpec(shape, lambda i: (0, 0, 0)) for shape, _ in shapes],
        out_shape=[jax.ShapeDtypeStruct(shape, kind) for shape, kind in shapes],
        compiler_params=pltpu.CompilerParams(vmem_limit_bytes=32 << 20),
        cost_estimate=pl.CostEstimate(flops=1 << 30, bytes_accessed=1 << 20, transcendentals=0),
        name="prepare",
    )(*args)


def warp_kernel(
    patch, slot, owner, weight, high_level, step_level, slope, rows_high, rows_low, col_weights,
    sort, unsort, image, above, below, out,
    terms, matched_terms, ready, place_of, seen, label, label_ready, sem, label_sem,
):
    grid_step = pl.program_id(0)
    grid_steps = pl.num_programs(0)
    devices = label.shape[0]
    ccd, _, has_above, has_below = whereabouts(devices)
    tall = BLOCK + 2 * RIM
    lane = iota((1, LANES), 1)
    label_copy = pltpu.make_async_copy(label_ready, out.at[:, pl.ds(CAP * BLOCK, LABEL)], label_sem)

    @pl.when(grid_step == 0)
    def _():
        terms[:, :, tall:] = jnp.zeros((TOGETHER, 4, TALL - tall, WIDTH), BF16)
        label[...] = jnp.zeros_like(label)

        def clear(p, _):
            seen[p] = 0
            return 0

        lax.fori_loop(0, owner.shape[0], clear, 0)
        own = jnp.where(iota(weight.shape, 1) == ccd, weight[...].astype(F32), 0.0)
        own = jnp.sum(own, axis=1, keepdims=True)
        for block in range(V * BLKC):
            p = patch[0, block]
            to = owner[p]
            rank = seen[p]
            seen[p] = rank + 1
            place_of[block] = to * CAP + rank
            line = label[pl.ds(to, 1), :]
            line = jnp.where(lane == rank * 2, own[block // BLKC : block // BLKC + 1], line)
            line = jnp.where(lane == rank * 2 + 1, slot[0, block].astype(F32), line)
            label[pl.ds(to, 1), :] = line
        label_ready[...] = jnp.broadcast_to(
            label[...].reshape(devices, 1, LANES), (devices, LABEL, LANES)
        ).astype(BF16)
        label_copy.start()

    col_pos = (2.0 * column_at(iota((1, WIDTH), 1)).astype(F32) + 1.0) / WIDTH - 1.0
    for i in range(TOGETHER):
        raw = jnp.concatenate(
            [jnp.where(has_above, above[i], 0.0), image[i], jnp.where(has_below, below[i], 0.0)],
            axis=0,
        )
        raw_high = raw.astype(BF16)
        raw_low = (raw - raw_high.astype(F32)).astype(BF16)
        sorted_terms = jnp.dot(
            jnp.concatenate([raw_high, raw_low], axis=0), sort[...], preferred_element_type=F32
        )
        high, low = sorted_terms[:tall], sorted_terms[tall:]
        tilted = (high + low) * col_pos
        tilted_high = tilted.astype(BF16)
        terms[i, 0, :tall] = high.astype(BF16)
        terms[i, 1, :tall] = low.astype(BF16)
        terms[i, 2, :tall] = tilted_high
        terms[i, 3, :tall] = (tilted - tilted_high.astype(F32)).astype(BF16)

    filler = jnp.zeros((BAND - GROUPS * STEP, WIDTH), BF16)
    for k in range(STRIPS):
        for i in range(TOGETHER):
            level = high_level[i]
            if k != MIDDLE:
                level = level + float(k - MIDDLE) * step_level[i]
            matrix = jnp.concatenate([level.astype(BF16), slope[i]], axis=1)
            rows = slice(k * STRIP, k * STRIP + STEP)
            columns = jnp.concatenate(
                [terms[i, h, rows] for h in (0, 1, 0, 2, 3, 2)] + [filler], axis=0
            )
            results = jnp.dot(matrix, columns, preferred_element_type=F32)
            blocks = lane_sum(
                lambda u, v, w: lane_block(results[u * STRIP : (u + 1) * STRIP], w),
                lane, TAPS, False,
            )
            matched = jnp.concatenate(blocks, axis=1)
            high = matched.astype(BF16)
            at = slice(k * STRIP, (k + 1) * STRIP)
            matched_terms[i, 0, at] = high
            matched_terms[i, 1, at] = (matched - high.astype(F32)).astype(BF16)

    empty = jnp.zeros((LANES - WINDOW, WIDTH), BF16)
    warped = []
    for i in range(TOGETHER):
        halves = []
        for h in range(HALVES):
            high = rows_high[i, h * ROWS : (h + 1) * ROWS]
            low = rows_low[i, h * ROWS : (h + 1) * ROWS]
            rows = slice(h * ROWS, h * ROWS + WINDOW)
            first = jnp.concatenate([matched_terms[i, 0, rows], empty], axis=0)
            second = jnp.concatenate([matched_terms[i, 1, rows], empty], axis=0)
            both = jnp.dot(
                jnp.concatenate([high, high], axis=1), jnp.concatenate([first, second], axis=0),
                preferred_element_type=F32,
            )
            halves.append(both + jnp.dot(low, first, preferred_element_type=F32))
        warped.append(jnp.concatenate(halves, axis=0))

    for i in range(TOGETHER):
        cols = col_weights[i]
        blocks = lane_sum(
            lambda s, v, w: lane_block(cols[s : s + 1], v) * lane_block(warped[i], w),
            lane, 2 * WARP + 1, True,
        )
        result = jnp.dot(
            jnp.concatenate(blocks, axis=1).astype(BF16), unsort[...], preferred_element_type=F32
        ).astype(BF16)
        for j in range(BLKC):
            block = (grid_step * TOGETHER + i) * BLKC + j
            ready[block] = result[:, j * BLOCK : (j + 1) * BLOCK]
            to = place_of[block]
            row = pl.multiple_of(to % CAP * BLOCK, BLOCK)
            pltpu.make_async_copy(
                ready.at[block], out.at[to // CAP, pl.ds(row, BLOCK)], sem.at[block]
            ).start()

    @pl.when(grid_step == grid_steps - 1)
    def _():
        label_copy.wait()
        for block in range(V * BLKC):
            pltpu.make_async_copy(ready.at[block], out.at[0, pl.ds(0, BLOCK)], sem.at[block]).wait()


def warp(patch, slot, owner, weight, ready, images, above, below, devices):
    smem = pl.BlockSpec(memory_space=pltpu.SMEM)
    hbm = pl.BlockSpec(memory_space=pl.ANY)
    sort = deinterleave()
    constants = [jnp.asarray(sort, BF16), jnp.asarray(sort.T, BF16)]

    def whole(x):
        return pl.BlockSpec(x.shape, lambda v: (0,) * x.ndim)

    def by_visit(x):
        return pl.BlockSpec((TOGETHER,) + x.shape[1:], lambda v: (v, 0, 0))

    return pl.pallas_call(
        warp_kernel,
        grid=(V // TOGETHER,),
        in_specs=[smem, smem, smem, whole(weight)]
        + [by_visit(x) for x in ready]
        + [whole(x) for x in constants]
        + [by_visit(x) for x in (images, above, below)],
        out_specs=hbm,
        scratch_shapes=[
            pltpu.VMEM((TOGETHER, 4, TALL, WIDTH), BF16),
            pltpu.VMEM((TOGETHER, 2, STRIPS * STRIP, WIDTH), BF16),
            pltpu.VMEM((V * BLKC, BLOCK, BLOCK), BF16),
            pltpu.SMEM((V * BLKC,), jnp.int32),
            pltpu.SMEM((owner.shape[0],), jnp.int32),
            pltpu.VMEM((devices, LANES), F32),
            pltpu.VMEM((devices, LABEL, LANES), BF16),
            pltpu.SemaphoreType.DMA((V * BLKC,)),
            pltpu.SemaphoreType.DMA(()),
        ],
        out_shape=jax.ShapeDtypeStruct((devices, CAP * BLOCK + LABEL, BLOCK), BF16),
        compiler_params=pltpu.CompilerParams(vmem_limit_bytes=32 << 20),
        cost_estimate=pl.CostEstimate(
            flops=V * 2 * STRIPS * TAPS * STRIP * BAND * WIDTH,
            bytes_accessed=V * (BLOCK * WIDTH * 6),
            transcendentals=0,
        ),
        name="match_warp",
    )(patch, slot, owner, weight, *ready, *constants, images, above, below)


def coadd_kernel(got, out, total, sums, out_sem):
    devices = got.shape[0]
    labels = got[:, CAP * BLOCK : CAP * BLOCK + LABEL].astype(F32)[:, 0]
    total[...] = jnp.zeros_like(total)
    for c in range(CELLS):
        sums[c] = 0.0
    for source in range(devices):
        for rank in range(CAP):
            weight = labels[source, rank * 2]

            @pl.when(weight > 0.0)
            def _(source=source, rank=rank, weight=weight):
                c = labels[source, rank * 2 + 1].astype(jnp.int32)
                sums[c] += weight
                rows = slice(rank * BLOCK, (rank + 1) * BLOCK)
                total[c] += weight * got[source, rows].astype(F32)

    copies = []
    for c in range(CELLS):
        inverse = 1.0 / jnp.maximum(jnp.full((1, BLOCK), sums[c], F32), 1.0)
        total[c] = total[c] * inverse
        rows = slice(c // PSIDE * BLOCK, (c // PSIDE + 1) * BLOCK)
        lanes = slice(c % PSIDE * BLOCK, (c % PSIDE + 1) * BLOCK)
        copies.append(pltpu.make_async_copy(total.at[c], out.at[0, rows, lanes], out_sem.at[c]))
        copies[-1].start()
    for copy in copies:
        copy.wait()


def coadd(got):
    return pl.pallas_call(
        coadd_kernel,
        in_specs=[pl.BlockSpec(memory_space=pltpu.VMEM)],
        out_specs=pl.BlockSpec(memory_space=pl.ANY),
        out_shape=jax.ShapeDtypeStruct((1, PSIDE * BLOCK, PSIDE * BLOCK), F32),
        scratch_shapes=[
            pltpu.VMEM((CELLS, BLOCK, BLOCK), F32),
            pltpu.SMEM((CELLS,), F32),
            pltpu.SemaphoreType.DMA((CELLS,)),
        ],
        compiler_params=pltpu.CompilerParams(vmem_limit_bytes=32 << 20),
        name="coadd",
    )(got)


def shards(
    images, basis_taps, psf_coef, affine, visit_weight, block_patch, block_slot, patch_owner
):
    devices = lax.axis_size("ccd")
    down = [(i, i + 1) for i in range(devices - 1)]
    up = [(i + 1, i) for i in range(devices - 1)]
    above = lax.ppermute(images[:, BLOCK - RIM :], "ccd", down)
    below = lax.ppermute(images[:, :RIM], "ccd", up)
    patch = block_patch[:, :, 0]
    ready = prepare(basis_taps, psf_coef, affine, devices)
    sent = warp(
        patch, block_slot, patch_owner, visit_weight, ready, images, above, below, devices
    )
    got = lax.all_to_all(sent, "ccd", split_axis=0, concat_axis=0, tiled=True)
    return coadd(got)


def solution(mesh):
    placed = (
        P(None, ("group", "ccd"), None),
        P(),
        P(None, "group", None, None),
        P(None, "group", None, None),
        P(None, "group"),
        P(("group", "ccd"), None, None),
        P(("group", "ccd"), None),
        P("group"),
    )
    return jax.shard_map(
        shards,
        mesh=mesh,
        in_specs=placed,
        out_specs=P(("group", "ccd"), None, None),
        check_vma=False,
    )
```

```python
import functools

import jax
import jax.numpy as jnp
import numpy as np
from jax import lax
from jax.experimental import pallas as pl
from jax.experimental.pallas import tpu as pltpu
from jax.sharding import PartitionSpec as P

V = 4
BLOCK = 128
BLKC = 4
SPLIT = 4
TAPS = 11
NBASIS = 9
PSIDE = 4
CELLS = PSIDE * PSIDE
CAP = 2

HALF = TAPS // 2
WARP = 3
RIM = HALF + WARP
HEIGHT = SPLIT * BLOCK
WIDTH = BLKC * BLOCK
LANES = 128
LANE_BLOCKS = WIDTH // LANES
STRIP = 16
STEP = 32
STRIPS = -(-(BLOCK + 2 * WARP) // STRIP)
MIDDLE = STRIPS // 2
GROUPS = 6
BAND = 256
TALL = (STRIPS - 1) * STRIP + STEP
HALVES = 2
PIECES = 3
ROWS = BLOCK // HALVES
WINDOW = ROWS + STRIP
LABEL = 16
F32 = jnp.float32
BF16 = jnp.bfloat16


def sin_pi(t):
    whole = jnp.round(t)
    f = t - whole
    odd = whole - 2.0 * jnp.floor(0.5 * whole)
    f2 = f * f
    out = 0.0
    for c in (
        0.00046630280576761, -0.0073704309457144, 0.0821458866111282,
        -0.599264529320792, 2.55016403987734, -5.16771278004997, 3.14159265358979,
    ):
        out = out * f2 + c
    return f * out * (1.0 - 2.0 * odd)


def lanczos(t):
    zero = t == 0.0
    safe = jnp.where(zero, 1.0, t)
    pt = jnp.pi * safe
    value = 3.0 * sin_pi(safe) * sin_pi(safe / 3.0) / (pt * pt)
    return jnp.where(jnp.abs(t) < 3.0, jnp.where(zero, 1.0, value), 0.0)


def iota(shape, dim):
    return lax.broadcasted_iota(jnp.int32, shape, dim)


def deinterleave():
    order = np.arange(WIDTH).reshape(LANES, LANE_BLOCKS).T.reshape(-1)
    return (np.arange(WIDTH)[:, None] == order[None, :]).astype(np.float32)


def column_at(lane):
    return lane % LANES * LANE_BLOCKS + lane // LANES


def lane_block(x, v):
    return x[:, v * LANES : (v + 1) * LANES]


def dot_exact(a, b, dims):
    return lax.dot_general(
        a, b, (dims, ((), ())), precision=lax.Precision.HIGHEST, preferred_element_type=F32
    )


def staircase(x, first):
    return jnp.concatenate(
        [
            pltpu.roll(x[g : g + 8], first + g, 1, stride=1, stride_axis=0)
            for g in range(0, x.shape[0], 8)
        ],
        axis=0,
    )


def lane_sum(terms_of, lane, count, weigh):
    blocks = []
    for v in range(LANE_BLOCKS):
        total = None
        half = count // 2
        for q in range(-(-half // LANE_BLOCKS) * -1, (half + LANE_BLOCKS - 1) // LANE_BLOCKS + 1):
            part = None
            for u in range(count):
                if (v + u - half) // LANE_BLOCKS != q:
                    continue
                piece = terms_of(u, v, (v + u - half) % LANE_BLOCKS)
                part = piece if part is None else part + piece
            if part is None:
                continue
            if q:
                part = pltpu.roll(part, -q % LANES, 1)
                if not weigh:
                    part = jnp.where((lane + q >= 0) & (lane + q < LANES), part, 0.0)
            total = part if total is None else total + part
        blocks.append(total)
    return blocks


def whereabouts(devices):
    band = lax.axis_index("ccd")
    quarter = (band + SPLIT // 2) % SPLIT
    has_above = (quarter > 0) & (band > 0)
    has_below = (quarter < SPLIT - 1) & (band < devices - 1)
    return (band + SPLIT // 2) // SPLIT, quarter * BLOCK, has_above, has_below


def prepare_kernel(devices, taps, psf, affine, high_level, step_level, slope, rows_high, rows_low, cols_out):
    ccd, top_row, has_above, has_below = whereabouts(devices)
    band_lane = iota((1, BAND), 1)
    seg = band_lane // STEP
    lane = iota((1, LANES), 1)
    tap = band_lane - seg * STEP
    onehot = (tap == iota((TAPS, BAND), 0)) & (seg < GROUPS)
    row_taps = dot_exact(taps[:, 0], onehot.astype(F32), ((1,), (0,)))
    eye = (iota((TAPS, STRIP), 0) == iota((TAPS, STRIP), 1)).astype(F32)
    turned_taps = dot_exact(eye, taps[:, 1], ((0,), (1,)))
    for visit in range(V):
        lhs = jnp.concatenate(
            [turned_taps * psf[ccd, c, visit : visit + 1, :] for c in range(3)], axis=0
        )
        kernels = dot_exact(lhs, row_taps, ((1,), (0,)))
        const, by_row, by_col = (kernels[c * STRIP : (c + 1) * STRIP] for c in range(3))
        is_level = seg < 3
        per_strip = 2.0 * STRIP / HEIGHT
        middle_row = (top_row + (MIDDLE * STRIP - WARP)).astype(F32)
        middle_pos = (2.0 * middle_row + 1.0) / HEIGHT - 1.0
        col_move = (iota((STRIP, 1), 0) - HALF).astype(F32) * (2.0 / WIDTH)
        by_row = jnp.where(is_level, by_row, 0.0)
        const = jnp.where(is_level, const + middle_pos * by_row - col_move * by_col, by_col)
        reach = per_strip * (STRIPS - MIDDLE)
        largest = jnp.max(jnp.abs(const) + reach * jnp.abs(by_row), axis=(0, 1), keepdims=True)
        unit = jnp.maximum(largest, 1e-30) * (1.0 / 200.0)
        const = const / unit
        by_row = (by_row * per_strip) / unit
        low_lanes = (lane // STEP) % 3 == 2
        low_band = seg % 3 == 2
        row_part = iota((STRIP, 1), 0).astype(F32) * (1.0 / STRIP)
        for u in range(TAPS):
            at = slice(u * STRIP, (u + 1) * STRIP)
            x = staircase(jnp.broadcast_to(const[u : u + 1], (STRIP, BAND)), 0)
            y = staircase(jnp.broadcast_to(by_row[u : u + 1, :LANES], (STRIP, LANES)), 0)
            tail = x[:, LANES:]
            high = tail.astype(BF16).astype(F32)
            slope[visit, at] = jnp.where(low_band[:, LANES:], tail - high, high).astype(BF16)
            x = x[:, :LANES] + row_part * y
            high = jnp.where(lane < 3 * STEP, jnp.round(x), x.astype(BF16).astype(F32))
            high_level[visit, at] = jnp.where(low_lanes, x - high, high)
            high = jnp.round(y)
            step_level[visit, at] = jnp.where(low_lanes, y - high, high)

        a = jnp.sum(
            jnp.where(iota((1, 1, affine.shape[3]), 2) == ccd, affine[visit], 0.0),
            axis=2, keepdims=True,
        )
        offset = iota((8, LANES), 0) - WARP
        row = (top_row + lane).astype(F32)
        shift = a[0, 0:1] + a[0, 1:2] * (row - (HEIGHT - 1) / 2.0) / HEIGHT
        band_row = lane + offset
        keep = (offset <= WARP) & ((band_row >= 0) | has_above) & ((band_row < BLOCK) | has_below)
        weights = jnp.where(keep, lanczos(shift - offset.astype(F32)), 0.0) * unit
        weights = jnp.concatenate([weights, jnp.zeros((LANES - 8, LANES), F32)], axis=0).T
        for h in range(HALVES):
            at = slice(h * ROWS, (h + 1) * ROWS)
            matrix = staircase(weights[at], 0)
            high = matrix.astype(BF16)
            rows_high[visit, at] = high
            rows_low[visit, at] = (matrix - high.astype(F32)).astype(BF16)

        lanes = iota((8, WIDTH), 1)
        step = iota((8, WIDTH), 0) - WARP
        block = lanes // LANES
        carry = (block + step + LANE_BLOCKS) // LANE_BLOCKS - 1
        from_lane = lanes % LANES - carry
        col = (from_lane * LANE_BLOCKS + block).astype(F32)
        col_shift = a[1, 0:1] + a[1, 1:2] * (col - (WIDTH - 1) / 2.0) / WIDTH
        within = (from_lane >= 0) & (from_lane < LANES) & (step <= WARP)
        cols_out[visit] = jnp.where(within, lanczos(col_shift - step.astype(F32)), 0.0)


def prepare(taps, psf, affine, devices):
    shapes = [
        ((V, TAPS * STRIP, LANES), F32),
        ((V, TAPS * STRIP, LANES), F32),
        ((V, TAPS * STRIP, BAND - LANES), BF16),
        ((V, BLOCK, LANES), BF16),
        ((V, BLOCK, LANES), BF16),
        ((V, 8, WIDTH), F32),
    ]
    args = [taps.transpose(1, 0, 2), psf.transpose(1, 3, 0, 2), affine.transpose(0, 2, 3, 1)]
    return pl.pallas_call(
        functools.partial(prepare_kernel, devices),
        grid=(1,),
        in_specs=[pl.BlockSpec(x.shape, lambda i, n=x.ndim: (0,) * n) for x in args],
        out_specs=[pl.BlockSpec(shape, lambda i: (0, 0, 0)) for shape, _ in shapes],
        out_shape=[jax.ShapeDtypeStruct(shape, kind) for shape, kind in shapes],
        compiler_params=pltpu.CompilerParams(vmem_limit_bytes=32 << 20),
        cost_estimate=pl.CostEstimate(flops=1 << 30, bytes_accessed=1 << 20, transcendentals=0),
        name="prepare",
    )(*args)


def warp_kernel(
    patch, slot, owner, weight, high_level, step_level, slope, rows_high, rows_low, col_weights,
    sort, unsort, image, above, below, out,
    terms, matched_terms, ready, place_of, seen, nothing, label, label_ready, sem, label_sem, clear_sem,
):
    devices = label.shape[0]
    ccd, _, has_above, has_below = whereabouts(devices)
    tall = BLOCK + 2 * RIM
    lane = iota((1, LANES), 1)

    nothing[...] = jnp.zeros_like(nothing)
    clears = [
        pltpu.make_async_copy(nothing, out.at[d, pl.ds(0, CAP * BLOCK)], clear_sem.at[d])
        for d in range(devices)
    ]
    for copy in clears:
        copy.start()
    label[...] = jnp.zeros_like(label)

    def forget(p, _):
        seen[p] = 0
        return 0

    lax.fori_loop(0, owner.shape[0], forget, 0)
    own = jnp.where(iota(weight.shape, 1) == ccd, weight[...].astype(F32), 0.0)
    own = jnp.sum(own, axis=1, keepdims=True)
    for block in range(V * BLKC):
        p = patch[0, block]
        to = owner[p]
        rank = seen[p]
        seen[p] = rank + 1
        place_of[block] = to * CAP + rank
        line = label[pl.ds(to, 1), :]
        line = jnp.where(lane == rank * 2, own[block // BLKC : block // BLKC + 1], line)
        line = jnp.where(lane == rank * 2 + 1, slot[0, block].astype(F32), line)
        label[pl.ds(to, 1), :] = line
    label_ready[...] = jnp.broadcast_to(
        label[...].reshape(devices, 1, LANES), (devices, LABEL, LANES)
    ).astype(BF16)
    label_copy = pltpu.make_async_copy(label_ready, out.at[:, pl.ds(CAP * BLOCK, LABEL)], label_sem)
    label_copy.start()

    terms[:, :, tall:] = jnp.zeros((V, 4, TALL - tall, WIDTH), BF16)
    col_pos = (2.0 * column_at(iota((1, WIDTH), 1)).astype(F32) + 1.0) / WIDTH - 1.0
    filler = jnp.zeros((BAND - GROUPS * STEP, WIDTH), BF16)
    empty = jnp.zeros((LANES - WINDOW, WIDTH), BF16)

    def sort_rows(i, piece):
        size = tall // PIECES
        low_row, high_row = piece * size - RIM, (piece + 1) * size - RIM
        raw = [image[i, max(low_row, 0) : min(high_row, BLOCK)]]
        if low_row < 0:
            raw = [jnp.where(has_above, above[i], 0.0)] + raw
        if high_row > BLOCK:
            raw = raw + [jnp.where(has_below, below[i], 0.0)]
        raw = jnp.concatenate(raw, axis=0)
        raw_high = raw.astype(BF16)
        raw_low = (raw - raw_high.astype(F32)).astype(BF16)
        both = jnp.dot(
            jnp.concatenate([raw_high, raw_low], axis=0), sort[...], preferred_element_type=F32
        )
        high, low = both[:size], both[size:]
        tilted = (high + low) * col_pos
        tilted_high = tilted.astype(BF16)
        at = slice(piece * size, (piece + 1) * size)
        terms[i, 0, at] = high.astype(BF16)
        terms[i, 1, at] = low.astype(BF16)
        terms[i, 2, at] = tilted_high
        terms[i, 3, at] = (tilted - tilted_high.astype(F32)).astype(BF16)

    def match_strip(i, k):
        level = high_level[i]
        if k != MIDDLE:
            level = level + float(k - MIDDLE) * step_level[i]
        matrix = jnp.concatenate([level.astype(BF16), slope[i]], axis=1)
        rows = slice(k * STRIP, k * STRIP + STEP)
        columns = jnp.concatenate([terms[i, h, rows] for h in (0, 1, 0, 2, 3, 2)] + [filler], axis=0)
        results = jnp.dot(matrix, columns, preferred_element_type=F32)
        blocks = lane_sum(
            lambda u, v, w: lane_block(results[u * STRIP : (u + 1) * STRIP], w), lane, TAPS, False
        )
        matched = jnp.concatenate(blocks, axis=1)
        high = matched.astype(BF16)
        at = slice(k * STRIP, (k + 1) * STRIP)
        matched_terms[i, 0, at] = high
        matched_terms[i, 1, at] = (matched - high.astype(F32)).astype(BF16)

    def warp_half(i, h):
        high = rows_high[i, h * ROWS : (h + 1) * ROWS]
        low = rows_low[i, h * ROWS : (h + 1) * ROWS]
        rows = slice(h * ROWS, h * ROWS + WINDOW)
        first = jnp.concatenate([matched_terms[i, 0, rows], empty], axis=0)
        second = jnp.concatenate([matched_terms[i, 1, rows], empty], axis=0)
        warped = jnp.dot(
            jnp.concatenate([high, high], axis=1), jnp.concatenate([first, second], axis=0),
            preferred_element_type=F32,
        )
        warped = warped + jnp.dot(low, first, preferred_element_type=F32)
        cols = col_weights[i]
        blocks = lane_sum(
            lambda s, v, w: lane_block(cols[s : s + 1], v) * lane_block(warped, w),
            lane, 2 * WARP + 1, True,
        )
        result = jnp.dot(
            jnp.concatenate(blocks, axis=1).astype(BF16), unsort[...], preferred_element_type=F32
        ).astype(BF16)
        for j in range(BLKC):
            ready[i * BLKC + j, h * ROWS : (h + 1) * ROWS] = lane_block(result, j)

    def send(i):
        if i == 0:
            for copy in clears:
                copy.wait()
        for block in range(i * BLKC, (i + 1) * BLKC):
            to = place_of[block]
            row = pl.multiple_of(to % CAP * BLOCK, BLOCK)
            pltpu.make_async_copy(
                ready.at[block], out.at[to // CAP, pl.ds(row, BLOCK)], sem.at[block]
            ).start()

    for piece in range(PIECES):
        sort_rows(0, piece)
    for i in range(V):
        between = {}
        if i > 0:
            between[1] = functools.partial(warp_half, i - 1, 0)
            between[3] = functools.partial(warp_half, i - 1, 1)
            between[4] = functools.partial(send, i - 1)
        if i < V - 1:
            for piece in range(PIECES):
                between[STRIPS - PIECES + piece] = functools.partial(sort_rows, i + 1, piece)
        for k in range(STRIPS):
            match_strip(i, k)
            if k in between:
                between[k]()
    for h in range(HALVES):
        warp_half(V - 1, h)
    send(V - 1)
    label_copy.wait()
    for block in range(V * BLKC):
        pltpu.make_async_copy(ready.at[block], out.at[0, pl.ds(0, BLOCK)], sem.at[block]).wait()


def warp(patch, slot, owner, weight, ready, images, above, below, devices):
    smem = pl.BlockSpec(memory_space=pltpu.SMEM)
    vmem = pl.BlockSpec(memory_space=pltpu.VMEM)
    sort = deinterleave()
    return pl.pallas_call(
        warp_kernel,
        in_specs=[smem] * 3 + [vmem] * 12,
        out_specs=pl.BlockSpec(memory_space=pl.ANY),
        scratch_shapes=[
            pltpu.VMEM((V, 4, TALL, WIDTH), BF16),
            pltpu.VMEM((V, 2, STRIPS * STRIP, WIDTH), BF16),
            pltpu.VMEM((V * BLKC, BLOCK, BLOCK), BF16),
            pltpu.SMEM((V * BLKC,), jnp.int32),
            pltpu.SMEM((owner.shape[0],), jnp.int32),
            pltpu.VMEM((CAP * BLOCK, BLOCK), BF16),
            pltpu.VMEM((devices, LANES), F32),
            pltpu.VMEM((devices, LABEL, LANES), BF16),
            pltpu.SemaphoreType.DMA((V * BLKC,)),
            pltpu.SemaphoreType.DMA(()),
            pltpu.SemaphoreType.DMA((devices,)),
        ],
        out_shape=jax.ShapeDtypeStruct((devices, CAP * BLOCK + LABEL, BLOCK), BF16),
        compiler_params=pltpu.CompilerParams(vmem_limit_bytes=32 << 20),
        cost_estimate=pl.CostEstimate(
            flops=V * 2 * STRIPS * TAPS * STRIP * BAND * WIDTH,
            bytes_accessed=V * (BLOCK * WIDTH * 6),
            transcendentals=0,
        ),
        name="match_warp",
    )(
        patch, slot, owner, weight, *ready,
        jnp.asarray(sort, BF16), jnp.asarray(sort.T, BF16), images, above, below,
    )


def coadd_kernel(got, out, total, out_sem):
    devices = got.shape[0]
    wide = devices * CAP * STRIP
    labels = got[:, CAP * BLOCK : CAP * BLOCK + LABEL][:, 0]
    lane = iota((1, wide), 1)
    rank = lane // STRIP % CAP
    source = lane // (STRIP * CAP)

    def spread(entry):
        onehot = (iota((LANES, wide), 0) == rank * 2 + entry).astype(F32).astype(BF16)
        every = jnp.dot(labels, onehot, preferred_element_type=F32)
        return jnp.sum(
            jnp.where(iota((devices, wide), 0) == source, every, 0.0), axis=0, keepdims=True
        )

    weights, cells = spread(0), spread(1)
    row = iota((CELLS * STRIP, 1), 0)
    mine = (cells == (row // STRIP).astype(F32)) & (lane % STRIP == row % STRIP)
    matrix = jnp.where(mine, weights, 0.0)
    sums = jnp.sum(matrix, axis=1, keepdims=True)
    inverse = 1.0 / jnp.maximum(sums, 1.0)
    matrix = matrix.astype(BF16)
    copies = []
    for pair in range(BLOCK // STRIP // 2):
        columns = jnp.concatenate(
            [
                jnp.concatenate(
                    [
                        got[s, r * BLOCK + k * STRIP : r * BLOCK + (k + 1) * STRIP]
                        for s in range(devices)
                        for r in range(CAP)
                    ],
                    axis=0,
                )
                for k in (2 * pair, 2 * pair + 1)
            ],
            axis=1,
        )
        result = jnp.dot(matrix, columns, preferred_element_type=F32) * inverse
        for c in range(CELLS):
            part = result[c * STRIP : (c + 1) * STRIP]
            lanes = slice(c % PSIDE * BLOCK, (c % PSIDE + 1) * BLOCK)
            for n in range(2):
                first = (2 * pair + n) * STRIP
                total[c // PSIDE, first : first + STRIP, lanes] = lane_block(part, n)
        size = 2 * STRIP
        for line in range(PSIDE):
            copies.append(
                pltpu.make_async_copy(
                    total.at[line, pl.ds(pair * size, size)],
                    out.at[0, pl.ds(line * BLOCK + pair * size, size)],
                    out_sem.at[pair, line],
                )
            )
            copies[-1].start()
    for copy in copies:
        copy.wait()


def coadd(got):
    return pl.pallas_call(
        coadd_kernel,
        in_specs=[pl.BlockSpec(memory_space=pltpu.VMEM)],
        out_specs=pl.BlockSpec(memory_space=pl.ANY),
        out_shape=jax.ShapeDtypeStruct((1, PSIDE * BLOCK, PSIDE * BLOCK), F32),
        scratch_shapes=[
            pltpu.VMEM((PSIDE, BLOCK, WIDTH), F32),
            pltpu.SemaphoreType.DMA((BLOCK // STRIP // 2, PSIDE)),
        ],
        compiler_params=pltpu.CompilerParams(vmem_limit_bytes=32 << 20),
        name="coadd",
    )(got)


def shards(
    images, basis_taps, psf_coef, affine, visit_weight, block_patch, block_slot, patch_owner
):
    devices = lax.axis_size("ccd")
    down = [(i, i + 1) for i in range(devices - 1)]
    up = [(i + 1, i) for i in range(devices - 1)]
    above = lax.ppermute(images[:, BLOCK - RIM :], "ccd", down)
    below = lax.ppermute(images[:, :RIM], "ccd", up)
    patch = block_patch[:, :, 0]
    ready = prepare(basis_taps, psf_coef, affine, devices)
    sent = warp(
        patch, block_slot, patch_owner, visit_weight, ready, images, above, below, devices
    )
    got = lax.all_to_all(sent, "ccd", split_axis=0, concat_axis=0, tiled=True)
    return coadd(got)


def solution(mesh):
    placed = (
        P(None, ("group", "ccd"), None),
        P(),
        P(None, "group", None, None),
        P(None, "group", None, None),
        P(None, "group"),
        P(("group", "ccd"), None, None),
        P(("group", "ccd"), None),
        P("group"),
    )
    return jax.shard_map(
        shards,
        mesh=mesh,
        in_specs=placed,
        out_specs=P(("group", "ccd"), None, None),
        check_vma=False,
    )
```

```python
import functools

import jax
import jax.numpy as jnp
import numpy as np
from jax import lax
from jax.experimental import pallas as pl
from jax.experimental.pallas import tpu as pltpu
from jax.sharding import PartitionSpec as P

V = 4
BLOCK = 128
BLKC = 4
SPLIT = 4
TAPS = 11
NBASIS = 9
PSIDE = 4
CELLS = PSIDE * PSIDE
CAP = 2

HALF = TAPS // 2
WARP = 3
RIM = HALF + WARP
HEIGHT = SPLIT * BLOCK
WIDTH = BLKC * BLOCK
LANES = 128
LANE_BLOCKS = WIDTH // LANES
STRIP = 16
STEP = 32
STRIPS = -(-(BLOCK + 2 * WARP) // STRIP)
MIDDLE = STRIPS // 2
GROUPS = 6
BAND = 256
TALL = (STRIPS - 1) * STRIP + STEP
HALVES = 2
TOGETHER = 2
PIECES = 3
ROWS = BLOCK // HALVES
WINDOW = ROWS + STRIP
LABEL = 16
F32 = jnp.float32
BF16 = jnp.bfloat16


def sin_pi(t):
    whole = jnp.round(t)
    f = t - whole
    odd = whole - 2.0 * jnp.floor(0.5 * whole)
    f2 = f * f
    out = 0.0
    for c in (
        0.00046630280576761, -0.0073704309457144, 0.0821458866111282,
        -0.599264529320792, 2.55016403987734, -5.16771278004997, 3.14159265358979,
    ):
        out = out * f2 + c
    return f * out * (1.0 - 2.0 * odd)


def lanczos(t):
    zero = t == 0.0
    safe = jnp.where(zero, 1.0, t)
    pt = jnp.pi * safe
    value = 3.0 * sin_pi(safe) * sin_pi(safe / 3.0) / (pt * pt)
    return jnp.where(jnp.abs(t) < 3.0, jnp.where(zero, 1.0, value), 0.0)


def iota(shape, dim):
    return lax.broadcasted_iota(jnp.int32, shape, dim)


def deinterleave():
    order = np.arange(WIDTH).reshape(LANES, LANE_BLOCKS).T.reshape(-1)
    return (np.arange(WIDTH)[:, None] == order[None, :]).astype(np.float32)


def column_at(lane):
    return lane % LANES * LANE_BLOCKS + lane // LANES


def lane_block(x, v):
    return x[:, v * LANES : (v + 1) * LANES]


def dot_exact(a, b, dims):
    return lax.dot_general(
        a, b, (dims, ((), ())), precision=lax.Precision.HIGHEST, preferred_element_type=F32
    )


def staircase(x, first):
    return jnp.concatenate(
        [
            pltpu.roll(x[g : g + 8], first + g, 1, stride=1, stride_axis=0)
            for g in range(0, x.shape[0], 8)
        ],
        axis=0,
    )


def lane_sum(terms_of, lane, count, weigh):
    blocks = []
    for v in range(LANE_BLOCKS):
        total = None
        half = count // 2
        for q in range(-(-half // LANE_BLOCKS) * -1, (half + LANE_BLOCKS - 1) // LANE_BLOCKS + 1):
            part = None
            for u in range(count):
                if (v + u - half) // LANE_BLOCKS != q:
                    continue
                piece = terms_of(u, v, (v + u - half) % LANE_BLOCKS)
                part = piece if part is None else part + piece
            if part is None:
                continue
            if q:
                part = pltpu.roll(part, -q % LANES, 1)
                if not weigh:
                    part = jnp.where((lane + q >= 0) & (lane + q < LANES), part, 0.0)
            total = part if total is None else total + part
        blocks.append(total)
    return blocks


def whereabouts(devices):
    band = lax.axis_index("ccd")
    quarter = (band + SPLIT // 2) % SPLIT
    has_above = (quarter > 0) & (band > 0)
    has_below = (quarter < SPLIT - 1) & (band < devices - 1)
    return (band + SPLIT // 2) // SPLIT, quarter * BLOCK, has_above, has_below


def prepare_kernel(devices, taps, psf, affine, high_level, step_level, slope, rows_high, rows_low, cols_out):
    ccd, top_row, has_above, has_below = whereabouts(devices)
    band_lane = iota((1, BAND), 1)
    seg = band_lane // STEP
    lane = iota((1, LANES), 1)
    tap = band_lane - seg * STEP
    onehot = (tap == iota((TAPS, BAND), 0)) & (seg < GROUPS)
    row_taps = dot_exact(taps[:, 0], onehot.astype(F32), ((1,), (0,)))
    eye = (iota((TAPS, STRIP), 0) == iota((TAPS, STRIP), 1)).astype(F32)
    turned_taps = dot_exact(eye, taps[:, 1], ((0,), (1,)))
    for visit in range(V):
        lhs = jnp.concatenate(
            [turned_taps * psf[ccd, c, visit : visit + 1, :] for c in range(3)], axis=0
        )
        kernels = dot_exact(lhs, row_taps, ((1,), (0,)))
        const, by_row, by_col = (kernels[c * STRIP : (c + 1) * STRIP] for c in range(3))
        is_level = seg < 3
        per_strip = 2.0 * STRIP / HEIGHT
        middle_row = (top_row + (MIDDLE * STRIP - WARP)).astype(F32)
        middle_pos = (2.0 * middle_row + 1.0) / HEIGHT - 1.0
        col_move = (iota((STRIP, 1), 0) - HALF).astype(F32) * (2.0 / WIDTH)
        by_row = jnp.where(is_level, by_row, 0.0)
        const = jnp.where(is_level, const + middle_pos * by_row - col_move * by_col, by_col)
        reach = per_strip * (STRIPS - MIDDLE)
        largest = jnp.max(jnp.abs(const) + reach * jnp.abs(by_row), axis=(0, 1), keepdims=True)
        unit = jnp.maximum(largest, 1e-30) * (1.0 / 200.0)
        const = const / unit
        by_row = (by_row * per_strip) / unit
        low_lanes = (lane // STEP) % 3 == 2
        low_band = seg % 3 == 2
        row_part = iota((STRIP, 1), 0).astype(F32) * (1.0 / STRIP)
        for u in range(TAPS):
            at = slice(u * STRIP, (u + 1) * STRIP)
            x = staircase(jnp.broadcast_to(const[u : u + 1], (STRIP, BAND)), 0)
            y = staircase(jnp.broadcast_to(by_row[u : u + 1, :LANES], (STRIP, LANES)), 0)
            tail = x[:, LANES:]
            high = tail.astype(BF16).astype(F32)
            slope[visit, at] = jnp.where(low_band[:, LANES:], tail - high, high).astype(BF16)
            x = x[:, :LANES] + row_part * y
            high = jnp.where(lane < 3 * STEP, jnp.round(x), x.astype(BF16).astype(F32))
            high_level[visit, at] = jnp.where(low_lanes, x - high, high)
            high = jnp.round(y)
            step_level[visit, at] = jnp.where(low_lanes, y - high, high)

        a = jnp.sum(
            jnp.where(iota((1, 1, affine.shape[3]), 2) == ccd, affine[visit], 0.0),
            axis=2, keepdims=True,
        )
        offset = iota((8, LANES), 0) - WARP
        row = (top_row + lane).astype(F32)
        shift = a[0, 0:1] + a[0, 1:2] * (row - (HEIGHT - 1) / 2.0) / HEIGHT
        band_row = lane + offset
        keep = (offset <= WARP) & ((band_row >= 0) | has_above) & ((band_row < BLOCK) | has_below)
        weights = jnp.where(keep, lanczos(shift - offset.astype(F32)), 0.0) * unit
        weights = jnp.concatenate([weights, jnp.zeros((LANES - 8, LANES), F32)], axis=0).T
        for h in range(HALVES):
            at = slice(h * ROWS, (h + 1) * ROWS)
            matrix = staircase(weights[at], 0)
            high = matrix.astype(BF16)
            rows_high[visit, at] = high
            rows_low[visit, at] = (matrix - high.astype(F32)).astype(BF16)

        lanes = iota((8, WIDTH), 1)
        step = iota((8, WIDTH), 0) - WARP
        block = lanes // LANES
        carry = (block + step + LANE_BLOCKS) // LANE_BLOCKS - 1
        from_lane = lanes % LANES - carry
        col = (from_lane * LANE_BLOCKS + block).astype(F32)
        col_shift = a[1, 0:1] + a[1, 1:2] * (col - (WIDTH - 1) / 2.0) / WIDTH
        within = (from_lane >= 0) & (from_lane < LANES) & (step <= WARP)
        cols_out[visit] = jnp.where(within, lanczos(col_shift - step.astype(F32)), 0.0)


def prepare(taps, psf, affine, devices):
    shapes = [
        ((V, TAPS * STRIP, LANES), F32),
        ((V, TAPS * STRIP, LANES), F32),
        ((V, TAPS * STRIP, BAND - LANES), BF16),
        ((V, BLOCK, LANES), BF16),
        ((V, BLOCK, LANES), BF16),
        ((V, 8, WIDTH), F32),
    ]
    args = [taps.transpose(1, 0, 2), psf.transpose(1, 3, 0, 2), affine.transpose(0, 2, 3, 1)]
    return pl.pallas_call(
        functools.partial(prepare_kernel, devices),
        grid=(1,),
        in_specs=[pl.BlockSpec(x.shape, lambda i, n=x.ndim: (0,) * n) for x in args],
        out_specs=[pl.BlockSpec(shape, lambda i: (0, 0, 0)) for shape, _ in shapes],
        out_shape=[jax.ShapeDtypeStruct(shape, kind) for shape, kind in shapes],
        compiler_params=pltpu.CompilerParams(vmem_limit_bytes=32 << 20),
        cost_estimate=pl.CostEstimate(flops=1 << 30, bytes_accessed=1 << 20, transcendentals=0),
        name="prepare",
    )(*args)


def warp_kernel(
    patch, slot, owner, weight, high_level, step_level, slope, rows_high, rows_low, col_weights,
    sort, unsort, image, above, below, out,
    raw, terms, matched_terms, ready, place_of, seen, nothing, label, label_ready, sem, label_sem, clear_sem,
):
    devices = label.shape[0]
    ccd, _, has_above, has_below = whereabouts(devices)
    tall = BLOCK + 2 * RIM
    lane = iota((1, LANES), 1)

    nothing[...] = jnp.zeros_like(nothing)
    clears = [
        pltpu.make_async_copy(nothing, out.at[d, pl.ds(0, CAP * BLOCK)], clear_sem.at[d])
        for d in range(devices)
    ]
    for copy in clears:
        copy.start()
    label[...] = jnp.zeros_like(label)

    def forget(p, _):
        seen[p] = 0
        return 0

    lax.fori_loop(0, owner.shape[0], forget, 0)
    own = jnp.where(iota(weight.shape, 1) == ccd, weight[...].astype(F32), 0.0)
    own = jnp.sum(own, axis=1, keepdims=True)
    for block in range(V * BLKC):
        p = patch[0, block]
        to = owner[p]
        rank = seen[p]
        seen[p] = rank + 1
        place_of[block] = to * CAP + rank
        line = label[pl.ds(to, 1), :]
        line = jnp.where(lane == rank * 2, own[block // BLKC : block // BLKC + 1], line)
        line = jnp.where(lane == rank * 2 + 1, slot[0, block].astype(F32), line)
        label[pl.ds(to, 1), :] = line
    label_ready[...] = jnp.broadcast_to(
        label[...].reshape(devices, 1, LANES), (devices, LABEL, LANES)
    ).astype(BF16)
    label_copy = pltpu.make_async_copy(label_ready, out.at[:, pl.ds(CAP * BLOCK, LABEL)], label_sem)
    label_copy.start()

    terms[:, :, tall:] = jnp.zeros((TOGETHER, 4, TALL - tall, WIDTH), BF16)
    col_pos = (2.0 * column_at(iota((1, WIDTH), 1)).astype(F32) + 1.0) / WIDTH - 1.0
    filler = jnp.zeros((BAND - GROUPS * STEP, WIDTH), BF16)
    empty = jnp.zeros((LANES - WINDOW, WIDTH), BF16)
    for copy in clears:
        copy.wait()

    def some_visits(turn, _):
        visits = [turn * TOGETHER + i for i in range(TOGETHER)]
        for i, visit in enumerate(visits):
            raw[i, :RIM] = jnp.where(has_above, above[visit], 0.0)
            raw[i, RIM : RIM + BLOCK] = image[visit]
            raw[i, RIM + BLOCK :] = jnp.where(has_below, below[visit], 0.0)

        def sort_rows(piece, _):
            size = tall // PIECES
            at = pl.ds(pl.multiple_of(piece * size, STRIP), size)
            for i in range(TOGETHER):
                rows = raw[i, at]
                rows_high = rows.astype(BF16)
                rows_low = (rows - rows_high.astype(F32)).astype(BF16)
                both = jnp.dot(
                    jnp.concatenate([rows_high, rows_low], axis=0), sort[...],
                    preferred_element_type=F32,
                )
                high, low = both[:size], both[size:]
                tilted = (high + low) * col_pos
                tilted_high = tilted.astype(BF16)
                terms[i, 0, at] = high.astype(BF16)
                terms[i, 1, at] = low.astype(BF16)
                terms[i, 2, at] = tilted_high
                terms[i, 3, at] = (tilted - tilted_high.astype(F32)).astype(BF16)
            return 0

        lax.fori_loop(0, PIECES, sort_rows, 0)

        def match_strip(k, _):
            first = pl.multiple_of(k * STRIP, STRIP)
            away = (k - MIDDLE).astype(F32)
            for i, visit in enumerate(visits):
                level = high_level[visit] + away * step_level[visit]
                matrix = jnp.concatenate([level.astype(BF16), slope[visit]], axis=1)
                columns = jnp.concatenate(
                    [terms[i, h, pl.ds(first, STEP)] for h in (0, 1, 0, 2, 3, 2)] + [filler], axis=0
                )
                results = jnp.dot(matrix, columns, preferred_element_type=F32)
                blocks = lane_sum(
                    lambda u, v, w: lane_block(results[u * STRIP : (u + 1) * STRIP], w),
                    lane, TAPS, False,
                )
                matched = jnp.concatenate(blocks, axis=1)
                high = matched.astype(BF16)
                at = pl.ds(first, STRIP)
                matched_terms[i, 0, at] = high
                matched_terms[i, 1, at] = (matched - high.astype(F32)).astype(BF16)
            return 0

        lax.fori_loop(0, STRIPS, match_strip, 0)

        def warp_half(h, _):
            first_row = pl.multiple_of(h * ROWS, ROWS)
            at = pl.ds(first_row, ROWS)
            rows = pl.ds(first_row, WINDOW)
            for i, visit in enumerate(visits):
                high = rows_high[visit, at]
                low = rows_low[visit, at]
                first = jnp.concatenate([matched_terms[i, 0, rows], empty], axis=0)
                second = jnp.concatenate([matched_terms[i, 1, rows], empty], axis=0)
                warped = jnp.dot(
                    jnp.concatenate([high, high], axis=1),
                    jnp.concatenate([first, second], axis=0),
                    preferred_element_type=F32,
                )
                warped = warped + jnp.dot(low, first, preferred_element_type=F32)
                cols = col_weights[visit]
                blocks = lane_sum(
                    lambda s, v, w: lane_block(cols[s : s + 1], v) * lane_block(warped, w),
                    lane, 2 * WARP + 1, True,
                )
                result = jnp.dot(
                    jnp.concatenate(blocks, axis=1).astype(BF16), unsort[...],
                    preferred_element_type=F32,
                ).astype(BF16)
                for j in range(BLKC):
                    ready[visit * BLKC + j, at] = lane_block(result, j)
            return 0

        lax.fori_loop(0, HALVES, warp_half, 0)
        for visit in visits:
            for j in range(BLKC):
                block = visit * BLKC + j
                to = place_of[block]
                row = pl.multiple_of(to % CAP * BLOCK, BLOCK)
                pltpu.make_async_copy(
                    ready.at[block], out.at[to // CAP, pl.ds(row, BLOCK)], sem.at[block]
                ).start()
        return 0

    lax.fori_loop(0, V // TOGETHER, some_visits, 0)
    label_copy.wait()
    for block in range(V * BLKC):
        pltpu.make_async_copy(ready.at[block], out.at[0, pl.ds(0, BLOCK)], sem.at[block]).wait()


def warp(patch, slot, owner, weight, ready, images, above, below, devices):
    smem = pl.BlockSpec(memory_space=pltpu.SMEM)
    vmem = pl.BlockSpec(memory_space=pltpu.VMEM)
    sort = deinterleave()
    return pl.pallas_call(
        warp_kernel,
        in_specs=[smem] * 3 + [vmem] * 12,
        out_specs=pl.BlockSpec(memory_space=pl.ANY),
        scratch_shapes=[
            pltpu.VMEM((TOGETHER, BLOCK + 2 * RIM, WIDTH), F32),
            pltpu.VMEM((TOGETHER, 4, TALL, WIDTH), BF16),
            pltpu.VMEM((TOGETHER, 2, STRIPS * STRIP, WIDTH), BF16),
            pltpu.VMEM((V * BLKC, BLOCK, BLOCK), BF16),
            pltpu.SMEM((V * BLKC,), jnp.int32),
            pltpu.SMEM((owner.shape[0],), jnp.int32),
            pltpu.VMEM((CAP * BLOCK, BLOCK), BF16),
            pltpu.VMEM((devices, LANES), F32),
            pltpu.VMEM((devices, LABEL, LANES), BF16),
            pltpu.SemaphoreType.DMA((V * BLKC,)),
            pltpu.SemaphoreType.DMA(()),
            pltpu.SemaphoreType.DMA((devices,)),
        ],
        out_shape=jax.ShapeDtypeStruct((devices, CAP * BLOCK + LABEL, BLOCK), BF16),
        compiler_params=pltpu.CompilerParams(vmem_limit_bytes=32 << 20),
        cost_estimate=pl.CostEstimate(
            flops=V * 2 * STRIPS * TAPS * STRIP * BAND * WIDTH,
            bytes_accessed=V * (BLOCK * WIDTH * 6),
            transcendentals=0,
        ),
        name="match_warp",
    )(
        patch, slot, owner, weight, *ready,
        jnp.asarray(sort, BF16), jnp.asarray(sort.T, BF16), images, above, below,
    )


def coadd_kernel(got, out, total, out_sem):
    devices = got.shape[0]
    wide = devices * CAP * STRIP
    labels = got[:, CAP * BLOCK : CAP * BLOCK + LABEL][:, 0]
    lane = iota((1, wide), 1)
    rank = lane // STRIP % CAP
    source = lane // (STRIP * CAP)

    def spread(entry):
        onehot = (iota((LANES, wide), 0) == rank * 2 + entry).astype(F32).astype(BF16)
        every = jnp.dot(labels, onehot, preferred_element_type=F32)
        return jnp.sum(
            jnp.where(iota((devices, wide), 0) == source, every, 0.0), axis=0, keepdims=True
        )

    weights, cells = spread(0), spread(1)
    row = iota((CELLS * STRIP, 1), 0)
    mine = (cells == (row // STRIP).astype(F32)) & (lane % STRIP == row % STRIP)
    matrix = jnp.where(mine, weights, 0.0)
    sums = jnp.sum(matrix, axis=1, keepdims=True)
    inverse = 1.0 / jnp.maximum(sums, 1.0)
    matrix = matrix.astype(BF16)
    copies = []
    for pair in range(BLOCK // STRIP // 2):
        columns = jnp.concatenate(
            [
                jnp.concatenate(
                    [
                        got[s, r * BLOCK + k * STRIP : r * BLOCK + (k + 1) * STRIP]
                        for s in range(devices)
                        for r in range(CAP)
                    ],
                    axis=0,
                )
                for k in (2 * pair, 2 * pair + 1)
            ],
            axis=1,
        )
        result = jnp.dot(matrix, columns, preferred_element_type=F32) * inverse
        for c in range(CELLS):
            part = result[c * STRIP : (c + 1) * STRIP]
            lanes = slice(c % PSIDE * BLOCK, (c % PSIDE + 1) * BLOCK)
            for n in range(2):
                first = (2 * pair + n) * STRIP
                total[c // PSIDE, first : first + STRIP, lanes] = lane_block(part, n)
        size = 2 * STRIP
        for line in range(PSIDE):
            copies.append(
                pltpu.make_async_copy(
                    total.at[line, pl.ds(pair * size, size)],
                    out.at[0, pl.ds(line * BLOCK + pair * size, size)],
                    out_sem.at[pair, line],
                )
            )
            copies[-1].start()
    for copy in copies:
        copy.wait()


def coadd(got):
    return pl.pallas_call(
        coadd_kernel,
        in_specs=[pl.BlockSpec(memory_space=pltpu.VMEM)],
        out_specs=pl.BlockSpec(memory_space=pl.ANY),
        out_shape=jax.ShapeDtypeStruct((1, PSIDE * BLOCK, PSIDE * BLOCK), F32),
        scratch_shapes=[
            pltpu.VMEM((PSIDE, BLOCK, WIDTH), F32),
            pltpu.SemaphoreType.DMA((BLOCK // STRIP // 2, PSIDE)),
        ],
        compiler_params=pltpu.CompilerParams(vmem_limit_bytes=32 << 20),
        name="coadd",
    )(got)


def shards(
    images, basis_taps, psf_coef, affine, visit_weight, block_patch, block_slot, patch_owner
):
    devices = lax.axis_size("ccd")
    down = [(i, i + 1) for i in range(devices - 1)]
    up = [(i + 1, i) for i in range(devices - 1)]
    above = lax.ppermute(images[:, BLOCK - RIM :], "ccd", down)
    below = lax.ppermute(images[:, :RIM], "ccd", up)
    patch = block_patch[:, :, 0]
    ready = prepare(basis_taps, psf_coef, affine, devices)
    sent = warp(
        patch, block_slot, patch_owner, visit_weight, ready, images, above, below, devices
    )
    got = lax.all_to_all(sent, "ccd", split_axis=0, concat_axis=0, tiled=True)
    return coadd(got)


def solution(mesh):
    placed = (
        P(None, ("group", "ccd"), None),
        P(),
        P(None, "group", None, None),
        P(None, "group", None, None),
        P(None, "group"),
        P(("group", "ccd"), None, None),
        P(("group", "ccd"), None),
        P("group"),
    )
    return jax.shard_map(
        shards,
        mesh=mesh,
        in_specs=placed,
        out_specs=P(("group", "ccd"), None, None),
        check_vma=False,
    )
```

```python
import functools

import jax
import jax.numpy as jnp
import numpy as np
from jax import lax
from jax.experimental import pallas as pl
from jax.experimental.pallas import tpu as pltpu
from jax.sharding import PartitionSpec as P

V = 4
BLOCK = 128
BLKC = 4
SPLIT = 4
TAPS = 11
NBASIS = 9
PSIDE = 4
CELLS = PSIDE * PSIDE
CAP = 2

HALF = TAPS // 2
WARP = 3
RIM = HALF + WARP
HEIGHT = SPLIT * BLOCK
WIDTH = BLKC * BLOCK
LANES = 128
LANE_BLOCKS = WIDTH // LANES
STRIP = 16
STEP = 32
STRIPS = -(-(BLOCK + 2 * WARP) // STRIP)
MIDDLE = STRIPS // 2
GROUPS = 6
BAND = 256
TALL = (STRIPS - 1) * STRIP + STEP
HALVES = 2
TOGETHER = 2
ROWS = BLOCK // HALVES
WINDOW = ROWS + STRIP
LABEL = 16
F32 = jnp.float32
BF16 = jnp.bfloat16


def sin_pi(t):
    whole = jnp.round(t)
    f = t - whole
    odd = whole - 2.0 * jnp.floor(0.5 * whole)
    f2 = f * f
    out = 0.0
    for c in (
        0.00046630280576761, -0.0073704309457144, 0.0821458866111282,
        -0.599264529320792, 2.55016403987734, -5.16771278004997, 3.14159265358979,
    ):
        out = out * f2 + c
    return f * out * (1.0 - 2.0 * odd)


def lanczos(t):
    zero = t == 0.0
    safe = jnp.where(zero, 1.0, t)
    pt = jnp.pi * safe
    value = 3.0 * sin_pi(safe) * sin_pi(safe / 3.0) / (pt * pt)
    return jnp.where(jnp.abs(t) < 3.0, jnp.where(zero, 1.0, value), 0.0)


def iota(shape, dim):
    return lax.broadcasted_iota(jnp.int32, shape, dim)


def deinterleave():
    order = np.arange(WIDTH).reshape(LANES, LANE_BLOCKS).T.reshape(-1)
    return (np.arange(WIDTH)[:, None] == order[None, :]).astype(np.float32)


def column_at(lane):
    return lane % LANES * LANE_BLOCKS + lane // LANES


def lane_block(x, v):
    return x[:, v * LANES : (v + 1) * LANES]


def dot_exact(a, b, dims):
    return lax.dot_general(
        a, b, (dims, ((), ())), precision=lax.Precision.HIGHEST, preferred_element_type=F32
    )


def staircase(x, first):
    return jnp.concatenate(
        [
            pltpu.roll(x[g : g + 8], first + g, 1, stride=1, stride_axis=0)
            for g in range(0, x.shape[0], 8)
        ],
        axis=0,
    )


def lane_sum(terms_of, lane, count, weigh):
    blocks = []
    for v in range(LANE_BLOCKS):
        total = None
        half = count // 2
        for q in range(-(-half // LANE_BLOCKS) * -1, (half + LANE_BLOCKS - 1) // LANE_BLOCKS + 1):
            part = None
            for u in range(count):
                if (v + u - half) // LANE_BLOCKS != q:
                    continue
                piece = terms_of(u, v, (v + u - half) % LANE_BLOCKS)
                part = piece if part is None else part + piece
            if part is None:
                continue
            if q:
                part = pltpu.roll(part, -q % LANES, 1)
                if not weigh:
                    part = jnp.where((lane + q >= 0) & (lane + q < LANES), part, 0.0)
            total = part if total is None else total + part
        blocks.append(total)
    return blocks


def whereabouts(devices):
    band = lax.axis_index("ccd")
    quarter = (band + SPLIT // 2) % SPLIT
    has_above = (quarter > 0) & (band > 0)
    has_below = (quarter < SPLIT - 1) & (band < devices - 1)
    return (band + SPLIT // 2) // SPLIT, quarter * BLOCK, has_above, has_below


def prepare_kernel(
    devices, taps, psf, affine,
    high_level, step_level, slope, rows_high, rows_low, cols_out, empty_out,
    nothing, sems,
):
    nothing[...] = jnp.zeros_like(nothing)
    clears = [
        pltpu.make_async_copy(nothing, empty_out.at[d], sems.at[d]) for d in range(devices)
    ]
    for copy in clears:
        copy.start()
    ccd, top_row, has_above, has_below = whereabouts(devices)
    band_lane = iota((1, BAND), 1)
    seg = band_lane // STEP
    lane = iota((1, LANES), 1)
    tap = band_lane - seg * STEP
    onehot = (tap == iota((TAPS, BAND), 0)) & (seg < GROUPS)
    row_taps = dot_exact(taps[:, 0], onehot.astype(F32), ((1,), (0,)))
    eye = (iota((TAPS, STRIP), 0) == iota((TAPS, STRIP), 1)).astype(F32)
    turned_taps = dot_exact(eye, taps[:, 1], ((0,), (1,)))
    for visit in range(V):
        lhs = jnp.concatenate(
            [turned_taps * psf[ccd, c, visit : visit + 1, :] for c in range(3)], axis=0
        )
        kernels = dot_exact(lhs, row_taps, ((1,), (0,)))
        const, by_row, by_col = (kernels[c * STRIP : (c + 1) * STRIP] for c in range(3))
        is_level = seg < 3
        per_strip = 2.0 * STRIP / HEIGHT
        middle_row = (top_row + (MIDDLE * STRIP - WARP)).astype(F32)
        middle_pos = (2.0 * middle_row + 1.0) / HEIGHT - 1.0
        col_move = (iota((STRIP, 1), 0) - HALF).astype(F32) * (2.0 / WIDTH)
        by_row = jnp.where(is_level, by_row, 0.0)
        const = jnp.where(is_level, const + middle_pos * by_row - col_move * by_col, by_col)
        reach = per_strip * (STRIPS - MIDDLE)
        largest = jnp.max(jnp.abs(const) + reach * jnp.abs(by_row), axis=(0, 1), keepdims=True)
        unit = jnp.maximum(largest, 1e-30) * (1.0 / 200.0)
        const = const / unit
        by_row = (by_row * per_strip) / unit
        low_lanes = (lane // STEP) % 3 == 2
        low_band = seg % 3 == 2
        row_part = iota((STRIP, 1), 0).astype(F32) * (1.0 / STRIP)
        for u in range(TAPS):
            at = slice(u * STRIP, (u + 1) * STRIP)
            x = staircase(jnp.broadcast_to(const[u : u + 1], (STRIP, BAND)), 0)
            y = staircase(jnp.broadcast_to(by_row[u : u + 1, :LANES], (STRIP, LANES)), 0)
            tail = x[:, LANES:]
            high = tail.astype(BF16).astype(F32)
            slope[visit, at] = jnp.where(low_band[:, LANES:], tail - high, high).astype(BF16)
            x = x[:, :LANES] + row_part * y
            high = jnp.where(lane < 3 * STEP, jnp.round(x), x.astype(BF16).astype(F32))
            high_level[visit, at] = jnp.where(low_lanes, x - high, high)
            high = jnp.round(y)
            step_level[visit, at] = jnp.where(low_lanes, y - high, high)

        a = jnp.sum(
            jnp.where(iota((1, 1, affine.shape[3]), 2) == ccd, affine[visit], 0.0),
            axis=2, keepdims=True,
        )
        offset = iota((8, LANES), 0) - WARP
        row = (top_row + lane).astype(F32)
        shift = a[0, 0:1] + a[0, 1:2] * (row - (HEIGHT - 1) / 2.0) / HEIGHT
        band_row = lane + offset
        keep = (offset <= WARP) & ((band_row >= 0) | has_above) & ((band_row < BLOCK) | has_below)
        weights = jnp.where(keep, lanczos(shift - offset.astype(F32)), 0.0) * unit
        weights = jnp.concatenate([weights, jnp.zeros((LANES - 8, LANES), F32)], axis=0).T
        for h in range(HALVES):
            at = slice(h * ROWS, (h + 1) * ROWS)
            matrix = staircase(weights[at], 0)
            high = matrix.astype(BF16)
            rows_high[visit, at] = high
            rows_low[visit, at] = (matrix - high.astype(F32)).astype(BF16)

        lanes = iota((8, WIDTH), 1)
        step = iota((8, WIDTH), 0) - WARP
        block = lanes // LANES
        carry = (block + step + LANE_BLOCKS) // LANE_BLOCKS - 1
        from_lane = lanes % LANES - carry
        col = (from_lane * LANE_BLOCKS + block).astype(F32)
        col_shift = a[1, 0:1] + a[1, 1:2] * (col - (WIDTH - 1) / 2.0) / WIDTH
        within = (from_lane >= 0) & (from_lane < LANES) & (step <= WARP)
        cols_out[visit] = jnp.where(within, lanczos(col_shift - step.astype(F32)), 0.0)
    for copy in clears:
        copy.wait()


def prepare(taps, psf, affine, devices):
    shapes = [
        ((V, TAPS * STRIP, LANES), F32),
        ((V, TAPS * STRIP, LANES), F32),
        ((V, TAPS * STRIP, BAND - LANES), BF16),
        ((V, BLOCK, LANES), BF16),
        ((V, BLOCK, LANES), BF16),
        ((V, 8, WIDTH), F32),
    ]
    places = (devices, CAP * BLOCK + LABEL, BLOCK)
    args = [taps.transpose(1, 0, 2), psf.transpose(1, 3, 0, 2), affine.transpose(0, 2, 3, 1)]
    return pl.pallas_call(
        functools.partial(prepare_kernel, devices),
        grid=(1,),
        in_specs=[pl.BlockSpec(x.shape, lambda i, n=x.ndim: (0,) * n) for x in args],
        out_specs=[pl.BlockSpec(shape, lambda i: (0, 0, 0)) for shape, _ in shapes]
        + [pl.BlockSpec(memory_space=pl.ANY)],
        out_shape=[jax.ShapeDtypeStruct(shape, kind) for shape, kind in shapes + [(places, BF16)]],
        scratch_shapes=[pltpu.VMEM(places[1:], BF16), pltpu.SemaphoreType.DMA((devices,))],
        compiler_params=pltpu.CompilerParams(vmem_limit_bytes=32 << 20),
        cost_estimate=pl.CostEstimate(flops=1 << 30, bytes_accessed=1 << 20, transcendentals=0),
        name="prepare",
    )(*args)


def warp_kernel(
    patch, slot, owner, weight, high_level, step_level, slope, rows_high, rows_low, col_weights,
    sort, unsort, image, above, below, _, out,
    terms, matched_terms, ready, place_of, seen, label, label_ready, sem, label_sem,
):
    grid_step = pl.program_id(0)
    grid_steps = pl.num_programs(0)
    devices = label.shape[0]
    ccd, _, has_above, has_below = whereabouts(devices)
    tall = BLOCK + 2 * RIM
    lane = iota((1, LANES), 1)
    label_copy = pltpu.make_async_copy(label_ready, out.at[:, pl.ds(CAP * BLOCK, LABEL)], label_sem)

    @pl.when(grid_step == 0)
    def _():
        terms[:, :, tall:] = jnp.zeros((TOGETHER, 4, TALL - tall, WIDTH), BF16)
        label[...] = jnp.zeros_like(label)

        def clear(p, _):
            seen[p] = 0
            return 0

        lax.fori_loop(0, owner.shape[0], clear, 0)
        own = jnp.where(iota(weight.shape, 1) == ccd, weight[...].astype(F32), 0.0)
        own = jnp.sum(own, axis=1, keepdims=True)
        for block in range(V * BLKC):
            p = patch[0, block]
            to = owner[p]
            rank = seen[p]
            seen[p] = rank + 1
            place_of[block] = to * CAP + rank
            line = label[pl.ds(to, 1), :]
            line = jnp.where(lane == rank * 2, own[block // BLKC : block // BLKC + 1], line)
            line = jnp.where(lane == rank * 2 + 1, slot[0, block].astype(F32), line)
            label[pl.ds(to, 1), :] = line
        label_ready[...] = jnp.broadcast_to(
            label[...].reshape(devices, 1, LANES), (devices, LABEL, LANES)
        ).astype(BF16)
        label_copy.start()

    col_pos = (2.0 * column_at(iota((1, WIDTH), 1)).astype(F32) + 1.0) / WIDTH - 1.0
    for i in range(TOGETHER):
        raw = jnp.concatenate(
            [jnp.where(has_above, above[i], 0.0), image[i], jnp.where(has_below, below[i], 0.0)],
            axis=0,
        )
        raw_high = raw.astype(BF16)
        raw_low = (raw - raw_high.astype(F32)).astype(BF16)
        sorted_terms = jnp.dot(
            jnp.concatenate([raw_high, raw_low], axis=0), sort[...], preferred_element_type=F32
        )
        high, low = sorted_terms[:tall], sorted_terms[tall:]
        tilted = (high + low) * col_pos
        tilted_high = tilted.astype(BF16)
        terms[i, 0, :tall] = high.astype(BF16)
        terms[i, 1, :tall] = low.astype(BF16)
        terms[i, 2, :tall] = tilted_high
        terms[i, 3, :tall] = (tilted - tilted_high.astype(F32)).astype(BF16)

    filler = jnp.zeros((BAND - GROUPS * STEP, WIDTH), BF16)
    for k in range(STRIPS):
        for i in range(TOGETHER):
            level = high_level[i]
            if k != MIDDLE:
                level = level + float(k - MIDDLE) * step_level[i]
            matrix = jnp.concatenate([level.astype(BF16), slope[i]], axis=1)
            rows = slice(k * STRIP, k * STRIP + STEP)
            columns = jnp.concatenate(
                [terms[i, h, rows] for h in (0, 1, 0, 2, 3, 2)] + [filler], axis=0
            )
            results = jnp.dot(matrix, columns, preferred_element_type=F32)
            blocks = lane_sum(
                lambda u, v, w: lane_block(results[u * STRIP : (u + 1) * STRIP], w),
                lane, TAPS, False,
            )
            matched = jnp.concatenate(blocks, axis=1)
            high = matched.astype(BF16)
            at = slice(k * STRIP, (k + 1) * STRIP)
            matched_terms[i, 0, at] = high
            matched_terms[i, 1, at] = (matched - high.astype(F32)).astype(BF16)

    empty = jnp.zeros((LANES - WINDOW, WIDTH), BF16)
    warped = []
    for i in range(TOGETHER):
        halves = []
        for h in range(HALVES):
            high = rows_high[i, h * ROWS : (h + 1) * ROWS]
            low = rows_low[i, h * ROWS : (h + 1) * ROWS]
            rows = slice(h * ROWS, h * ROWS + WINDOW)
            first = jnp.concatenate([matched_terms[i, 0, rows], empty], axis=0)
            second = jnp.concatenate([matched_terms[i, 1, rows], empty], axis=0)
            both = jnp.dot(
                jnp.concatenate([high, high], axis=1), jnp.concatenate([first, second], axis=0),
                preferred_element_type=F32,
            )
            halves.append(both + jnp.dot(low, first, preferred_element_type=F32))
        warped.append(jnp.concatenate(halves, axis=0))

    for i in range(TOGETHER):
        cols = col_weights[i]
        blocks = lane_sum(
            lambda s, v, w: lane_block(cols[s : s + 1], v) * lane_block(warped[i], w),
            lane, 2 * WARP + 1, True,
        )
        result = jnp.dot(
            jnp.concatenate(blocks, axis=1).astype(BF16), unsort[...], preferred_element_type=F32
        ).astype(BF16)
        for j in range(BLKC):
            block = (grid_step * TOGETHER + i) * BLKC + j
            ready[block] = result[:, j * BLOCK : (j + 1) * BLOCK]
            to = place_of[block]
            row = pl.multiple_of(to % CAP * BLOCK, BLOCK)
            pltpu.make_async_copy(
                ready.at[block], out.at[to // CAP, pl.ds(row, BLOCK)], sem.at[block]
            ).start()

    @pl.when(grid_step == grid_steps - 1)
    def _():
        label_copy.wait()
        for block in range(V * BLKC):
            pltpu.make_async_copy(ready.at[block], out.at[0, pl.ds(0, BLOCK)], sem.at[block]).wait()


def warp(patch, slot, owner, weight, ready, images, above, below, devices):
    smem = pl.BlockSpec(memory_space=pltpu.SMEM)
    hbm = pl.BlockSpec(memory_space=pl.ANY)
    sort = deinterleave()
    constants = [jnp.asarray(sort, BF16), jnp.asarray(sort.T, BF16)]
    *ready, places = ready
    args = [patch, slot, owner, weight, *ready, *constants, images, above, below, places]

    def whole(x):
        return pl.BlockSpec(x.shape, lambda v: (0,) * x.ndim)

    def by_visit(x):
        return pl.BlockSpec((TOGETHER,) + x.shape[1:], lambda v: (v, 0, 0))

    return pl.pallas_call(
        warp_kernel,
        grid=(V // TOGETHER,),
        in_specs=[smem, smem, smem, whole(weight)]
        + [by_visit(x) for x in ready]
        + [whole(x) for x in constants]
        + [by_visit(x) for x in (images, above, below)]
        + [hbm],
        out_specs=hbm,
        scratch_shapes=[
            pltpu.VMEM((TOGETHER, 4, TALL, WIDTH), BF16),
            pltpu.VMEM((TOGETHER, 2, STRIPS * STRIP, WIDTH), BF16),
            pltpu.VMEM((V * BLKC, BLOCK, BLOCK), BF16),
            pltpu.SMEM((V * BLKC,), jnp.int32),
            pltpu.SMEM((owner.shape[0],), jnp.int32),
            pltpu.VMEM((devices, LANES), F32),
            pltpu.VMEM((devices, LABEL, LANES), BF16),
            pltpu.SemaphoreType.DMA((V * BLKC,)),
            pltpu.SemaphoreType.DMA(()),
        ],
        out_shape=jax.ShapeDtypeStruct(places.shape, BF16),
        input_output_aliases={len(args) - 1: 0},
        compiler_params=pltpu.CompilerParams(vmem_limit_bytes=32 << 20),
        cost_estimate=pl.CostEstimate(
            flops=V * 2 * STRIPS * TAPS * STRIP * BAND * WIDTH,
            bytes_accessed=V * (BLOCK * WIDTH * 6),
            transcendentals=0,
        ),
        name="match_warp",
    )(*args)


def coadd_kernel(got, out, total, out_sem):
    devices = got.shape[0]
    wide = devices * CAP * STRIP
    labels = got[:, CAP * BLOCK : CAP * BLOCK + LABEL][:, 0]
    lane = iota((1, wide), 1)
    rank = lane // STRIP % CAP
    source = lane // (STRIP * CAP)

    def spread(entry):
        onehot = (iota((LANES, wide), 0) == rank * 2 + entry).astype(F32).astype(BF16)
        every = jnp.dot(labels, onehot, preferred_element_type=F32)
        return jnp.sum(
            jnp.where(iota((devices, wide), 0) == source, every, 0.0), axis=0, keepdims=True
        )

    weights, cells = spread(0), spread(1)
    row = iota((CELLS * STRIP, 1), 0)
    mine = (cells == (row // STRIP).astype(F32)) & (lane % STRIP == row % STRIP)
    matrix = jnp.where(mine, weights, 0.0)
    sums = jnp.sum(matrix, axis=1, keepdims=True)
    inverse = 1.0 / jnp.maximum(sums, 1.0)
    matrix = matrix.astype(BF16)
    copies = []
    for pair in range(BLOCK // STRIP // 2):
        columns = jnp.concatenate(
            [
                jnp.concatenate(
                    [
                        got[s, r * BLOCK + k * STRIP : r * BLOCK + (k + 1) * STRIP]
                        for s in range(devices)
                        for r in range(CAP)
                    ],
                    axis=0,
                )
                for k in (2 * pair, 2 * pair + 1)
            ],
            axis=1,
        )
        result = jnp.dot(matrix, columns, preferred_element_type=F32) * inverse
        for c in range(CELLS):
            part = result[c * STRIP : (c + 1) * STRIP]
            lanes = slice(c % PSIDE * BLOCK, (c % PSIDE + 1) * BLOCK)
            for n in range(2):
                first = (2 * pair + n) * STRIP
                total[c // PSIDE, first : first + STRIP, lanes] = lane_block(part, n)
        size = 2 * STRIP
        for line in range(PSIDE):
            copies.append(
                pltpu.make_async_copy(
                    total.at[line, pl.ds(pair * size, size)],
                    out.at[0, pl.ds(line * BLOCK + pair * size, size)],
                    out_sem.at[pair, line],
                )
            )
            copies[-1].start()
    for copy in copies:
        copy.wait()


def coadd(got):
    return pl.pallas_call(
        coadd_kernel,
        in_specs=[pl.BlockSpec(memory_space=pltpu.VMEM)],
        out_specs=pl.BlockSpec(memory_space=pl.ANY),
        out_shape=jax.ShapeDtypeStruct((1, PSIDE * BLOCK, PSIDE * BLOCK), F32),
        scratch_shapes=[
            pltpu.VMEM((PSIDE, BLOCK, WIDTH), F32),
            pltpu.SemaphoreType.DMA((BLOCK // STRIP // 2, PSIDE)),
        ],
        compiler_params=pltpu.CompilerParams(vmem_limit_bytes=32 << 20),
        name="coadd",
    )(got)


def shards(
    images, basis_taps, psf_coef, affine, visit_weight, block_patch, block_slot, patch_owner
):
    devices = lax.axis_size("ccd")
    down = [(i, i + 1) for i in range(devices - 1)]
    up = [(i + 1, i) for i in range(devices - 1)]
    above = lax.ppermute(images[:, BLOCK - RIM :], "ccd", down)
    below = lax.ppermute(images[:, :RIM], "ccd", up)
    patch = block_patch[:, :, 0]
    ready = prepare(basis_taps, psf_coef, affine, devices)
    sent = warp(
        patch, block_slot, patch_owner, visit_weight, ready, images, above, below, devices
    )
    got = lax.all_to_all(sent, "ccd", split_axis=0, concat_axis=0, tiled=True)
    return coadd(got)


def solution(mesh):
    placed = (
        P(None, ("group", "ccd"), None),
        P(),
        P(None, "group", None, None),
        P(None, "group", None, None),
        P(None, "group"),
        P(("group", "ccd"), None, None),
        P(("group", "ccd"), None),
        P("group"),
    )
    return jax.shard_map(
        shards,
        mesh=mesh,
        in_specs=placed,
        out_specs=P(("group", "ccd"), None, None),
        check_vma=False,
    )
```

```python
import functools

import jax
import jax.numpy as jnp
import numpy as np
from jax import lax
from jax.experimental import pallas as pl
from jax.experimental.pallas import tpu as pltpu
from jax.sharding import PartitionSpec as P

V = 4
BLOCK = 128
BLKC = 4
SPLIT = 4
TAPS = 11
NBASIS = 9
PSIDE = 4
CELLS = PSIDE * PSIDE
CAP = 2

HALF = TAPS // 2
WARP = 3
RIM = HALF + WARP
HEIGHT = SPLIT * BLOCK
WIDTH = BLKC * BLOCK
LANES = 128
LANE_BLOCKS = WIDTH // LANES
STRIP = 16
STEP = 32
STRIPS = -(-(BLOCK + 2 * WARP) // STRIP)
MIDDLE = STRIPS // 2
GROUPS = 6
BAND = 256
TALL = (STRIPS - 1) * STRIP + STEP
HALVES = 2
TOGETHER = 2
ROWS = BLOCK // HALVES
WINDOW = ROWS + STRIP
LABEL = 16
F32 = jnp.float32
BF16 = jnp.bfloat16


def sin_pi(t):
    whole = jnp.round(t)
    f = t - whole
    odd = whole - 2.0 * jnp.floor(0.5 * whole)
    f2 = f * f
    out = 0.0
    for c in (
        0.00046630280576761, -0.0073704309457144, 0.0821458866111282,
        -0.599264529320792, 2.55016403987734, -5.16771278004997, 3.14159265358979,
    ):
        out = out * f2 + c
    return f * out * (1.0 - 2.0 * odd)


def lanczos(t):
    zero = t == 0.0
    safe = jnp.where(zero, 1.0, t)
    pt = jnp.pi * safe
    value = 3.0 * sin_pi(safe) * sin_pi(safe / 3.0) / (pt * pt)
    return jnp.where(jnp.abs(t) < 3.0, jnp.where(zero, 1.0, value), 0.0)


def iota(shape, dim):
    return lax.broadcasted_iota(jnp.int32, shape, dim)


def deinterleave():
    order = np.arange(WIDTH).reshape(LANES, LANE_BLOCKS).T.reshape(-1)
    return (np.arange(WIDTH)[:, None] == order[None, :]).astype(np.float32)


def column_at(lane):
    return lane % LANES * LANE_BLOCKS + lane // LANES


def lane_block(x, v):
    return x[:, v * LANES : (v + 1) * LANES]


def dot_exact(a, b, dims):
    return lax.dot_general(
        a, b, (dims, ((), ())), precision=lax.Precision.HIGHEST, preferred_element_type=F32
    )


def staircase(x, first):
    return jnp.concatenate(
        [
            pltpu.roll(x[g : g + 8], first + g, 1, stride=1, stride_axis=0)
            for g in range(0, x.shape[0], 8)
        ],
        axis=0,
    )


def lane_sum(terms_of, lane, count, weigh):
    blocks = []
    for v in range(LANE_BLOCKS):
        total = None
        half = count // 2
        for q in range(-(-half // LANE_BLOCKS) * -1, (half + LANE_BLOCKS - 1) // LANE_BLOCKS + 1):
            part = None
            for u in range(count):
                if (v + u - half) // LANE_BLOCKS != q:
                    continue
                piece = terms_of(u, v, (v + u - half) % LANE_BLOCKS)
                part = piece if part is None else part + piece
            if part is None:
                continue
            if q:
                part = pltpu.roll(part, -q % LANES, 1)
                if not weigh:
                    part = jnp.where((lane + q >= 0) & (lane + q < LANES), part, 0.0)
            total = part if total is None else total + part
        blocks.append(total)
    return blocks


def whereabouts(devices):
    band = lax.axis_index("ccd")
    quarter = (band + SPLIT // 2) % SPLIT
    has_above = (quarter > 0) & (band > 0)
    has_below = (quarter < SPLIT - 1) & (band < devices - 1)
    return (band + SPLIT // 2) // SPLIT, quarter * BLOCK, has_above, has_below


def lanczos_kernel(devices, affine, rows_out, cols_out):
    ccd, top_row, has_above, has_below = whereabouts(devices)
    lane = iota((1, LANES), 1)
    for visit in range(V):
        a = jnp.sum(
            jnp.where(iota((1, 1, affine.shape[3]), 2) == ccd, affine[visit], 0.0),
            axis=2, keepdims=True,
        )
        offset = iota((8, LANES), 0) - WARP
        row = (top_row + lane).astype(F32)
        shift = a[0, 0:1] + a[0, 1:2] * (row - (HEIGHT - 1) / 2.0) / HEIGHT
        band_row = lane + offset
        keep = (offset <= WARP) & ((band_row >= 0) | has_above) & ((band_row < BLOCK) | has_below)
        weights = jnp.where(keep, lanczos(shift - offset.astype(F32)), 0.0)
        rows_out[visit] = jnp.concatenate([weights, jnp.zeros((LANES - 8, LANES), F32)], axis=0).T
        lanes = iota((8, WIDTH), 1)
        step = iota((8, WIDTH), 0) - WARP
        block = lanes // LANES
        carry = (block + step + LANE_BLOCKS) // LANE_BLOCKS - 1
        from_lane = lanes % LANES - carry
        col = (from_lane * LANE_BLOCKS + block).astype(F32)
        col_shift = a[1, 0:1] + a[1, 1:2] * (col - (WIDTH - 1) / 2.0) / WIDTH
        within = (from_lane >= 0) & (from_lane < LANES) & (step <= WARP)
        cols_out[visit] = jnp.where(within, lanczos(col_shift - step.astype(F32)), 0.0)


def prepare_kernel(
    devices, taps, psf, row_weights, high_level, step_level, slope, rows_high, rows_low
):
    ccd, top_row, _, _ = whereabouts(devices)
    band_lane = iota((1, BAND), 1)
    seg = band_lane // STEP
    lane = iota((1, LANES), 1)
    tap = band_lane - seg * STEP
    onehot = (tap == iota((TAPS, BAND), 0)) & (seg < GROUPS)
    row_taps = dot_exact(taps[:, 0], onehot.astype(F32), ((1,), (0,)))
    eye = (iota((TAPS, STRIP), 0) == iota((TAPS, STRIP), 1)).astype(F32)
    turned_taps = dot_exact(eye, taps[:, 1], ((0,), (1,)))
    for visit in range(V):
        lhs = jnp.concatenate(
            [turned_taps * psf[ccd, c, visit : visit + 1, :] for c in range(3)], axis=0
        )
        kernels = dot_exact(lhs, row_taps, ((1,), (0,)))
        const, by_row, by_col = (kernels[c * STRIP : (c + 1) * STRIP] for c in range(3))
        is_level = seg < 3
        per_strip = 2.0 * STRIP / HEIGHT
        middle_row = (top_row + (MIDDLE * STRIP - WARP)).astype(F32)
        middle_pos = (2.0 * middle_row + 1.0) / HEIGHT - 1.0
        col_move = (iota((STRIP, 1), 0) - HALF).astype(F32) * (2.0 / WIDTH)
        by_row = jnp.where(is_level, by_row, 0.0)
        const = jnp.where(is_level, const + middle_pos * by_row - col_move * by_col, by_col)
        reach = per_strip * (STRIPS - MIDDLE)
        largest = jnp.max(jnp.abs(const) + reach * jnp.abs(by_row), axis=(0, 1), keepdims=True)
        unit = jnp.maximum(largest, 1e-30) * (1.0 / 200.0)
        const = const / unit
        by_row = (by_row * per_strip) / unit
        low_lanes = (lane // STEP) % 3 == 2
        low_band = seg % 3 == 2
        row_part = iota((STRIP, 1), 0).astype(F32) * (1.0 / STRIP)
        for u in range(TAPS):
            at = slice(u * STRIP, (u + 1) * STRIP)
            x = staircase(jnp.broadcast_to(const[u : u + 1], (STRIP, BAND)), 0)
            y = staircase(jnp.broadcast_to(by_row[u : u + 1, :LANES], (STRIP, LANES)), 0)
            tail = x[:, LANES:]
            high = tail.astype(BF16).astype(F32)
            slope[visit, at] = jnp.where(low_band[:, LANES:], tail - high, high).astype(BF16)
            x = x[:, :LANES] + row_part * y
            high = jnp.where(lane < 3 * STEP, jnp.round(x), x.astype(BF16).astype(F32))
            high_level[visit, at] = jnp.where(low_lanes, x - high, high)
            high = jnp.round(y)
            step_level[visit, at] = jnp.where(low_lanes, y - high, high)

        for h in range(HALVES):
            at = slice(h * ROWS, (h + 1) * ROWS)
            matrix = staircase(row_weights[visit, at] * unit, 0)
            high = matrix.astype(BF16)
            rows_high[visit, at] = high
            rows_low[visit, at] = (matrix - high.astype(F32)).astype(BF16)


def small_kernel(body, name, args, shapes):
    return pl.pallas_call(
        body,
        grid=(1,),
        in_specs=[pl.BlockSpec(x.shape, lambda i, n=x.ndim: (0,) * n) for x in args],
        out_specs=[pl.BlockSpec(shape, lambda i: (0, 0, 0)) for shape, _ in shapes],
        out_shape=[jax.ShapeDtypeStruct(shape, kind) for shape, kind in shapes],
        compiler_params=pltpu.CompilerParams(vmem_limit_bytes=32 << 20),
        cost_estimate=pl.CostEstimate(flops=1 << 30, bytes_accessed=1 << 20, transcendentals=0),
        name=name,
    )(*args)


def prepare(taps, psf, affine, devices):
    row_weights, col_weights = small_kernel(
        functools.partial(lanczos_kernel, devices), "lanczos_weights",
        [affine.transpose(0, 2, 3, 1)],
        [((V, BLOCK, LANES), F32), ((V, 8, WIDTH), F32)],
    )
    matrices = small_kernel(
        functools.partial(prepare_kernel, devices), "matrices",
        [taps.transpose(1, 0, 2), psf.transpose(1, 3, 0, 2), row_weights],
        [
            ((V, TAPS * STRIP, LANES), F32),
            ((V, TAPS * STRIP, LANES), F32),
            ((V, TAPS * STRIP, BAND - LANES), BF16),
            ((V, BLOCK, LANES), BF16),
            ((V, BLOCK, LANES), BF16),
        ],
    )
    return [*matrices, col_weights]


def warp_kernel(
    patch, slot, owner, weight, high_level, step_level, slope, rows_high, rows_low, col_weights,
    sort, unsort, image, above, below, out,
    terms, matched_terms, ready, place_of, seen, label, label_ready, sem, label_sem,
):
    grid_step = pl.program_id(0)
    grid_steps = pl.num_programs(0)
    devices = label.shape[0]
    ccd, _, has_above, has_below = whereabouts(devices)
    tall = BLOCK + 2 * RIM
    lane = iota((1, LANES), 1)
    label_copy = pltpu.make_async_copy(label_ready, out.at[:, pl.ds(CAP * BLOCK, LABEL)], label_sem)

    @pl.when(grid_step == 0)
    def _():
        terms[:, :, tall:] = jnp.zeros((TOGETHER, 4, TALL - tall, WIDTH), BF16)
        label[...] = jnp.zeros_like(label)

        def clear(p, _):
            seen[p] = 0
            return 0

        lax.fori_loop(0, owner.shape[0], clear, 0)
        own = jnp.where(iota(weight.shape, 1) == ccd, weight[...].astype(F32), 0.0)
        own = jnp.sum(own, axis=1, keepdims=True)
        for block in range(V * BLKC):
            p = patch[0, block]
            to = owner[p]
            rank = seen[p]
            seen[p] = rank + 1
            place_of[block] = to * CAP + rank
            line = label[pl.ds(to, 1), :]
            line = jnp.where(lane == rank * 2, own[block // BLKC : block // BLKC + 1], line)
            line = jnp.where(lane == rank * 2 + 1, slot[0, block].astype(F32), line)
            label[pl.ds(to, 1), :] = line
        label_ready[...] = jnp.broadcast_to(
            label[...].reshape(devices, 1, LANES), (devices, LABEL, LANES)
        ).astype(BF16)
        label_copy.start()

    col_pos = (2.0 * column_at(iota((1, WIDTH), 1)).astype(F32) + 1.0) / WIDTH - 1.0
    for i in range(TOGETHER):
        raw = jnp.concatenate(
            [jnp.where(has_above, above[i], 0.0), image[i], jnp.where(has_below, below[i], 0.0)],
            axis=0,
        )
        raw_high = raw.astype(BF16)
        raw_low = (raw - raw_high.astype(F32)).astype(BF16)
        sorted_terms = jnp.dot(
            jnp.concatenate([raw_high, raw_low], axis=0), sort[...], preferred_element_type=F32
        )
        high, low = sorted_terms[:tall], sorted_terms[tall:]
        tilted = (high + low) * col_pos
        tilted_high = tilted.astype(BF16)
        terms[i, 0, :tall] = high.astype(BF16)
        terms[i, 1, :tall] = low.astype(BF16)
        terms[i, 2, :tall] = tilted_high
        terms[i, 3, :tall] = (tilted - tilted_high.astype(F32)).astype(BF16)

    filler = jnp.zeros((BAND - GROUPS * STEP, WIDTH), BF16)
    for k in range(STRIPS):
        for i in range(TOGETHER):
            level = high_level[i]
            if k != MIDDLE:
                level = level + float(k - MIDDLE) * step_level[i]
            matrix = jnp.concatenate([level.astype(BF16), slope[i]], axis=1)
            rows = slice(k * STRIP, k * STRIP + STEP)
            columns = jnp.concatenate(
                [terms[i, h, rows] for h in (0, 1, 0, 2, 3, 2)] + [filler], axis=0
            )
            results = jnp.dot(matrix, columns, preferred_element_type=F32)
            blocks = lane_sum(
                lambda u, v, w: lane_block(results[u * STRIP : (u + 1) * STRIP], w),
                lane, TAPS, False,
            )
            matched = jnp.concatenate(blocks, axis=1)
            high = matched.astype(BF16)
            at = slice(k * STRIP, (k + 1) * STRIP)
            matched_terms[i, 0, at] = high
            matched_terms[i, 1, at] = (matched - high.astype(F32)).astype(BF16)

    empty = jnp.zeros((LANES - WINDOW, WIDTH), BF16)
    warped = []
    for i in range(TOGETHER):
        halves = []
        for h in range(HALVES):
            high = rows_high[i, h * ROWS : (h + 1) * ROWS]
            low = rows_low[i, h * ROWS : (h + 1) * ROWS]
            rows = slice(h * ROWS, h * ROWS + WINDOW)
            first = jnp.concatenate([matched_terms[i, 0, rows], empty], axis=0)
            second = jnp.concatenate([matched_terms[i, 1, rows], empty], axis=0)
            both = jnp.dot(
                jnp.concatenate([high, high], axis=1), jnp.concatenate([first, second], axis=0),
                preferred_element_type=F32,
            )
            halves.append(both + jnp.dot(low, first, preferred_element_type=F32))
        warped.append(jnp.concatenate(halves, axis=0))

    for i in range(TOGETHER):
        cols = col_weights[i]
        blocks = lane_sum(
            lambda s, v, w: lane_block(cols[s : s + 1], v) * lane_block(warped[i], w),
            lane, 2 * WARP + 1, True,
        )
        result = jnp.dot(
            jnp.concatenate(blocks, axis=1).astype(BF16), unsort[...], preferred_element_type=F32
        ).astype(BF16)
        for j in range(BLKC):
            block = (grid_step * TOGETHER + i) * BLKC + j
            ready[block] = result[:, j * BLOCK : (j + 1) * BLOCK]
            to = place_of[block]
            row = pl.multiple_of(to % CAP * BLOCK, BLOCK)
            pltpu.make_async_copy(
                ready.at[block], out.at[to // CAP, pl.ds(row, BLOCK)], sem.at[block]
            ).start()

    @pl.when(grid_step == grid_steps - 1)
    def _():
        label_copy.wait()
        for block in range(V * BLKC):
            pltpu.make_async_copy(ready.at[block], out.at[0, pl.ds(0, BLOCK)], sem.at[block]).wait()


def warp(patch, slot, owner, weight, ready, images, above, below, devices):
    smem = pl.BlockSpec(memory_space=pltpu.SMEM)
    hbm = pl.BlockSpec(memory_space=pl.ANY)
    sort = deinterleave()
    constants = [jnp.asarray(sort, BF16), jnp.asarray(sort.T, BF16)]

    def whole(x):
        return pl.BlockSpec(x.shape, lambda v: (0,) * x.ndim)

    def by_visit(x):
        return pl.BlockSpec((TOGETHER,) + x.shape[1:], lambda v: (v, 0, 0))

    return pl.pallas_call(
        warp_kernel,
        grid=(V // TOGETHER,),
        in_specs=[smem, smem, smem, whole(weight)]
        + [by_visit(x) for x in ready]
        + [whole(x) for x in constants]
        + [by_visit(x) for x in (images, above, below)],
        out_specs=hbm,
        scratch_shapes=[
            pltpu.VMEM((TOGETHER, 4, TALL, WIDTH), BF16),
            pltpu.VMEM((TOGETHER, 2, STRIPS * STRIP, WIDTH), BF16),
            pltpu.VMEM((V * BLKC, BLOCK, BLOCK), BF16),
            pltpu.SMEM((V * BLKC,), jnp.int32),
            pltpu.SMEM((owner.shape[0],), jnp.int32),
            pltpu.VMEM((devices, LANES), F32),
            pltpu.VMEM((devices, LABEL, LANES), BF16),
            pltpu.SemaphoreType.DMA((V * BLKC,)),
            pltpu.SemaphoreType.DMA(()),
        ],
        out_shape=jax.ShapeDtypeStruct((devices, CAP * BLOCK + LABEL, BLOCK), BF16),
        compiler_params=pltpu.CompilerParams(vmem_limit_bytes=32 << 20),
        cost_estimate=pl.CostEstimate(
            flops=V * 2 * STRIPS * TAPS * STRIP * BAND * WIDTH,
            bytes_accessed=V * (BLOCK * WIDTH * 6),
            transcendentals=0,
        ),
        name="match_warp",
    )(patch, slot, owner, weight, *ready, *constants, images, above, below)


def coadd_kernel(got, out, total, out_sem):
    devices = got.shape[0]
    wide = devices * CAP * STRIP
    labels = got[:, CAP * BLOCK : CAP * BLOCK + LABEL][:, 0]
    lane = iota((1, wide), 1)
    rank = lane // STRIP % CAP
    source = lane // (STRIP * CAP)

    def spread(entry):
        onehot = (iota((LANES, wide), 0) == rank * 2 + entry).astype(F32).astype(BF16)
        every = jnp.dot(labels, onehot, preferred_element_type=F32)
        return jnp.sum(
            jnp.where(iota((devices, wide), 0) == source, every, 0.0), axis=0, keepdims=True
        )

    weights, cells = spread(0), spread(1)
    row = iota((CELLS * STRIP, 1), 0)
    mine = (cells == (row // STRIP).astype(F32)) & (lane % STRIP == row % STRIP)
    matrix = jnp.where(mine, weights, 0.0)
    sums = jnp.sum(matrix, axis=1, keepdims=True)
    inverse = 1.0 / jnp.maximum(sums, 1.0)
    matrix = matrix.astype(BF16)
    taken = {}
    for r in range(CAP):
        column = jnp.broadcast_to(labels[:, 2 * r : 2 * r + 1].astype(F32), (devices, LANES))
        for s in range(devices):
            taken[s, r] = jnp.broadcast_to(column[s : s + 1], (STRIP, LANES)).astype(BF16) > 0

    def tile(s, r, k):
        first = r * BLOCK + k * STRIP
        return jnp.where(taken[s, r], got[s, first : first + STRIP], jnp.zeros((), BF16))

    copies = []
    for pair in range(BLOCK // STRIP // 2):
        columns = jnp.concatenate(
            [
                jnp.concatenate(
                    [tile(s, r, k) for s in range(devices) for r in range(CAP)], axis=0
                )
                for k in (2 * pair, 2 * pair + 1)
            ],
            axis=1,
        )
        result = jnp.dot(matrix, columns, preferred_element_type=F32) * inverse
        for c in range(CELLS):
            part = result[c * STRIP : (c + 1) * STRIP]
            lanes = slice(c % PSIDE * BLOCK, (c % PSIDE + 1) * BLOCK)
            for n in range(2):
                first = (2 * pair + n) * STRIP
                total[c // PSIDE, first : first + STRIP, lanes] = lane_block(part, n)
        size = 2 * STRIP
        for line in range(PSIDE):
            copies.append(
                pltpu.make_async_copy(
                    total.at[line, pl.ds(pair * size, size)],
                    out.at[0, pl.ds(line * BLOCK + pair * size, size)],
                    out_sem.at[pair, line],
                )
            )
            copies[-1].start()
    for copy in copies:
        copy.wait()


def coadd(got):
    return pl.pallas_call(
        coadd_kernel,
        in_specs=[pl.BlockSpec(memory_space=pltpu.VMEM)],
        out_specs=pl.BlockSpec(memory_space=pl.ANY),
        out_shape=jax.ShapeDtypeStruct((1, PSIDE * BLOCK, PSIDE * BLOCK), F32),
        scratch_shapes=[
            pltpu.VMEM((PSIDE, BLOCK, WIDTH), F32),
            pltpu.SemaphoreType.DMA((BLOCK // STRIP // 2, PSIDE)),
        ],
        compiler_params=pltpu.CompilerParams(vmem_limit_bytes=32 << 20),
        name="coadd",
    )(got)


def shards(
    images, basis_taps, psf_coef, affine, visit_weight, block_patch, block_slot, patch_owner
):
    devices = lax.axis_size("ccd")
    down = [(i, i + 1) for i in range(devices - 1)]
    up = [(i + 1, i) for i in range(devices - 1)]
    above = lax.ppermute(images[:, BLOCK - RIM :], "ccd", down)
    below = lax.ppermute(images[:, :RIM], "ccd", up)
    patch = block_patch[:, :, 0]
    ready = prepare(basis_taps, psf_coef, affine, devices)
    sent = warp(
        patch, block_slot, patch_owner, visit_weight, ready, images, above, below, devices
    )
    got = lax.all_to_all(sent, "ccd", split_axis=0, concat_axis=0, tiled=True)
    return coadd(got)


def solution(mesh):
    placed = (
        P(None, ("group", "ccd"), None),
        P(),
        P(None, "group", None, None),
        P(None, "group", None, None),
        P(None, "group"),
        P(("group", "ccd"), None, None),
        P(("group", "ccd"), None),
        P("group"),
    )
    return jax.shard_map(
        shards,
        mesh=mesh,
        in_specs=placed,
        out_specs=P(("group", "ccd"), None, None),
        check_vma=False,
    )
```

```python
import functools

import jax
import jax.numpy as jnp
import numpy as np
from jax import lax
from jax.experimental import pallas as pl
from jax.experimental.pallas import tpu as pltpu
from jax.sharding import PartitionSpec as P

V = 4
BLOCK = 128
BLKC = 4
SPLIT = 4
TAPS = 11
NBASIS = 9
PSIDE = 4
CELLS = PSIDE * PSIDE
CAP = 2

HALF = TAPS // 2
WARP = 3
RIM = HALF + WARP
HEIGHT = SPLIT * BLOCK
WIDTH = BLKC * BLOCK
LANES = 128
LANE_BLOCKS = WIDTH // LANES
STRIP = 16
STEP = 32
STRIPS = -(-(BLOCK + 2 * WARP) // STRIP)
MIDDLE = STRIPS // 2
GROUPS = 6
BAND = 256
TALL = (STRIPS - 1) * STRIP + STEP
HALVES = 2
TOGETHER = 2
ROWS = BLOCK // HALVES
WINDOW = ROWS + STRIP
LABEL = 16
F32 = jnp.float32
BF16 = jnp.bfloat16


def sin_pi(t):
    whole = jnp.round(t)
    f = t - whole
    odd = whole - 2.0 * jnp.floor(0.5 * whole)
    f2 = f * f
    out = 0.0
    for c in (
        0.00046630280576761, -0.0073704309457144, 0.0821458866111282,
        -0.599264529320792, 2.55016403987734, -5.16771278004997, 3.14159265358979,
    ):
        out = out * f2 + c
    return f * out * (1.0 - 2.0 * odd)


def lanczos(t):
    zero = t == 0.0
    safe = jnp.where(zero, 1.0, t)
    pt = jnp.pi * safe
    value = 3.0 * sin_pi(safe) * sin_pi(safe / 3.0) / (pt * pt)
    return jnp.where(jnp.abs(t) < 3.0, jnp.where(zero, 1.0, value), 0.0)


def iota(shape, dim):
    return lax.broadcasted_iota(jnp.int32, shape, dim)


def deinterleave():
    order = np.arange(WIDTH).reshape(LANES, LANE_BLOCKS).T.reshape(-1)
    return (np.arange(WIDTH)[:, None] == order[None, :]).astype(np.float32)


def column_at(lane):
    return lane % LANES * LANE_BLOCKS + lane // LANES


def lane_block(x, v):
    return x[:, v * LANES : (v + 1) * LANES]


def dot_exact(a, b, dims):
    return lax.dot_general(
        a, b, (dims, ((), ())), precision=lax.Precision.HIGHEST, preferred_element_type=F32
    )


def staircase(x, first):
    return jnp.concatenate(
        [
            pltpu.roll(x[g : g + 8], first + g, 1, stride=1, stride_axis=0)
            for g in range(0, x.shape[0], 8)
        ],
        axis=0,
    )


def lane_sum(terms_of, lane, count, weigh):
    blocks = []
    for v in range(LANE_BLOCKS):
        total = None
        half = count // 2
        for q in range(-(-half // LANE_BLOCKS) * -1, (half + LANE_BLOCKS - 1) // LANE_BLOCKS + 1):
            part = None
            for u in range(count):
                if (v + u - half) // LANE_BLOCKS != q:
                    continue
                piece = terms_of(u, v, (v + u - half) % LANE_BLOCKS)
                part = piece if part is None else part + piece
            if part is None:
                continue
            if q:
                part = pltpu.roll(part, -q % LANES, 1)
                if not weigh:
                    part = jnp.where((lane + q >= 0) & (lane + q < LANES), part, 0.0)
            total = part if total is None else total + part
        blocks.append(total)
    return blocks


def whereabouts(devices):
    band = lax.axis_index("ccd")
    quarter = (band + SPLIT // 2) % SPLIT
    has_above = (quarter > 0) & (band > 0)
    has_below = (quarter < SPLIT - 1) & (band < devices - 1)
    return (band + SPLIT // 2) // SPLIT, quarter * BLOCK, has_above, has_below


def lanczos_kernel(devices, affine, rows_out, cols_out):
    ccd, top_row, has_above, has_below = whereabouts(devices)
    lane = iota((1, LANES), 1)
    for visit in range(V):
        a = jnp.sum(
            jnp.where(iota((1, 1, affine.shape[3]), 2) == ccd, affine[visit], 0.0),
            axis=2, keepdims=True,
        )
        offset = iota((8, LANES), 0) - WARP
        row = (top_row + lane).astype(F32)
        shift = a[0, 0:1] + a[0, 1:2] * (row - (HEIGHT - 1) / 2.0) / HEIGHT
        band_row = lane + offset
        keep = (offset <= WARP) & ((band_row >= 0) | has_above) & ((band_row < BLOCK) | has_below)
        weights = jnp.where(keep, lanczos(shift - offset.astype(F32)), 0.0)
        rows_out[visit] = jnp.concatenate([weights, jnp.zeros((LANES - 8, LANES), F32)], axis=0).T
        lanes = iota((8, WIDTH), 1)
        step = iota((8, WIDTH), 0) - WARP
        block = lanes // LANES
        carry = (block + step + LANE_BLOCKS) // LANE_BLOCKS - 1
        from_lane = lanes % LANES - carry
        col = (from_lane * LANE_BLOCKS + block).astype(F32)
        col_shift = a[1, 0:1] + a[1, 1:2] * (col - (WIDTH - 1) / 2.0) / WIDTH
        within = (from_lane >= 0) & (from_lane < LANES) & (step <= WARP)
        cols_out[visit] = jnp.where(within, lanczos(col_shift - step.astype(F32)), 0.0)


def prepare_kernel(
    devices, taps, psf, row_weights, high_level, step_level, slope, rows_high, rows_low
):
    ccd, top_row, _, _ = whereabouts(devices)
    band_lane = iota((1, BAND), 1)
    seg = band_lane // STEP
    lane = iota((1, LANES), 1)
    tap = band_lane - seg * STEP
    onehot = (tap == iota((TAPS, BAND), 0)) & (seg < GROUPS)
    row_taps = dot_exact(taps[:, 0], onehot.astype(F32), ((1,), (0,)))
    eye = (iota((TAPS, STRIP), 0) == iota((TAPS, STRIP), 1)).astype(F32)
    turned_taps = dot_exact(eye, taps[:, 1], ((0,), (1,)))
    for visit in range(V):
        lhs = jnp.concatenate(
            [turned_taps * psf[ccd, c, visit : visit + 1, :] for c in range(3)], axis=0
        )
        kernels = dot_exact(lhs, row_taps, ((1,), (0,)))
        const, by_row, by_col = (kernels[c * STRIP : (c + 1) * STRIP] for c in range(3))
        is_level = seg < 3
        per_strip = 2.0 * STRIP / HEIGHT
        middle_row = (top_row + (MIDDLE * STRIP - WARP)).astype(F32)
        middle_pos = (2.0 * middle_row + 1.0) / HEIGHT - 1.0
        col_move = (iota((STRIP, 1), 0) - HALF).astype(F32) * (2.0 / WIDTH)
        by_row = jnp.where(is_level, by_row, 0.0)
        const = jnp.where(is_level, const + middle_pos * by_row - col_move * by_col, by_col)
        reach = per_strip * (STRIPS - MIDDLE)
        largest = jnp.max(jnp.abs(const) + reach * jnp.abs(by_row), axis=(0, 1), keepdims=True)
        unit = jnp.maximum(largest, 1e-30) * (1.0 / 200.0)
        const = const / unit
        by_row = (by_row * per_strip) / unit
        low_lanes = (lane // STEP) % 3 == 2
        low_band = seg % 3 == 2
        row_part = iota((STRIP, 1), 0).astype(F32) * (1.0 / STRIP)
        for u in range(TAPS):
            at = slice(u * STRIP, (u + 1) * STRIP)
            x = staircase(jnp.broadcast_to(const[u : u + 1], (STRIP, BAND)), 0)
            y = staircase(jnp.broadcast_to(by_row[u : u + 1, :LANES], (STRIP, LANES)), 0)
            tail = x[:, LANES:]
            high = tail.astype(BF16).astype(F32)
            slope[visit, at] = jnp.where(low_band[:, LANES:], tail - high, high).astype(BF16)
            x = x[:, :LANES] + row_part * y
            high = jnp.where(lane < 3 * STEP, jnp.round(x), x.astype(BF16).astype(F32))
            high_level[visit, at] = jnp.where(low_lanes, x - high, high)
            high = jnp.round(y)
            step_level[visit, at] = jnp.where(low_lanes, y - high, high)

        for h in range(HALVES):
            at = slice(h * ROWS, (h + 1) * ROWS)
            matrix = staircase(row_weights[visit, at] * unit, 0)
            high = matrix.astype(BF16)
            rows_high[visit, at] = high
            rows_low[visit, at] = (matrix - high.astype(F32)).astype(BF16)


def small_kernel(body, name, args, shapes):
    return pl.pallas_call(
        body,
        grid=(1,),
        in_specs=[pl.BlockSpec(x.shape, lambda i, n=x.ndim: (0,) * n) for x in args],
        out_specs=[pl.BlockSpec(shape, lambda i: (0, 0, 0)) for shape, _ in shapes],
        out_shape=[jax.ShapeDtypeStruct(shape, kind) for shape, kind in shapes],
        compiler_params=pltpu.CompilerParams(vmem_limit_bytes=32 << 20),
        cost_estimate=pl.CostEstimate(flops=1 << 30, bytes_accessed=1 << 20, transcendentals=0),
        name=name,
    )(*args)


def prepare(taps, psf, affine, devices):
    row_weights, col_weights = small_kernel(
        functools.partial(lanczos_kernel, devices), "lanczos_weights",
        [affine.transpose(0, 2, 3, 1)],
        [((V, BLOCK, LANES), F32), ((V, 8, WIDTH), F32)],
    )
    matrices = small_kernel(
        functools.partial(prepare_kernel, devices), "matrices",
        [taps.transpose(1, 0, 2), psf.transpose(1, 3, 0, 2), row_weights],
        [
            ((V, TAPS * STRIP, LANES), F32),
            ((V, TAPS * STRIP, LANES), F32),
            ((V, TAPS * STRIP, BAND - LANES), BF16),
            ((V, BLOCK, LANES), BF16),
            ((V, BLOCK, LANES), BF16),
        ],
    )
    return [*matrices, col_weights]


def warp_kernel(
    patch, slot, owner, weight, high_level, step_level, slope, rows_high, rows_low, col_weights,
    sort, unsort, image, above, below, out,
    terms, matched_terms, place_of, seen, label,
):
    devices = label.shape[0]
    ccd, _, has_above, has_below = whereabouts(devices)
    tall = BLOCK + 2 * RIM
    lane = iota((1, LANES), 1)
    terms[:, :, tall:] = jnp.zeros((TOGETHER, 4, TALL - tall, WIDTH), BF16)
    label[...] = jnp.zeros_like(label)

    def clear(p, _):
        seen[p] = 0
        return 0

    lax.fori_loop(0, owner.shape[0], clear, 0)
    own = jnp.where(iota(weight.shape, 1) == ccd, weight[...].astype(F32), 0.0)
    own = jnp.sum(own, axis=1, keepdims=True)
    for block in range(V * BLKC):
        p = patch[0, block]
        to = owner[p]
        rank = seen[p]
        seen[p] = rank + 1
        place_of[block] = to * CAP + rank
        line = label[pl.ds(to, 1), :]
        line = jnp.where(lane == rank * 2, own[block // BLKC : block // BLKC + 1], line)
        line = jnp.where(lane == rank * 2 + 1, slot[0, block].astype(F32), line)
        label[pl.ds(to, 1), :] = line
    out[:, CAP * BLOCK :] = jnp.broadcast_to(
        label[...].reshape(devices, 1, LANES), (devices, LABEL, LANES)
    ).astype(BF16)

    def some_visits(turn, _):
        col_pos = (2.0 * column_at(iota((1, WIDTH), 1)).astype(F32) + 1.0) / WIDTH - 1.0
        for i in range(TOGETHER):
            raw = jnp.concatenate(
                [jnp.where(has_above, above[turn * TOGETHER + i], 0.0), image[turn * TOGETHER + i], jnp.where(has_below, below[turn * TOGETHER + i], 0.0)],
                axis=0,
            )
            raw_high = raw.astype(BF16)
            raw_low = (raw - raw_high.astype(F32)).astype(BF16)
            sorted_terms = jnp.dot(
                jnp.concatenate([raw_high, raw_low], axis=0), sort[...], preferred_element_type=F32
            )
            high, low = sorted_terms[:tall], sorted_terms[tall:]
            tilted = (high + low) * col_pos
            tilted_high = tilted.astype(BF16)
            terms[i, 0, :tall] = high.astype(BF16)
            terms[i, 1, :tall] = low.astype(BF16)
            terms[i, 2, :tall] = tilted_high
            terms[i, 3, :tall] = (tilted - tilted_high.astype(F32)).astype(BF16)

        filler = jnp.zeros((BAND - GROUPS * STEP, WIDTH), BF16)
        for k in range(STRIPS):
            for i in range(TOGETHER):
                level = high_level[turn * TOGETHER + i]
                if k != MIDDLE:
                    level = level + float(k - MIDDLE) * step_level[turn * TOGETHER + i]
                matrix = jnp.concatenate([level.astype(BF16), slope[turn * TOGETHER + i]], axis=1)
                rows = slice(k * STRIP, k * STRIP + STEP)
                columns = jnp.concatenate(
                    [terms[i, h, rows] for h in (0, 1, 0, 2, 3, 2)] + [filler], axis=0
                )
                results = jnp.dot(matrix, columns, preferred_element_type=F32)
                blocks = lane_sum(
                    lambda u, v, w: lane_block(results[u * STRIP : (u + 1) * STRIP], w),
                    lane, TAPS, False,
                )
                matched = jnp.concatenate(blocks, axis=1)
                high = matched.astype(BF16)
                at = slice(k * STRIP, (k + 1) * STRIP)
                matched_terms[i, 0, at] = high
                matched_terms[i, 1, at] = (matched - high.astype(F32)).astype(BF16)

        empty = jnp.zeros((LANES - WINDOW, WIDTH), BF16)
        warped = []
        for i in range(TOGETHER):
            halves = []
            for h in range(HALVES):
                high = rows_high[turn * TOGETHER + i, h * ROWS : (h + 1) * ROWS]
                low = rows_low[turn * TOGETHER + i, h * ROWS : (h + 1) * ROWS]
                rows = slice(h * ROWS, h * ROWS + WINDOW)
                first = jnp.concatenate([matched_terms[i, 0, rows], empty], axis=0)
                second = jnp.concatenate([matched_terms[i, 1, rows], empty], axis=0)
                both = jnp.dot(
                    jnp.concatenate([high, high], axis=1), jnp.concatenate([first, second], axis=0),
                    preferred_element_type=F32,
                )
                halves.append(both + jnp.dot(low, first, preferred_element_type=F32))
            warped.append(jnp.concatenate(halves, axis=0))

        for i in range(TOGETHER):
            cols = col_weights[turn * TOGETHER + i]
            blocks = lane_sum(
                lambda s, v, w: lane_block(cols[s : s + 1], v) * lane_block(warped[i], w),
                lane, 2 * WARP + 1, True,
            )
            result = jnp.dot(
                jnp.concatenate(blocks, axis=1).astype(BF16), unsort[...], preferred_element_type=F32
            ).astype(BF16)
            for j in range(BLKC):
                to = place_of[(turn * TOGETHER + i) * BLKC + j]
                rows = pl.ds(pl.multiple_of(to % CAP * BLOCK, BLOCK), BLOCK)
                out[to // CAP, rows] = lane_block(result, j)
        return 0

    lax.fori_loop(0, V // TOGETHER, some_visits, 0)


def warp(patch, slot, owner, weight, ready, images, above, below, devices):
    smem = pl.BlockSpec(memory_space=pltpu.SMEM)
    vmem = pl.BlockSpec(memory_space=pltpu.VMEM)
    sort = deinterleave()
    args = [
        patch, slot, owner, weight, *ready,
        jnp.asarray(sort, BF16), jnp.asarray(sort.T, BF16), images, above, below,
    ]
    return pl.pallas_call(
        warp_kernel,
        in_specs=[smem] * 3 + [vmem] * (len(args) - 3),
        out_specs=vmem,
        scratch_shapes=[
            pltpu.VMEM((TOGETHER, 4, TALL, WIDTH), BF16),
            pltpu.VMEM((TOGETHER, 2, STRIPS * STRIP, WIDTH), BF16),
            pltpu.SMEM((V * BLKC,), jnp.int32),
            pltpu.SMEM((owner.shape[0],), jnp.int32),
            pltpu.VMEM((devices, LANES), F32),
        ],
        out_shape=jax.ShapeDtypeStruct((devices, CAP * BLOCK + LABEL, BLOCK), BF16),
        compiler_params=pltpu.CompilerParams(vmem_limit_bytes=32 << 20),
        cost_estimate=pl.CostEstimate(
            flops=V * 2 * STRIPS * TAPS * STRIP * BAND * WIDTH,
            bytes_accessed=V * (BLOCK * WIDTH * 6),
            transcendentals=0,
        ),
        name="match_warp",
    )(*args)


def coadd_kernel(got, out, total, out_sem):
    devices = got.shape[0]
    wide = devices * CAP * STRIP
    labels = got[:, CAP * BLOCK : CAP * BLOCK + LABEL][:, 0]
    lane = iota((1, wide), 1)
    rank = lane // STRIP % CAP
    source = lane // (STRIP * CAP)

    def spread(entry):
        onehot = (iota((LANES, wide), 0) == rank * 2 + entry).astype(F32).astype(BF16)
        every = jnp.dot(labels, onehot, preferred_element_type=F32)
        return jnp.sum(
            jnp.where(iota((devices, wide), 0) == source, every, 0.0), axis=0, keepdims=True
        )

    weights, cells = spread(0), spread(1)
    row = iota((CELLS * STRIP, 1), 0)
    mine = (cells == (row // STRIP).astype(F32)) & (lane % STRIP == row % STRIP)
    matrix = jnp.where(mine, weights, 0.0)
    sums = jnp.sum(matrix, axis=1, keepdims=True)
    inverse = 1.0 / jnp.maximum(sums, 1.0)
    matrix = matrix.astype(BF16)
    taken = {}
    for r in range(CAP):
        column = jnp.broadcast_to(labels[:, 2 * r : 2 * r + 1].astype(F32), (devices, LANES))
        for s in range(devices):
            taken[s, r] = jnp.broadcast_to(column[s : s + 1], (STRIP, LANES)).astype(BF16) > 0

    def tile(s, r, k):
        first = r * BLOCK + k * STRIP
        return jnp.where(taken[s, r], got[s, first : first + STRIP], jnp.zeros((), BF16))

    copies = []
    for pair in range(BLOCK // STRIP // 2):
        columns = jnp.concatenate(
            [
                jnp.concatenate(
                    [tile(s, r, k) for s in range(devices) for r in range(CAP)], axis=0
                )
                for k in (2 * pair, 2 * pair + 1)
            ],
            axis=1,
        )
        result = jnp.dot(matrix, columns, preferred_element_type=F32) * inverse
        for c in range(CELLS):
            part = result[c * STRIP : (c + 1) * STRIP]
            lanes = slice(c % PSIDE * BLOCK, (c % PSIDE + 1) * BLOCK)
            for n in range(2):
                first = (2 * pair + n) * STRIP
                total[c // PSIDE, first : first + STRIP, lanes] = lane_block(part, n)
        size = 2 * STRIP
        for line in range(PSIDE):
            copies.append(
                pltpu.make_async_copy(
                    total.at[line, pl.ds(pair * size, size)],
                    out.at[0, pl.ds(line * BLOCK + pair * size, size)],
                    out_sem.at[pair, line],
                )
            )
            copies[-1].start()
    for copy in copies:
        copy.wait()


def coadd(got):
    return pl.pallas_call(
        coadd_kernel,
        in_specs=[pl.BlockSpec(memory_space=pltpu.VMEM)],
        out_specs=pl.BlockSpec(memory_space=pl.ANY),
        out_shape=jax.ShapeDtypeStruct((1, PSIDE * BLOCK, PSIDE * BLOCK), F32),
        scratch_shapes=[
            pltpu.VMEM((PSIDE, BLOCK, WIDTH), F32),
            pltpu.SemaphoreType.DMA((BLOCK // STRIP // 2, PSIDE)),
        ],
        compiler_params=pltpu.CompilerParams(vmem_limit_bytes=32 << 20),
        name="coadd",
    )(got)


def shards(
    images, basis_taps, psf_coef, affine, visit_weight, block_patch, block_slot, patch_owner
):
    devices = lax.axis_size("ccd")
    down = [(i, i + 1) for i in range(devices - 1)]
    up = [(i + 1, i) for i in range(devices - 1)]
    above = lax.ppermute(images[:, BLOCK - RIM :], "ccd", down)
    below = lax.ppermute(images[:, :RIM], "ccd", up)
    patch = block_patch[:, :, 0]
    ready = prepare(basis_taps, psf_coef, affine, devices)
    sent = warp(
        patch, block_slot, patch_owner, visit_weight, ready, images, above, below, devices
    )
    got = lax.all_to_all(sent, "ccd", split_axis=0, concat_axis=0, tiled=True)
    return coadd(got)


def solution(mesh):
    placed = (
        P(None, ("group", "ccd"), None),
        P(),
        P(None, "group", None, None),
        P(None, "group", None, None),
        P(None, "group"),
        P(("group", "ccd"), None, None),
        P(("group", "ccd"), None),
        P("group"),
    )
    return jax.shard_map(
        shards,
        mesh=mesh,
        in_specs=placed,
        out_specs=P(("group", "ccd"), None, None),
        check_vma=False,
    )
```

```python
import functools
import itertools

import jax
import jax.numpy as jnp
import numpy as np
from jax import lax
from jax.experimental import pallas as pl
from jax.experimental.pallas import tpu as pltpu
from jax.sharding import PartitionSpec as P

V = 4
BLOCK = 128
BLKC = 4
SPLIT = 4
TAPS = 11
NBASIS = 9
PSIDE = 4
CELLS = PSIDE * PSIDE
CAP = 2

HALF = TAPS // 2
WARP = 3
RIM = HALF + WARP
HEAD = 16
HEIGHT = SPLIT * BLOCK
WIDTH = BLKC * BLOCK
LANES = 128
LANE_BLOCKS = WIDTH // LANES
STRIP = 16
STEP = 32
STRIPS = -(-(BLOCK + 2 * WARP) // STRIP)
MIDDLE = STRIPS // 2
GROUPS = 6
BAND = 256
OWN_STRIPS = STRIPS - 1
NEXT_STRIPS = 2
NEXT_FIRST = (STRIPS - NEXT_STRIPS) * STRIP
HALVES = 2
TOGETHER = 2
ROWS = BLOCK // HALVES
WINDOW = ROWS + STRIP
BODY = BLOCK - HEAD
LABEL = 16
F32 = jnp.float32
BF16 = jnp.bfloat16


def sin_pi(t):
    whole = jnp.round(t)
    f = t - whole
    odd = whole - 2.0 * jnp.floor(0.5 * whole)
    f2 = f * f
    out = 0.0
    for c in (
        0.00046630280576761, -0.0073704309457144, 0.0821458866111282,
        -0.599264529320792, 2.55016403987734, -5.16771278004997, 3.14159265358979,
    ):
        out = out * f2 + c
    return f * out * (1.0 - 2.0 * odd)


def lanczos(t):
    zero = t == 0.0
    safe = jnp.where(zero, 1.0, t)
    pt = jnp.pi * safe
    value = 3.0 * sin_pi(safe) * sin_pi(safe / 3.0) / (pt * pt)
    return jnp.where(jnp.abs(t) < 3.0, jnp.where(zero, 1.0, value), 0.0)


def iota(shape, dim):
    return lax.broadcasted_iota(jnp.int32, shape, dim)


def deinterleave():
    order = np.arange(WIDTH).reshape(LANES, LANE_BLOCKS).T.reshape(-1)
    return (np.arange(WIDTH)[:, None] == order[None, :]).astype(np.float32)


def column_at(lane):
    return lane % LANES * LANE_BLOCKS + lane // LANES


def lane_block(x, v):
    return x[:, v * LANES : (v + 1) * LANES]


def dot_exact(a, b, dims):
    return lax.dot_general(
        a, b, (dims, ((), ())), precision=lax.Precision.HIGHEST, preferred_element_type=F32
    )


def staircase(x, first):
    return jnp.concatenate(
        [
            pltpu.roll(x[g : g + 8], first + g, 1, stride=1, stride_axis=0)
            for g in range(0, x.shape[0], 8)
        ],
        axis=0,
    )


def lane_sum(terms_of, lane, count, weigh):
    blocks = []
    for v in range(LANE_BLOCKS):
        total = None
        half = count // 2
        for q in range(-(-half // LANE_BLOCKS) * -1, (half + LANE_BLOCKS - 1) // LANE_BLOCKS + 1):
            part = None
            for u in range(count):
                if (v + u - half) // LANE_BLOCKS != q:
                    continue
                piece = terms_of(u, v, (v + u - half) % LANE_BLOCKS)
                part = piece if part is None else part + piece
            if part is None:
                continue
            if q:
                part = pltpu.roll(part, -q % LANES, 1)
                if not weigh:
                    part = jnp.where((lane + q >= 0) & (lane + q < LANES), part, 0.0)
            total = part if total is None else total + part
        blocks.append(total)
    return blocks


def whereabouts(devices):
    band = lax.axis_index("ccd")
    after = lax.rem(band + 1, devices)
    quarter = (band + SPLIT // 2) % SPLIT
    own = ((band + SPLIT // 2) // SPLIT, quarter * BLOCK + HEAD)
    following = (
        (after + SPLIT // 2) // SPLIT,
        (after + SPLIT // 2) % SPLIT * BLOCK - BODY,
    )
    return (own, following), (quarter < SPLIT - 1) & (band < devices - 1)


def lanczos_kernel(devices, affine, rows_out, cols_out):
    bands, same = whereabouts(devices)
    lane = iota((1, LANES), 1)
    lanes = iota((8, WIDTH), 1)
    step = iota((8, WIDTH), 0) - WARP
    block = lanes // LANES
    carry = (block + step + LANE_BLOCKS) // LANE_BLOCKS - 1
    from_lane = lanes % LANES - carry
    col = (from_lane * LANE_BLOCKS + block).astype(F32)
    within = (from_lane >= 0) & (from_lane < LANES) & (step <= WARP)
    offset = iota((8, LANES), 0) - WARP
    crosses = (lane + offset >= BODY) != (lane >= BODY)
    keep = (offset <= WARP) & (same | jnp.logical_not(crosses))
    for visit in range(V):
        shifts = []
        for n, (ccd, top_row) in enumerate(bands):
            a = jnp.sum(
                jnp.where(iota((1, 1, affine.shape[3]), 2) == ccd, affine[visit], 0.0),
                axis=2, keepdims=True,
            )
            row = (top_row + lane).astype(F32)
            shifts.append(a[0, 0:1] + a[0, 1:2] * (row - (HEIGHT - 1) / 2.0) / HEIGHT)
            col_shift = a[1, 0:1] + a[1, 1:2] * (col - (WIDTH - 1) / 2.0) / WIDTH
            cols_out[n * V + visit] = jnp.where(within, lanczos(col_shift - step.astype(F32)), 0.0)
        shift = jnp.where(lane < BODY, shifts[0], shifts[1])
        weights = jnp.where(keep, lanczos(shift - offset.astype(F32)), 0.0)
        rows_out[visit] = jnp.concatenate([weights, jnp.zeros((LANES - 8, LANES), F32)], axis=0).T


def prepare_kernel(
    devices, taps, psf, row_weights, high_level, step_level, slope, rows_high, rows_low
):
    bands, _ = whereabouts(devices)
    band_lane = iota((1, BAND), 1)
    seg = band_lane // STEP
    lane = iota((1, LANES), 1)
    tap = band_lane - seg * STEP
    onehot = (tap == iota((TAPS, BAND), 0)) & (seg < GROUPS)
    row_taps = dot_exact(taps[:, 0], onehot.astype(F32), ((1,), (0,)))
    eye = (iota((TAPS, STRIP), 0) == iota((TAPS, STRIP), 1)).astype(F32)
    turned_taps = dot_exact(eye, taps[:, 1], ((0,), (1,)))
    units = []
    for n, visit in itertools.product(range(2), range(V)):
        ccd, top_row = bands[n]
        lhs = jnp.concatenate(
            [turned_taps * psf[ccd, c, visit : visit + 1, :] for c in range(3)], axis=0
        )
        kernels = dot_exact(lhs, row_taps, ((1,), (0,)))
        const, by_row, by_col = (kernels[c * STRIP : (c + 1) * STRIP] for c in range(3))
        is_level = seg < 3
        per_strip = 2.0 * STRIP / HEIGHT
        middle_row = (top_row + (MIDDLE * STRIP - WARP)).astype(F32)
        middle_pos = (2.0 * middle_row + 1.0) / HEIGHT - 1.0
        col_move = (iota((STRIP, 1), 0) - HALF).astype(F32) * (2.0 / WIDTH)
        by_row = jnp.where(is_level, by_row, 0.0)
        const = jnp.where(is_level, const + middle_pos * by_row - col_move * by_col, by_col)
        reach = per_strip * (STRIPS - MIDDLE)
        largest = jnp.max(jnp.abs(const) + reach * jnp.abs(by_row), axis=(0, 1), keepdims=True)
        unit = jnp.maximum(largest, 1e-30) * (1.0 / 200.0)
        units.append(unit)
        const = const / unit
        by_row = (by_row * per_strip) / unit
        low_lanes = (lane // STEP) % 3 == 2
        low_band = seg % 3 == 2
        row_part = iota((STRIP, 1), 0).astype(F32) * (1.0 / STRIP)
        for u in range(TAPS):
            at = slice(u * STRIP, (u + 1) * STRIP)
            x = staircase(jnp.broadcast_to(const[u : u + 1], (STRIP, BAND)), 0)
            y = staircase(jnp.broadcast_to(by_row[u : u + 1, :LANES], (STRIP, LANES)), 0)
            tail = x[:, LANES:]
            high = tail.astype(BF16).astype(F32)
            slope[n * V + visit, at] = jnp.where(low_band[:, LANES:], tail - high, high).astype(BF16)
            x = x[:, :LANES] + row_part * y
            high = jnp.where(lane < 3 * STEP, jnp.round(x), x.astype(BF16).astype(F32))
            high_level[n * V + visit, at] = jnp.where(low_lanes, x - high, high)
            high = jnp.round(y)
            step_level[n * V + visit, at] = jnp.where(low_lanes, y - high, high)

    for visit in range(V):
        weights = row_weights[visit]
        matrix = jnp.concatenate(
            [
                staircase(weights[:ROWS] * units[visit], 0),
                staircase(weights[ROWS:BODY] * units[visit], 0),
                staircase(weights[BODY:] * units[V + visit], ROWS),
            ],
            axis=0,
        )
        high = matrix.astype(BF16)
        rows_high[visit] = high
        rows_low[visit] = (matrix - high.astype(F32)).astype(BF16)


def small_kernel(body, name, args, shapes):
    return pl.pallas_call(
        body,
        grid=(1,),
        in_specs=[pl.BlockSpec(x.shape, lambda i, n=x.ndim: (0,) * n) for x in args],
        out_specs=[pl.BlockSpec(shape, lambda i: (0, 0, 0)) for shape, _ in shapes],
        out_shape=[jax.ShapeDtypeStruct(shape, kind) for shape, kind in shapes],
        compiler_params=pltpu.CompilerParams(vmem_limit_bytes=32 << 20),
        cost_estimate=pl.CostEstimate(flops=1 << 30, bytes_accessed=1 << 20, transcendentals=0),
        name=name,
    )(*args)


def prepare(taps, psf, affine, devices):
    row_weights, col_weights = small_kernel(
        functools.partial(lanczos_kernel, devices), "lanczos_weights",
        [affine.transpose(0, 2, 3, 1)],
        [((V, BLOCK, LANES), F32), ((2 * V, 8, WIDTH), F32)],
    )
    matrices = small_kernel(
        functools.partial(prepare_kernel, devices), "matrices",
        [taps.transpose(1, 0, 2), psf.transpose(1, 3, 0, 2), row_weights],
        [
            ((2 * V, TAPS * STRIP, LANES), F32),
            ((2 * V, TAPS * STRIP, LANES), F32),
            ((2 * V, TAPS * STRIP, BAND - LANES), BF16),
            ((V, BLOCK, LANES), BF16),
            ((V, BLOCK, LANES), BF16),
        ],
    )
    return [*matrices, col_weights]


def warp_kernel(
    patch, slot, owner, weight, high_level, step_level, slope, rows_high, rows_low, col_weights,
    sort, unsort, image, below, out,
    terms, next_terms, matched_terms, next_matched, next_names, place_of, seen, label, name_sem,
):
    devices = label.shape[0]
    blocks_here = V * BLKC
    ((ccd, _), _), same = whereabouts(devices)
    names_copy = pltpu.make_async_copy(
        below.at[0, pl.ds(HEAD + RIM, 8), pl.ds(0, LANES)], next_names, name_sem
    )
    names_copy.start()
    lane = iota((1, LANES), 1)
    next_terms[:, :, STEP:] = jnp.zeros((TOGETHER, 4, STRIP, WIDTH), BF16)
    label[...] = jnp.zeros_like(label)

    def forget():
        def clear(p, _):
            seen[p] = 0
            return 0

        lax.fori_loop(0, owner.shape[0], clear, 0)

    def take(p):
        rank = seen[p]
        seen[p] = rank + 1
        return owner[p], rank

    forget()
    own = jnp.where(iota(weight.shape, 1) == ccd, weight[...].astype(F32), 0.0)
    own = jnp.sum(own, axis=1, keepdims=True)
    for block in range(blocks_here):
        to, rank = take(patch[0, block])
        place_of[block] = to * CAP + rank
        line = label[pl.ds(to, 1), :]
        line = jnp.where(lane == rank * 2, own[block // BLKC : block // BLKC + 1], line)
        line = jnp.where(lane == rank * 2 + 1, slot[0, block].astype(F32), line)
        label[pl.ds(to, 1), :] = line
    out[:, CAP * BLOCK :] = jnp.broadcast_to(
        label[...].reshape(devices, 1, LANES), (devices, LABEL, LANES)
    ).astype(BF16)
    forget()
    names_copy.wait()
    for block in range(blocks_here):
        to, rank = take(next_names[0, block].astype(jnp.int32))
        place_of[blocks_here + block] = to * CAP + rank

    seam_row = iota((STEP, 1), 0) < STEP - HEAD - RIM
    both = jnp.where(same, 1.0, 0.0)
    own_sees = jnp.where(seam_row, 1.0, both)
    next_sees = jnp.where(seam_row, both, 1.0)
    col_pos = (2.0 * column_at(iota((1, WIDTH), 1)).astype(F32) + 1.0) / WIDTH - 1.0
    filler = jnp.zeros((BAND - GROUPS * STEP, WIDTH), BF16)
    tall = BLOCK + 2 * RIM
    seam = tall - STEP

    def some_visits(turn, _):
        visits = [turn * TOGETHER + i for i in range(TOGETHER)]

        for i, visit in enumerate(visits):
            raw = jnp.concatenate([image[visit, RIM:], below[visit, : HEAD + RIM]], axis=0)
            raw_high = raw.astype(BF16)
            raw_low = (raw - raw_high.astype(F32)).astype(BF16)
            sorted_terms = jnp.dot(
                jnp.concatenate([raw_high, raw_low], axis=0), sort[...], preferred_element_type=F32
            )
            high, low = sorted_terms[:tall], sorted_terms[tall:]
            tilted = (high + low) * col_pos
            tilted_high = tilted.astype(BF16).astype(F32)
            for h, value in enumerate((high, low, tilted_high, tilted - tilted_high)):
                terms[i, h, :seam] = value[:seam].astype(BF16)
                terms[i, h, seam:] = (value[seam:] * own_sees).astype(BF16)
                next_terms[i, h, :STEP] = (value[seam:] * next_sees).astype(BF16)

        def strip(matrices, source, rows, k):
            level = high_level[matrices]
            if k != MIDDLE:
                level = level + float(k - MIDDLE) * step_level[matrices]
            matrix = jnp.concatenate([level.astype(BF16), slope[matrices]], axis=1)
            columns = jnp.concatenate(
                [source[h, rows] for h in (0, 1, 0, 2, 3, 2)] + [filler], axis=0
            )
            results = jnp.dot(matrix, columns, preferred_element_type=F32)
            blocks = lane_sum(
                lambda u, v, w: lane_block(results[u * STRIP : (u + 1) * STRIP], w),
                lane, TAPS, False,
            )
            matched = jnp.concatenate(blocks, axis=1)
            high = matched.astype(BF16)
            return high, (matched - high.astype(F32)).astype(BF16)

        for k in range(OWN_STRIPS):
            for i, visit in enumerate(visits):
                at = slice(k * STRIP, (k + 1) * STRIP)
                matched_terms[i, 0, at], matched_terms[i, 1, at] = strip(
                    visit, terms.at[i], slice(k * STRIP, k * STRIP + STEP), k
                )
        for k in range(NEXT_STRIPS):
            for i, visit in enumerate(visits):
                at = slice(k * STRIP, (k + 1) * STRIP)
                next_matched[i, 0, at], next_matched[i, 1, at] = strip(
                    V + visit, next_terms.at[i], slice(k * STRIP, k * STRIP + STEP),
                    STRIPS - NEXT_STRIPS + k,
                )

        warped = []
        for i, visit in enumerate(visits):
            halves = []
            for h in range(HALVES):
                at = slice(h * ROWS, (h + 1) * ROWS)
                high, low = rows_high[visit, at], rows_low[visit, at]

                def under(term):
                    if h == 0:
                        parts = [matched_terms[i, term, :WINDOW]]
                    else:
                        parts = [matched_terms[i, term, ROWS:], next_matched[i, term]]
                    left = LANES - sum([x.shape[0] for x in parts])
                    return jnp.concatenate(parts + [jnp.zeros((left, WIDTH), BF16)], axis=0)

                first = under(0)
                total = jnp.dot(
                    jnp.concatenate([high, high], axis=1),
                    jnp.concatenate([first, under(1)], axis=0),
                    preferred_element_type=F32,
                )
                halves.append(total + jnp.dot(low, first, preferred_element_type=F32))
            warped.append(jnp.concatenate(halves, axis=0))

        for i, visit in enumerate(visits):
            parts = []
            for rows, weights in (
                (slice(0, BODY), col_weights[visit]),
                (slice(BODY, BLOCK), col_weights[V + visit]),
            ):
                some = warped[i][rows]
                blocks = lane_sum(
                    lambda s, v, w: lane_block(weights[s : s + 1], v) * lane_block(some, w),
                    lane, 2 * WARP + 1, True,
                )
                parts.append(jnp.concatenate(blocks, axis=1).astype(BF16))
            result = jnp.dot(
                jnp.concatenate(parts, axis=0), unsort[...], preferred_element_type=F32
            ).astype(BF16)
            for j in range(BLKC):
                piece = lane_block(result, j)
                to = place_of[visit * BLKC + j]
                rows = pl.ds(pl.multiple_of(to % CAP * BODY, HEAD), BODY)
                out[to // CAP, rows] = piece[:BODY]
                to = place_of[blocks_here + visit * BLKC + j]
                rows = pl.ds(pl.multiple_of(CAP * BODY + to % CAP * HEAD, HEAD), HEAD)
                out[to // CAP, rows] = piece[BODY:]
        return 0

    lax.fori_loop(0, V // TOGETHER, some_visits, 0)


def warp(patch, slot, owner, weight, ready, images, below, devices):
    smem = pl.BlockSpec(memory_space=pltpu.SMEM)
    vmem = pl.BlockSpec(memory_space=pltpu.VMEM)
    sort = deinterleave()
    args = [
        patch, slot, owner, weight, *ready,
        jnp.asarray(sort, BF16), jnp.asarray(sort.T, BF16), images, below,
    ]
    return pl.pallas_call(
        warp_kernel,
        in_specs=[smem] * 3 + [vmem] * (len(args) - 3),
        out_specs=vmem,
        scratch_shapes=[
            pltpu.VMEM((TOGETHER, 4, BLOCK + 2 * RIM, WIDTH), BF16),
            pltpu.VMEM((TOGETHER, 4, STEP + STRIP, WIDTH), BF16),
            pltpu.VMEM((TOGETHER, 2, OWN_STRIPS * STRIP, WIDTH), BF16),
            pltpu.VMEM((TOGETHER, 2, NEXT_STRIPS * STRIP, WIDTH), BF16),
            pltpu.SMEM((8, LANES), F32),
            pltpu.SMEM((2 * V * BLKC,), jnp.int32),
            pltpu.SMEM((owner.shape[0],), jnp.int32),
            pltpu.VMEM((devices, LANES), F32),
            pltpu.SemaphoreType.DMA(()),
        ],
        out_shape=jax.ShapeDtypeStruct((devices, CAP * BLOCK + LABEL, BLOCK), BF16),
        compiler_params=pltpu.CompilerParams(vmem_limit_bytes=32 << 20),
        cost_estimate=pl.CostEstimate(
            flops=V * 2 * STRIPS * TAPS * STRIP * BAND * WIDTH,
            bytes_accessed=V * (BLOCK * WIDTH * 6),
            transcendentals=0,
        ),
        name="match_warp",
    )(*args)


def coadd_kernel(got, out, total, out_sem):
    devices = got.shape[0]
    wide = devices * CAP * STRIP
    labels = got[:, CAP * BLOCK : CAP * BLOCK + LABEL][:, 0]
    lane = iota((1, wide), 1)
    rank = lane // STRIP % CAP
    source = lane // (STRIP * CAP)

    def spread(entry):
        onehot = (iota((LANES, wide), 0) == rank * 2 + entry).astype(F32).astype(BF16)
        every = jnp.dot(labels, onehot, preferred_element_type=F32)
        return jnp.sum(
            jnp.where(iota((devices, wide), 0) == source, every, 0.0), axis=0, keepdims=True
        )

    weights, cells = spread(0), spread(1)
    row = iota((CELLS * STRIP, 1), 0)
    mine = (cells == (row // STRIP).astype(F32)) & (lane % STRIP == row % STRIP)
    matrix = jnp.where(mine, weights, 0.0)
    sums = jnp.sum(matrix, axis=1, keepdims=True)
    inverse = 1.0 / jnp.maximum(sums, 1.0)
    matrix = matrix.astype(BF16)
    taken = {}
    for r in range(CAP):
        column = jnp.broadcast_to(labels[:, 2 * r : 2 * r + 1].astype(F32), (devices, LANES))
        for s in range(devices):
            taken[s, r] = jnp.broadcast_to(column[s : s + 1], (STRIP, LANES)).astype(BF16) > 0

    def tile(s, r, k):
        device, first = s, r * BODY + k * STRIP - HEAD
        if k == 0:
            device, first = (s - 1) % devices, CAP * BODY + r * HEAD
        return jnp.where(taken[s, r], got[device, first : first + STRIP], jnp.zeros((), BF16))

    copies = []
    for pair in range(BLOCK // STRIP // 2):
        columns = jnp.concatenate(
            [
                jnp.concatenate(
                    [tile(s, r, k) for s in range(devices) for r in range(CAP)], axis=0
                )
                for k in (2 * pair, 2 * pair + 1)
            ],
            axis=1,
        )
        result = jnp.dot(matrix, columns, preferred_element_type=F32) * inverse
        for c in range(CELLS):
            part = result[c * STRIP : (c + 1) * STRIP]
            lanes = slice(c % PSIDE * BLOCK, (c % PSIDE + 1) * BLOCK)
            for n in range(2):
                first = (2 * pair + n) * STRIP
                total[c // PSIDE, first : first + STRIP, lanes] = lane_block(part, n)
        size = 2 * STRIP
        for line in range(PSIDE):
            copies.append(
                pltpu.make_async_copy(
                    total.at[line, pl.ds(pair * size, size)],
                    out.at[0, pl.ds(line * BLOCK + pair * size, size)],
                    out_sem.at[pair, line],
                )
            )
            copies[-1].start()
    for copy in copies:
        copy.wait()


def coadd(got):
    return pl.pallas_call(
        coadd_kernel,
        in_specs=[pl.BlockSpec(memory_space=pltpu.VMEM)],
        out_specs=pl.BlockSpec(memory_space=pl.ANY),
        out_shape=jax.ShapeDtypeStruct((1, PSIDE * BLOCK, PSIDE * BLOCK), F32),
        scratch_shapes=[
            pltpu.VMEM((PSIDE, BLOCK, WIDTH), F32),
            pltpu.SemaphoreType.DMA((BLOCK // STRIP // 2, PSIDE)),
        ],
        compiler_params=pltpu.CompilerParams(vmem_limit_bytes=32 << 20),
        name="coadd",
    )(got)


def shards(
    images, basis_taps, psf_coef, affine, visit_weight, block_patch, block_slot, patch_owner
):
    devices = lax.axis_size("ccd")
    patch = block_patch[:, :, 0]
    names = lax.pad(
        patch.astype(F32)[:, None, :], jnp.zeros((), F32),
        ((0, V - 1, 0), (0, 7, 0), (0, WIDTH - V * BLKC, 0)),
    )
    head = jnp.concatenate([images[:, : HEAD + RIM], names], axis=1)
    below = lax.ppermute(head, "ccd", [((i + 1) % devices, i) for i in range(devices)])
    ready = prepare(basis_taps, psf_coef, affine, devices)
    sent = warp(
        patch, block_slot, patch_owner, visit_weight, ready, images, below, devices
    )
    got = lax.all_to_all(sent, "ccd", split_axis=0, concat_axis=0, tiled=True)
    return coadd(got)


def solution(mesh):
    placed = (
        P(None, ("group", "ccd"), None),
        P(),
        P(None, "group", None, None),
        P(None, "group", None, None),
        P(None, "group"),
        P(("group", "ccd"), None, None),
        P(("group", "ccd"), None),
        P("group"),
    )
    return jax.shard_map(
        shards,
        mesh=mesh,
        in_specs=placed,
        out_specs=P(("group", "ccd"), None, None),
        check_vma=False,
    )
```

```python
import functools
import itertools

import jax
import jax.numpy as jnp
import numpy as np
from jax import lax
from jax.experimental import pallas as pl
from jax.experimental.pallas import tpu as pltpu
from jax.sharding import PartitionSpec as P

V = 4
BLOCK = 128
BLKC = 4
SPLIT = 4
TAPS = 11
NBASIS = 9
PSIDE = 4
CELLS = PSIDE * PSIDE
CAP = 2

HALF = TAPS // 2
WARP = 3
RIM = HALF + WARP
HEAD = 16
HEIGHT = SPLIT * BLOCK
WIDTH = BLKC * BLOCK
LANES = 128
LANE_BLOCKS = WIDTH // LANES
STRIP = 16
STEP = 32
STRIPS = -(-(BLOCK + 2 * WARP) // STRIP)
MIDDLE = STRIPS // 2
GROUPS = 6
BAND = 256
FIRST_STRIPS = 6
OWN_STRIPS = STRIPS - 1
NEXT_STRIPS = 2
NEXT_FIRST = (STRIPS - NEXT_STRIPS) * STRIP
HALVES = 2
TOGETHER = 2
ROWS = BLOCK // HALVES
WINDOW = ROWS + STRIP
BODY = BLOCK - HEAD
SEEN = -(-(FIRST_STRIPS * STRIP + TAPS - 1) // STRIP) * STRIP
LABEL = 16
F32 = jnp.float32
BF16 = jnp.bfloat16


def sin_pi(t):
    whole = jnp.round(t)
    f = t - whole
    odd = whole - 2.0 * jnp.floor(0.5 * whole)
    f2 = f * f
    out = 0.0
    for c in (
        0.00046630280576761, -0.0073704309457144, 0.0821458866111282,
        -0.599264529320792, 2.55016403987734, -5.16771278004997, 3.14159265358979,
    ):
        out = out * f2 + c
    return f * out * (1.0 - 2.0 * odd)


def lanczos(t):
    zero = t == 0.0
    safe = jnp.where(zero, 1.0, t)
    pt = jnp.pi * safe
    value = 3.0 * sin_pi(safe) * sin_pi(safe / 3.0) / (pt * pt)
    return jnp.where(jnp.abs(t) < 3.0, jnp.where(zero, 1.0, value), 0.0)


def iota(shape, dim):
    return lax.broadcasted_iota(jnp.int32, shape, dim)


def deinterleave():
    order = np.arange(WIDTH).reshape(LANES, LANE_BLOCKS).T.reshape(-1)
    return (np.arange(WIDTH)[:, None] == order[None, :]).astype(np.float32)


def column_at(lane):
    return lane % LANES * LANE_BLOCKS + lane // LANES


def lane_block(x, v):
    return x[:, v * LANES : (v + 1) * LANES]


def dot_exact(a, b, dims):
    return lax.dot_general(
        a, b, (dims, ((), ())), precision=lax.Precision.HIGHEST, preferred_element_type=F32
    )


def staircase(x, first):
    return jnp.concatenate(
        [
            pltpu.roll(x[g : g + 8], first + g, 1, stride=1, stride_axis=0)
            for g in range(0, x.shape[0], 8)
        ],
        axis=0,
    )


def lane_sum(terms_of, lane, count, weigh):
    blocks = []
    for v in range(LANE_BLOCKS):
        total = None
        half = count // 2
        for q in range(-(-half // LANE_BLOCKS) * -1, (half + LANE_BLOCKS - 1) // LANE_BLOCKS + 1):
            part = None
            for u in range(count):
                if (v + u - half) // LANE_BLOCKS != q:
                    continue
                piece = terms_of(u, v, (v + u - half) % LANE_BLOCKS)
                part = piece if part is None else part + piece
            if part is None:
                continue
            if q:
                part = pltpu.roll(part, -q % LANES, 1)
                if not weigh:
                    part = jnp.where((lane + q >= 0) & (lane + q < LANES), part, 0.0)
            total = part if total is None else total + part
        blocks.append(total)
    return blocks


def whereabouts(devices):
    band = lax.axis_index("ccd")
    after = lax.rem(band + 1, devices)
    quarter = (band + SPLIT // 2) % SPLIT
    own = ((band + SPLIT // 2) // SPLIT, quarter * BLOCK + HEAD)
    following = (
        (after + SPLIT // 2) // SPLIT,
        (after + SPLIT // 2) % SPLIT * BLOCK - BODY,
    )
    return (own, following), (quarter < SPLIT - 1) & (band < devices - 1)


def lanczos_kernel(devices, affine, rows_out, cols_out):
    bands, same = whereabouts(devices)
    lane = iota((1, LANES), 1)
    lanes = iota((8, WIDTH), 1)
    step = iota((8, WIDTH), 0) - WARP
    block = lanes // LANES
    carry = (block + step + LANE_BLOCKS) // LANE_BLOCKS - 1
    from_lane = lanes % LANES - carry
    col = (from_lane * LANE_BLOCKS + block).astype(F32)
    within = (from_lane >= 0) & (from_lane < LANES) & (step <= WARP)
    offset = iota((8, LANES), 0) - WARP
    crosses = (lane + offset >= BODY) != (lane >= BODY)
    keep = (offset <= WARP) & (same | jnp.logical_not(crosses))
    for visit in range(V):
        shifts = []
        for n, (ccd, top_row) in enumerate(bands):
            a = jnp.sum(
                jnp.where(iota((1, 1, affine.shape[3]), 2) == ccd, affine[visit], 0.0),
                axis=2, keepdims=True,
            )
            row = (top_row + lane).astype(F32)
            shifts.append(a[0, 0:1] + a[0, 1:2] * (row - (HEIGHT - 1) / 2.0) / HEIGHT)
            col_shift = a[1, 0:1] + a[1, 1:2] * (col - (WIDTH - 1) / 2.0) / WIDTH
            cols_out[n * V + visit] = jnp.where(within, lanczos(col_shift - step.astype(F32)), 0.0)
        shift = jnp.where(lane < BODY, shifts[0], shifts[1])
        weights = jnp.where(keep, lanczos(shift - offset.astype(F32)), 0.0)
        rows_out[visit] = jnp.concatenate([weights, jnp.zeros((LANES - 8, LANES), F32)], axis=0).T


def prepare_kernel(
    devices, taps, psf, row_weights, high_level, step_level, slope, rows_high, rows_low
):
    bands, _ = whereabouts(devices)
    band_lane = iota((1, BAND), 1)
    seg = band_lane // STEP
    lane = iota((1, LANES), 1)
    tap = band_lane - seg * STEP
    onehot = (tap == iota((TAPS, BAND), 0)) & (seg < GROUPS)
    row_taps = dot_exact(taps[:, 0], onehot.astype(F32), ((1,), (0,)))
    eye = (iota((TAPS, STRIP), 0) == iota((TAPS, STRIP), 1)).astype(F32)
    turned_taps = dot_exact(eye, taps[:, 1], ((0,), (1,)))
    units = []
    for n, visit in itertools.product(range(2), range(V)):
        ccd, top_row = bands[n]
        lhs = jnp.concatenate(
            [turned_taps * psf[ccd, c, visit : visit + 1, :] for c in range(3)], axis=0
        )
        kernels = dot_exact(lhs, row_taps, ((1,), (0,)))
        const, by_row, by_col = (kernels[c * STRIP : (c + 1) * STRIP] for c in range(3))
        is_level = seg < 3
        per_strip = 2.0 * STRIP / HEIGHT
        middle_row = (top_row + (MIDDLE * STRIP - WARP)).astype(F32)
        middle_pos = (2.0 * middle_row + 1.0) / HEIGHT - 1.0
        col_move = (iota((STRIP, 1), 0) - HALF).astype(F32) * (2.0 / WIDTH)
        by_row = jnp.where(is_level, by_row, 0.0)
        const = jnp.where(is_level, const + middle_pos * by_row - col_move * by_col, by_col)
        reach = per_strip * (STRIPS - MIDDLE)
        largest = jnp.max(jnp.abs(const) + reach * jnp.abs(by_row), axis=(0, 1), keepdims=True)
        unit = jnp.maximum(largest, 1e-30) * (1.0 / 200.0)
        units.append(unit)
        const = const / unit
        by_row = (by_row * per_strip) / unit
        low_lanes = (lane // STEP) % 3 == 2
        low_band = seg % 3 == 2
        row_part = iota((STRIP, 1), 0).astype(F32) * (1.0 / STRIP)
        for u in range(TAPS):
            at = slice(u * STRIP, (u + 1) * STRIP)
            x = staircase(jnp.broadcast_to(const[u : u + 1], (STRIP, BAND)), 0)
            y = staircase(jnp.broadcast_to(by_row[u : u + 1, :LANES], (STRIP, LANES)), 0)
            tail = x[:, LANES:]
            high = tail.astype(BF16).astype(F32)
            slope[n * V + visit, at] = jnp.where(low_band[:, LANES:], tail - high, high).astype(BF16)
            x = x[:, :LANES] + row_part * y
            high = jnp.where(lane < 3 * STEP, jnp.round(x), x.astype(BF16).astype(F32))
            high_level[n * V + visit, at] = jnp.where(low_lanes, x - high, high)
            high = jnp.round(y)
            step_level[n * V + visit, at] = jnp.where(low_lanes, y - high, high)

    for visit in range(V):
        weights = row_weights[visit]
        matrix = jnp.concatenate(
            [
                staircase(weights[:ROWS] * units[visit], 0),
                staircase(weights[ROWS:BODY] * units[visit], 0),
                staircase(weights[BODY:] * units[V + visit], ROWS),
            ],
            axis=0,
        )
        high = matrix.astype(BF16)
        rows_high[visit] = high
        rows_low[visit] = (matrix - high.astype(F32)).astype(BF16)


def small_kernel(body, name, args, shapes):
    return pl.pallas_call(
        body,
        grid=(1,),
        in_specs=[pl.BlockSpec(x.shape, lambda i, n=x.ndim: (0,) * n) for x in args],
        out_specs=[pl.BlockSpec(shape, lambda i: (0, 0, 0)) for shape, _ in shapes],
        out_shape=[jax.ShapeDtypeStruct(shape, kind) for shape, kind in shapes],
        compiler_params=pltpu.CompilerParams(vmem_limit_bytes=32 << 20),
        cost_estimate=pl.CostEstimate(flops=1 << 30, bytes_accessed=1 << 20, transcendentals=0),
        name=name,
    )(*args)


def prepare(taps, psf, affine, devices):
    row_weights, col_weights = small_kernel(
        functools.partial(lanczos_kernel, devices), "lanczos_weights",
        [affine.transpose(0, 2, 3, 1)],
        [((V, BLOCK, LANES), F32), ((2 * V, 8, WIDTH), F32)],
    )
    matrices = small_kernel(
        functools.partial(prepare_kernel, devices), "matrices",
        [taps.transpose(1, 0, 2), psf.transpose(1, 3, 0, 2), row_weights],
        [
            ((2 * V, TAPS * STRIP, LANES), F32),
            ((2 * V, TAPS * STRIP, LANES), F32),
            ((2 * V, TAPS * STRIP, BAND - LANES), BF16),
            ((V, BLOCK, LANES), BF16),
            ((V, BLOCK, LANES), BF16),
        ],
    )
    return [*matrices, col_weights]


def sorted_rows(raw, sort):
    col_pos = (2.0 * column_at(iota((1, WIDTH), 1)).astype(F32) + 1.0) / WIDTH - 1.0
    count = raw.shape[0]
    raw_high = raw.astype(BF16)
    raw_low = (raw - raw_high.astype(F32)).astype(BF16)
    both = jnp.dot(
        jnp.concatenate([raw_high, raw_low], axis=0), sort, preferred_element_type=F32
    )
    high, low = both[:count], both[count:]
    tilted = (high + low) * col_pos
    tilted_high = tilted.astype(BF16).astype(F32)
    return high, low, tilted_high, tilted - tilted_high


def match_strip(level, step, slope, source, first, k):
    lane = iota((1, LANES), 1)
    if k != MIDDLE:
        level = level + float(k - MIDDLE) * step
    matrix = jnp.concatenate([level.astype(BF16), slope], axis=1)
    filler = jnp.zeros((BAND - GROUPS * STEP, WIDTH), BF16)
    rows = slice(first, first + STEP)
    columns = jnp.concatenate([source[h, rows] for h in (0, 1, 0, 2, 3, 2)] + [filler], axis=0)
    results = jnp.dot(matrix, columns, preferred_element_type=F32)
    blocks = lane_sum(
        lambda u, v, w: lane_block(results[u * STRIP : (u + 1) * STRIP], w), lane, TAPS, False
    )
    matched = jnp.concatenate(blocks, axis=1)
    high = matched.astype(BF16)
    return high, (matched - high.astype(F32)).astype(BF16)


def forget(seen):
    def clear(p, _):
        seen[p] = 0
        return 0

    lax.fori_loop(0, seen.shape[0], clear, 0)


def take(p, owner, seen):
    rank = seen[p]
    seen[p] = rank + 1
    return owner[p], rank


def match_kernel(
    patch, slot, owner, weight, high_level, step_level, slope, sort, image,
    place_of, label, matched_terms, terms, seen,
):
    devices = label.shape[0]
    ((ccd, _), _), _ = whereabouts(devices)
    lane = iota((1, LANES), 1)
    label[...] = jnp.zeros_like(label)
    forget(seen)
    own = jnp.where(iota(weight.shape, 1) == ccd, weight[...].astype(F32), 0.0)
    own = jnp.sum(own, axis=1, keepdims=True)
    for block in range(V * BLKC):
        to, rank = take(patch[0, block], owner, seen)
        place_of[block] = to * CAP + rank
        line = label[pl.ds(to, 1), :]
        line = jnp.where(lane == rank * 2, own[block // BLKC : block // BLKC + 1], line)
        line = jnp.where(lane == rank * 2 + 1, slot[0, block].astype(F32), line)
        label[pl.ds(to, 1), :] = line

    def some_visits(turn, _):
        visits = [turn * TOGETHER + i for i in range(TOGETHER)]
        for i, visit in enumerate(visits):
            for h, value in enumerate(sorted_rows(image[visit, RIM : RIM + SEEN], sort[...])):
                terms[i, h] = value.astype(BF16)
        for k in range(FIRST_STRIPS):
            for i, visit in enumerate(visits):
                at = slice(k * STRIP, (k + 1) * STRIP)
                matched_terms[visit, 0, at], matched_terms[visit, 1, at] = match_strip(
                    high_level[visit], step_level[visit], slope[visit],
                    terms.at[i], k * STRIP, k,
                )
        return 0

    lax.fori_loop(0, V // TOGETHER, some_visits, 0)


def warp_kernel(
    owner, place_of, label, high_level, step_level, slope, rows_high, rows_low, col_weights,
    sort, unsort, image, below, matched_first, out,
    terms, next_terms, matched_terms, next_matched, next_names, next_place, seen, name_sem,
):
    devices = label.shape[0]
    _, same = whereabouts(devices)
    names_copy = pltpu.make_async_copy(
        below.at[pl.ds(V * (HEAD + RIM), 8), pl.ds(0, LANES)], next_names, name_sem
    )
    names_copy.start()
    lane = iota((1, LANES), 1)
    next_terms[:, :, STEP:] = jnp.zeros((TOGETHER, 4, STRIP, WIDTH), BF16)
    out[:, CAP * BLOCK :] = jnp.broadcast_to(
        label[...].reshape(devices, 1, LANES), (devices, LABEL, LANES)
    ).astype(BF16)
    forget(seen)
    names_copy.wait()
    for block in range(V * BLKC):
        to, rank = take(next_names[0, block].astype(jnp.int32), owner, seen)
        next_place[block] = to * CAP + rank

    first_row = FIRST_STRIPS * STRIP
    tall = BLOCK + 2 * RIM
    seam = tall - STEP - first_row
    seam_row = iota((STEP, 1), 0) < STEP - HEAD - RIM
    both = jnp.where(same, 1.0, 0.0)
    own_sees = jnp.where(seam_row, 1.0, both)
    next_sees = jnp.where(seam_row, both, 1.0)

    def some_visits(turn, _):
        visits = [turn * TOGETHER + i for i in range(TOGETHER)]
        for i, visit in enumerate(visits):
            head = pl.ds(pl.multiple_of(visit * (HEAD + RIM), 8), HEAD + RIM)
            raw = jnp.concatenate([image[visit, RIM + first_row :], below[head]], axis=0)
            for h, value in enumerate(sorted_rows(raw, sort[...])):
                terms[i, h, :seam] = value[:seam].astype(BF16)
                terms[i, h, seam:] = (value[seam:] * own_sees).astype(BF16)
                next_terms[i, h, :STEP] = (value[seam:] * next_sees).astype(BF16)
        for k in range(FIRST_STRIPS, OWN_STRIPS):
            for i, visit in enumerate(visits):
                first = k * STRIP - first_row
                at = slice(first, first + STRIP)
                matched_terms[i, 0, at], matched_terms[i, 1, at] = match_strip(
                    high_level[visit], step_level[visit], slope[visit], terms.at[i], first, k
                )
        for k in range(NEXT_STRIPS):
            for i, visit in enumerate(visits):
                at = slice(k * STRIP, (k + 1) * STRIP)
                next_matched[i, 0, at], next_matched[i, 1, at] = match_strip(
                    high_level[V + visit], step_level[V + visit], slope[V + visit],
                    next_terms.at[i], k * STRIP, STRIPS - NEXT_STRIPS + k,
                )

        warped = []
        for i, visit in enumerate(visits):
            halves = []
            for h in range(HALVES):
                at = slice(h * ROWS, (h + 1) * ROWS)
                high, low = rows_high[visit, at], rows_low[visit, at]

                def under(term):
                    if h == 0:
                        parts = [matched_first[visit, term, :WINDOW]]
                    else:
                        parts = [
                            matched_first[visit, term, ROWS:],
                            matched_terms[i, term],
                            next_matched[i, term],
                        ]
                    left = LANES - sum([x.shape[0] for x in parts])
                    return jnp.concatenate(parts + [jnp.zeros((left, WIDTH), BF16)], axis=0)

                first = under(0)
                total = jnp.dot(
                    jnp.concatenate([high, high], axis=1),
                    jnp.concatenate([first, under(1)], axis=0),
                    preferred_element_type=F32,
                )
                halves.append(total + jnp.dot(low, first, preferred_element_type=F32))
            warped.append(jnp.concatenate(halves, axis=0))

        for i, visit in enumerate(visits):
            parts = []
            for rows, weights in (
                (slice(0, BODY), col_weights[visit]),
                (slice(BODY, BLOCK), col_weights[V + visit]),
            ):
                some = warped[i][rows]
                blocks = lane_sum(
                    lambda s, v, w: lane_block(weights[s : s + 1], v) * lane_block(some, w),
                    lane, 2 * WARP + 1, True,
                )
                parts.append(jnp.concatenate(blocks, axis=1).astype(BF16))
            result = jnp.dot(
                jnp.concatenate(parts, axis=0), unsort[...], preferred_element_type=F32
            ).astype(BF16)
            for j in range(BLKC):
                piece = lane_block(result, j)
                to = place_of[visit * BLKC + j]
                rows = pl.ds(pl.multiple_of(to % CAP * BODY, HEAD), BODY)
                out[to // CAP, rows] = piece[:BODY]
                to = next_place[visit * BLKC + j]
                rows = pl.ds(pl.multiple_of(CAP * BODY + to % CAP * HEAD, HEAD), HEAD)
                out[to // CAP, rows] = piece[BODY:]
        return 0

    lax.fori_loop(0, V // TOGETHER, some_visits, 0)


def warp(patch, slot, owner, weight, ready, images, below, devices):
    smem = pl.BlockSpec(memory_space=pltpu.SMEM)
    vmem = pl.BlockSpec(memory_space=pltpu.VMEM)
    order = deinterleave()
    sort, unsort = jnp.asarray(order, BF16), jnp.asarray(order.T, BF16)
    *matrices, rows_high, rows_low, col_weights = ready
    args = [patch, slot, owner, weight, *matrices, sort, images]
    place_of, label, matched = pl.pallas_call(
        match_kernel,
        in_specs=[smem] * 3 + [vmem] * (len(args) - 3),
        out_specs=[smem, vmem, vmem],
        out_shape=[
            jax.ShapeDtypeStruct((V * BLKC,), jnp.int32),
            jax.ShapeDtypeStruct((devices, LANES), F32),
            jax.ShapeDtypeStruct((V, 2, FIRST_STRIPS * STRIP, WIDTH), BF16),
        ],
        scratch_shapes=[
            pltpu.VMEM((TOGETHER, 4, SEEN, WIDTH), BF16),
            pltpu.SMEM((owner.shape[0],), jnp.int32),
        ],
        compiler_params=pltpu.CompilerParams(vmem_limit_bytes=32 << 20),
        cost_estimate=pl.CostEstimate(
            flops=V * 2 * FIRST_STRIPS * TAPS * STRIP * BAND * WIDTH,
            bytes_accessed=V * (BLOCK * WIDTH * 6),
            transcendentals=0,
        ),
        name="match",
    )(*args)
    args = [
        owner, place_of, label, *matrices, rows_high, rows_low, col_weights,
        sort, unsort, images, below, matched,
    ]
    return pl.pallas_call(
        warp_kernel,
        in_specs=[smem] * 2 + [vmem] * (len(args) - 2),
        out_specs=vmem,
        scratch_shapes=[
            pltpu.VMEM((TOGETHER, 4, BLOCK + 2 * RIM - FIRST_STRIPS * STRIP, WIDTH), BF16),
            pltpu.VMEM((TOGETHER, 4, STEP + STRIP, WIDTH), BF16),
            pltpu.VMEM((TOGETHER, 2, (OWN_STRIPS - FIRST_STRIPS) * STRIP, WIDTH), BF16),
            pltpu.VMEM((TOGETHER, 2, NEXT_STRIPS * STRIP, WIDTH), BF16),
            pltpu.SMEM((8, LANES), F32),
            pltpu.SMEM((V * BLKC,), jnp.int32),
            pltpu.SMEM((owner.shape[0],), jnp.int32),
            pltpu.SemaphoreType.DMA(()),
        ],
        out_shape=jax.ShapeDtypeStruct((devices, CAP * BLOCK + LABEL, BLOCK), BF16),
        compiler_params=pltpu.CompilerParams(vmem_limit_bytes=32 << 20),
        cost_estimate=pl.CostEstimate(
            flops=V * 2 * STRIPS * TAPS * STRIP * BAND * WIDTH,
            bytes_accessed=V * (BLOCK * WIDTH * 6),
            transcendentals=0,
        ),
        name="warp",
    )(*args)


def coadd_kernel(got, out, total, out_sem):
    devices = got.shape[0]
    wide = devices * CAP * STRIP
    labels = got[:, CAP * BLOCK : CAP * BLOCK + LABEL][:, 0]
    lane = iota((1, wide), 1)
    rank = lane // STRIP % CAP
    source = lane // (STRIP * CAP)

    def spread(entry):
        onehot = (iota((LANES, wide), 0) == rank * 2 + entry).astype(F32).astype(BF16)
        every = jnp.dot(labels, onehot, preferred_element_type=F32)
        return jnp.sum(
            jnp.where(iota((devices, wide), 0) == source, every, 0.0), axis=0, keepdims=True
        )

    weights, cells = spread(0), spread(1)
    row = iota((CELLS * STRIP, 1), 0)
    mine = (cells == (row // STRIP).astype(F32)) & (lane % STRIP == row % STRIP)
    matrix = jnp.where(mine, weights, 0.0)
    sums = jnp.sum(matrix, axis=1, keepdims=True)
    inverse = 1.0 / jnp.maximum(sums, 1.0)
    matrix = matrix.astype(BF16)
    taken = {}
    for r in range(CAP):
        column = jnp.broadcast_to(labels[:, 2 * r : 2 * r + 1].astype(F32), (devices, LANES))
        for s in range(devices):
            taken[s, r] = jnp.broadcast_to(column[s : s + 1], (STRIP, LANES)).astype(BF16) > 0

    def tile(s, r, k):
        device, first = s, r * BODY + k * STRIP - HEAD
        if k == 0:
            device, first = (s - 1) % devices, CAP * BODY + r * HEAD
        return jnp.where(taken[s, r], got[device, first : first + STRIP], jnp.zeros((), BF16))

    copies = []
    for pair in range(BLOCK // STRIP // 2):
        columns = jnp.concatenate(
            [
                jnp.concatenate(
                    [tile(s, r, k) for s in range(devices) for r in range(CAP)], axis=0
                )
                for k in (2 * pair, 2 * pair + 1)
            ],
            axis=1,
        )
        result = jnp.dot(matrix, columns, preferred_element_type=F32) * inverse
        for c in range(CELLS):
            part = result[c * STRIP : (c + 1) * STRIP]
            lanes = slice(c % PSIDE * BLOCK, (c % PSIDE + 1) * BLOCK)
            for n in range(2):
                first = (2 * pair + n) * STRIP
                total[c // PSIDE, first : first + STRIP, lanes] = lane_block(part, n)
        size = 2 * STRIP
        for line in range(PSIDE):
            copies.append(
                pltpu.make_async_copy(
                    total.at[line, pl.ds(pair * size, size)],
                    out.at[0, pl.ds(line * BLOCK + pair * size, size)],
                    out_sem.at[pair, line],
                )
            )
            copies[-1].start()
    for copy in copies:
        copy.wait()


def coadd(got):
    return pl.pallas_call(
        coadd_kernel,
        in_specs=[pl.BlockSpec(memory_space=pltpu.VMEM)],
        out_specs=pl.BlockSpec(memory_space=pl.ANY),
        out_shape=jax.ShapeDtypeStruct((1, PSIDE * BLOCK, PSIDE * BLOCK), F32),
        scratch_shapes=[
            pltpu.VMEM((PSIDE, BLOCK, WIDTH), F32),
            pltpu.SemaphoreType.DMA((BLOCK // STRIP // 2, PSIDE)),
        ],
        compiler_params=pltpu.CompilerParams(vmem_limit_bytes=32 << 20),
        name="coadd",
    )(got)


def shards(
    images, basis_taps, psf_coef, affine, visit_weight, block_patch, block_slot, patch_owner
):
    devices = lax.axis_size("ccd")
    patch = block_patch[:, :, 0]
    names = lax.pad(
        patch.astype(F32), jnp.zeros((), F32), ((0, 7, 0), (0, WIDTH - V * BLKC, 0))
    )
    head = jnp.concatenate([images[:, : HEAD + RIM].reshape(-1, WIDTH), names], axis=0)
    below = lax.ppermute(head, "ccd", [((i + 1) % devices, i) for i in range(devices)])
    ready = prepare(basis_taps, psf_coef, affine, devices)
    sent = warp(
        patch, block_slot, patch_owner, visit_weight, ready, images, below, devices
    )
    got = lax.all_to_all(sent, "ccd", split_axis=0, concat_axis=0, tiled=True)
    return coadd(got)


def solution(mesh):
    placed = (
        P(None, ("group", "ccd"), None),
        P(),
        P(None, "group", None, None),
        P(None, "group", None, None),
        P(None, "group"),
        P(("group", "ccd"), None, None),
        P(("group", "ccd"), None),
        P("group"),
    )
    return jax.shard_map(
        shards,
        mesh=mesh,
        in_specs=placed,
        out_specs=P(("group", "ccd"), None, None),
        check_vma=False,
    )
```

```python
import functools
import itertools

import jax
import jax.numpy as jnp
import numpy as np
from jax import lax
from jax.experimental import pallas as pl
from jax.experimental.pallas import tpu as pltpu
from jax.sharding import PartitionSpec as P

V = 4
BLOCK = 128
BLKC = 4
SPLIT = 4
TAPS = 11
NBASIS = 9
PSIDE = 4
CELLS = PSIDE * PSIDE
CAP = 2

HALF = TAPS // 2
WARP = 3
RIM = HALF + WARP
HEAD = 16
HEIGHT = SPLIT * BLOCK
WIDTH = BLKC * BLOCK
LANES = 128
LANE_BLOCKS = WIDTH // LANES
STRIP = 16
STEP = 32
STRIPS = -(-(BLOCK + 2 * WARP) // STRIP)
MIDDLE = STRIPS // 2
GROUPS = 6
BAND = 256
FIRST_STRIPS = 6
OWN_STRIPS = STRIPS - 1
NEXT_STRIPS = 2
NEXT_FIRST = (STRIPS - NEXT_STRIPS) * STRIP
HALVES = 2
TOGETHER = 2
ROWS = BLOCK // HALVES
WINDOW = ROWS + STRIP
BODY = BLOCK - HEAD
SEEN = -(-(FIRST_STRIPS * STRIP + TAPS - 1) // STRIP) * STRIP
LABEL = 16
F32 = jnp.float32
BF16 = jnp.bfloat16


def sin_pi(t):
    whole = jnp.round(t)
    f = t - whole
    odd = whole - 2.0 * jnp.floor(0.5 * whole)
    f2 = f * f
    out = 0.0
    for c in (
        0.00046630280576761, -0.0073704309457144, 0.0821458866111282,
        -0.599264529320792, 2.55016403987734, -5.16771278004997, 3.14159265358979,
    ):
        out = out * f2 + c
    return f * out * (1.0 - 2.0 * odd)


def lanczos(t):
    zero = t == 0.0
    safe = jnp.where(zero, 1.0, t)
    pt = jnp.pi * safe
    value = 3.0 * sin_pi(safe) * sin_pi(safe / 3.0) / (pt * pt)
    return jnp.where(jnp.abs(t) < 3.0, jnp.where(zero, 1.0, value), 0.0)


def iota(shape, dim):
    return lax.broadcasted_iota(jnp.int32, shape, dim)


def deinterleave():
    order = np.arange(WIDTH).reshape(LANES, LANE_BLOCKS).T.reshape(-1)
    return (np.arange(WIDTH)[:, None] == order[None, :]).astype(np.float32)


def column_at(lane):
    return lane % LANES * LANE_BLOCKS + lane // LANES


def lane_block(x, v):
    return x[:, v * LANES : (v + 1) * LANES]


def dot_exact(a, b, dims):
    return lax.dot_general(
        a, b, (dims, ((), ())), precision=lax.Precision.HIGHEST, preferred_element_type=F32
    )


def staircase(x, first):
    return jnp.concatenate(
        [
            pltpu.roll(x[g : g + 8], first + g, 1, stride=1, stride_axis=0)
            for g in range(0, x.shape[0], 8)
        ],
        axis=0,
    )


def lane_sum(terms_of, lane, count, weigh):
    blocks = []
    for v in range(LANE_BLOCKS):
        total = None
        half = count // 2
        for q in range(-(-half // LANE_BLOCKS) * -1, (half + LANE_BLOCKS - 1) // LANE_BLOCKS + 1):
            part = None
            for u in range(count):
                if (v + u - half) // LANE_BLOCKS != q:
                    continue
                piece = terms_of(u, v, (v + u - half) % LANE_BLOCKS)
                part = piece if part is None else part + piece
            if part is None:
                continue
            if q:
                part = pltpu.roll(part, -q % LANES, 1)
                if not weigh:
                    part = jnp.where((lane + q >= 0) & (lane + q < LANES), part, 0.0)
            total = part if total is None else total + part
        blocks.append(total)
    return blocks


def whereabouts(devices):
    band = lax.axis_index("ccd")
    after = lax.rem(band + 1, devices)
    quarter = (band + SPLIT // 2) % SPLIT
    own = ((band + SPLIT // 2) // SPLIT, quarter * BLOCK + HEAD)
    following = (
        (after + SPLIT // 2) // SPLIT,
        (after + SPLIT // 2) % SPLIT * BLOCK - BODY,
    )
    return (own, following), (quarter < SPLIT - 1) & (band < devices - 1)


def lanczos_kernel(devices, affine, rows_out, cols_out):
    bands, same = whereabouts(devices)
    lane = iota((1, LANES), 1)
    lanes = iota((8, WIDTH), 1)
    step = iota((8, WIDTH), 0) - WARP
    block = lanes // LANES
    carry = (block + step + LANE_BLOCKS) // LANE_BLOCKS - 1
    from_lane = lanes % LANES - carry
    col = (from_lane * LANE_BLOCKS + block).astype(F32)
    within = (from_lane >= 0) & (from_lane < LANES) & (step <= WARP)
    offset = iota((8, LANES), 0) - WARP
    crosses = (lane + offset >= BODY) != (lane >= BODY)
    keep = (offset <= WARP) & (same | jnp.logical_not(crosses))
    for visit in range(V):
        shifts = []
        for n, (ccd, top_row) in enumerate(bands):
            a = jnp.sum(
                jnp.where(iota((1, 1, affine.shape[3]), 2) == ccd, affine[visit], 0.0),
                axis=2, keepdims=True,
            )
            row = (top_row + lane).astype(F32)
            shifts.append(a[0, 0:1] + a[0, 1:2] * (row - (HEIGHT - 1) / 2.0) / HEIGHT)
            col_shift = a[1, 0:1] + a[1, 1:2] * (col - (WIDTH - 1) / 2.0) / WIDTH
            cols_out[n * V + visit] = jnp.where(within, lanczos(col_shift - step.astype(F32)), 0.0)
        shift = jnp.where(lane < BODY, shifts[0], shifts[1])
        weights = jnp.where(keep, lanczos(shift - offset.astype(F32)), 0.0)
        rows_out[visit] = jnp.concatenate([weights, jnp.zeros((LANES - 8, LANES), F32)], axis=0).T


def prepare_kernel(
    devices, taps, psf, row_weights, high_level, step_level, slope, rows_high, rows_low
):
    bands, _ = whereabouts(devices)
    band_lane = iota((1, BAND), 1)
    seg = band_lane // STEP
    lane = iota((1, LANES), 1)
    tap = band_lane - seg * STEP
    onehot = (tap == iota((TAPS, BAND), 0)) & (seg < GROUPS)
    row_taps = dot_exact(taps[:, 0], onehot.astype(F32), ((1,), (0,)))
    eye = (iota((TAPS, STRIP), 0) == iota((TAPS, STRIP), 1)).astype(F32)
    turned_taps = dot_exact(eye, taps[:, 1], ((0,), (1,)))
    units = []
    for n, visit in itertools.product(range(2), range(V)):
        ccd, top_row = bands[n]
        lhs = jnp.concatenate(
            [turned_taps * psf[ccd, c, visit : visit + 1, :] for c in range(3)], axis=0
        )
        kernels = dot_exact(lhs, row_taps, ((1,), (0,)))
        const, by_row, by_col = (kernels[c * STRIP : (c + 1) * STRIP] for c in range(3))
        is_level = seg < 3
        per_strip = 2.0 * STRIP / HEIGHT
        middle_row = (top_row + (MIDDLE * STRIP - WARP)).astype(F32)
        middle_pos = (2.0 * middle_row + 1.0) / HEIGHT - 1.0
        col_move = (iota((STRIP, 1), 0) - HALF).astype(F32) * (2.0 / WIDTH)
        by_row = jnp.where(is_level, by_row, 0.0)
        const = jnp.where(is_level, const + middle_pos * by_row - col_move * by_col, by_col)
        reach = per_strip * (STRIPS - MIDDLE)
        largest = jnp.max(jnp.abs(const) + reach * jnp.abs(by_row), axis=(0, 1), keepdims=True)
        unit = jnp.maximum(largest, 1e-30) * (1.0 / 200.0)
        units.append(unit)
        const = const / unit
        by_row = (by_row * per_strip) / unit
        low_lanes = (lane // STEP) % 3 == 2
        low_band = seg % 3 == 2
        row_part = iota((STRIP, 1), 0).astype(F32) * (1.0 / STRIP)
        for u in range(TAPS):
            at = slice(u * STRIP, (u + 1) * STRIP)
            x = staircase(jnp.broadcast_to(const[u : u + 1], (STRIP, BAND)), 0)
            y = staircase(jnp.broadcast_to(by_row[u : u + 1, :LANES], (STRIP, LANES)), 0)
            tail = x[:, LANES:]
            high = tail.astype(BF16).astype(F32)
            slope[n * V + visit, at] = jnp.where(low_band[:, LANES:], tail - high, high).astype(BF16)
            x = x[:, :LANES] + row_part * y
            high = jnp.where(lane < 3 * STEP, jnp.round(x), x.astype(BF16).astype(F32))
            high_level[n * V + visit, at] = jnp.where(low_lanes, x - high, high)
            high = jnp.round(y)
            step_level[n * V + visit, at] = jnp.where(low_lanes, y - high, high)

    for visit in range(V):
        weights = row_weights[visit]
        matrix = jnp.concatenate(
            [
                staircase(weights[:ROWS] * units[visit], 0),
                staircase(weights[ROWS:BODY] * units[visit], 0),
                staircase(weights[BODY:] * units[V + visit], ROWS),
            ],
            axis=0,
        )
        high = matrix.astype(BF16)
        rows_high[visit] = high
        rows_low[visit] = (matrix - high.astype(F32)).astype(BF16)


def small_kernel(body, name, args, shapes):
    vmem = pl.BlockSpec(memory_space=pltpu.VMEM)
    return pl.pallas_call(
        body,
        in_specs=[vmem] * len(args),
        out_specs=[vmem] * len(shapes),
        out_shape=[jax.ShapeDtypeStruct(shape, kind) for shape, kind in shapes],
        compiler_params=pltpu.CompilerParams(vmem_limit_bytes=32 << 20),
        cost_estimate=pl.CostEstimate(flops=1 << 30, bytes_accessed=1 << 20, transcendentals=0),
        name=name,
    )(*args)


def prepare(taps, psf, affine, devices):
    row_weights, col_weights = small_kernel(
        functools.partial(lanczos_kernel, devices), "lanczos_weights",
        [affine.transpose(0, 2, 3, 1)],
        [((V, BLOCK, LANES), F32), ((2 * V, 8, WIDTH), F32)],
    )
    matrices = small_kernel(
        functools.partial(prepare_kernel, devices), "matrices",
        [taps.transpose(1, 0, 2), psf.transpose(1, 3, 0, 2), row_weights],
        [
            ((2 * V, TAPS * STRIP, LANES), F32),
            ((2 * V, TAPS * STRIP, LANES), F32),
            ((2 * V, TAPS * STRIP, BAND - LANES), BF16),
            ((V, BLOCK, LANES), BF16),
            ((V, BLOCK, LANES), BF16),
        ],
    )
    return [*matrices, col_weights]


def sorted_rows(raw, sort):
    col_pos = (2.0 * column_at(iota((1, WIDTH), 1)).astype(F32) + 1.0) / WIDTH - 1.0
    count = raw.shape[0]
    raw_high = raw.astype(BF16)
    raw_low = (raw - raw_high.astype(F32)).astype(BF16)
    both = jnp.dot(
        jnp.concatenate([raw_high, raw_low], axis=0), sort, preferred_element_type=F32
    )
    high, low = both[:count], both[count:]
    tilted = (high + low) * col_pos
    tilted_high = tilted.astype(BF16).astype(F32)
    return high, low, tilted_high, tilted - tilted_high


def match_strip(level, step, slope, source, first, k):
    lane = iota((1, LANES), 1)
    if k != MIDDLE:
        level = level + float(k - MIDDLE) * step
    matrix = jnp.concatenate([level.astype(BF16), slope], axis=1)
    filler = jnp.zeros((BAND - GROUPS * STEP, WIDTH), BF16)
    rows = slice(first, first + STEP)
    columns = jnp.concatenate([source[h, rows] for h in (0, 1, 0, 2, 3, 2)] + [filler], axis=0)
    results = jnp.dot(matrix, columns, preferred_element_type=F32)
    blocks = lane_sum(
        lambda u, v, w: lane_block(results[u * STRIP : (u + 1) * STRIP], w), lane, TAPS, False
    )
    matched = jnp.concatenate(blocks, axis=1)
    high = matched.astype(BF16)
    return high, (matched - high.astype(F32)).astype(BF16)


def upright(line):
    count = line.shape[1]
    square = (count, count)
    return jnp.sum(
        jnp.where(iota(square, 0) == iota(square, 1), jnp.broadcast_to(line, square), 0),
        axis=1, keepdims=True,
    )


def route(patch, owner):
    square = (patch.shape[1], patch.shape[1])
    earlier = (iota(square, 0) < iota(square, 1)) & (upright(patch) == patch)
    rank = jnp.sum(earlier.astype(jnp.int32), axis=0, keepdims=True)
    named = iota((owner.shape[1], patch.shape[1]), 0) == patch
    to = jnp.sum(jnp.where(named, upright(owner), 0), axis=0, keepdims=True)
    return to, rank


def match_kernel(
    patch, slot, owner, weight, high_level, step_level, slope, sort, image,
    places, label, matched_terms, terms,
):
    ((ccd, _), _), _ = whereabouts(label.shape[0])
    to, rank = route(patch[...], owner[...])
    places[...] = to * CAP + rank

    own = jnp.where(iota(weight.shape, 1) == ccd, weight[...].astype(F32), 0.0)
    own = jnp.sum(own, axis=1, keepdims=True)
    each = (V, V * BLKC)
    weights = jnp.sum(
        jnp.where(iota(each, 1) // BLKC == iota(each, 0), own, 0.0), axis=0, keepdims=True
    )
    goes = iota((label.shape[0], V * BLKC), 0) == to
    lane = iota(label.shape, 1)
    lines = jnp.zeros(label.shape, F32)
    for r in range(CAP):
        for n, value in enumerate((weights, slot[...].astype(F32))):
            column = jnp.sum(jnp.where(goes & (rank == r), value, 0.0), axis=1, keepdims=True)
            lines = jnp.where(lane == 2 * r + n, column, lines)
    label[...] = lines

    def some_visits(turn, _):
        visits = [turn * TOGETHER + i for i in range(TOGETHER)]
        for i, visit in enumerate(visits):
            for h, value in enumerate(sorted_rows(image[visit, RIM : RIM + SEEN], sort[...])):
                terms[i, h] = value.astype(BF16)
        for k in range(FIRST_STRIPS):
            for i, visit in enumerate(visits):
                at = slice(k * STRIP, (k + 1) * STRIP)
                matched_terms[visit, 0, at], matched_terms[visit, 1, at] = match_strip(
                    high_level[visit], step_level[visit], slope[visit],
                    terms.at[i], k * STRIP, k,
                )
        return 0

    lax.fori_loop(0, V // TOGETHER, some_visits, 0)


def warp_kernel(
    owner, places, label, high_level, step_level, slope, rows_high, rows_low, col_weights,
    sort, unsort, image, below, matched_first, out,
    terms, next_terms, matched_terms, next_matched, both_places, place_of, place_sem,
):
    devices = label.shape[0]
    _, same = whereabouts(devices)
    next_patch = below[V * (HEAD + RIM) : V * (HEAD + RIM) + 1, : V * BLKC].astype(jnp.int32)
    to, rank = route(next_patch, owner[...])
    both_places[0:1, : V * BLKC] = places[...]
    both_places[1:2, : V * BLKC] = to * CAP + rank
    place_copy = pltpu.make_async_copy(both_places, place_of, place_sem)
    place_copy.start()
    lane = iota((1, LANES), 1)
    next_terms[:, :, STEP:] = jnp.zeros((TOGETHER, 4, STRIP, WIDTH), BF16)
    out[:, CAP * BLOCK :] = jnp.broadcast_to(
        label[...].reshape(devices, 1, LANES), (devices, LABEL, LANES)
    ).astype(BF16)

    first_row = FIRST_STRIPS * STRIP
    tall = BLOCK + 2 * RIM
    seam = tall - STEP - first_row
    seam_row = iota((STEP, 1), 0) < STEP - HEAD - RIM
    both = jnp.where(same, 1.0, 0.0)
    own_sees = jnp.where(seam_row, 1.0, both)
    next_sees = jnp.where(seam_row, both, 1.0)

    def some_visits(turn, _):
        visits = [turn * TOGETHER + i for i in range(TOGETHER)]
        for i, visit in enumerate(visits):
            head = pl.ds(pl.multiple_of(visit * (HEAD + RIM), 8), HEAD + RIM)
            raw = jnp.concatenate([image[visit, RIM + first_row :], below[head]], axis=0)
            for h, value in enumerate(sorted_rows(raw, sort[...])):
                terms[i, h, :seam] = value[:seam].astype(BF16)
                terms[i, h, seam:] = (value[seam:] * own_sees).astype(BF16)
                next_terms[i, h, :STEP] = (value[seam:] * next_sees).astype(BF16)
        for k in range(FIRST_STRIPS, OWN_STRIPS):
            for i, visit in enumerate(visits):
                first = k * STRIP - first_row
                at = slice(first, first + STRIP)
                matched_terms[i, 0, at], matched_terms[i, 1, at] = match_strip(
                    high_level[visit], step_level[visit], slope[visit], terms.at[i], first, k
                )
        for k in range(NEXT_STRIPS):
            for i, visit in enumerate(visits):
                at = slice(k * STRIP, (k + 1) * STRIP)
                next_matched[i, 0, at], next_matched[i, 1, at] = match_strip(
                    high_level[V + visit], step_level[V + visit], slope[V + visit],
                    next_terms.at[i], k * STRIP, STRIPS - NEXT_STRIPS + k,
                )

        warped = []
        for i, visit in enumerate(visits):
            halves = []
            for h in range(HALVES):
                at = slice(h * ROWS, (h + 1) * ROWS)
                high, low = rows_high[visit, at], rows_low[visit, at]

                def under(term):
                    if h == 0:
                        parts = [matched_first[visit, term, :WINDOW]]
                    else:
                        parts = [
                            matched_first[visit, term, ROWS:],
                            matched_terms[i, term],
                            next_matched[i, term],
                        ]
                    left = LANES - sum([x.shape[0] for x in parts])
                    return jnp.concatenate(parts + [jnp.zeros((left, WIDTH), BF16)], axis=0)

                first = under(0)
                total = jnp.dot(
                    jnp.concatenate([high, high], axis=1),
                    jnp.concatenate([first, under(1)], axis=0),
                    preferred_element_type=F32,
                )
                halves.append(total + jnp.dot(low, first, preferred_element_type=F32))
            warped.append(jnp.concatenate(halves, axis=0))

        @pl.when(turn == 0)
        def _():
            place_copy.wait()

        for i, visit in enumerate(visits):
            parts = []
            for rows, weights in (
                (slice(0, BODY), col_weights[visit]),
                (slice(BODY, BLOCK), col_weights[V + visit]),
            ):
                some = warped[i][rows]
                blocks = lane_sum(
                    lambda s, v, w: lane_block(weights[s : s + 1], v) * lane_block(some, w),
                    lane, 2 * WARP + 1, True,
                )
                parts.append(jnp.concatenate(blocks, axis=1).astype(BF16))
            result = jnp.dot(
                jnp.concatenate(parts, axis=0), unsort[...], preferred_element_type=F32
            ).astype(BF16)
            for j in range(BLKC):
                piece = lane_block(result, j)
                to = place_of[0, visit * BLKC + j]
                rows = pl.ds(pl.multiple_of(to % CAP * BODY, HEAD), BODY)
                out[to // CAP, rows] = piece[:BODY]
                to = place_of[1, visit * BLKC + j]
                rows = pl.ds(pl.multiple_of(CAP * BODY + to % CAP * HEAD, HEAD), HEAD)
                out[to // CAP, rows] = piece[BODY:]
        return 0

    lax.fori_loop(0, V // TOGETHER, some_visits, 0)


def warp(patch, slot, owner, weight, ready, images, below, devices):
    vmem = pl.BlockSpec(memory_space=pltpu.VMEM)
    order = deinterleave()
    sort, unsort = jnp.asarray(order, BF16), jnp.asarray(order.T, BF16)
    *matrices, rows_high, rows_low, col_weights = ready
    owner = owner.reshape(1, -1)
    args = [patch, slot, owner, weight, *matrices, sort, images]
    places, label, matched = pl.pallas_call(
        match_kernel,
        in_specs=[vmem] * len(args),
        out_specs=[vmem, vmem, vmem],
        out_shape=[
            jax.ShapeDtypeStruct((1, V * BLKC), jnp.int32),
            jax.ShapeDtypeStruct((devices, LANES), F32),
            jax.ShapeDtypeStruct((V, 2, FIRST_STRIPS * STRIP, WIDTH), BF16),
        ],
        scratch_shapes=[
            pltpu.VMEM((TOGETHER, 4, SEEN, WIDTH), BF16),
        ],
        compiler_params=pltpu.CompilerParams(vmem_limit_bytes=32 << 20),
        cost_estimate=pl.CostEstimate(
            flops=V * 2 * FIRST_STRIPS * TAPS * STRIP * BAND * WIDTH,
            bytes_accessed=V * (BLOCK * WIDTH * 6),
            transcendentals=0,
        ),
        name="match",
    )(*args)
    args = [
        owner, places, label, *matrices, rows_high, rows_low, col_weights,
        sort, unsort, images, below, matched,
    ]
    return pl.pallas_call(
        warp_kernel,
        in_specs=[vmem] * len(args),
        out_specs=vmem,
        scratch_shapes=[
            pltpu.VMEM((TOGETHER, 4, BLOCK + 2 * RIM - FIRST_STRIPS * STRIP, WIDTH), BF16),
            pltpu.VMEM((TOGETHER, 4, STEP + STRIP, WIDTH), BF16),
            pltpu.VMEM((TOGETHER, 2, (OWN_STRIPS - FIRST_STRIPS) * STRIP, WIDTH), BF16),
            pltpu.VMEM((TOGETHER, 2, NEXT_STRIPS * STRIP, WIDTH), BF16),
            pltpu.VMEM((8, LANES), jnp.int32),
            pltpu.SMEM((8, LANES), jnp.int32),
            pltpu.SemaphoreType.DMA(()),
        ],
        out_shape=jax.ShapeDtypeStruct((devices, CAP * BLOCK + LABEL, BLOCK), BF16),
        compiler_params=pltpu.CompilerParams(vmem_limit_bytes=32 << 20),
        cost_estimate=pl.CostEstimate(
            flops=V * 2 * STRIPS * TAPS * STRIP * BAND * WIDTH,
            bytes_accessed=V * (BLOCK * WIDTH * 6),
            transcendentals=0,
        ),
        name="warp",
    )(*args)


def coadd_kernel(got, out, total, out_sem):
    devices = got.shape[0]
    wide = devices * CAP * STRIP
    labels = got[:, CAP * BLOCK : CAP * BLOCK + LABEL][:, 0]
    lane = iota((1, wide), 1)
    rank = lane // STRIP % CAP
    source = lane // (STRIP * CAP)

    def spread(entry):
        onehot = (iota((LANES, wide), 0) == rank * 2 + entry).astype(F32).astype(BF16)
        every = jnp.dot(labels, onehot, preferred_element_type=F32)
        return jnp.sum(
            jnp.where(iota((devices, wide), 0) == source, every, 0.0), axis=0, keepdims=True
        )

    weights, cells = spread(0), spread(1)
    row = iota((CELLS * STRIP, 1), 0)
    mine = (cells == (row // STRIP).astype(F32)) & (lane % STRIP == row % STRIP)
    matrix = jnp.where(mine, weights, 0.0)
    sums = jnp.sum(matrix, axis=1, keepdims=True)
    inverse = 1.0 / jnp.maximum(sums, 1.0)
    matrix = matrix.astype(BF16)
    taken = {}
    for r in range(CAP):
        column = jnp.broadcast_to(labels[:, 2 * r : 2 * r + 1].astype(F32), (devices, LANES))
        for s in range(devices):
            taken[s, r] = jnp.broadcast_to(column[s : s + 1], (STRIP, LANES)).astype(BF16) > 0

    def tile(s, r, k):
        device, first = s, r * BODY + k * STRIP - HEAD
        if k == 0:
            device, first = (s - 1) % devices, CAP * BODY + r * HEAD
        return jnp.where(taken[s, r], got[device, first : first + STRIP], jnp.zeros((), BF16))

    copies = []
    for pair in range(BLOCK // STRIP // 2):
        columns = jnp.concatenate(
            [
                jnp.concatenate(
                    [tile(s, r, k) for s in range(devices) for r in range(CAP)], axis=0
                )
                for k in (2 * pair, 2 * pair + 1)
            ],
            axis=1,
        )
        result = jnp.dot(matrix, columns, preferred_element_type=F32) * inverse
        for c in range(CELLS):
            part = result[c * STRIP : (c + 1) * STRIP]
            lanes = slice(c % PSIDE * BLOCK, (c % PSIDE + 1) * BLOCK)
            for n in range(2):
                first = (2 * pair + n) * STRIP
                total[c // PSIDE, first : first + STRIP, lanes] = lane_block(part, n)
        size = 2 * STRIP
        for line in range(PSIDE):
            copies.append(
                pltpu.make_async_copy(
                    total.at[line, pl.ds(pair * size, size)],
                    out.at[0, pl.ds(line * BLOCK + pair * size, size)],
                    out_sem.at[pair, line],
                )
            )
            copies[-1].start()
    for copy in copies:
        copy.wait()


def coadd(got):
    return pl.pallas_call(
        coadd_kernel,
        in_specs=[pl.BlockSpec(memory_space=pltpu.VMEM)],
        out_specs=pl.BlockSpec(memory_space=pl.ANY),
        out_shape=jax.ShapeDtypeStruct((1, PSIDE * BLOCK, PSIDE * BLOCK), F32),
        scratch_shapes=[
            pltpu.VMEM((PSIDE, BLOCK, WIDTH), F32),
            pltpu.SemaphoreType.DMA((BLOCK // STRIP // 2, PSIDE)),
        ],
        compiler_params=pltpu.CompilerParams(vmem_limit_bytes=32 << 20),
        name="coadd",
    )(got)


def shards(
    images, basis_taps, psf_coef, affine, visit_weight, block_patch, block_slot, patch_owner
):
    devices = lax.axis_size("ccd")
    patch = block_patch[:, :, 0]
    zero = jnp.zeros((), F32)
    rows = V * (HEAD + RIM)
    head = lax.pad(
        images[:, : HEAD + RIM].reshape(rows, WIDTH), zero, ((0, 8, 0), (0, 0, 0))
    ) + lax.pad(patch.astype(F32), zero, ((rows, 7, 0), (0, WIDTH - V * BLKC, 0)))
    below = lax.ppermute(head, "ccd", [((i + 1) % devices, i) for i in range(devices)])
    ready = prepare(basis_taps, psf_coef, affine, devices)
    sent = warp(
        patch, block_slot, patch_owner, visit_weight, ready, images, below, devices
    )
    got = lax.all_to_all(sent, "ccd", split_axis=0, concat_axis=0, tiled=True)
    return coadd(got)


def solution(mesh):
    placed = (
        P(None, ("group", "ccd"), None),
        P(),
        P(None, "group", None, None),
        P(None, "group", None, None),
        P(None, "group"),
        P(("group", "ccd"), None, None),
        P(("group", "ccd"), None),
        P("group"),
    )
    return jax.shard_map(
        shards,
        mesh=mesh,
        in_specs=placed,
        out_specs=P(("group", "ccd"), None, None),
        check_vma=False,
    )
```

```python
import functools
import itertools

import jax
import jax.numpy as jnp
import numpy as np
from jax import lax
from jax.experimental import pallas as pl
from jax.experimental.pallas import tpu as pltpu
from jax.sharding import PartitionSpec as P

V = 4
BLOCK = 128
BLKC = 4
SPLIT = 4
TAPS = 11
NBASIS = 9
PSIDE = 4
CELLS = PSIDE * PSIDE
CAP = 2

HALF = TAPS // 2
WARP = 3
RIM = HALF + WARP
TAIL = 16
HEIGHT = SPLIT * BLOCK
WIDTH = BLKC * BLOCK
LANES = 128
LANE_BLOCKS = WIDTH // LANES
STRIP = 16
STEP = 32
STRIPS = -(-(BLOCK + 2 * WARP) // STRIP)
MIDDLE = STRIPS // 2
GROUPS = 6
BAND = 256
PAST_STRIPS = 2
OWN_FIRST = 1
FREE_FIRST = 2
HALVES = 2
TOGETHER = 2
ROWS = BLOCK // HALVES
WINDOW = ROWS + STRIP
BODY = BLOCK - TAIL
GOT = TAIL + RIM
OPEN = (STRIPS - 1) * STRIP + STEP - FREE_FIRST * STRIP
LABEL = 16
F32 = jnp.float32
BF16 = jnp.bfloat16


def sin_pi(t):
    whole = jnp.round(t)
    f = t - whole
    odd = whole - 2.0 * jnp.floor(0.5 * whole)
    f2 = f * f
    out = 0.0
    for c in (
        0.00046630280576761, -0.0073704309457144, 0.0821458866111282,
        -0.599264529320792, 2.55016403987734, -5.16771278004997, 3.14159265358979,
    ):
        out = out * f2 + c
    return f * out * (1.0 - 2.0 * odd)


def lanczos(t):
    zero = t == 0.0
    safe = jnp.where(zero, 1.0, t)
    pt = jnp.pi * safe
    value = 3.0 * sin_pi(safe) * sin_pi(safe / 3.0) / (pt * pt)
    return jnp.where(jnp.abs(t) < 3.0, jnp.where(zero, 1.0, value), 0.0)


def iota(shape, dim):
    return lax.broadcasted_iota(jnp.int32, shape, dim)


def deinterleave():
    order = np.arange(WIDTH).reshape(LANES, LANE_BLOCKS).T.reshape(-1)
    return (np.arange(WIDTH)[:, None] == order[None, :]).astype(np.float32)


def column_at(lane):
    return lane % LANES * LANE_BLOCKS + lane // LANES


def lane_block(x, v):
    return x[:, v * LANES : (v + 1) * LANES]


def dot_exact(a, b, dims):
    return lax.dot_general(
        a, b, (dims, ((), ())), precision=lax.Precision.HIGHEST, preferred_element_type=F32
    )


def staircase(x, first):
    return jnp.concatenate(
        [
            pltpu.roll(x[g : g + 8], first + g, 1, stride=1, stride_axis=0)
            for g in range(0, x.shape[0], 8)
        ],
        axis=0,
    )


def lane_sum(terms_of, lane, count, weigh):
    blocks = []
    for v in range(LANE_BLOCKS):
        total = None
        half = count // 2
        for q in range(-(-half // LANE_BLOCKS) * -1, (half + LANE_BLOCKS - 1) // LANE_BLOCKS + 1):
            part = None
            for u in range(count):
                if (v + u - half) // LANE_BLOCKS != q:
                    continue
                piece = terms_of(u, v, (v + u - half) % LANE_BLOCKS)
                part = piece if part is None else part + piece
            if part is None:
                continue
            if q:
                part = pltpu.roll(part, -q % LANES, 1)
                if not weigh:
                    part = jnp.where((lane + q >= 0) & (lane + q < LANES), part, 0.0)
            total = part if total is None else total + part
        blocks.append(total)
    return blocks


def whereabouts(devices):
    band = lax.axis_index("ccd")
    past = lax.rem(band + devices - 1, devices)
    quarter = (band + SPLIT // 2) % SPLIT
    own = ((band + SPLIT // 2) // SPLIT, quarter * BLOCK - TAIL)
    before = ((past + SPLIT // 2) // SPLIT, (past + SPLIT // 2) % SPLIT * BLOCK + BODY)
    return (own, before), (quarter > 0) & (band > 0)


def collect_kernel(images, patch, *refs):
    count = (len(refs) - 3) // 2
    small, head, copies_out, numbers, sems = (
        refs[:count], refs[count], refs[count + 1 : 2 * count + 1], refs[-2], refs[-1]
    )
    copies = [
        pltpu.make_async_copy(
            images.at[v, pl.ds(BLOCK - GOT, GOT)], head.at[pl.ds(v * GOT, GOT)], sems.at[v]
        )
        for v in range(V)
    ]
    copies += [
        pltpu.make_async_copy(a, b, sems.at[V + 1 + n])
        for n, (a, b) in enumerate(zip(small, copies_out))
    ]
    names = pltpu.make_async_copy(patch, numbers, sems.at[V])
    names.start()
    for copy in copies:
        copy.start()
    head[V * GOT :] = jnp.zeros((8, WIDTH), F32)
    names.wait()
    head[V * GOT : V * GOT + 1, : V * BLKC] = numbers[...].astype(F32)
    for copy in copies:
        copy.wait()


def collect(images, patch, small):
    hbm = pl.BlockSpec(memory_space=pl.ANY)
    vmem = pl.BlockSpec(memory_space=pltpu.VMEM)
    return pl.pallas_call(
        collect_kernel,
        in_specs=[hbm] * (2 + len(small)),
        out_specs=[vmem] * (1 + len(small)),
        out_shape=[jax.ShapeDtypeStruct((V * GOT + 8, WIDTH), F32)]
        + [jax.ShapeDtypeStruct(x.shape, x.dtype) for x in small],
        scratch_shapes=[
            pltpu.VMEM(patch.shape, jnp.int32),
            pltpu.SemaphoreType.DMA((V + 1 + len(small),)),
        ],
        name="collect",
    )(images, patch, *small)


def lanczos_kernel(devices, affine, rows_out, cols_out):
    bands, same = whereabouts(devices)
    lane = iota((1, LANES), 1)
    lanes = iota((8, WIDTH), 1)
    step = iota((8, WIDTH), 0) - WARP
    block = lanes // LANES
    carry = (block + step + LANE_BLOCKS) // LANE_BLOCKS - 1
    from_lane = lanes % LANES - carry
    col = (from_lane * LANE_BLOCKS + block).astype(F32)
    within = (from_lane >= 0) & (from_lane < LANES) & (step <= WARP)
    offset = iota((8, LANES), 0) - WARP
    crosses = (lane + offset >= TAIL) != (lane >= TAIL)
    keep = (offset <= WARP) & (same | jnp.logical_not(crosses))
    for visit in range(V):
        shifts = []
        for n, (ccd, top_row) in enumerate(bands):
            a = jnp.sum(
                jnp.where(iota((1, 1, affine.shape[3]), 2) == ccd, affine[visit], 0.0),
                axis=2, keepdims=True,
            )
            row = (top_row + lane).astype(F32)
            shifts.append(a[0, 0:1] + a[0, 1:2] * (row - (HEIGHT - 1) / 2.0) / HEIGHT)
            col_shift = a[1, 0:1] + a[1, 1:2] * (col - (WIDTH - 1) / 2.0) / WIDTH
            cols_out[n * V + visit] = jnp.where(within, lanczos(col_shift - step.astype(F32)), 0.0)
        shift = jnp.where(lane < TAIL, shifts[1], shifts[0])
        weights = jnp.where(keep, lanczos(shift - offset.astype(F32)), 0.0)
        rows_out[visit] = jnp.concatenate([weights, jnp.zeros((LANES - 8, LANES), F32)], axis=0).T


def prepare_kernel(
    devices, taps, psf, row_weights, high_level, step_level, slope, rows_high, rows_low
):
    bands, _ = whereabouts(devices)
    band_lane = iota((1, BAND), 1)
    seg = band_lane // STEP
    lane = iota((1, LANES), 1)
    tap = band_lane - seg * STEP
    onehot = (tap == iota((TAPS, BAND), 0)) & (seg < GROUPS)
    row_taps = dot_exact(taps[:, 0], onehot.astype(F32), ((1,), (0,)))
    eye = (iota((TAPS, STRIP), 0) == iota((TAPS, STRIP), 1)).astype(F32)
    turned_taps = dot_exact(eye, taps[:, 1], ((0,), (1,)))
    units = []
    for n, visit in itertools.product(range(2), range(V)):
        ccd, top_row = bands[n]
        lhs = jnp.concatenate(
            [turned_taps * psf[ccd, c, visit : visit + 1, :] for c in range(3)], axis=0
        )
        kernels = dot_exact(lhs, row_taps, ((1,), (0,)))
        const, by_row, by_col = (kernels[c * STRIP : (c + 1) * STRIP] for c in range(3))
        is_level = seg < 3
        per_strip = 2.0 * STRIP / HEIGHT
        middle_row = (top_row + (MIDDLE * STRIP - WARP)).astype(F32)
        middle_pos = (2.0 * middle_row + 1.0) / HEIGHT - 1.0
        col_move = (iota((STRIP, 1), 0) - HALF).astype(F32) * (2.0 / WIDTH)
        by_row = jnp.where(is_level, by_row, 0.0)
        const = jnp.where(is_level, const + middle_pos * by_row - col_move * by_col, by_col)
        reach = per_strip * (STRIPS - MIDDLE)
        largest = jnp.max(jnp.abs(const) + reach * jnp.abs(by_row), axis=(0, 1), keepdims=True)
        unit = jnp.maximum(largest, 1e-30) * (1.0 / 200.0)
        units.append(unit)
        const = const / unit
        by_row = (by_row * per_strip) / unit
        low_lanes = (lane // STEP) % 3 == 2
        low_band = seg % 3 == 2
        row_part = iota((STRIP, 1), 0).astype(F32) * (1.0 / STRIP)
        for u in range(TAPS):
            at = slice(u * STRIP, (u + 1) * STRIP)
            x = staircase(jnp.broadcast_to(const[u : u + 1], (STRIP, BAND)), 0)
            y = staircase(jnp.broadcast_to(by_row[u : u + 1, :LANES], (STRIP, LANES)), 0)
            tail = x[:, LANES:]
            high = tail.astype(BF16).astype(F32)
            slope[n * V + visit, at] = jnp.where(low_band[:, LANES:], tail - high, high).astype(BF16)
            x = x[:, :LANES] + row_part * y
            high = jnp.where(lane < 3 * STEP, jnp.round(x), x.astype(BF16).astype(F32))
            high_level[n * V + visit, at] = jnp.where(low_lanes, x - high, high)
            high = jnp.round(y)
            step_level[n * V + visit, at] = jnp.where(low_lanes, y - high, high)

    for visit in range(V):
        weights = row_weights[visit]
        matrix = jnp.concatenate(
            [
                staircase(weights[:TAIL] * units[V + visit], 0),
                staircase(weights[TAIL:ROWS] * units[visit], PAST_STRIPS * STRIP),
                staircase(weights[ROWS:] * units[visit], 0),
            ],
            axis=0,
        )
        high = matrix.astype(BF16)
        rows_high[visit] = high
        rows_low[visit] = (matrix - high.astype(F32)).astype(BF16)


def small_kernel(body, name, args, shapes):
    vmem = pl.BlockSpec(memory_space=pltpu.VMEM)
    return pl.pallas_call(
        body,
        in_specs=[vmem] * len(args),
        out_specs=[vmem] * len(shapes),
        out_shape=[jax.ShapeDtypeStruct(shape, kind) for shape, kind in shapes],
        compiler_params=pltpu.CompilerParams(vmem_limit_bytes=32 << 20),
        cost_estimate=pl.CostEstimate(flops=1 << 30, bytes_accessed=1 << 20, transcendentals=0),
        name=name,
    )(*args)


def prepare(taps, psf, affine, devices):
    row_weights, col_weights = small_kernel(
        functools.partial(lanczos_kernel, devices), "lanczos_weights",
        [affine],
        [((V, BLOCK, LANES), F32), ((2 * V, 8, WIDTH), F32)],
    )
    matrices = small_kernel(
        functools.partial(prepare_kernel, devices), "matrices",
        [taps, psf, row_weights],
        [
            ((2 * V, TAPS * STRIP, LANES), F32),
            ((2 * V, TAPS * STRIP, LANES), F32),
            ((2 * V, TAPS * STRIP, BAND - LANES), BF16),
            ((V, BLOCK, LANES), BF16),
            ((V, BLOCK, LANES), BF16),
        ],
    )
    return [*matrices, col_weights]


def sorted_rows(raw, sort):
    col_pos = (2.0 * column_at(iota((1, WIDTH), 1)).astype(F32) + 1.0) / WIDTH - 1.0
    count = raw.shape[0]
    raw_high = raw.astype(BF16)
    raw_low = (raw - raw_high.astype(F32)).astype(BF16)
    both = jnp.dot(
        jnp.concatenate([raw_high, raw_low], axis=0), sort, preferred_element_type=F32
    )
    high, low = both[:count], both[count:]
    tilted = (high + low) * col_pos
    tilted_high = tilted.astype(BF16).astype(F32)
    return high, low, tilted_high, tilted - tilted_high


def match_strip(level, step, slope, source, first, k):
    lane = iota((1, LANES), 1)
    if k != MIDDLE:
        level = level + float(k - MIDDLE) * step
    matrix = jnp.concatenate([level.astype(BF16), slope], axis=1)
    filler = jnp.zeros((BAND - GROUPS * STEP, WIDTH), BF16)
    rows = slice(first, first + STEP)
    columns = jnp.concatenate([source[h, rows] for h in (0, 1, 0, 2, 3, 2)] + [filler], axis=0)
    results = jnp.dot(matrix, columns, preferred_element_type=F32)
    blocks = lane_sum(
        lambda u, v, w: lane_block(results[u * STRIP : (u + 1) * STRIP], w), lane, TAPS, False
    )
    matched = jnp.concatenate(blocks, axis=1)
    high = matched.astype(BF16)
    return high, (matched - high.astype(F32)).astype(BF16)


def upright(line):
    count = line.shape[1]
    square = (count, count)
    return jnp.sum(
        jnp.where(iota(square, 0) == iota(square, 1), jnp.broadcast_to(line, square), 0),
        axis=1, keepdims=True,
    )


def route(patch, owner):
    square = (patch.shape[1], patch.shape[1])
    earlier = (iota(square, 0) < iota(square, 1)) & (upright(patch) == patch)
    rank = jnp.sum(earlier.astype(jnp.int32), axis=0, keepdims=True)
    named = iota((owner.shape[1], patch.shape[1]), 0) == patch
    to = jnp.sum(jnp.where(named, upright(owner), 0), axis=0, keepdims=True)
    return to, rank


def match_kernel(
    patch, slot, owner, weight, high_level, step_level, slope, sort, image,
    places, label, matched_terms, terms,
):
    ((ccd, _), _), _ = whereabouts(label.shape[0])
    to, rank = route(patch[...], owner[...])
    places[...] = to * CAP + rank

    own = jnp.where(iota(weight.shape, 1) == ccd, weight[...].astype(F32), 0.0)
    own = jnp.sum(own, axis=1, keepdims=True)
    each = (V, V * BLKC)
    weights = jnp.sum(
        jnp.where(iota(each, 1) // BLKC == iota(each, 0), own, 0.0), axis=0, keepdims=True
    )
    goes = iota((label.shape[0], V * BLKC), 0) == to
    lane = iota(label.shape, 1)
    lines = jnp.zeros(label.shape, F32)
    for r in range(CAP):
        for n, value in enumerate((weights, slot[...].astype(F32))):
            column = jnp.sum(jnp.where(goes & (rank == r), value, 0.0), axis=1, keepdims=True)
            lines = jnp.where(lane == 2 * r + n, column, lines)
    label[...] = lines

    open_row = FREE_FIRST * STRIP - GOT
    seen = OPEN - STRIP
    terms[:, :, seen:] = jnp.zeros((TOGETHER, 4, STRIP, WIDTH), BF16)

    def some_visits(turn, _):
        visits = [turn * TOGETHER + i for i in range(TOGETHER)]
        for i, visit in enumerate(visits):
            rows = sorted_rows(image[visit, open_row : open_row + seen], sort[...])
            for h, value in enumerate(rows):
                terms[i, h, :seen] = value.astype(BF16)
        for k in range(FREE_FIRST, STRIPS):
            first = (k - FREE_FIRST) * STRIP
            for i, visit in enumerate(visits):
                at = slice(first, first + STRIP)
                matched_terms[visit, 0, at], matched_terms[visit, 1, at] = match_strip(
                    high_level[visit], step_level[visit], slope[visit], terms.at[i], first, k
                )
        return 0

    lax.fori_loop(0, V // TOGETHER, some_visits, 0)


def warp_kernel(
    owner, places, label, high_level, step_level, slope, rows_high, rows_low, col_weights,
    sort, unsort, image, above, matched_free, out,
    own_terms, past_terms, own_matched, past_matched, both_places, place_of, place_sem,
):
    devices = label.shape[0]
    _, same = whereabouts(devices)
    past_patch = above[V * GOT : V * GOT + 1, : V * BLKC].astype(jnp.int32)
    to, rank = route(past_patch, owner[...])
    both_places[0:1, : V * BLKC] = places[...]
    both_places[1:2, : V * BLKC] = to * CAP + rank
    place_copy = pltpu.make_async_copy(both_places, place_of, place_sem)
    place_copy.start()
    lane = iota((1, LANES), 1)
    out[:, CAP * BLOCK :] = jnp.broadcast_to(
        label[...].reshape(devices, 1, LANES), (devices, LABEL, LANES)
    ).astype(BF16)

    seam = STRIP + STEP
    foreign = iota((seam, 1), 0) < GOT
    both = jnp.where(same, 1.0, 0.0)
    own_sees = jnp.where(foreign, both, 1.0)
    past_sees = jnp.where(foreign, 1.0, both)

    def some_visits(turn, _):
        visits = [turn * TOGETHER + i for i in range(TOGETHER)]
        for i, visit in enumerate(visits):
            tail = pl.ds(pl.multiple_of(visit * GOT, 8), GOT)
            raw = jnp.concatenate([above[tail], image[visit, : seam - GOT]], axis=0)
            for h, value in enumerate(sorted_rows(raw, sort[...])):
                own_terms[i, h] = (value * own_sees).astype(BF16)
                past_terms[i, h] = (value * past_sees).astype(BF16)
        for i, visit in enumerate(visits):
            own_matched[i, 0], own_matched[i, 1] = match_strip(
                high_level[visit], step_level[visit], slope[visit],
                own_terms.at[i], OWN_FIRST * STRIP, OWN_FIRST,
            )
        for k in range(PAST_STRIPS):
            for i, visit in enumerate(visits):
                at = slice(k * STRIP, (k + 1) * STRIP)
                past_matched[i, 0, at], past_matched[i, 1, at] = match_strip(
                    high_level[V + visit], step_level[V + visit], slope[V + visit],
                    past_terms.at[i], k * STRIP, k,
                )

        warped = []
        for i, visit in enumerate(visits):
            halves = []
            for h in range(HALVES):
                at = slice(h * ROWS, (h + 1) * ROWS)
                high, low = rows_high[visit, at], rows_low[visit, at]
                free = FREE_FIRST * STRIP

                def under(term):
                    if h == 0:
                        parts = [
                            past_matched[i, term],
                            own_matched[i, term],
                            matched_free[visit, term, : WINDOW - free],
                        ]
                    else:
                        parts = [matched_free[visit, term, ROWS - free :]]
                    left = LANES - sum([x.shape[0] for x in parts])
                    return jnp.concatenate(parts + [jnp.zeros((left, WIDTH), BF16)], axis=0)

                first = under(0)
                total = jnp.dot(
                    jnp.concatenate([high, high], axis=1),
                    jnp.concatenate([first, under(1)], axis=0),
                    preferred_element_type=F32,
                )
                halves.append(total + jnp.dot(low, first, preferred_element_type=F32))
            warped.append(jnp.concatenate(halves, axis=0))

        @pl.when(turn == 0)
        def _():
            place_copy.wait()

        for i, visit in enumerate(visits):
            parts = []
            for rows, weights in (
                (slice(0, TAIL), col_weights[V + visit]),
                (slice(TAIL, BLOCK), col_weights[visit]),
            ):
                some = warped[i][rows]
                blocks = lane_sum(
                    lambda s, v, w: lane_block(weights[s : s + 1], v) * lane_block(some, w),
                    lane, 2 * WARP + 1, True,
                )
                parts.append(jnp.concatenate(blocks, axis=1).astype(BF16))
            result = jnp.dot(
                jnp.concatenate(parts, axis=0), unsort[...], preferred_element_type=F32
            ).astype(BF16)
            for j in range(BLKC):
                piece = lane_block(result, j)
                to = place_of[0, visit * BLKC + j]
                rows = pl.ds(pl.multiple_of(to % CAP * BODY, TAIL), BODY)
                out[to // CAP, rows] = piece[TAIL:]
                to = place_of[1, visit * BLKC + j]
                rows = pl.ds(pl.multiple_of(CAP * BODY + to % CAP * TAIL, TAIL), TAIL)
                out[to // CAP, rows] = piece[:TAIL]
        return 0

    lax.fori_loop(0, V // TOGETHER, some_visits, 0)


def warp(patch, slot, owner, weight, ready, images, above, devices):
    vmem = pl.BlockSpec(memory_space=pltpu.VMEM)
    order = deinterleave()
    sort, unsort = jnp.asarray(order, BF16), jnp.asarray(order.T, BF16)
    *matrices, rows_high, rows_low, col_weights = ready
    owner = owner.reshape(1, -1)
    args = [patch, slot, owner, weight, *matrices, sort, images]
    places, label, matched = pl.pallas_call(
        match_kernel,
        in_specs=[vmem] * len(args),
        out_specs=[vmem, vmem, vmem],
        out_shape=[
            jax.ShapeDtypeStruct((1, V * BLKC), jnp.int32),
            jax.ShapeDtypeStruct((devices, LANES), F32),
            jax.ShapeDtypeStruct((V, 2, (STRIPS - FREE_FIRST) * STRIP, WIDTH), BF16),
        ],
        scratch_shapes=[
            pltpu.VMEM((TOGETHER, 4, OPEN, WIDTH), BF16),
        ],
        compiler_params=pltpu.CompilerParams(vmem_limit_bytes=32 << 20),
        cost_estimate=pl.CostEstimate(
            flops=V * 2 * (STRIPS - FREE_FIRST) * TAPS * STRIP * BAND * WIDTH,
            bytes_accessed=V * (BLOCK * WIDTH * 6),
            transcendentals=0,
        ),
        name="match",
    )(*args)
    args = [
        owner, places, label, *matrices, rows_high, rows_low, col_weights,
        sort, unsort, images, above, matched,
    ]
    return pl.pallas_call(
        warp_kernel,
        in_specs=[vmem] * len(args),
        out_specs=vmem,
        scratch_shapes=[
            pltpu.VMEM((TOGETHER, 4, STRIP + STEP, WIDTH), BF16),
            pltpu.VMEM((TOGETHER, 4, STRIP + STEP, WIDTH), BF16),
            pltpu.VMEM((TOGETHER, 2, STRIP, WIDTH), BF16),
            pltpu.VMEM((TOGETHER, 2, PAST_STRIPS * STRIP, WIDTH), BF16),
            pltpu.VMEM((8, LANES), jnp.int32),
            pltpu.SMEM((8, LANES), jnp.int32),
            pltpu.SemaphoreType.DMA(()),
        ],
        out_shape=jax.ShapeDtypeStruct((devices, CAP * BLOCK + LABEL, BLOCK), BF16),
        compiler_params=pltpu.CompilerParams(vmem_limit_bytes=32 << 20),
        cost_estimate=pl.CostEstimate(
            flops=V * 2 * STRIPS * TAPS * STRIP * BAND * WIDTH,
            bytes_accessed=V * (BLOCK * WIDTH * 6),
            transcendentals=0,
        ),
        name="warp",
    )(*args)


def coadd_kernel(got, out, total, out_sem):
    devices = got.shape[0]
    wide = devices * CAP * STRIP
    labels = got[:, CAP * BLOCK : CAP * BLOCK + LABEL][:, 0]
    lane = iota((1, wide), 1)
    rank = lane // STRIP % CAP
    source = lane // (STRIP * CAP)

    def spread(entry):
        onehot = (iota((LANES, wide), 0) == rank * 2 + entry).astype(F32).astype(BF16)
        every = jnp.dot(labels, onehot, preferred_element_type=F32)
        return jnp.sum(
            jnp.where(iota((devices, wide), 0) == source, every, 0.0), axis=0, keepdims=True
        )

    weights, cells = spread(0), spread(1)
    row = iota((CELLS * STRIP, 1), 0)
    mine = (cells == (row // STRIP).astype(F32)) & (lane % STRIP == row % STRIP)
    matrix = jnp.where(mine, weights, 0.0)
    sums = jnp.sum(matrix, axis=1, keepdims=True)
    inverse = 1.0 / jnp.maximum(sums, 1.0)
    matrix = matrix.astype(BF16)
    taken = {}
    for r in range(CAP):
        column = jnp.broadcast_to(labels[:, 2 * r : 2 * r + 1].astype(F32), (devices, LANES))
        for s in range(devices):
            taken[s, r] = jnp.broadcast_to(column[s : s + 1], (STRIP, LANES)).astype(BF16) > 0

    def tile(s, r, k):
        device, first = s, r * BODY + k * STRIP
        if first - r * BODY >= BODY:
            device, first = (s + 1) % devices, CAP * BODY + r * TAIL
        return jnp.where(taken[s, r], got[device, first : first + STRIP], jnp.zeros((), BF16))

    copies = []
    for pair in range(BLOCK // STRIP // 2):
        columns = jnp.concatenate(
            [
                jnp.concatenate(
                    [tile(s, r, k) for s in range(devices) for r in range(CAP)], axis=0
                )
                for k in (2 * pair, 2 * pair + 1)
            ],
            axis=1,
        )
        result = jnp.dot(matrix, columns, preferred_element_type=F32) * inverse
        for c in range(CELLS):
            part = result[c * STRIP : (c + 1) * STRIP]
            lanes = slice(c % PSIDE * BLOCK, (c % PSIDE + 1) * BLOCK)
            for n in range(2):
                first = (2 * pair + n) * STRIP
                total[c // PSIDE, first : first + STRIP, lanes] = lane_block(part, n)
        size = 2 * STRIP
        for line in range(PSIDE):
            copies.append(
                pltpu.make_async_copy(
                    total.at[line, pl.ds(pair * size, size)],
                    out.at[0, pl.ds(line * BLOCK + pair * size, size)],
                    out_sem.at[pair, line],
                )
            )
            copies[-1].start()
    for copy in copies:
        copy.wait()


def coadd(got):
    return pl.pallas_call(
        coadd_kernel,
        in_specs=[pl.BlockSpec(memory_space=pltpu.VMEM)],
        out_specs=pl.BlockSpec(memory_space=pl.ANY),
        out_shape=jax.ShapeDtypeStruct((1, PSIDE * BLOCK, PSIDE * BLOCK), F32),
        scratch_shapes=[
            pltpu.VMEM((PSIDE, BLOCK, WIDTH), F32),
            pltpu.SemaphoreType.DMA((BLOCK // STRIP // 2, PSIDE)),
        ],
        compiler_params=pltpu.CompilerParams(vmem_limit_bytes=32 << 20),
        name="coadd",
    )(got)


def shards(
    images, basis_taps, psf_coef, affine, visit_weight, block_patch, block_slot, patch_owner
):
    devices = lax.axis_size("ccd")
    patch = block_patch[:, :, 0]
    head, taps, psf, affine = collect(
        images, patch,
        [basis_taps.transpose(1, 0, 2), psf_coef.transpose(1, 3, 0, 2), affine.transpose(0, 2, 3, 1)],
    )
    above = lax.ppermute(head, "ccd", [(i, (i + 1) % devices) for i in range(devices)])
    ready = prepare(taps, psf, affine, devices)
    sent = warp(
        patch, block_slot, patch_owner, visit_weight, ready, images, above, devices
    )
    got = lax.all_to_all(sent, "ccd", split_axis=0, concat_axis=0, tiled=True)
    return coadd(got)


def solution(mesh):
    placed = (
        P(None, ("group", "ccd"), None),
        P(),
        P(None, "group", None, None),
        P(None, "group", None, None),
        P(None, "group"),
        P(("group", "ccd"), None, None),
        P(("group", "ccd"), None),
        P("group"),
    )
    return jax.shard_map(
        shards,
        mesh=mesh,
        in_specs=placed,
        out_specs=P(("group", "ccd"), None, None),
        check_vma=False,
    )
```

```python
import functools
import itertools

import jax
import jax.numpy as jnp
from jax import lax
from jax.experimental import pallas as pl
from jax.experimental.pallas import tpu as pltpu
from jax.sharding import PartitionSpec as P

V = 4
BLOCK = 128
BLKC = 4
SPLIT = 4
TAPS = 11
NBASIS = 9
PSIDE = 4
CELLS = PSIDE * PSIDE
CAP = 2

HALF = TAPS // 2
WARP = 3
RIM = HALF + WARP
TAIL = 16
HEIGHT = SPLIT * BLOCK
WIDTH = BLKC * BLOCK
LANES = 128
LANE_BLOCKS = WIDTH // LANES
STRIP = 16
STEP = 32
STRIPS = -(-(BLOCK + 2 * WARP) // STRIP)
MIDDLE = STRIPS // 2
GROUPS = 6
BAND = 256
PAST_STRIPS = 2
OWN_FIRST = 1
FREE_FIRST = 2
HALVES = 2
MATCHED = 4
WARPED = 1
ROWS = BLOCK // HALVES
WINDOW = ROWS + STRIP
BODY = BLOCK - TAIL
GOT = TAIL + RIM
OPEN = (STRIPS - 1) * STRIP + STEP - FREE_FIRST * STRIP
LABEL = 16
F32 = jnp.float32
BF16 = jnp.bfloat16


def sin_pi(t):
    whole = jnp.round(t)
    f = t - whole
    odd = whole - 2.0 * jnp.floor(0.5 * whole)
    f2 = f * f
    out = 0.0
    for c in (
        0.00046630280576761, -0.0073704309457144, 0.0821458866111282,
        -0.599264529320792, 2.55016403987734, -5.16771278004997, 3.14159265358979,
    ):
        out = out * f2 + c
    return f * out * (1.0 - 2.0 * odd)


def lanczos(t):
    zero = t == 0.0
    safe = jnp.where(zero, 1.0, t)
    pt = jnp.pi * safe
    value = 3.0 * sin_pi(safe) * sin_pi(safe / 3.0) / (pt * pt)
    return jnp.where(jnp.abs(t) < 3.0, jnp.where(zero, 1.0, value), 0.0)


def iota(shape, dim):
    return lax.broadcasted_iota(jnp.int32, shape, dim)


def column_at(lane):
    return lane % LANES * LANE_BLOCKS + lane // LANES


def order_kernel(sort, unsort):
    square = (WIDTH, WIDTH)
    one, none = jnp.ones((), F32), jnp.zeros((), F32)
    goes = iota(square, 0) == column_at(iota((1, WIDTH), 1))
    sort[...] = jnp.where(goes, one, none).astype(BF16)
    comes = iota(square, 1) == column_at(iota((WIDTH, 1), 0))
    unsort[...] = jnp.where(comes, one, none).astype(BF16)


def orders():
    return small_kernel(order_kernel, "orders", [], [((WIDTH, WIDTH), BF16)] * 2)


def lane_block(x, v):
    return x[:, v * LANES : (v + 1) * LANES]


def dot_exact(a, b, dims):
    return lax.dot_general(
        a, b, (dims, ((), ())), precision=lax.Precision.HIGHEST, preferred_element_type=F32
    )


def staircase(x, first):
    return jnp.concatenate(
        [
            pltpu.roll(x[g : g + 8], first + g, 1, stride=1, stride_axis=0)
            for g in range(0, x.shape[0], 8)
        ],
        axis=0,
    )


def lane_sum(terms_of, lane, count, weigh):
    blocks = []
    for v in range(LANE_BLOCKS):
        total = None
        half = count // 2
        for q in range(-(-half // LANE_BLOCKS) * -1, (half + LANE_BLOCKS - 1) // LANE_BLOCKS + 1):
            part = None
            for u in range(count):
                if (v + u - half) // LANE_BLOCKS != q:
                    continue
                piece = terms_of(u, v, (v + u - half) % LANE_BLOCKS)
                part = piece if part is None else part + piece
            if part is None:
                continue
            if q:
                part = pltpu.roll(part, -q % LANES, 1)
                if not weigh:
                    part = jnp.where((lane + q >= 0) & (lane + q < LANES), part, 0.0)
            total = part if total is None else total + part
        blocks.append(total)
    return blocks


def whereabouts(devices):
    band = lax.axis_index("ccd")
    past = lax.rem(band + devices - 1, devices)
    quarter = (band + SPLIT // 2) % SPLIT
    own = ((band + SPLIT // 2) // SPLIT, quarter * BLOCK - TAIL)
    before = ((past + SPLIT // 2) // SPLIT, (past + SPLIT // 2) % SPLIT * BLOCK + BODY)
    return (own, before), (quarter > 0) & (band > 0)


def collect_kernel(images, patch, head, numbers, line, sems):
    copies = [
        pltpu.make_async_copy(
            images.at[v, pl.ds(BLOCK - GOT, GOT)], head.at[pl.ds(v * GOT, GOT)], sems.at[v]
        )
        for v in range(V)
    ]
    names = pltpu.make_async_copy(patch, numbers, sems.at[V])
    names.start()
    for copy in copies:
        copy.start()
    line[...] = jnp.zeros_like(line)
    names.wait()
    line[0:1, : V * BLKC] = numbers[...].astype(F32)
    last = pltpu.make_async_copy(line, head.at[pl.ds(V * GOT, 8)], sems.at[V + 1])
    last.start()
    for copy in copies + [last]:
        copy.wait()


def collect(images, patch):
    hbm = pl.BlockSpec(memory_space=pl.ANY)
    return pl.pallas_call(
        collect_kernel,
        in_specs=[hbm] * 2,
        out_specs=hbm,
        out_shape=jax.ShapeDtypeStruct((V * GOT + 8, WIDTH), F32),
        scratch_shapes=[
            pltpu.VMEM(patch.shape, jnp.int32),
            pltpu.VMEM((8, WIDTH), F32),
            pltpu.SemaphoreType.DMA((V + 2,)),
        ],
        name="collect",
    )(images, patch)


def lanczos_weights(devices, affine, cols_out):
    bands, same = whereabouts(devices)
    lane = iota((1, LANES), 1)
    lanes = iota((8, WIDTH), 1)
    step = iota((8, WIDTH), 0) - WARP
    block = lanes // LANES
    carry = (block + step + LANE_BLOCKS) // LANE_BLOCKS - 1
    from_lane = lanes % LANES - carry
    col = (from_lane * LANE_BLOCKS + block).astype(F32)
    within = (from_lane >= 0) & (from_lane < LANES) & (step <= WARP)
    offset = iota((8, LANES), 0) - WARP
    crosses = (lane + offset >= TAIL) != (lane >= TAIL)
    keep = (offset <= WARP) & (same | jnp.logical_not(crosses))
    by_row = []
    for visit in range(V):
        shifts = []
        for n, (ccd, top_row) in enumerate(bands):
            a = jnp.sum(
                jnp.where(iota((1, 1, affine.shape[3]), 2) == ccd, affine[visit], 0.0),
                axis=2, keepdims=True,
            )
            row = (top_row + lane).astype(F32)
            shifts.append(a[0, 0:1] + a[0, 1:2] * (row - (HEIGHT - 1) / 2.0) / HEIGHT)
            col_shift = a[1, 0:1] + a[1, 1:2] * (col - (WIDTH - 1) / 2.0) / WIDTH
            cols_out[n * V + visit] = jnp.where(within, lanczos(col_shift - step.astype(F32)), 0.0)
        shift = jnp.where(lane < TAIL, shifts[1], shifts[0])
        weights = jnp.where(keep, lanczos(shift - offset.astype(F32)), 0.0)
        by_row.append(jnp.concatenate([weights, jnp.zeros((LANES - 8, LANES), F32)], axis=0).T)
    return by_row


def prepare_kernel(
    devices, taps, psf, affine, high_level, step_level, slope, rows_high, rows_low, cols_out
):
    row_weights = lanczos_weights(devices, affine, cols_out)
    bands, _ = whereabouts(devices)
    band_lane = iota((1, BAND), 1)
    seg = band_lane // STEP
    lane = iota((1, LANES), 1)
    tap = band_lane - seg * STEP
    onehot = (tap == iota((TAPS, BAND), 0)) & (seg < GROUPS)
    row_taps = dot_exact(taps[:, 0], onehot.astype(F32), ((1,), (0,)))
    eye = (iota((TAPS, STRIP), 0) == iota((TAPS, STRIP), 1)).astype(F32)
    turned_taps = dot_exact(eye, taps[:, 1], ((0,), (1,)))
    units = []
    for n, visit in itertools.product(range(2), range(V)):
        ccd, top_row = bands[n]
        lhs = jnp.concatenate(
            [turned_taps * psf[ccd, c, visit : visit + 1, :] for c in range(3)], axis=0
        )
        kernels = dot_exact(lhs, row_taps, ((1,), (0,)))
        const, by_row, by_col = (kernels[c * STRIP : (c + 1) * STRIP] for c in range(3))
        is_level = seg < 3
        per_strip = 2.0 * STRIP / HEIGHT
        middle_row = (top_row + (MIDDLE * STRIP - WARP)).astype(F32)
        middle_pos = (2.0 * middle_row + 1.0) / HEIGHT - 1.0
        col_move = (iota((STRIP, 1), 0) - HALF).astype(F32) * (2.0 / WIDTH)
        by_row = jnp.where(is_level, by_row, 0.0)
        const = jnp.where(is_level, const + middle_pos * by_row - col_move * by_col, by_col)
        reach = per_strip * (STRIPS - MIDDLE)
        largest = jnp.max(jnp.abs(const) + reach * jnp.abs(by_row), axis=(0, 1), keepdims=True)
        unit = jnp.maximum(largest, 1e-30) * (1.0 / 200.0)
        units.append(unit)
        const = const / unit
        by_row = (by_row * per_strip) / unit
        low_lanes = (lane // STEP) % 3 == 2
        low_band = seg % 3 == 2
        row_part = iota((STRIP, 1), 0).astype(F32) * (1.0 / STRIP)
        for u in range(TAPS):
            at = slice(u * STRIP, (u + 1) * STRIP)
            one = jnp.broadcast_to(const[u : u + 1], (STRIP, BAND))
            x, tail = staircase(one[:, :LANES], 0), staircase(one[:, LANES:], 0)
            y = staircase(jnp.broadcast_to(by_row[u : u + 1, :LANES], (STRIP, LANES)), 0)
            high = tail.astype(BF16).astype(F32)
            slope[n * V + visit, at] = jnp.where(low_band[:, LANES:], tail - high, high).astype(BF16)
            x = x + row_part * y
            high = jnp.where(lane < 3 * STEP, jnp.round(x), x.astype(BF16).astype(F32))
            high_level[n * V + visit, at] = jnp.where(low_lanes, x - high, high)
            high = jnp.round(y)
            step_level[n * V + visit, at] = jnp.where(low_lanes, y - high, high)

    for visit in range(V):
        weights = row_weights[visit]
        matrix = jnp.concatenate(
            [
                staircase(weights[:TAIL] * units[V + visit], 0),
                staircase(weights[TAIL:ROWS] * units[visit], PAST_STRIPS * STRIP),
                staircase(weights[ROWS:] * units[visit], 0),
            ],
            axis=0,
        )
        high = matrix.astype(BF16)
        rows_high[visit] = high
        rows_low[visit] = (matrix - high.astype(F32)).astype(BF16)


def small_kernel(body, name, args, shapes):
    vmem = pl.BlockSpec(memory_space=pltpu.VMEM)
    return pl.pallas_call(
        body,
        in_specs=[vmem] * len(args),
        out_specs=[vmem] * len(shapes),
        out_shape=[jax.ShapeDtypeStruct(shape, kind) for shape, kind in shapes],
        compiler_params=pltpu.CompilerParams(vmem_limit_bytes=32 << 20),
        cost_estimate=pl.CostEstimate(flops=1 << 30, bytes_accessed=1 << 20, transcendentals=0),
        name=name,
    )(*args)


def prepare(taps, psf, affine, devices):
    return small_kernel(
        functools.partial(prepare_kernel, devices), "matrices", [taps, psf, affine],
        [
            ((2 * V, TAPS * STRIP, LANES), F32),
            ((2 * V, TAPS * STRIP, LANES), F32),
            ((2 * V, TAPS * STRIP, BAND - LANES), BF16),
            ((V, BLOCK, LANES), BF16),
            ((V, BLOCK, LANES), BF16),
            ((2 * V, 8, WIDTH), F32),
        ],
    )


def sorted_rows(raw, sort):
    col_pos = (2.0 * column_at(iota((1, WIDTH), 1)).astype(F32) + 1.0) / WIDTH - 1.0
    count = raw.shape[0]
    raw_high = raw.astype(BF16)
    raw_low = (raw - raw_high.astype(F32)).astype(BF16)
    both = jnp.dot(
        jnp.concatenate([raw_high, raw_low], axis=0), sort, preferred_element_type=F32
    )
    high, low = both[:count], both[count:]
    tilted = (high + low) * col_pos
    tilted_high = tilted.astype(BF16).astype(F32)
    return high, low, tilted_high, tilted - tilted_high


def match_strip(level, step, slope, source, first, k):
    lane = iota((1, LANES), 1)
    if k != MIDDLE:
        level = level + float(k - MIDDLE) * step
    matrix = jnp.concatenate([level.astype(BF16), slope], axis=1)
    filler = jnp.zeros((BAND - GROUPS * STEP, WIDTH), BF16)
    rows = slice(first, first + STEP)
    columns = jnp.concatenate([source[h, rows] for h in (0, 1, 0, 2, 3, 2)] + [filler], axis=0)
    results = jnp.dot(matrix, columns, preferred_element_type=F32)
    blocks = lane_sum(
        lambda u, v, w: lane_block(results[u * STRIP : (u + 1) * STRIP], w), lane, TAPS, False
    )
    matched = jnp.concatenate(blocks, axis=1)
    high = matched.astype(BF16)
    return high, (matched - high.astype(F32)).astype(BF16)


def upright(line):
    count = line.shape[1]
    square = (count, count)
    return jnp.sum(
        jnp.where(iota(square, 0) == iota(square, 1), jnp.broadcast_to(line, square), 0),
        axis=1, keepdims=True,
    )


def route(patch, owner):
    square = (patch.shape[1], patch.shape[1])
    earlier = (iota(square, 0) < iota(square, 1)) & (upright(patch) == patch)
    rank = jnp.sum(earlier.astype(jnp.int32), axis=0, keepdims=True)
    named = iota((owner.shape[1], patch.shape[1]), 0) == patch
    to = jnp.sum(jnp.where(named, upright(owner), 0), axis=0, keepdims=True)
    return to, rank


def match_kernel(
    patch, slot, owner, weight, high_level, step_level, slope, sort, image,
    places, label, matched_terms, terms,
):
    ((ccd, _), _), _ = whereabouts(label.shape[0])
    to, rank = route(patch[...], owner[...])
    places[...] = to * CAP + rank

    own = jnp.where(iota(weight.shape, 1) == ccd, weight[...].astype(F32), 0.0)
    own = jnp.sum(own, axis=1, keepdims=True)
    each = (V, V * BLKC)
    weights = jnp.sum(
        jnp.where(iota(each, 1) // BLKC == iota(each, 0), own, 0.0), axis=0, keepdims=True
    )
    goes = iota((label.shape[0], V * BLKC), 0) == to
    lane = iota(label.shape, 1)
    lines = jnp.zeros(label.shape, F32)
    for r in range(CAP):
        for n, value in enumerate((weights, slot[...].astype(F32))):
            column = jnp.sum(jnp.where(goes & (rank == r), value, 0.0), axis=1, keepdims=True)
            lines = jnp.where(lane == 2 * r + n, column, lines)
    label[...] = lines

    open_row = FREE_FIRST * STRIP - GOT
    seen = OPEN - STRIP
    terms[:, :, seen:] = jnp.zeros((MATCHED, 4, STRIP, WIDTH), BF16)

    def some_visits(turn, _):
        visits = [turn * MATCHED + i for i in range(MATCHED)]
        for i, visit in enumerate(visits):
            rows = sorted_rows(image[visit, open_row : open_row + seen], sort[...])
            for h, value in enumerate(rows):
                terms[i, h, :seen] = value.astype(BF16)
        for k in range(FREE_FIRST, STRIPS):
            first = (k - FREE_FIRST) * STRIP
            for i, visit in enumerate(visits):
                at = slice(first, first + STRIP)
                matched_terms[visit, 0, at], matched_terms[visit, 1, at] = match_strip(
                    high_level[visit], step_level[visit], slope[visit], terms.at[i], first, k
                )
        return 0

    lax.fori_loop(0, V // MATCHED, some_visits, 0)


def warp_kernel(
    owner, places, label, high_level, step_level, slope, rows_high, rows_low, col_weights,
    sort, unsort, image, above, matched_free, out,
    own_terms, past_terms, own_matched, past_matched, both_places, place_of, place_sem,
):
    devices = label.shape[0]
    _, same = whereabouts(devices)
    past_patch = above[V * GOT : V * GOT + 1, : V * BLKC].astype(jnp.int32)
    to, rank = route(past_patch, owner[...])
    both_places[0:1, : V * BLKC] = places[...]
    both_places[1:2, : V * BLKC] = to * CAP + rank
    place_copy = pltpu.make_async_copy(both_places, place_of, place_sem)
    place_copy.start()
    lane = iota((1, LANES), 1)
    out[:, CAP * BLOCK :] = jnp.broadcast_to(
        label[...].reshape(devices, 1, LANES), (devices, LABEL, LANES)
    ).astype(BF16)

    seam = STRIP + STEP
    foreign = iota((seam, 1), 0) < GOT
    both = jnp.where(same, 1.0, 0.0)
    own_sees = jnp.where(foreign, both, 1.0)
    past_sees = jnp.where(foreign, 1.0, both)

    def some_visits(turn, _):
        visits = [turn * WARPED + i for i in range(WARPED)]
        for i, visit in enumerate(visits):
            tail = pl.ds(pl.multiple_of(visit * GOT, 8), GOT)
            raw = jnp.concatenate([above[tail], image[visit, : seam - GOT]], axis=0)
            for h, value in enumerate(sorted_rows(raw, sort[...])):
                own_terms[i, h] = (value * own_sees).astype(BF16)
                past_terms[i, h] = (value * past_sees).astype(BF16)
        for i, visit in enumerate(visits):
            own_matched[i, 0], own_matched[i, 1] = match_strip(
                high_level[visit], step_level[visit], slope[visit],
                own_terms.at[i], OWN_FIRST * STRIP, OWN_FIRST,
            )
        for k in range(PAST_STRIPS):
            for i, visit in enumerate(visits):
                at = slice(k * STRIP, (k + 1) * STRIP)
                past_matched[i, 0, at], past_matched[i, 1, at] = match_strip(
                    high_level[V + visit], step_level[V + visit], slope[V + visit],
                    past_terms.at[i], k * STRIP, k,
                )

        warped = []
        for i, visit in enumerate(visits):
            halves = []
            for h in range(HALVES):
                at = slice(h * ROWS, (h + 1) * ROWS)
                high, low = rows_high[visit, at], rows_low[visit, at]
                free = FREE_FIRST * STRIP

                def under(term):
                    if h == 0:
                        parts = [
                            past_matched[i, term],
                            own_matched[i, term],
                            matched_free[visit, term, : WINDOW - free],
                        ]
                    else:
                        parts = [matched_free[visit, term, ROWS - free :]]
                    left = LANES - sum([x.shape[0] for x in parts])
                    return jnp.concatenate(parts + [jnp.zeros((left, WIDTH), BF16)], axis=0)

                first = under(0)
                total = jnp.dot(
                    jnp.concatenate([high, high], axis=1),
                    jnp.concatenate([first, under(1)], axis=0),
                    preferred_element_type=F32,
                )
                halves.append(total + jnp.dot(low, first, preferred_element_type=F32))
            warped.append(jnp.concatenate(halves, axis=0))

        @pl.when(turn == 0)
        def _():
            place_copy.wait()

        for i, visit in enumerate(visits):
            parts = []
            for rows, weights in (
                (slice(0, TAIL), col_weights[V + visit]),
                (slice(TAIL, BLOCK), col_weights[visit]),
            ):
                some = warped[i][rows]
                blocks = lane_sum(
                    lambda s, v, w: lane_block(weights[s : s + 1], v) * lane_block(some, w),
                    lane, 2 * WARP + 1, True,
                )
                parts.append(jnp.concatenate(blocks, axis=1).astype(BF16))
            result = jnp.dot(
                jnp.concatenate(parts, axis=0), unsort[...], preferred_element_type=F32
            ).astype(BF16)
            for j in range(BLKC):
                piece = lane_block(result, j)
                to = place_of[0, visit * BLKC + j]
                rows = pl.ds(pl.multiple_of(to % CAP * BODY, TAIL), BODY)
                out[to // CAP, rows] = piece[TAIL:]
                to = place_of[1, visit * BLKC + j]
                rows = pl.ds(pl.multiple_of(CAP * BODY + to % CAP * TAIL, TAIL), TAIL)
                out[to // CAP, rows] = piece[:TAIL]
        return 0

    lax.fori_loop(0, V // WARPED, some_visits, 0)


def warp(patch, slot, owner, weight, ready, order, images, above, devices):
    vmem = pl.BlockSpec(memory_space=pltpu.VMEM)
    sort, unsort = order
    *matrices, rows_high, rows_low, col_weights = ready
    owner = owner.reshape(1, -1)
    args = [patch, slot, owner, weight, *matrices, sort, images]
    places, label, matched = pl.pallas_call(
        match_kernel,
        in_specs=[vmem] * len(args),
        out_specs=[vmem, vmem, vmem],
        out_shape=[
            jax.ShapeDtypeStruct((1, V * BLKC), jnp.int32),
            jax.ShapeDtypeStruct((devices, LANES), F32),
            jax.ShapeDtypeStruct((V, 2, (STRIPS - FREE_FIRST) * STRIP, WIDTH), BF16),
        ],
        scratch_shapes=[
            pltpu.VMEM((MATCHED, 4, OPEN, WIDTH), BF16),
        ],
        compiler_params=pltpu.CompilerParams(vmem_limit_bytes=32 << 20),
        cost_estimate=pl.CostEstimate(
            flops=V * 2 * (STRIPS - FREE_FIRST) * TAPS * STRIP * BAND * WIDTH,
            bytes_accessed=V * (BLOCK * WIDTH * 6),
            transcendentals=0,
        ),
        name="match",
    )(*args)
    args = [
        owner, places, label, *matrices, rows_high, rows_low, col_weights,
        sort, unsort, images, above, matched,
    ]
    return pl.pallas_call(
        warp_kernel,
        in_specs=[vmem] * len(args),
        out_specs=vmem,
        scratch_shapes=[
            pltpu.VMEM((WARPED, 4, STRIP + STEP, WIDTH), BF16),
            pltpu.VMEM((WARPED, 4, STRIP + STEP, WIDTH), BF16),
            pltpu.VMEM((WARPED, 2, STRIP, WIDTH), BF16),
            pltpu.VMEM((WARPED, 2, PAST_STRIPS * STRIP, WIDTH), BF16),
            pltpu.VMEM((8, LANES), jnp.int32),
            pltpu.SMEM((8, LANES), jnp.int32),
            pltpu.SemaphoreType.DMA(()),
        ],
        out_shape=jax.ShapeDtypeStruct((devices, CAP * BLOCK + LABEL, BLOCK), BF16),
        compiler_params=pltpu.CompilerParams(vmem_limit_bytes=32 << 20),
        cost_estimate=pl.CostEstimate(
            flops=V * 2 * STRIPS * TAPS * STRIP * BAND * WIDTH,
            bytes_accessed=V * (BLOCK * WIDTH * 6),
            transcendentals=0,
        ),
        name="warp",
    )(*args)


def coadd_kernel(got, out, total, out_sem):
    devices = got.shape[0]
    wide = devices * CAP * STRIP
    labels = got[:, CAP * BLOCK : CAP * BLOCK + LABEL][:, 0]
    lane = iota((1, wide), 1)
    rank = lane // STRIP % CAP
    source = lane // (STRIP * CAP)

    def spread(entry):
        onehot = (iota((LANES, wide), 0) == rank * 2 + entry).astype(F32).astype(BF16)
        every = jnp.dot(labels, onehot, preferred_element_type=F32)
        return jnp.sum(
            jnp.where(iota((devices, wide), 0) == source, every, 0.0), axis=0, keepdims=True
        )

    weights, cells = spread(0), spread(1)
    row = iota((CELLS * STRIP, 1), 0)
    mine = (cells == (row // STRIP).astype(F32)) & (lane % STRIP == row % STRIP)
    matrix = jnp.where(mine, weights, 0.0)
    sums = jnp.sum(matrix, axis=1, keepdims=True)
    inverse = 1.0 / jnp.maximum(sums, 1.0)
    matrix = matrix.astype(BF16)
    taken = {}
    for r in range(CAP):
        column = jnp.broadcast_to(labels[:, 2 * r : 2 * r + 1].astype(F32), (devices, LANES))
        for s in range(devices):
            taken[s, r] = jnp.broadcast_to(column[s : s + 1], (STRIP, LANES)).astype(BF16) > 0

    def tile(s, r, k):
        device, first = s, r * BODY + k * STRIP
        if first - r * BODY >= BODY:
            device, first = (s + 1) % devices, CAP * BODY + r * TAIL
        return jnp.where(taken[s, r], got[device, first : first + STRIP], jnp.zeros((), BF16))

    copies = []
    for pair in range(BLOCK // STRIP // 2):
        columns = jnp.concatenate(
            [
                jnp.concatenate(
                    [tile(s, r, k) for s in range(devices) for r in range(CAP)], axis=0
                )
                for k in (2 * pair, 2 * pair + 1)
            ],
            axis=1,
        )
        result = jnp.dot(matrix, columns, preferred_element_type=F32) * inverse
        for c in range(CELLS):
            part = result[c * STRIP : (c + 1) * STRIP]
            lanes = slice(c % PSIDE * BLOCK, (c % PSIDE + 1) * BLOCK)
            for n in range(2):
                first = (2 * pair + n) * STRIP
                total[c // PSIDE, first : first + STRIP, lanes] = lane_block(part, n)
        size = 2 * STRIP
        for line in range(PSIDE):
            copies.append(
                pltpu.make_async_copy(
                    total.at[line, pl.ds(pair * size, size)],
                    out.at[0, pl.ds(line * BLOCK + pair * size, size)],
                    out_sem.at[pair, line],
                )
            )
            copies[-1].start()
    for copy in copies:
        copy.wait()


def coadd(got):
    return pl.pallas_call(
        coadd_kernel,
        in_specs=[pl.BlockSpec(memory_space=pltpu.VMEM)],
        out_specs=pl.BlockSpec(memory_space=pl.ANY),
        out_shape=jax.ShapeDtypeStruct((1, PSIDE * BLOCK, PSIDE * BLOCK), F32),
        scratch_shapes=[
            pltpu.VMEM((PSIDE, BLOCK, WIDTH), F32),
            pltpu.SemaphoreType.DMA((BLOCK // STRIP // 2, PSIDE)),
        ],
        compiler_params=pltpu.CompilerParams(vmem_limit_bytes=32 << 20),
        name="coadd",
    )(got)


def shards(
    images, basis_taps, psf_coef, affine, visit_weight, block_patch, block_slot, patch_owner
):
    devices = lax.axis_size("ccd")
    patch = block_patch[:, :, 0]
    head = collect(images, patch)
    above = lax.ppermute(head, "ccd", [(i, (i + 1) % devices) for i in range(devices)])
    order = orders()
    ready = prepare(
        basis_taps.transpose(1, 0, 2), psf_coef.transpose(1, 3, 0, 2), affine.transpose(0, 2, 3, 1),
        devices,
    )
    sent = warp(
        patch, block_slot, patch_owner, visit_weight, ready, order, images, above, devices
    )
    got = lax.all_to_all(sent, "ccd", split_axis=0, concat_axis=0, tiled=True)
    return coadd(got)


def solution(mesh):
    placed = (
        P(None, ("group", "ccd"), None),
        P(),
        P(None, "group", None, None),
        P(None, "group", None, None),
        P(None, "group"),
        P(("group", "ccd"), None, None),
        P(("group", "ccd"), None),
        P("group"),
    )
    return jax.shard_map(
        shards,
        mesh=mesh,
        in_specs=placed,
        out_specs=P(("group", "ccd"), None, None),
        check_vma=False,
    )
```

```python
import functools
import itertools

import jax
import jax.numpy as jnp
from jax import lax
from jax.experimental import pallas as pl
from jax.experimental.pallas import tpu as pltpu
from jax.sharding import PartitionSpec as P

V = 4
BLOCK = 128
BLKC = 4
SPLIT = 4
TAPS = 11
NBASIS = 9
PSIDE = 4
CELLS = PSIDE * PSIDE
CAP = 2

HALF = TAPS // 2
WARP = 3
RIM = HALF + WARP
TAIL = 16
HEIGHT = SPLIT * BLOCK
WIDTH = BLKC * BLOCK
LANES = 128
LANE_BLOCKS = WIDTH // LANES
STRIP = 16
STEP = 32
STRIPS = -(-(BLOCK + 2 * WARP) // STRIP)
MIDDLE = STRIPS // 2
GROUPS = 6
BAND = 256
PAST_STRIPS = 2
OWN_FIRST = 1
FREE_FIRST = 2
HALVES = 2
MATCHED = 4
WARPED = 4
ROWS = BLOCK // HALVES
WINDOW = ROWS + STRIP
BODY = BLOCK - TAIL
GOT = TAIL + RIM
OPEN = (STRIPS - 1) * STRIP + STEP - FREE_FIRST * STRIP
LABEL = 16
F32 = jnp.float32
BF16 = jnp.bfloat16


def sin_pi(t):
    whole = jnp.round(t)
    f = t - whole
    odd = whole - 2.0 * jnp.floor(0.5 * whole)
    f2 = f * f
    out = 0.0
    for c in (
        0.00046630280576761, -0.0073704309457144, 0.0821458866111282,
        -0.599264529320792, 2.55016403987734, -5.16771278004997, 3.14159265358979,
    ):
        out = out * f2 + c
    return f * out * (1.0 - 2.0 * odd)


def lanczos(t):
    zero = t == 0.0
    safe = jnp.where(zero, 1.0, t)
    pt = jnp.pi * safe
    value = 3.0 * sin_pi(safe) * sin_pi(safe / 3.0) / (pt * pt)
    return jnp.where(jnp.abs(t) < 3.0, jnp.where(zero, 1.0, value), 0.0)


def iota(shape, dim):
    return lax.broadcasted_iota(jnp.int32, shape, dim)


def column_at(lane):
    return lane % LANES * LANE_BLOCKS + lane // LANES


def order_kernel(sort, unsort):
    square = (WIDTH, WIDTH)
    one, none = jnp.ones((), F32), jnp.zeros((), F32)
    goes = iota(square, 0) == column_at(iota((1, WIDTH), 1))
    sort[...] = jnp.where(goes, one, none).astype(BF16)
    comes = iota(square, 1) == column_at(iota((WIDTH, 1), 0))
    unsort[...] = jnp.where(comes, one, none).astype(BF16)


def orders():
    return small_kernel(order_kernel, "orders", [], [((WIDTH, WIDTH), BF16)] * 2)


def lane_block(x, v):
    return x[:, v * LANES : (v + 1) * LANES]


def dot_exact(a, b, dims):
    return lax.dot_general(
        a, b, (dims, ((), ())), precision=lax.Precision.HIGHEST, preferred_element_type=F32
    )


def staircase(x, first):
    return jnp.concatenate(
        [
            pltpu.roll(x[g : g + 8], first + g, 1, stride=1, stride_axis=0)
            for g in range(0, x.shape[0], 8)
        ],
        axis=0,
    )


def lane_sum(terms_of, lane, count, weigh):
    blocks = []
    for v in range(LANE_BLOCKS):
        total = None
        half = count // 2
        for q in range(-(-half // LANE_BLOCKS) * -1, (half + LANE_BLOCKS - 1) // LANE_BLOCKS + 1):
            part = None
            for u in range(count):
                if (v + u - half) // LANE_BLOCKS != q:
                    continue
                piece = terms_of(u, v, (v + u - half) % LANE_BLOCKS)
                part = piece if part is None else part + piece
            if part is None:
                continue
            if q:
                part = pltpu.roll(part, -q % LANES, 1)
                if not weigh:
                    part = jnp.where((lane + q >= 0) & (lane + q < LANES), part, 0.0)
            total = part if total is None else total + part
        blocks.append(total)
    return blocks


def whereabouts(devices):
    band = lax.axis_index("ccd")
    past = lax.rem(band + devices - 1, devices)
    quarter = (band + SPLIT // 2) % SPLIT
    own = ((band + SPLIT // 2) // SPLIT, quarter * BLOCK - TAIL)
    before = ((past + SPLIT // 2) // SPLIT, (past + SPLIT // 2) % SPLIT * BLOCK + BODY)
    return (own, before), (quarter > 0) & (band > 0)


def collect_kernel(images, patch, head, numbers, sems):
    copies = [
        pltpu.make_async_copy(
            images.at[v, pl.ds(BLOCK - GOT, GOT)], head.at[pl.ds(v * GOT, GOT)], sems.at[v]
        )
        for v in range(V)
    ]
    names = pltpu.make_async_copy(patch, numbers, sems.at[V])
    names.start()
    for copy in copies:
        copy.start()
    head[V * GOT :] = jnp.zeros((8, WIDTH), F32)
    names.wait()
    head[V * GOT : V * GOT + 1, : V * BLKC] = numbers[...].astype(F32)
    for copy in copies:
        copy.wait()


def collect(images, patch):
    return pl.pallas_call(
        collect_kernel,
        in_specs=[pl.BlockSpec(memory_space=pl.ANY)] * 2,
        out_specs=pl.BlockSpec(memory_space=pltpu.VMEM),
        out_shape=jax.ShapeDtypeStruct((V * GOT + 8, WIDTH), F32),
        scratch_shapes=[pltpu.VMEM(patch.shape, jnp.int32), pltpu.SemaphoreType.DMA((V + 1,))],
        name="collect",
    )(images, patch)


def lanczos_weights(devices, affine, cols_out):
    bands, same = whereabouts(devices)
    lane = iota((1, LANES), 1)
    lanes = iota((8, WIDTH), 1)
    step = iota((8, WIDTH), 0) - WARP
    block = lanes // LANES
    carry = (block + step + LANE_BLOCKS) // LANE_BLOCKS - 1
    from_lane = lanes % LANES - carry
    col = (from_lane * LANE_BLOCKS + block).astype(F32)
    within = (from_lane >= 0) & (from_lane < LANES) & (step <= WARP)
    offset = iota((8, LANES), 0) - WARP
    crosses = (lane + offset >= TAIL) != (lane >= TAIL)
    keep = (offset <= WARP) & (same | jnp.logical_not(crosses))
    by_row = []
    for visit in range(V):
        shifts = []
        for n, (ccd, top_row) in enumerate(bands):
            a = jnp.sum(
                jnp.where(iota((1, 1, affine.shape[3]), 2) == ccd, affine[visit], 0.0),
                axis=2, keepdims=True,
            )
            row = (top_row + lane).astype(F32)
            shifts.append(a[0, 0:1] + a[0, 1:2] * (row - (HEIGHT - 1) / 2.0) / HEIGHT)
            col_shift = a[1, 0:1] + a[1, 1:2] * (col - (WIDTH - 1) / 2.0) / WIDTH
            cols_out[n * V + visit] = jnp.where(within, lanczos(col_shift - step.astype(F32)), 0.0)
        shift = jnp.where(lane < TAIL, shifts[1], shifts[0])
        weights = jnp.where(keep, lanczos(shift - offset.astype(F32)), 0.0)
        by_row.append(jnp.concatenate([weights, jnp.zeros((LANES - 8, LANES), F32)], axis=0).T)
    return by_row


def prepare_kernel(
    devices, taps, psf, affine, high_level, step_level, slope, rows_high, rows_low, cols_out
):
    row_weights = lanczos_weights(devices, affine, cols_out)
    bands, _ = whereabouts(devices)
    band_lane = iota((1, BAND), 1)
    seg = band_lane // STEP
    lane = iota((1, LANES), 1)
    tap = band_lane - seg * STEP
    onehot = (tap == iota((TAPS, BAND), 0)) & (seg < GROUPS)
    row_taps = dot_exact(taps[:, 0], onehot.astype(F32), ((1,), (0,)))
    eye = (iota((TAPS, STRIP), 0) == iota((TAPS, STRIP), 1)).astype(F32)
    turned_taps = dot_exact(eye, taps[:, 1], ((0,), (1,)))
    units = []
    for n, visit in itertools.product(range(2), range(V)):
        ccd, top_row = bands[n]
        lhs = jnp.concatenate(
            [turned_taps * psf[ccd, c, visit : visit + 1, :] for c in range(3)], axis=0
        )
        kernels = dot_exact(lhs, row_taps, ((1,), (0,)))
        const, by_row, by_col = (kernels[c * STRIP : (c + 1) * STRIP] for c in range(3))
        is_level = seg < 3
        per_strip = 2.0 * STRIP / HEIGHT
        middle_row = (top_row + (MIDDLE * STRIP - WARP)).astype(F32)
        middle_pos = (2.0 * middle_row + 1.0) / HEIGHT - 1.0
        col_move = (iota((STRIP, 1), 0) - HALF).astype(F32) * (2.0 / WIDTH)
        by_row = jnp.where(is_level, by_row, 0.0)
        const = jnp.where(is_level, const + middle_pos * by_row - col_move * by_col, by_col)
        reach = per_strip * (STRIPS - MIDDLE)
        largest = jnp.max(jnp.abs(const) + reach * jnp.abs(by_row), axis=(0, 1), keepdims=True)
        unit = jnp.maximum(largest, 1e-30) * (1.0 / 200.0)
        units.append(unit)
        const = const / unit
        by_row = (by_row * per_strip) / unit
        low_lanes = (lane // STEP) % 3 == 2
        low_band = seg % 3 == 2
        row_part = iota((STRIP, 1), 0).astype(F32) * (1.0 / STRIP)
        for u in range(TAPS):
            at = slice(u * STRIP, (u + 1) * STRIP)
            one = jnp.broadcast_to(const[u : u + 1], (STRIP, BAND))
            x, tail = staircase(one[:, :LANES], 0), staircase(one[:, LANES:], 0)
            y = staircase(jnp.broadcast_to(by_row[u : u + 1, :LANES], (STRIP, LANES)), 0)
            high = tail.astype(BF16).astype(F32)
            slope[n * V + visit, at] = jnp.where(low_band[:, LANES:], tail - high, high).astype(BF16)
            x = x + row_part * y
            high = jnp.where(lane < 3 * STEP, jnp.round(x), x.astype(BF16).astype(F32))
            high_level[n * V + visit, at] = jnp.where(low_lanes, x - high, high)
            high = jnp.round(y)
            step_level[n * V + visit, at] = jnp.where(low_lanes, y - high, high)

    for visit in range(V):
        weights = row_weights[visit]
        matrix = jnp.concatenate(
            [
                staircase(weights[:TAIL] * units[V + visit], 0),
                staircase(weights[TAIL:ROWS] * units[visit], PAST_STRIPS * STRIP),
                staircase(weights[ROWS:] * units[visit], 0),
            ],
            axis=0,
        )
        high = matrix.astype(BF16)
        rows_high[visit] = high
        rows_low[visit] = (matrix - high.astype(F32)).astype(BF16)


def small_kernel(body, name, args, shapes):
    vmem = pl.BlockSpec(memory_space=pltpu.VMEM)
    return pl.pallas_call(
        body,
        in_specs=[vmem] * len(args),
        out_specs=[vmem] * len(shapes),
        out_shape=[jax.ShapeDtypeStruct(shape, kind) for shape, kind in shapes],
        compiler_params=pltpu.CompilerParams(vmem_limit_bytes=32 << 20),
        cost_estimate=pl.CostEstimate(flops=1 << 30, bytes_accessed=1 << 20, transcendentals=0),
        name=name,
    )(*args)


def prepare(taps, psf, affine, devices):
    return small_kernel(
        functools.partial(prepare_kernel, devices), "matrices", [taps, psf, affine],
        [
            ((2 * V, TAPS * STRIP, LANES), F32),
            ((2 * V, TAPS * STRIP, LANES), F32),
            ((2 * V, TAPS * STRIP, BAND - LANES), BF16),
            ((V, BLOCK, LANES), BF16),
            ((V, BLOCK, LANES), BF16),
            ((2 * V, 8, WIDTH), F32),
        ],
    )


def sorted_rows(raw, sort):
    col_pos = (2.0 * column_at(iota((1, WIDTH), 1)).astype(F32) + 1.0) / WIDTH - 1.0
    count = raw.shape[0]
    raw_high = raw.astype(BF16)
    raw_low = (raw - raw_high.astype(F32)).astype(BF16)
    both = jnp.dot(
        jnp.concatenate([raw_high, raw_low], axis=0), sort, preferred_element_type=F32
    )
    high, low = both[:count], both[count:]
    tilted = (high + low) * col_pos
    tilted_high = tilted.astype(BF16).astype(F32)
    return high, low, tilted_high, tilted - tilted_high


def match_strip(level, step, slope, source, first, k):
    lane = iota((1, LANES), 1)
    if k != MIDDLE:
        level = level + float(k - MIDDLE) * step
    matrix = jnp.concatenate([level.astype(BF16), slope], axis=1)
    filler = jnp.zeros((BAND - GROUPS * STEP, WIDTH), BF16)
    rows = slice(first, first + STEP)
    columns = jnp.concatenate([source[h, rows] for h in (0, 1, 0, 2, 3, 2)] + [filler], axis=0)
    results = jnp.dot(matrix, columns, preferred_element_type=F32)
    blocks = lane_sum(
        lambda u, v, w: lane_block(results[u * STRIP : (u + 1) * STRIP], w), lane, TAPS, False
    )
    matched = jnp.concatenate(blocks, axis=1)
    high = matched.astype(BF16)
    return high, (matched - high.astype(F32)).astype(BF16)


def upright(line):
    count = line.shape[1]
    square = (count, count)
    return jnp.sum(
        jnp.where(iota(square, 0) == iota(square, 1), jnp.broadcast_to(line, square), 0),
        axis=1, keepdims=True,
    )


def route(patch, owner):
    square = (patch.shape[1], patch.shape[1])
    earlier = (iota(square, 0) < iota(square, 1)) & (upright(patch) == patch)
    rank = jnp.sum(earlier.astype(jnp.int32), axis=0, keepdims=True)
    named = iota((owner.shape[1], patch.shape[1]), 0) == patch
    to = jnp.sum(jnp.where(named, upright(owner), 0), axis=0, keepdims=True)
    return to, rank


def match_kernel(
    patch, slot, owner, weight, high_level, step_level, slope, sort, image,
    places, label, matched_terms, terms,
):
    ((ccd, _), _), _ = whereabouts(label.shape[0])
    to, rank = route(patch[...], owner[...])
    places[...] = to * CAP + rank

    own = jnp.where(iota(weight.shape, 1) == ccd, weight[...].astype(F32), 0.0)
    own = jnp.sum(own, axis=1, keepdims=True)
    each = (V, V * BLKC)
    weights = jnp.sum(
        jnp.where(iota(each, 1) // BLKC == iota(each, 0), own, 0.0), axis=0, keepdims=True
    )
    goes = iota((label.shape[0], V * BLKC), 0) == to
    lane = iota(label.shape, 1)
    lines = jnp.zeros(label.shape, F32)
    for r in range(CAP):
        for n, value in enumerate((weights, slot[...].astype(F32))):
            column = jnp.sum(jnp.where(goes & (rank == r), value, 0.0), axis=1, keepdims=True)
            lines = jnp.where(lane == 2 * r + n, column, lines)
    label[...] = lines

    open_row = FREE_FIRST * STRIP - GOT
    seen = OPEN - STRIP
    terms[:, :, seen:] = jnp.zeros((MATCHED, 4, STRIP, WIDTH), BF16)

    def some_visits(turn, _):
        visits = [turn * MATCHED + i for i in range(MATCHED)]
        for i, visit in enumerate(visits):
            rows = sorted_rows(image[visit, open_row : open_row + seen], sort[...])
            for h, value in enumerate(rows):
                terms[i, h, :seen] = value.astype(BF16)
        for k in range(FREE_FIRST, STRIPS):
            first = (k - FREE_FIRST) * STRIP
            for i, visit in enumerate(visits):
                at = slice(first, first + STRIP)
                matched_terms[visit, 0, at], matched_terms[visit, 1, at] = match_strip(
                    high_level[visit], step_level[visit], slope[visit], terms.at[i], first, k
                )
        return 0

    lax.fori_loop(0, V // MATCHED, some_visits, 0)


def warp_kernel(
    owner, places, label, high_level, step_level, slope, rows_high, rows_low, col_weights,
    sort, unsort, image, above, matched_free, out,
    own_terms, past_terms, own_matched, past_matched, both_places, place_of, place_sem,
):
    devices = label.shape[0]
    _, same = whereabouts(devices)
    past_patch = above[V * GOT : V * GOT + 1, : V * BLKC].astype(jnp.int32)
    to, rank = route(past_patch, owner[...])
    both_places[0:1, : V * BLKC] = places[...]
    both_places[1:2, : V * BLKC] = to * CAP + rank
    place_copy = pltpu.make_async_copy(both_places, place_of, place_sem)
    place_copy.start()
    lane = iota((1, LANES), 1)
    out[:, CAP * BLOCK :] = jnp.broadcast_to(
        label[...].reshape(devices, 1, LANES), (devices, LABEL, LANES)
    ).astype(BF16)

    seam = STRIP + STEP
    foreign = iota((seam, 1), 0) < GOT
    both = jnp.where(same, 1.0, 0.0)
    own_sees = jnp.where(foreign, both, 1.0)
    past_sees = jnp.where(foreign, 1.0, both)

    def some_visits(turn, _):
        visits = [turn * WARPED + i for i in range(WARPED)]
        for i, visit in enumerate(visits):
            tail = pl.ds(pl.multiple_of(visit * GOT, 8), GOT)
            raw = jnp.concatenate([above[tail], image[visit, : seam - GOT]], axis=0)
            for h, value in enumerate(sorted_rows(raw, sort[...])):
                own_terms[i, h] = (value * own_sees).astype(BF16)
                past_terms[i, h] = (value * past_sees).astype(BF16)
        for i, visit in enumerate(visits):
            own_matched[i, 0], own_matched[i, 1] = match_strip(
                high_level[visit], step_level[visit], slope[visit],
                own_terms.at[i], OWN_FIRST * STRIP, OWN_FIRST,
            )
        for k in range(PAST_STRIPS):
            for i, visit in enumerate(visits):
                at = slice(k * STRIP, (k + 1) * STRIP)
                past_matched[i, 0, at], past_matched[i, 1, at] = match_strip(
                    high_level[V + visit], step_level[V + visit], slope[V + visit],
                    past_terms.at[i], k * STRIP, k,
                )

        warped = []
        for i, visit in enumerate(visits):
            halves = []
            for h in range(HALVES):
                at = slice(h * ROWS, (h + 1) * ROWS)
                high, low = rows_high[visit, at], rows_low[visit, at]
                free = FREE_FIRST * STRIP

                def under(term):
                    if h == 0:
                        parts = [
                            past_matched[i, term],
                            own_matched[i, term],
                            matched_free[visit, term, : WINDOW - free],
                        ]
                    else:
                        parts = [matched_free[visit, term, ROWS - free :]]
                    left = LANES - sum([x.shape[0] for x in parts])
                    return jnp.concatenate(parts + [jnp.zeros((left, WIDTH), BF16)], axis=0)

                first = under(0)
                total = jnp.dot(
                    jnp.concatenate([high, high], axis=1),
                    jnp.concatenate([first, under(1)], axis=0),
                    preferred_element_type=F32,
                )
                halves.append(total + jnp.dot(low, first, preferred_element_type=F32))
            warped.append(jnp.concatenate(halves, axis=0))

        @pl.when(turn == 0)
        def _():
            place_copy.wait()

        for i, visit in enumerate(visits):
            parts = []
            for rows, weights in (
                (slice(0, TAIL), col_weights[V + visit]),
                (slice(TAIL, BLOCK), col_weights[visit]),
            ):
                some = warped[i][rows]
                blocks = lane_sum(
                    lambda s, v, w: lane_block(weights[s : s + 1], v) * lane_block(some, w),
                    lane, 2 * WARP + 1, True,
                )
                parts.append(jnp.concatenate(blocks, axis=1).astype(BF16))
            result = jnp.dot(
                jnp.concatenate(parts, axis=0), unsort[...], preferred_element_type=F32
            ).astype(BF16)
            for j in range(BLKC):
                piece = lane_block(result, j)
                to = place_of[0, visit * BLKC + j]
                rows = pl.ds(pl.multiple_of(to % CAP * BODY, TAIL), BODY)
                out[to // CAP, rows] = piece[TAIL:]
                to = place_of[1, visit * BLKC + j]
                rows = pl.ds(pl.multiple_of(CAP * BODY + to % CAP * TAIL, TAIL), TAIL)
                out[to // CAP, rows] = piece[:TAIL]
        return 0

    lax.fori_loop(0, V // WARPED, some_visits, 0)


def warp(patch, slot, owner, weight, ready, order, images, above, devices):
    vmem = pl.BlockSpec(memory_space=pltpu.VMEM)
    sort, unsort = order
    *matrices, rows_high, rows_low, col_weights = ready
    owner = owner.reshape(1, -1)
    args = [patch, slot, owner, weight, *matrices, sort, images]
    places, label, matched = pl.pallas_call(
        match_kernel,
        in_specs=[vmem] * len(args),
        out_specs=[vmem, vmem, vmem],
        out_shape=[
            jax.ShapeDtypeStruct((1, V * BLKC), jnp.int32),
            jax.ShapeDtypeStruct((devices, LANES), F32),
            jax.ShapeDtypeStruct((V, 2, (STRIPS - FREE_FIRST) * STRIP, WIDTH), BF16),
        ],
        scratch_shapes=[
            pltpu.VMEM((MATCHED, 4, OPEN, WIDTH), BF16),
        ],
        compiler_params=pltpu.CompilerParams(vmem_limit_bytes=32 << 20),
        cost_estimate=pl.CostEstimate(
            flops=V * 2 * (STRIPS - FREE_FIRST) * TAPS * STRIP * BAND * WIDTH,
            bytes_accessed=V * (BLOCK * WIDTH * 6),
            transcendentals=0,
        ),
        name="match",
    )(*args)
    args = [
        owner, places, label, *matrices, rows_high, rows_low, col_weights,
        sort, unsort, images, above, matched,
    ]
    return pl.pallas_call(
        warp_kernel,
        in_specs=[vmem] * len(args),
        out_specs=vmem,
        scratch_shapes=[
            pltpu.VMEM((WARPED, 4, STRIP + STEP, WIDTH), BF16),
            pltpu.VMEM((WARPED, 4, STRIP + STEP, WIDTH), BF16),
            pltpu.VMEM((WARPED, 2, STRIP, WIDTH), BF16),
            pltpu.VMEM((WARPED, 2, PAST_STRIPS * STRIP, WIDTH), BF16),
            pltpu.VMEM((8, LANES), jnp.int32),
            pltpu.SMEM((8, LANES), jnp.int32),
            pltpu.SemaphoreType.DMA(()),
        ],
        out_shape=jax.ShapeDtypeStruct((devices, CAP * BLOCK + LABEL, BLOCK), BF16),
        compiler_params=pltpu.CompilerParams(vmem_limit_bytes=32 << 20),
        cost_estimate=pl.CostEstimate(
            flops=V * 2 * STRIPS * TAPS * STRIP * BAND * WIDTH,
            bytes_accessed=V * (BLOCK * WIDTH * 6),
            transcendentals=0,
        ),
        name="warp",
    )(*args)


def coadd_kernel(got, out, total, out_sem):
    devices = got.shape[0]
    wide = devices * CAP * STRIP
    labels = got[:, CAP * BLOCK : CAP * BLOCK + LABEL][:, 0]
    lane = iota((1, wide), 1)
    rank = lane // STRIP % CAP
    source = lane // (STRIP * CAP)

    def spread(entry):
        onehot = (iota((LANES, wide), 0) == rank * 2 + entry).astype(F32).astype(BF16)
        every = jnp.dot(labels, onehot, preferred_element_type=F32)
        return jnp.sum(
            jnp.where(iota((devices, wide), 0) == source, every, 0.0), axis=0, keepdims=True
        )

    weights, cells = spread(0), spread(1)
    row = iota((CELLS * STRIP, 1), 0)
    mine = (cells == (row // STRIP).astype(F32)) & (lane % STRIP == row % STRIP)
    matrix = jnp.where(mine, weights, 0.0)
    sums = jnp.sum(matrix, axis=1, keepdims=True)
    inverse = 1.0 / jnp.maximum(sums, 1.0)
    matrix = matrix.astype(BF16)
    taken = {}
    for r in range(CAP):
        column = jnp.broadcast_to(labels[:, 2 * r : 2 * r + 1].astype(F32), (devices, LANES))
        for s in range(devices):
            taken[s, r] = jnp.broadcast_to(column[s : s + 1], (STRIP, LANES)).astype(BF16) > 0

    def tile(s, r, k):
        device, first = s, r * BODY + k * STRIP
        if first - r * BODY >= BODY:
            device, first = (s + 1) % devices, CAP * BODY + r * TAIL
        return jnp.where(taken[s, r], got[device, first : first + STRIP], jnp.zeros((), BF16))

    copies = []
    for pair in range(BLOCK // STRIP // 2):
        columns = jnp.concatenate(
            [
                jnp.concatenate(
                    [tile(s, r, k) for s in range(devices) for r in range(CAP)], axis=0
                )
                for k in (2 * pair, 2 * pair + 1)
            ],
            axis=1,
        )
        result = jnp.dot(matrix, columns, preferred_element_type=F32) * inverse
        for c in range(CELLS):
            part = result[c * STRIP : (c + 1) * STRIP]
            lanes = slice(c % PSIDE * BLOCK, (c % PSIDE + 1) * BLOCK)
            for n in range(2):
                first = (2 * pair + n) * STRIP
                total[c // PSIDE, first : first + STRIP, lanes] = lane_block(part, n)
        size = 2 * STRIP
        for line in range(PSIDE):
            copies.append(
                pltpu.make_async_copy(
                    total.at[line, pl.ds(pair * size, size)],
                    out.at[0, pl.ds(line * BLOCK + pair * size, size)],
                    out_sem.at[pair, line],
                )
            )
            copies[-1].start()
    for copy in copies:
        copy.wait()


def coadd(got):
    return pl.pallas_call(
        coadd_kernel,
        in_specs=[pl.BlockSpec(memory_space=pltpu.VMEM)],
        out_specs=pl.BlockSpec(memory_space=pl.ANY),
        out_shape=jax.ShapeDtypeStruct((1, PSIDE * BLOCK, PSIDE * BLOCK), F32),
        scratch_shapes=[
            pltpu.VMEM((PSIDE, BLOCK, WIDTH), F32),
            pltpu.SemaphoreType.DMA((BLOCK // STRIP // 2, PSIDE)),
        ],
        compiler_params=pltpu.CompilerParams(vmem_limit_bytes=32 << 20),
        name="coadd",
    )(got)


def shards(
    images, basis_taps, psf_coef, affine, visit_weight, block_patch, block_slot, patch_owner
):
    devices = lax.axis_size("ccd")
    patch = block_patch[:, :, 0]
    head = collect(images, patch)
    above = lax.ppermute(head, "ccd", [(i, (i + 1) % devices) for i in range(devices)])
    order = orders()
    ready = prepare(
        basis_taps.transpose(1, 0, 2), psf_coef.transpose(1, 3, 0, 2), affine.transpose(0, 2, 3, 1),
        devices,
    )
    sent = warp(
        patch, block_slot, patch_owner, visit_weight, ready, order, images, above, devices
    )
    got = lax.all_to_all(sent, "ccd", split_axis=0, concat_axis=0, tiled=True)
    return coadd(got)


def solution(mesh):
    placed = (
        P(None, ("group", "ccd"), None),
        P(),
        P(None, "group", None, None),
        P(None, "group", None, None),
        P(None, "group"),
        P(("group", "ccd"), None, None),
        P(("group", "ccd"), None),
        P("group"),
    )
    return jax.shard_map(
        shards,
        mesh=mesh,
        in_specs=placed,
        out_specs=P(("group", "ccd"), None, None),
        check_vma=False,
    )
```

```python
import functools

import jax
import jax.numpy as jnp
from jax import lax
from jax.experimental import pallas as pl
from jax.experimental.pallas import tpu as pltpu
from jax.sharding import PartitionSpec as P

V = 4
BLOCK = 128
BLKC = 4
SPLIT = 4
TAPS = 11
NBASIS = 9
PSIDE = 4
CELLS = PSIDE * PSIDE
CAP = 2

HALF = TAPS // 2
WARP = 3
RIM = HALF + WARP
TAIL = 16
HEIGHT = SPLIT * BLOCK
WIDTH = BLKC * BLOCK
LANES = 128
LANE_BLOCKS = WIDTH // LANES
STRIP = 16
STEP = 32
STRIPS = -(-(BLOCK + 2 * WARP) // STRIP)
MIDDLE = STRIPS // 2
GROUPS = 6
BAND = 256
PAST_STRIPS = 2
OWN_FIRST = 1
FREE_FIRST = 2
HALVES = 2
MATCHED = 4
WARPED = 4
ROWS = BLOCK // HALVES
WINDOW = ROWS + STRIP
BODY = BLOCK - TAIL
GOT = TAIL + RIM
OPEN = (STRIPS - 1) * STRIP + STEP - FREE_FIRST * STRIP
LABEL = 8
F32 = jnp.float32
BF16 = jnp.bfloat16


def sin_pi(t):
    whole = jnp.round(t)
    f = t - whole
    odd = whole - 2.0 * jnp.floor(0.5 * whole)
    f2 = f * f
    out = 0.0
    for c in (
        0.00046630280576761, -0.0073704309457144, 0.0821458866111282,
        -0.599264529320792, 2.55016403987734, -5.16771278004997, 3.14159265358979,
    ):
        out = out * f2 + c
    return f * out * (1.0 - 2.0 * odd)


def lanczos(t):
    zero = t == 0.0
    safe = jnp.where(zero, 1.0, t)
    pt = jnp.pi * safe
    value = 3.0 * sin_pi(safe) * sin_pi(safe / 3.0) / (pt * pt)
    return jnp.where(jnp.abs(t) < 3.0, jnp.where(zero, 1.0, value), 0.0)


def iota(shape, dim):
    return lax.broadcasted_iota(jnp.int32, shape, dim)


def column_at(lane):
    return lane % LANES * LANE_BLOCKS + lane // LANES


def order_kernel(sort, unsort):
    square = (WIDTH, WIDTH)
    one, none = jnp.ones((), F32), jnp.zeros((), F32)
    goes = iota(square, 0) == column_at(iota((1, WIDTH), 1))
    sort[...] = jnp.where(goes, one, none).astype(BF16)
    comes = iota(square, 1) == column_at(iota((WIDTH, 1), 0))
    unsort[...] = jnp.where(comes, one, none).astype(BF16)


def orders():
    return small_kernel(order_kernel, "orders", [], [((WIDTH, WIDTH), BF16)] * 2)


def lane_block(x, v):
    return x[:, v * LANES : (v + 1) * LANES]


def dot_exact(a, b, dims):
    return lax.dot_general(
        a, b, (dims, ((), ())), precision=lax.Precision.HIGHEST, preferred_element_type=F32
    )


def staircase(x, first):
    return jnp.concatenate(
        [
            pltpu.roll(x[g : g + 8], first + g, 1, stride=1, stride_axis=0)
            for g in range(0, x.shape[0], 8)
        ],
        axis=0,
    )


def lane_sum(terms_of, lane, count, weigh):
    blocks = []
    for v in range(LANE_BLOCKS):
        total = None
        half = count // 2
        for q in range(-(-half // LANE_BLOCKS) * -1, (half + LANE_BLOCKS - 1) // LANE_BLOCKS + 1):
            part = None
            for u in range(count):
                if (v + u - half) // LANE_BLOCKS != q:
                    continue
                piece = terms_of(u, v, (v + u - half) % LANE_BLOCKS)
                part = piece if part is None else part + piece
            if part is None:
                continue
            if q:
                part = pltpu.roll(part, -q % LANES, 1)
                if not weigh:
                    part = jnp.where((lane + q >= 0) & (lane + q < LANES), part, 0.0)
            total = part if total is None else total + part
        blocks.append(total)
    return blocks


def whereabouts(devices):
    band = lax.axis_index("ccd")
    past = lax.rem(band + devices - 1, devices)
    quarter = (band + SPLIT // 2) % SPLIT
    own = ((band + SPLIT // 2) // SPLIT, quarter * BLOCK - TAIL)
    before = ((past + SPLIT // 2) // SPLIT, (past + SPLIT // 2) % SPLIT * BLOCK + BODY)
    return (own, before), (quarter > 0) & (band > 0)


def collect_kernel(images, patch, head, numbers, sems):
    copies = [
        pltpu.make_async_copy(
            images.at[v, pl.ds(BLOCK - GOT, GOT)], head.at[pl.ds(v * GOT, GOT)], sems.at[v]
        )
        for v in range(V)
    ]
    names = pltpu.make_async_copy(patch, numbers, sems.at[V])
    names.start()
    for copy in copies:
        copy.start()
    head[V * GOT :] = jnp.zeros((8, WIDTH), F32)
    names.wait()
    head[V * GOT : V * GOT + 1, : V * BLKC] = numbers[...].astype(F32)
    for copy in copies:
        copy.wait()


def collect(images, patch):
    return pl.pallas_call(
        collect_kernel,
        in_specs=[pl.BlockSpec(memory_space=pl.ANY)] * 2,
        out_specs=pl.BlockSpec(memory_space=pltpu.VMEM),
        out_shape=jax.ShapeDtypeStruct((V * GOT + 8, WIDTH), F32),
        scratch_shapes=[pltpu.VMEM(patch.shape, jnp.int32), pltpu.SemaphoreType.DMA((V + 1,))],
        name="collect",
    )(images, patch)


def lanczos_weights(devices, affine, cols_out):
    bands, same = whereabouts(devices)
    lane = iota((1, LANES), 1)
    lanes = iota((8, WIDTH), 1)
    step = iota((8, WIDTH), 0) - WARP
    block = lanes // LANES
    carry = (block + step + LANE_BLOCKS) // LANE_BLOCKS - 1
    from_lane = lanes % LANES - carry
    col = (from_lane * LANE_BLOCKS + block).astype(F32)
    within = (from_lane >= 0) & (from_lane < LANES) & (step <= WARP)
    offset = iota((8, LANES), 0) - WARP
    crosses = (lane + offset >= TAIL) != (lane >= TAIL)
    keep = (offset <= WARP) & (same | jnp.logical_not(crosses))
    def terms_of(n, visit):
        here = iota((1, 1, affine.shape[3]), 2) == bands[n][0]
        return jnp.sum(jnp.where(here, affine[visit], 0.0), axis=2, keepdims=True)

    def columns(n, visit):
        a = terms_of(n, visit)
        col_shift = a[1, 0:1] + a[1, 1:2] * (col - (WIDTH - 1) / 2.0) / WIDTH
        cols_out[n * V + visit] = jnp.where(within, lanczos(col_shift - step.astype(F32)), 0.0)

    by_row = []
    for visit in range(V):
        columns(0, visit)
        shifts = []
        for n, (_, top_row) in enumerate(bands):
            a = terms_of(n, visit)
            row = (top_row + lane).astype(F32)
            shifts.append(a[0, 0:1] + a[0, 1:2] * (row - (HEIGHT - 1) / 2.0) / HEIGHT)
        shift = jnp.where(lane < TAIL, shifts[1], shifts[0])
        weights = jnp.where(keep, lanczos(shift - offset.astype(F32)), 0.0)
        by_row.append(jnp.concatenate([weights, jnp.zeros((LANES - 8, LANES), F32)], axis=0).T)

    @pl.when(jnp.logical_not(same))
    def _():
        for visit in range(V):
            columns(1, visit)

    return by_row


def prepare_kernel(
    devices, taps, psf, affine, high_level, step_level, slope, rows_high, rows_low, cols_out
):
    row_weights = lanczos_weights(devices, affine, cols_out)
    bands, same = whereabouts(devices)
    band_lane = iota((1, BAND), 1)
    seg = band_lane // STEP
    lane = iota((1, LANES), 1)
    tap = band_lane - seg * STEP
    onehot = (tap == iota((TAPS, BAND), 0)) & (seg < GROUPS)
    row_taps = dot_exact(taps[:, 0], onehot.astype(F32), ((1,), (0,)))
    eye = (iota((TAPS, STRIP), 0) == iota((TAPS, STRIP), 1)).astype(F32)
    turned_taps = dot_exact(eye, taps[:, 1], ((0,), (1,)))
    def make(n, visit):
        ccd, top_row = bands[n]
        lhs = jnp.concatenate(
            [turned_taps * psf[ccd, c, visit : visit + 1, :] for c in range(3)], axis=0
        )
        kernels = dot_exact(lhs, row_taps, ((1,), (0,)))
        const, by_row, by_col = (kernels[c * STRIP : (c + 1) * STRIP] for c in range(3))
        is_level = seg < 3
        per_strip = 2.0 * STRIP / HEIGHT
        middle_row = (top_row + (MIDDLE * STRIP - WARP)).astype(F32)
        middle_pos = (2.0 * middle_row + 1.0) / HEIGHT - 1.0
        col_move = (iota((STRIP, 1), 0) - HALF).astype(F32) * (2.0 / WIDTH)
        by_row = jnp.where(is_level, by_row, 0.0)
        const = jnp.where(is_level, const + middle_pos * by_row - col_move * by_col, by_col)
        reach = per_strip * (STRIPS - MIDDLE)
        largest = jnp.max(jnp.abs(const) + reach * jnp.abs(by_row), axis=(0, 1), keepdims=True)
        unit = jnp.maximum(largest, 1e-30) * (1.0 / 200.0)
        const = const / unit
        by_row = (by_row * per_strip) / unit
        low_lanes = (lane // STEP) % 3 == 2
        low_band = seg % 3 == 2
        row_part = iota((STRIP, 1), 0).astype(F32) * (1.0 / STRIP)
        for u in range(TAPS):
            at = slice(u * STRIP, (u + 1) * STRIP)
            one = jnp.broadcast_to(const[u : u + 1], (STRIP, BAND))
            x, tail = staircase(one[:, :LANES], 0), staircase(one[:, LANES:], 0)
            y = staircase(jnp.broadcast_to(by_row[u : u + 1, :LANES], (STRIP, LANES)), 0)
            high = tail.astype(BF16).astype(F32)
            slope[n * V + visit, at] = jnp.where(low_band[:, LANES:], tail - high, high).astype(BF16)
            x = x + row_part * y
            high = jnp.where(lane < 3 * STEP, jnp.round(x), x.astype(BF16).astype(F32))
            high_level[n * V + visit, at] = jnp.where(low_lanes, x - high, high)
            high = jnp.round(y)
            step_level[n * V + visit, at] = jnp.where(low_lanes, y - high, high)
        return unit

    def put(visit, at, matrix):
        high = matrix.astype(BF16)
        rows_high[visit, at] = high
        rows_low[visit, at] = (matrix - high.astype(F32)).astype(BF16)

    for visit in range(V):
        weights = row_weights[visit] * make(0, visit)
        put(visit, slice(0, TAIL), staircase(weights[:TAIL], 0))
        put(visit, slice(TAIL, ROWS), staircase(weights[TAIL:ROWS], PAST_STRIPS * STRIP))
        put(visit, slice(ROWS, BLOCK), staircase(weights[ROWS:], 0))

    @pl.when(jnp.logical_not(same))
    def _():
        for visit in range(V):
            weights = row_weights[visit][:TAIL] * make(1, visit)
            put(visit, slice(0, TAIL), staircase(weights, 0))


def small_kernel(body, name, args, shapes):
    vmem = pl.BlockSpec(memory_space=pltpu.VMEM)
    return pl.pallas_call(
        body,
        in_specs=[vmem] * len(args),
        out_specs=[vmem] * len(shapes),
        out_shape=[jax.ShapeDtypeStruct(shape, kind) for shape, kind in shapes],
        compiler_params=pltpu.CompilerParams(vmem_limit_bytes=32 << 20),
        cost_estimate=pl.CostEstimate(flops=1 << 30, bytes_accessed=1 << 20, transcendentals=0),
        name=name,
    )(*args)


def prepare(taps, psf, affine, devices):
    return small_kernel(
        functools.partial(prepare_kernel, devices), "matrices", [taps, psf, affine],
        [
            ((2 * V, TAPS * STRIP, LANES), F32),
            ((2 * V, TAPS * STRIP, LANES), F32),
            ((2 * V, TAPS * STRIP, BAND - LANES), BF16),
            ((V, BLOCK, LANES), BF16),
            ((V, BLOCK, LANES), BF16),
            ((2 * V, 8, WIDTH), F32),
        ],
    )


def sorted_rows(raw, sort):
    col_pos = (2.0 * column_at(iota((1, WIDTH), 1)).astype(F32) + 1.0) / WIDTH - 1.0
    count = raw.shape[0]
    raw_high = raw.astype(BF16)
    raw_low = (raw - raw_high.astype(F32)).astype(BF16)
    both = jnp.dot(
        jnp.concatenate([raw_high, raw_low], axis=0), sort, preferred_element_type=F32
    )
    high, low = both[:count], both[count:]
    tilted = (high + low) * col_pos
    tilted_high = tilted.astype(BF16).astype(F32)
    return high, low, tilted_high, tilted - tilted_high


def match_strip(level, step, slope, source, first, k):
    lane = iota((1, LANES), 1)
    if k != MIDDLE:
        level = level + float(k - MIDDLE) * step
    matrix = jnp.concatenate([level.astype(BF16), slope], axis=1)
    filler = jnp.zeros((BAND - GROUPS * STEP, WIDTH), BF16)
    rows = slice(first, first + STEP)
    columns = jnp.concatenate([source[h, rows] for h in (0, 1, 0, 2, 3, 2)] + [filler], axis=0)
    results = jnp.dot(matrix, columns, preferred_element_type=F32)
    blocks = lane_sum(
        lambda u, v, w: lane_block(results[u * STRIP : (u + 1) * STRIP], w), lane, TAPS, False
    )
    matched = jnp.concatenate(blocks, axis=1)
    high = matched.astype(BF16)
    return high, (matched - high.astype(F32)).astype(BF16)


def upright(line):
    count = line.shape[1]
    square = (count, count)
    return jnp.sum(
        jnp.where(iota(square, 0) == iota(square, 1), jnp.broadcast_to(line, square), 0),
        axis=1, keepdims=True,
    )


def route(patch, owner):
    square = (patch.shape[1], patch.shape[1])
    earlier = (iota(square, 0) < iota(square, 1)) & (upright(patch) == patch)
    rank = jnp.sum(earlier.astype(jnp.int32), axis=0, keepdims=True)
    named = iota((owner.shape[1], patch.shape[1]), 0) == patch
    to = jnp.sum(jnp.where(named, upright(owner), 0), axis=0, keepdims=True)
    return to, rank


def warp_rows(high, low, first, second, weights, unsort):
    lane = iota((1, LANES), 1)

    def filled(x):
        return jnp.concatenate([x, jnp.zeros((LANES - x.shape[0], WIDTH), BF16)], axis=0)

    first = filled(first)
    total = jnp.dot(
        jnp.concatenate([high, high], axis=1),
        jnp.concatenate([first, filled(second)], axis=0),
        preferred_element_type=F32,
    )
    total = total + jnp.dot(low, first, preferred_element_type=F32)
    parts = []
    for rows, cols in weights:
        some = total[rows]
        blocks = lane_sum(
            lambda s, v, w: lane_block(cols[s : s + 1], v) * lane_block(some, w),
            lane, 2 * WARP + 1, True,
        )
        parts.append(jnp.concatenate(blocks, axis=1).astype(BF16))
    return jnp.dot(
        jnp.concatenate(parts, axis=0), unsort, preferred_element_type=F32
    ).astype(BF16)


def match_kernel(
    patch, slot, owner, weight, high_level, step_level, slope, rows_high, rows_low, col_weights,
    sort, unsort, image,
    places, label, matched_out, second_half, terms, matched_terms,
):
    ((ccd, _), _), _ = whereabouts(label.shape[0])
    to, rank = route(patch[...], owner[...])
    places[...] = to * CAP + rank

    own = jnp.where(iota(weight.shape, 1) == ccd, weight[...].astype(F32), 0.0)
    own = jnp.sum(own, axis=1, keepdims=True)
    each = (V, V * BLKC)
    weights = jnp.sum(
        jnp.where(iota(each, 1) // BLKC == iota(each, 0), own, 0.0), axis=0, keepdims=True
    )
    goes = iota((label.shape[0], V * BLKC), 0) == to
    lane = iota(label.shape, 1)
    lines = jnp.zeros(label.shape, F32)
    for r in range(CAP):
        for n, value in enumerate((weights, slot[...].astype(F32))):
            column = jnp.sum(jnp.where(goes & (rank == r), value, 0.0), axis=1, keepdims=True)
            lines = jnp.where(lane == 2 * r + n, column, lines)
    label[...] = lines

    open_row = FREE_FIRST * STRIP - GOT
    seen = OPEN - STRIP
    terms[:, :, seen:] = jnp.zeros((MATCHED, 4, STRIP, WIDTH), BF16)

    def some_visits(turn, _):
        visits = [turn * MATCHED + i for i in range(MATCHED)]
        for i, visit in enumerate(visits):
            rows = sorted_rows(image[visit, open_row : open_row + seen], sort[...])
            for h, value in enumerate(rows):
                terms[i, h, :seen] = value.astype(BF16)
        for k in range(FREE_FIRST, STRIPS):
            first = (k - FREE_FIRST) * STRIP
            for i, visit in enumerate(visits):
                at = slice(first, first + STRIP)
                matched_terms[i, 0, at], matched_terms[i, 1, at] = match_strip(
                    high_level[visit], step_level[visit], slope[visit], terms.at[i], first, k
                )
        half = slice(ROWS, BLOCK)
        for i, visit in enumerate(visits):
            matched_out[visit] = matched_terms[i, :, : WINDOW - FREE_FIRST * STRIP]
            under = [matched_terms[i, term, ROWS - FREE_FIRST * STRIP :] for term in range(2)]
            second_half[visit] = warp_rows(
                rows_high[visit, half], rows_low[visit, half], *under,
                [(slice(0, ROWS), col_weights[visit])], unsort[...],
            )
        return 0

    lax.fori_loop(0, V // MATCHED, some_visits, 0)


def warp_kernel(
    owner, places, label, high_level, step_level, slope, rows_high, rows_low, col_weights,
    sort, unsort, image, above, matched_free, second_half, out,
    own_terms, past_terms, own_matched, past_matched, both_places, place_of, place_sem,
):
    devices = label.shape[0]
    _, same = whereabouts(devices)
    past_patch = above[V * GOT : V * GOT + 1, : V * BLKC].astype(jnp.int32)
    to, rank = route(past_patch, owner[...])
    both_places[0:1, : V * BLKC] = places[...]
    both_places[1:2, : V * BLKC] = to * CAP + rank
    place_copy = pltpu.make_async_copy(both_places, place_of, place_sem)
    place_copy.start()
    lane = iota((1, LANES), 1)
    out[:, CAP * BLOCK :] = jnp.broadcast_to(
        label[...].reshape(devices, 1, LANES), (devices, LABEL, LANES)
    ).astype(BF16)

    seam = STRIP + STEP
    foreign = iota((seam, 1), 0) < GOT
    both = jnp.where(same, 1.0, 0.0)
    past = jnp.where(same, 0, V)
    own_sees = jnp.where(foreign, both, 1.0)
    past_sees = jnp.where(foreign, 1.0, both)

    def some_visits(turn, _):
        visits = [turn * WARPED + i for i in range(WARPED)]
        for i, visit in enumerate(visits):
            tail = pl.ds(pl.multiple_of(visit * GOT, 8), GOT)
            raw = jnp.concatenate([above[tail], image[visit, : seam - GOT]], axis=0)
            for h, value in enumerate(sorted_rows(raw, sort[...])):
                own_terms[i, h] = (value * own_sees).astype(BF16)
                past_terms[i, h] = (value * past_sees).astype(BF16)
        for i, visit in enumerate(visits):
            own_matched[i, 0], own_matched[i, 1] = match_strip(
                high_level[visit], step_level[visit], slope[visit],
                own_terms.at[i], OWN_FIRST * STRIP, OWN_FIRST,
            )
        for k in range(PAST_STRIPS):
            for i, visit in enumerate(visits):
                at = slice(k * STRIP, (k + 1) * STRIP)
                past_matched[i, 0, at], past_matched[i, 1, at] = match_strip(
                    high_level[past + visit], step_level[past + visit], slope[past + visit],
                    past_terms.at[i], k * STRIP, k,
                )

        @pl.when(turn == 0)
        def _():
            place_copy.wait()

        half = slice(0, ROWS)
        for i, visit in enumerate(visits):
            under = [
                jnp.concatenate(
                    [past_matched[i, term], own_matched[i, term], matched_free[visit, term]], axis=0
                )
                for term in range(2)
            ]
            result = warp_rows(
                rows_high[visit, half], rows_low[visit, half], *under,
                [
                    (slice(0, TAIL), col_weights[past + visit]),
                    (slice(TAIL, ROWS), col_weights[visit]),
                ],
                unsort[...],
            )
            rest = second_half[visit]
            for j in range(BLKC):
                piece = lane_block(result, j)
                to = place_of[0, visit * BLKC + j]
                row = to % CAP * BODY
                rows = pl.ds(pl.multiple_of(row, TAIL), ROWS - TAIL)
                out[to // CAP, rows] = piece[TAIL:]
                rows = pl.ds(pl.multiple_of(row + ROWS - TAIL, TAIL), BLOCK - ROWS)
                out[to // CAP, rows] = lane_block(rest, j)
                to = place_of[1, visit * BLKC + j]
                rows = pl.ds(pl.multiple_of(CAP * BODY + to % CAP * TAIL, TAIL), TAIL)
                out[to // CAP, rows] = piece[:TAIL]
        return 0

    lax.fori_loop(0, V // WARPED, some_visits, 0)


def warp(patch, slot, owner, weight, ready, order, images, above, devices):
    vmem = pl.BlockSpec(memory_space=pltpu.VMEM)
    sort, unsort = order
    *matrices, rows_high, rows_low, col_weights = ready
    owner = owner.reshape(1, -1)
    ready = [*matrices, rows_high, rows_low, col_weights, sort, unsort, images]
    args = [patch, slot, owner, weight, *ready]
    places, label, matched, second_half = pl.pallas_call(
        match_kernel,
        in_specs=[vmem] * len(args),
        out_specs=[vmem] * 4,
        out_shape=[
            jax.ShapeDtypeStruct((1, V * BLKC), jnp.int32),
            jax.ShapeDtypeStruct((devices, LANES), F32),
            jax.ShapeDtypeStruct((V, 2, WINDOW - FREE_FIRST * STRIP, WIDTH), BF16),
            jax.ShapeDtypeStruct((V, BLOCK - ROWS, WIDTH), BF16),
        ],
        scratch_shapes=[
            pltpu.VMEM((MATCHED, 4, OPEN, WIDTH), BF16),
            pltpu.VMEM((MATCHED, 2, (STRIPS - FREE_FIRST) * STRIP, WIDTH), BF16),
        ],
        compiler_params=pltpu.CompilerParams(vmem_limit_bytes=32 << 20),
        cost_estimate=pl.CostEstimate(
            flops=V * 2 * (STRIPS - FREE_FIRST) * TAPS * STRIP * BAND * WIDTH,
            bytes_accessed=V * (BLOCK * WIDTH * 6),
            transcendentals=0,
        ),
        name="match",
    )(*args)
    args = [owner, places, label, *ready, above, matched, second_half]
    return pl.pallas_call(
        warp_kernel,
        in_specs=[vmem] * len(args),
        out_specs=vmem,
        scratch_shapes=[
            pltpu.VMEM((WARPED, 4, STRIP + STEP, WIDTH), BF16),
            pltpu.VMEM((WARPED, 4, STRIP + STEP, WIDTH), BF16),
            pltpu.VMEM((WARPED, 2, STRIP, WIDTH), BF16),
            pltpu.VMEM((WARPED, 2, PAST_STRIPS * STRIP, WIDTH), BF16),
            pltpu.VMEM((8, LANES), jnp.int32),
            pltpu.SMEM((8, LANES), jnp.int32),
            pltpu.SemaphoreType.DMA(()),
        ],
        out_shape=jax.ShapeDtypeStruct((devices, CAP * BLOCK + LABEL, BLOCK), BF16),
        compiler_params=pltpu.CompilerParams(vmem_limit_bytes=32 << 20),
        cost_estimate=pl.CostEstimate(
            flops=V * 2 * STRIPS * TAPS * STRIP * BAND * WIDTH,
            bytes_accessed=V * (BLOCK * WIDTH * 6),
            transcendentals=0,
        ),
        name="warp",
    )(*args)


def coadd_kernel(got, out, total, out_sem):
    devices = got.shape[0]
    wide = devices * CAP * STRIP
    labels = got[:, CAP * BLOCK : CAP * BLOCK + LABEL][:, 0]
    lane = iota((1, wide), 1)
    rank = lane // STRIP % CAP
    source = lane // (STRIP * CAP)

    def spread(entry):
        onehot = (iota((LANES, wide), 0) == rank * 2 + entry).astype(F32).astype(BF16)
        every = jnp.dot(labels, onehot, preferred_element_type=F32)
        return jnp.sum(
            jnp.where(iota((devices, wide), 0) == source, every, 0.0), axis=0, keepdims=True
        )

    weights, cells = spread(0), spread(1)
    row = iota((CELLS * STRIP, 1), 0)
    mine = (cells == (row // STRIP).astype(F32)) & (lane % STRIP == row % STRIP)
    matrix = jnp.where(mine, weights, 0.0)
    sums = jnp.sum(matrix, axis=1, keepdims=True)
    inverse = 1.0 / jnp.maximum(sums, 1.0)
    matrix = matrix.astype(BF16)
    taken = {}
    for r in range(CAP):
        column = jnp.broadcast_to(labels[:, 2 * r : 2 * r + 1].astype(F32), (devices, LANES))
        for s in range(devices):
            taken[s, r] = jnp.broadcast_to(column[s : s + 1], (STRIP, LANES)).astype(BF16) > 0

    def tile(s, r, k):
        device, first = s, r * BODY + k * STRIP
        if first - r * BODY >= BODY:
            device, first = (s + 1) % devices, CAP * BODY + r * TAIL
        return jnp.where(taken[s, r], got[device, first : first + STRIP], jnp.zeros((), BF16))

    copies = []
    for pair in range(BLOCK // STRIP // 2):
        columns = jnp.concatenate(
            [
                jnp.concatenate(
                    [tile(s, r, k) for s in range(devices) for r in range(CAP)], axis=0
                )
                for k in (2 * pair, 2 * pair + 1)
            ],
            axis=1,
        )
        result = jnp.dot(matrix, columns, preferred_element_type=F32) * inverse
        for c in range(CELLS):
            part = result[c * STRIP : (c + 1) * STRIP]
            lanes = slice(c % PSIDE * BLOCK, (c % PSIDE + 1) * BLOCK)
            for n in range(2):
                first = (2 * pair + n) * STRIP
                total[c // PSIDE, first : first + STRIP, lanes] = lane_block(part, n)
        size = 2 * STRIP
        for line in range(PSIDE):
            copies.append(
                pltpu.make_async_copy(
                    total.at[line, pl.ds(pair * size, size)],
                    out.at[0, pl.ds(line * BLOCK + pair * size, size)],
                    out_sem.at[pair, line],
                )
            )
            copies[-1].start()
    for copy in copies:
        copy.wait()


def coadd(got):
    return pl.pallas_call(
        coadd_kernel,
        in_specs=[pl.BlockSpec(memory_space=pltpu.VMEM)],
        out_specs=pl.BlockSpec(memory_space=pl.ANY),
        out_shape=jax.ShapeDtypeStruct((1, PSIDE * BLOCK, PSIDE * BLOCK), F32),
        scratch_shapes=[
            pltpu.VMEM((PSIDE, BLOCK, WIDTH), F32),
            pltpu.SemaphoreType.DMA((BLOCK // STRIP // 2, PSIDE)),
        ],
        compiler_params=pltpu.CompilerParams(vmem_limit_bytes=32 << 20),
        name="coadd",
    )(got)


def shards(
    images, basis_taps, psf_coef, affine, visit_weight, block_patch, block_slot, patch_owner
):
    devices = lax.axis_size("ccd")
    patch = block_patch[:, :, 0]
    head = collect(images, patch)
    above = lax.ppermute(head, "ccd", [(i, (i + 1) % devices) for i in range(devices)])
    order = orders()
    ready = prepare(
        basis_taps.transpose(1, 0, 2), psf_coef.transpose(1, 3, 0, 2), affine.transpose(0, 2, 3, 1),
        devices,
    )
    sent = warp(
        patch, block_slot, patch_owner, visit_weight, ready, order, images, above, devices
    )
    got = lax.all_to_all(sent, "ccd", split_axis=0, concat_axis=0, tiled=True)
    return coadd(got)


def solution(mesh):
    placed = (
        P(None, ("group", "ccd"), None),
        P(),
        P(None, "group", None, None),
        P(None, "group", None, None),
        P(None, "group"),
        P(("group", "ccd"), None, None),
        P(("group", "ccd"), None),
        P("group"),
    )
    return jax.shard_map(
        shards,
        mesh=mesh,
        in_specs=placed,
        out_specs=P(("group", "ccd"), None, None),
        check_vma=False,
    )
```

```python
import functools

import jax
import jax.numpy as jnp
from jax import lax
from jax.experimental import pallas as pl
from jax.experimental.pallas import tpu as pltpu
from jax.sharding import PartitionSpec as P

V = 4
BLOCK = 128
BLKC = 4
SPLIT = 4
TAPS = 11
NBASIS = 9
PSIDE = 4
CELLS = PSIDE * PSIDE
CAP = 2

HALF = TAPS // 2
WARP = 3
RIM = HALF + WARP
TAIL = 16
HEIGHT = SPLIT * BLOCK
WIDTH = BLKC * BLOCK
LANES = 128
LANE_BLOCKS = WIDTH // LANES
STRIP = 16
STEP = 32
STRIPS = -(-(BLOCK + 2 * WARP) // STRIP)
MIDDLE = STRIPS // 2
GROUPS = 6
BAND = 256
PAST_STRIPS = 2
OWN_FIRST = 1
FREE_FIRST = 2
HALVES = 2
MATCHED = 4
WARPED = 4
ROWS = BLOCK // HALVES
WINDOW = ROWS + STRIP
BODY = BLOCK - TAIL
GOT = TAIL + RIM
OPEN = (STRIPS - 1) * STRIP + STEP - FREE_FIRST * STRIP
LABEL = 8
F32 = jnp.float32
BF16 = jnp.bfloat16


def sin_pi(t):
    whole = jnp.round(t)
    f = t - whole
    odd = whole - 2.0 * jnp.floor(0.5 * whole)
    f2 = f * f
    out = 0.0
    for c in (
        0.00046630280576761, -0.0073704309457144, 0.0821458866111282,
        -0.599264529320792, 2.55016403987734, -5.16771278004997, 3.14159265358979,
    ):
        out = out * f2 + c
    return f * out * (1.0 - 2.0 * odd)


def lanczos(t):
    zero = t == 0.0
    safe = jnp.where(zero, 1.0, t)
    pt = jnp.pi * safe
    value = 3.0 * sin_pi(safe) * sin_pi(safe / 3.0) / (pt * pt)
    return jnp.where(jnp.abs(t) < 3.0, jnp.where(zero, 1.0, value), 0.0)


def iota(shape, dim):
    return lax.broadcasted_iota(jnp.int32, shape, dim)


def column_at(lane):
    return lane % LANES * LANE_BLOCKS + lane // LANES


def order_kernel(sort, unsort):
    square = (WIDTH, WIDTH)
    one, none = jnp.ones((), F32), jnp.zeros((), F32)
    goes = iota(square, 0) == column_at(iota((1, WIDTH), 1))
    sort[...] = jnp.where(goes, one, none).astype(BF16)
    comes = iota(square, 1) == column_at(iota((WIDTH, 1), 0))
    unsort[...] = jnp.where(comes, one, none).astype(BF16)


def orders():
    return small_kernel(order_kernel, "orders", [], [((WIDTH, WIDTH), BF16)] * 2)


def lane_block(x, v):
    return x[:, v * LANES : (v + 1) * LANES]


def dot_exact(a, b, dims):
    return lax.dot_general(
        a, b, (dims, ((), ())), precision=lax.Precision.HIGHEST, preferred_element_type=F32
    )


def staircase(x, first):
    return jnp.concatenate(
        [
            pltpu.roll(x[g : g + 8], first + g, 1, stride=1, stride_axis=0)
            for g in range(0, x.shape[0], 8)
        ],
        axis=0,
    )


def lane_sum(terms_of, lane, count, weigh):
    blocks = []
    for v in range(LANE_BLOCKS):
        total = None
        half = count // 2
        for q in range(-(-half // LANE_BLOCKS) * -1, (half + LANE_BLOCKS - 1) // LANE_BLOCKS + 1):
            part = None
            for u in range(count):
                if (v + u - half) // LANE_BLOCKS != q:
                    continue
                piece = terms_of(u, v, (v + u - half) % LANE_BLOCKS)
                part = piece if part is None else part + piece
            if part is None:
                continue
            if q:
                part = pltpu.roll(part, -q % LANES, 1)
                if not weigh:
                    part = jnp.where((lane + q >= 0) & (lane + q < LANES), part, 0.0)
            total = part if total is None else total + part
        blocks.append(total)
    return blocks


def whereabouts(devices):
    band = lax.axis_index("ccd")
    past = lax.rem(band + devices - 1, devices)
    quarter = (band + SPLIT // 2) % SPLIT
    own = ((band + SPLIT // 2) // SPLIT, quarter * BLOCK - TAIL)
    before = ((past + SPLIT // 2) // SPLIT, (past + SPLIT // 2) % SPLIT * BLOCK + BODY)
    return (own, before), (quarter > 0) & (band > 0)


def collect_kernel(images, patch, head, numbers, sems):
    copies = [
        pltpu.make_async_copy(
            images.at[v, pl.ds(BLOCK - GOT, GOT)], head.at[pl.ds(v * GOT, GOT)], sems.at[v]
        )
        for v in range(V)
    ]
    names = pltpu.make_async_copy(patch, numbers, sems.at[V])
    names.start()
    for copy in copies:
        copy.start()
    head[V * GOT :] = jnp.zeros((8, WIDTH), F32)
    names.wait()
    head[V * GOT : V * GOT + 1, : V * BLKC] = numbers[...].astype(F32)
    for copy in copies:
        copy.wait()


def collect(images, patch):
    return pl.pallas_call(
        collect_kernel,
        in_specs=[pl.BlockSpec(memory_space=pl.ANY)] * 2,
        out_specs=pl.BlockSpec(memory_space=pltpu.VMEM),
        out_shape=jax.ShapeDtypeStruct((V * GOT + 8, WIDTH), F32),
        scratch_shapes=[pltpu.VMEM(patch.shape, jnp.int32), pltpu.SemaphoreType.DMA((V + 1,))],
        name="collect",
    )(images, patch)


def lanczos_weights(devices, affine, cols_out):
    bands, same = whereabouts(devices)
    lane = iota((1, LANES), 1)
    lanes = iota((8, WIDTH), 1)
    step = iota((8, WIDTH), 0) - WARP
    block = lanes // LANES
    carry = (block + step + LANE_BLOCKS) // LANE_BLOCKS - 1
    from_lane = lanes % LANES - carry
    col = (from_lane * LANE_BLOCKS + block).astype(F32)
    within = (from_lane >= 0) & (from_lane < LANES) & (step <= WARP)
    offset = iota((8, LANES), 0) - WARP
    crosses = (lane + offset >= TAIL) != (lane >= TAIL)
    keep = (offset <= WARP) & (same | jnp.logical_not(crosses))
    def terms_of(n, visit):
        here = iota((1, 1, affine.shape[3]), 2) == bands[n][0]
        return jnp.sum(jnp.where(here, affine[visit], 0.0), axis=2, keepdims=True)

    def columns(n, visit):
        a = terms_of(n, visit)
        col_shift = a[1, 0:1] + a[1, 1:2] * (col - (WIDTH - 1) / 2.0) / WIDTH
        cols_out[n * V + visit] = jnp.where(within, lanczos(col_shift - step.astype(F32)), 0.0)

    by_row = []
    for visit in range(V):
        columns(0, visit)
        shifts = []
        for n, (_, top_row) in enumerate(bands):
            a = terms_of(n, visit)
            row = (top_row + lane).astype(F32)
            shifts.append(a[0, 0:1] + a[0, 1:2] * (row - (HEIGHT - 1) / 2.0) / HEIGHT)
        shift = jnp.where(lane < TAIL, shifts[1], shifts[0])
        weights = jnp.where(keep, lanczos(shift - offset.astype(F32)), 0.0)
        by_row.append(jnp.concatenate([weights, jnp.zeros((LANES - 8, LANES), F32)], axis=0).T)

    @pl.when(jnp.logical_not(same))
    def _():
        for visit in range(V):
            columns(1, visit)

    return by_row


def prepare_kernel(
    devices, taps, psf, affine, high_level, step_level, slope, rows_high, rows_low, cols_out
):
    row_weights = lanczos_weights(devices, affine, cols_out)
    bands, same = whereabouts(devices)
    band_lane = iota((1, BAND), 1)
    seg = band_lane // STEP
    lane = iota((1, LANES), 1)
    tap = band_lane - seg * STEP
    onehot = (tap == iota((TAPS, BAND), 0)) & (seg < GROUPS)
    row_taps = dot_exact(taps[:, 0], onehot.astype(F32), ((1,), (0,)))
    eye = (iota((TAPS, STRIP), 0) == iota((TAPS, STRIP), 1)).astype(F32)
    turned_taps = dot_exact(eye, taps[:, 1], ((0,), (1,)))
    def make(n, visit):
        ccd, top_row = bands[n]
        lhs = jnp.concatenate(
            [turned_taps * psf[ccd, c, visit : visit + 1, :] for c in range(3)], axis=0
        )
        kernels = dot_exact(lhs, row_taps, ((1,), (0,)))
        const, by_row, by_col = (kernels[c * STRIP : (c + 1) * STRIP] for c in range(3))
        is_level = seg < 3
        per_strip = 2.0 * STRIP / HEIGHT
        middle_row = (top_row + (MIDDLE * STRIP - WARP)).astype(F32)
        middle_pos = (2.0 * middle_row + 1.0) / HEIGHT - 1.0
        col_move = (iota((STRIP, 1), 0) - HALF).astype(F32) * (2.0 / WIDTH)
        by_row = jnp.where(is_level, by_row, 0.0)
        const = jnp.where(is_level, const + middle_pos * by_row - col_move * by_col, by_col)
        reach = per_strip * (STRIPS - MIDDLE)
        largest = jnp.max(jnp.abs(const) + reach * jnp.abs(by_row), axis=(0, 1), keepdims=True)
        unit = jnp.maximum(largest, 1e-30) * (1.0 / 200.0)
        const = const / unit
        by_row = (by_row * per_strip) / unit
        low_lanes = (lane // STEP) % 3 == 2
        low_band = seg % 3 == 2
        row_part = iota((STRIP, 1), 0).astype(F32) * (1.0 / STRIP)
        for u in range(TAPS):
            at = slice(u * STRIP, (u + 1) * STRIP)
            one = jnp.broadcast_to(const[u : u + 1], (STRIP, BAND))
            x, tail = staircase(one[:, :LANES], 0), staircase(one[:, LANES:], 0)
            y = staircase(jnp.broadcast_to(by_row[u : u + 1, :LANES], (STRIP, LANES)), 0)
            high = tail.astype(BF16).astype(F32)
            slope[n * V + visit, at] = jnp.where(low_band[:, LANES:], tail - high, high).astype(BF16)
            x = x + row_part * y
            high = jnp.where(lane < 3 * STEP, jnp.round(x), x.astype(BF16).astype(F32))
            high_level[n * V + visit, at] = jnp.where(low_lanes, x - high, high)
            high = jnp.round(y)
            step_level[n * V + visit, at] = jnp.where(low_lanes, y - high, high)
        return unit

    def put(visit, at, matrix):
        high = matrix.astype(BF16)
        rows_high[visit, at] = high
        rows_low[visit, at] = (matrix - high.astype(F32)).astype(BF16)

    for visit in range(V):
        weights = row_weights[visit] * make(0, visit)
        put(visit, slice(0, TAIL), staircase(weights[:TAIL], 0))
        put(visit, slice(TAIL, ROWS), staircase(weights[TAIL:ROWS], PAST_STRIPS * STRIP))
        put(visit, slice(ROWS, BLOCK), staircase(weights[ROWS:], 0))

    @pl.when(jnp.logical_not(same))
    def _():
        for visit in range(V):
            weights = row_weights[visit][:TAIL] * make(1, visit)
            put(visit, slice(0, TAIL), staircase(weights, 0))


def small_kernel(body, name, args, shapes):
    vmem = pl.BlockSpec(memory_space=pltpu.VMEM)
    return pl.pallas_call(
        body,
        in_specs=[vmem] * len(args),
        out_specs=[vmem] * len(shapes),
        out_shape=[jax.ShapeDtypeStruct(shape, kind) for shape, kind in shapes],
        compiler_params=pltpu.CompilerParams(vmem_limit_bytes=32 << 20),
        cost_estimate=pl.CostEstimate(flops=1 << 30, bytes_accessed=1 << 20, transcendentals=0),
        name=name,
    )(*args)


def prepare(taps, psf, affine, devices):
    return small_kernel(
        functools.partial(prepare_kernel, devices), "matrices", [taps, psf, affine],
        [
            ((2 * V, TAPS * STRIP, LANES), F32),
            ((2 * V, TAPS * STRIP, LANES), F32),
            ((2 * V, TAPS * STRIP, BAND - LANES), BF16),
            ((V, BLOCK, LANES), BF16),
            ((V, BLOCK, LANES), BF16),
            ((2 * V, 8, WIDTH), F32),
        ],
    )


def sorted_rows(raw, sort):
    col_pos = (2.0 * column_at(iota((1, WIDTH), 1)).astype(F32) + 1.0) / WIDTH - 1.0
    count = raw.shape[0]
    raw_high = raw.astype(BF16)
    raw_low = (raw - raw_high.astype(F32)).astype(BF16)
    both = jnp.dot(
        jnp.concatenate([raw_high, raw_low], axis=0), sort, preferred_element_type=F32
    )
    high, low = both[:count], both[count:]
    tilted = (high + low) * col_pos
    tilted_high = tilted.astype(BF16).astype(F32)
    return high, low, tilted_high, tilted - tilted_high


def match_strip(level, step, slope, source, first, k):
    lane = iota((1, LANES), 1)
    if k != MIDDLE:
        level = level + float(k - MIDDLE) * step
    matrix = jnp.concatenate([level.astype(BF16), slope], axis=1)
    filler = jnp.zeros((BAND - GROUPS * STEP, WIDTH), BF16)
    rows = slice(first, first + STEP)
    columns = jnp.concatenate([source[h, rows] for h in (0, 1, 0, 2, 3, 2)] + [filler], axis=0)
    results = jnp.dot(matrix, columns, preferred_element_type=F32)
    blocks = lane_sum(
        lambda u, v, w: lane_block(results[u * STRIP : (u + 1) * STRIP], w), lane, TAPS, False
    )
    matched = jnp.concatenate(blocks, axis=1)
    high = matched.astype(BF16)
    return high, (matched - high.astype(F32)).astype(BF16)


def upright(line):
    count = line.shape[1]
    square = (count, count)
    return jnp.sum(
        jnp.where(iota(square, 0) == iota(square, 1), jnp.broadcast_to(line, square), 0),
        axis=1, keepdims=True,
    )


def route(patch, owner):
    square = (patch.shape[1], patch.shape[1])
    earlier = (iota(square, 0) < iota(square, 1)) & (upright(patch) == patch)
    rank = jnp.sum(earlier.astype(jnp.int32), axis=0, keepdims=True)
    named = iota((owner.shape[1], patch.shape[1]), 0) == patch
    to = jnp.sum(jnp.where(named, upright(owner), 0), axis=0, keepdims=True)
    return to, rank


def match_kernel(
    patch, slot, owner, weight, high_level, step_level, slope, sort, image,
    places, label, matched_terms, terms,
):
    ((ccd, _), _), _ = whereabouts(label.shape[0])
    to, rank = route(patch[...], owner[...])
    places[...] = to * CAP + rank

    own = jnp.where(iota(weight.shape, 1) == ccd, weight[...].astype(F32), 0.0)
    own = jnp.sum(own, axis=1, keepdims=True)
    each = (V, V * BLKC)
    weights = jnp.sum(
        jnp.where(iota(each, 1) // BLKC == iota(each, 0), own, 0.0), axis=0, keepdims=True
    )
    goes = iota((label.shape[0], V * BLKC), 0) == to
    lane = iota(label.shape, 1)
    lines = jnp.zeros(label.shape, F32)
    for r in range(CAP):
        for n, value in enumerate((weights, slot[...].astype(F32))):
            column = jnp.sum(jnp.where(goes & (rank == r), value, 0.0), axis=1, keepdims=True)
            lines = jnp.where(lane == 2 * r + n, column, lines)
    label[...] = lines

    open_row = FREE_FIRST * STRIP - GOT
    seen = OPEN - STRIP
    terms[:, :, seen:] = jnp.zeros((MATCHED, 4, STRIP, WIDTH), BF16)

    def some_visits(turn, _):
        visits = [turn * MATCHED + i for i in range(MATCHED)]
        for i, visit in enumerate(visits):
            rows = sorted_rows(image[visit, open_row : open_row + seen], sort[...])
            for h, value in enumerate(rows):
                terms[i, h, :seen] = value.astype(BF16)
        for k in range(FREE_FIRST, STRIPS):
            first = (k - FREE_FIRST) * STRIP
            for i, visit in enumerate(visits):
                at = slice(first, first + STRIP)
                matched_terms[visit, 0, at], matched_terms[visit, 1, at] = match_strip(
                    high_level[visit], step_level[visit], slope[visit], terms.at[i], first, k
                )
        return 0

    lax.fori_loop(0, V // MATCHED, some_visits, 0)


def warp_kernel(
    owner, places, label, high_level, step_level, slope, rows_high, rows_low, col_weights,
    sort, unsort, image, above, matched_free, out,
    own_terms, past_terms, own_matched, past_matched, both_places, place_of, place_sem,
):
    devices = label.shape[0]
    _, same = whereabouts(devices)
    past_patch = above[V * GOT : V * GOT + 1, : V * BLKC].astype(jnp.int32)
    to, rank = route(past_patch, owner[...])
    both_places[0:1, : V * BLKC] = places[...]
    both_places[1:2, : V * BLKC] = to * CAP + rank
    place_copy = pltpu.make_async_copy(both_places, place_of, place_sem)
    place_copy.start()
    lane = iota((1, LANES), 1)
    out[:, CAP * BLOCK :] = jnp.broadcast_to(
        label[...].reshape(devices, 1, LANES), (devices, LABEL, LANES)
    ).astype(BF16)

    seam = STRIP + STEP
    foreign = iota((seam, 1), 0) < GOT
    both = jnp.where(same, 1.0, 0.0)
    past = jnp.where(same, 0, V)
    own_sees = jnp.where(foreign, both, 1.0)
    past_sees = jnp.where(foreign, 1.0, both)

    def some_visits(turn, _):
        visits = [turn * WARPED + i for i in range(WARPED)]
        for i, visit in enumerate(visits):
            tail = pl.ds(pl.multiple_of(visit * GOT, 8), GOT)
            raw = jnp.concatenate([above[tail], image[visit, : seam - GOT]], axis=0)
            for h, value in enumerate(sorted_rows(raw, sort[...])):
                own_terms[i, h] = (value * own_sees).astype(BF16)
                past_terms[i, h] = (value * past_sees).astype(BF16)
        for i, visit in enumerate(visits):
            own_matched[i, 0], own_matched[i, 1] = match_strip(
                high_level[visit], step_level[visit], slope[visit],
                own_terms.at[i], OWN_FIRST * STRIP, OWN_FIRST,
            )
        for k in range(PAST_STRIPS):
            for i, visit in enumerate(visits):
                at = slice(k * STRIP, (k + 1) * STRIP)
                past_matched[i, 0, at], past_matched[i, 1, at] = match_strip(
                    high_level[past + visit], step_level[past + visit], slope[past + visit],
                    past_terms.at[i], k * STRIP, k,
                )

        warped = []
        for i, visit in enumerate(visits):
            halves = []
            for h in range(HALVES):
                at = slice(h * ROWS, (h + 1) * ROWS)
                high, low = rows_high[visit, at], rows_low[visit, at]
                free = FREE_FIRST * STRIP

                def under(term):
                    if h == 0:
                        parts = [
                            past_matched[i, term],
                            own_matched[i, term],
                            matched_free[visit, term, : WINDOW - free],
                        ]
                    else:
                        parts = [matched_free[visit, term, ROWS - free :]]
                    left = LANES - sum([x.shape[0] for x in parts])
                    return jnp.concatenate(parts + [jnp.zeros((left, WIDTH), BF16)], axis=0)

                first = under(0)
                total = jnp.dot(
                    jnp.concatenate([high, high], axis=1),
                    jnp.concatenate([first, under(1)], axis=0),
                    preferred_element_type=F32,
                )
                halves.append(total + jnp.dot(low, first, preferred_element_type=F32))
            warped.append(jnp.concatenate(halves, axis=0))

        @pl.when(turn == 0)
        def _():
            place_copy.wait()

        for i, visit in enumerate(visits):
            parts = []
            for rows, weights in (
                (slice(0, TAIL), col_weights[past + visit]),
                (slice(TAIL, BLOCK), col_weights[visit]),
            ):
                some = warped[i][rows]
                blocks = lane_sum(
                    lambda s, v, w: lane_block(weights[s : s + 1], v) * lane_block(some, w),
                    lane, 2 * WARP + 1, True,
                )
                parts.append(jnp.concatenate(blocks, axis=1).astype(BF16))
            result = jnp.dot(
                jnp.concatenate(parts, axis=0), unsort[...], preferred_element_type=F32
            ).astype(BF16)
            for j in range(BLKC):
                piece = lane_block(result, j)
                to = place_of[0, visit * BLKC + j]
                rows = pl.ds(pl.multiple_of(to % CAP * BODY, TAIL), BODY)
                out[to // CAP, rows] = piece[TAIL:]
                to = place_of[1, visit * BLKC + j]
                rows = pl.ds(pl.multiple_of(CAP * BODY + to % CAP * TAIL, TAIL), TAIL)
                out[to // CAP, rows] = piece[:TAIL]
        return 0

    lax.fori_loop(0, V // WARPED, some_visits, 0)


def warp(patch, slot, owner, weight, ready, order, images, above, devices):
    vmem = pl.BlockSpec(memory_space=pltpu.VMEM)
    sort, unsort = order
    *matrices, rows_high, rows_low, col_weights = ready
    owner = owner.reshape(1, -1)
    args = [patch, slot, owner, weight, *matrices, sort, images]
    places, label, matched = pl.pallas_call(
        match_kernel,
        in_specs=[vmem] * len(args),
        out_specs=[vmem, vmem, vmem],
        out_shape=[
            jax.ShapeDtypeStruct((1, V * BLKC), jnp.int32),
            jax.ShapeDtypeStruct((devices, LANES), F32),
            jax.ShapeDtypeStruct((V, 2, (STRIPS - FREE_FIRST) * STRIP, WIDTH), BF16),
        ],
        scratch_shapes=[
            pltpu.VMEM((MATCHED, 4, OPEN, WIDTH), BF16),
        ],
        compiler_params=pltpu.CompilerParams(vmem_limit_bytes=32 << 20),
        cost_estimate=pl.CostEstimate(
            flops=V * 2 * (STRIPS - FREE_FIRST) * TAPS * STRIP * BAND * WIDTH,
            bytes_accessed=V * (BLOCK * WIDTH * 6),
            transcendentals=0,
        ),
        name="match",
    )(*args)
    args = [
        owner, places, label, *matrices, rows_high, rows_low, col_weights,
        sort, unsort, images, above, matched,
    ]
    return pl.pallas_call(
        warp_kernel,
        in_specs=[vmem] * len(args),
        out_specs=vmem,
        scratch_shapes=[
            pltpu.VMEM((WARPED, 4, STRIP + STEP, WIDTH), BF16),
            pltpu.VMEM((WARPED, 4, STRIP + STEP, WIDTH), BF16),
            pltpu.VMEM((WARPED, 2, STRIP, WIDTH), BF16),
            pltpu.VMEM((WARPED, 2, PAST_STRIPS * STRIP, WIDTH), BF16),
            pltpu.VMEM((8, LANES), jnp.int32),
            pltpu.SMEM((8, LANES), jnp.int32),
            pltpu.SemaphoreType.DMA(()),
        ],
        out_shape=jax.ShapeDtypeStruct((devices, CAP * BLOCK + LABEL, BLOCK), BF16),
        compiler_params=pltpu.CompilerParams(vmem_limit_bytes=32 << 20),
        cost_estimate=pl.CostEstimate(
            flops=V * 2 * STRIPS * TAPS * STRIP * BAND * WIDTH,
            bytes_accessed=V * (BLOCK * WIDTH * 6),
            transcendentals=0,
        ),
        name="warp",
    )(*args)


def coadd_kernel(got, out, total, out_sem):
    devices = got.shape[0]
    wide = devices * CAP * STRIP
    labels = got[:, CAP * BLOCK : CAP * BLOCK + LABEL][:, 0]
    lane = iota((1, wide), 1)
    rank = lane // STRIP % CAP
    source = lane // (STRIP * CAP)

    def spread(entry):
        onehot = (iota((LANES, wide), 0) == rank * 2 + entry).astype(F32).astype(BF16)
        every = jnp.dot(labels, onehot, preferred_element_type=F32)
        return jnp.sum(
            jnp.where(iota((devices, wide), 0) == source, every, 0.0), axis=0, keepdims=True
        )

    weights, cells = spread(0), spread(1)
    row = iota((CELLS * STRIP, 1), 0)
    mine = (cells == (row // STRIP).astype(F32)) & (lane % STRIP == row % STRIP)
    matrix = jnp.where(mine, weights, 0.0)
    sums = jnp.sum(matrix, axis=1, keepdims=True)
    inverse = 1.0 / jnp.maximum(sums, 1.0)
    matrix = matrix.astype(BF16)
    taken = {}
    for r in range(CAP):
        column = jnp.broadcast_to(labels[:, 2 * r : 2 * r + 1].astype(F32), (devices, LANES))
        for s in range(devices):
            taken[s, r] = jnp.broadcast_to(column[s : s + 1], (STRIP, LANES)).astype(BF16) > 0

    def tile(s, r, k):
        device, first = s, r * BODY + k * STRIP
        if first - r * BODY >= BODY:
            device, first = (s + 1) % devices, CAP * BODY + r * TAIL
        return jnp.where(taken[s, r], got[device, first : first + STRIP], jnp.zeros((), BF16))

    copies = []
    for pair in range(BLOCK // STRIP // 2):
        columns = jnp.concatenate(
            [
                jnp.concatenate(
                    [tile(s, r, k) for s in range(devices) for r in range(CAP)], axis=0
                )
                for k in (2 * pair, 2 * pair + 1)
            ],
            axis=1,
        )
        result = jnp.dot(matrix, columns, preferred_element_type=F32) * inverse
        for c in range(CELLS):
            part = result[c * STRIP : (c + 1) * STRIP]
            lanes = slice(c % PSIDE * BLOCK, (c % PSIDE + 1) * BLOCK)
            for n in range(2):
                first = (2 * pair + n) * STRIP
                total[c // PSIDE, first : first + STRIP, lanes] = lane_block(part, n)
        size = 2 * STRIP
        for line in range(PSIDE):
            copies.append(
                pltpu.make_async_copy(
                    total.at[line, pl.ds(pair * size, size)],
                    out.at[0, pl.ds(line * BLOCK + pair * size, size)],
                    out_sem.at[pair, line],
                )
            )
            copies[-1].start()
    for copy in copies:
        copy.wait()


def coadd(got):
    return pl.pallas_call(
        coadd_kernel,
        in_specs=[pl.BlockSpec(memory_space=pltpu.VMEM)],
        out_specs=pl.BlockSpec(memory_space=pl.ANY),
        out_shape=jax.ShapeDtypeStruct((1, PSIDE * BLOCK, PSIDE * BLOCK), F32),
        scratch_shapes=[
            pltpu.VMEM((PSIDE, BLOCK, WIDTH), F32),
            pltpu.SemaphoreType.DMA((BLOCK // STRIP // 2, PSIDE)),
        ],
        compiler_params=pltpu.CompilerParams(vmem_limit_bytes=32 << 20),
        name="coadd",
    )(got)


def shards(
    images, basis_taps, psf_coef, affine, visit_weight, block_patch, block_slot, patch_owner
):
    devices = lax.axis_size("ccd")
    patch = block_patch[:, :, 0]
    head = collect(images, patch)
    above = lax.ppermute(head, "ccd", [(i, (i + 1) % devices) for i in range(devices)])
    order = orders()
    ready = prepare(
        basis_taps.transpose(1, 0, 2), psf_coef.transpose(1, 3, 0, 2), affine.transpose(0, 2, 3, 1),
        devices,
    )
    sent = warp(
        patch, block_slot, patch_owner, visit_weight, ready, order, images, above, devices
    )
    got = lax.all_to_all(sent, "ccd", split_axis=0, concat_axis=0, tiled=True)
    return coadd(got)


def solution(mesh):
    placed = (
        P(None, ("group", "ccd"), None),
        P(),
        P(None, "group", None, None),
        P(None, "group", None, None),
        P(None, "group"),
        P(("group", "ccd"), None, None),
        P(("group", "ccd"), None),
        P("group"),
    )
    return jax.shard_map(
        shards,
        mesh=mesh,
        in_specs=placed,
        out_specs=P(("group", "ccd"), None, None),
        check_vma=False,
    )
```

```python
import functools

import jax
import jax.numpy as jnp
from jax import lax
from jax.experimental import pallas as pl
from jax.experimental.pallas import tpu as pltpu
from jax.sharding import PartitionSpec as P

V = 4
BLOCK = 128
BLKC = 4
SPLIT = 4
TAPS = 11
NBASIS = 9
PSIDE = 4
CELLS = PSIDE * PSIDE
CAP = 2

HALF = TAPS // 2
WARP = 3
RIM = HALF + WARP
TAIL = 16
HEIGHT = SPLIT * BLOCK
WIDTH = BLKC * BLOCK
LANES = 128
LANE_BLOCKS = WIDTH // LANES
STRIP = 16
STEP = 32
STRIPS = -(-(BLOCK + 2 * WARP) // STRIP)
MIDDLE = STRIPS // 2
GROUPS = 6
BAND = 256
PAST_STRIPS = 2
OWN_FIRST = 1
FREE_FIRST = 2
HALVES = 2
MATCHED = 4
WARPED = 4
ROWS = BLOCK // HALVES
WINDOW = ROWS + STRIP
BODY = BLOCK - TAIL
GOT = TAIL + RIM
OPEN = (STRIPS - 1) * STRIP + STEP - FREE_FIRST * STRIP
LABEL = 8
F32 = jnp.float32
BF16 = jnp.bfloat16


def sin_pi(t):
    whole = jnp.round(t)
    f = t - whole
    odd = whole - 2.0 * jnp.floor(0.5 * whole)
    f2 = f * f
    out = 0.0
    for c in (
        0.00046630280576761, -0.0073704309457144, 0.0821458866111282,
        -0.599264529320792, 2.55016403987734, -5.16771278004997, 3.14159265358979,
    ):
        out = out * f2 + c
    return f * out * (1.0 - 2.0 * odd)


def lanczos(t):
    zero = t == 0.0
    safe = jnp.where(zero, 1.0, t)
    pt = jnp.pi * safe
    value = 3.0 * sin_pi(safe) * sin_pi(safe / 3.0) / (pt * pt)
    return jnp.where(jnp.abs(t) < 3.0, jnp.where(zero, 1.0, value), 0.0)


def iota(shape, dim):
    return lax.broadcasted_iota(jnp.int32, shape, dim)


def column_at(lane):
    return lane % LANES * LANE_BLOCKS + lane // LANES


def order_kernel(sort, unsort):
    square = (WIDTH, WIDTH)
    one, none = jnp.ones((), F32), jnp.zeros((), F32)
    goes = iota(square, 0) == column_at(iota((1, WIDTH), 1))
    sort[...] = jnp.where(goes, one, none).astype(BF16)
    comes = iota(square, 1) == column_at(iota((WIDTH, 1), 0))
    unsort[...] = jnp.where(comes, one, none).astype(BF16)


def orders():
    return small_kernel(order_kernel, "orders", [], [((WIDTH, WIDTH), BF16)] * 2)


def lane_block(x, v):
    return x[:, v * LANES : (v + 1) * LANES]


def dot_exact(a, b, dims):
    return lax.dot_general(
        a, b, (dims, ((), ())), precision=lax.Precision.HIGHEST, preferred_element_type=F32
    )


def staircase(x, first):
    return jnp.concatenate(
        [
            pltpu.roll(x[g : g + 8], first + g, 1, stride=1, stride_axis=0)
            for g in range(0, x.shape[0], 8)
        ],
        axis=0,
    )


def lane_sum(terms_of, lane, count, weigh):
    blocks = []
    for v in range(LANE_BLOCKS):
        total = None
        half = count // 2
        for q in range(-(-half // LANE_BLOCKS) * -1, (half + LANE_BLOCKS - 1) // LANE_BLOCKS + 1):
            part = None
            for u in range(count):
                if (v + u - half) // LANE_BLOCKS != q:
                    continue
                piece = terms_of(u, v, (v + u - half) % LANE_BLOCKS)
                part = piece if part is None else part + piece
            if part is None:
                continue
            if q:
                part = pltpu.roll(part, -q % LANES, 1)
                if not weigh:
                    part = jnp.where((lane + q >= 0) & (lane + q < LANES), part, 0.0)
            total = part if total is None else total + part
        blocks.append(total)
    return blocks


def whereabouts(devices):
    band = lax.axis_index("ccd")
    past = lax.rem(band + devices - 1, devices)
    quarter = (band + SPLIT // 2) % SPLIT
    own = ((band + SPLIT // 2) // SPLIT, quarter * BLOCK - TAIL)
    before = ((past + SPLIT // 2) // SPLIT, (past + SPLIT // 2) % SPLIT * BLOCK + BODY)
    return (own, before), (quarter > 0) & (band > 0)


def collect_kernel(images, patch, head, numbers, sems):
    copies = [
        pltpu.make_async_copy(
            images.at[v, pl.ds(BLOCK - GOT, GOT)], head.at[pl.ds(v * GOT, GOT)], sems.at[v]
        )
        for v in range(V)
    ]
    names = pltpu.make_async_copy(patch, numbers, sems.at[V])
    names.start()
    for copy in copies:
        copy.start()
    head[V * GOT :] = jnp.zeros((8, WIDTH), F32)
    names.wait()
    head[V * GOT : V * GOT + 1, : V * BLKC] = numbers[...].astype(F32)
    for copy in copies:
        copy.wait()


def collect(images, patch):
    return pl.pallas_call(
        collect_kernel,
        in_specs=[pl.BlockSpec(memory_space=pl.ANY)] * 2,
        out_specs=pl.BlockSpec(memory_space=pltpu.VMEM),
        out_shape=jax.ShapeDtypeStruct((V * GOT + 8, WIDTH), F32),
        scratch_shapes=[pltpu.VMEM(patch.shape, jnp.int32), pltpu.SemaphoreType.DMA((V + 1,))],
        name="collect",
    )(images, patch)


def lanczos_weights(devices, affine, cols_out):
    bands, same = whereabouts(devices)
    lane = iota((1, LANES), 1)
    lanes = iota((8, WIDTH), 1)
    step = iota((8, WIDTH), 0) - WARP
    block = lanes // LANES
    carry = (block + step + LANE_BLOCKS) // LANE_BLOCKS - 1
    from_lane = lanes % LANES - carry
    col = (from_lane * LANE_BLOCKS + block).astype(F32)
    within = (from_lane >= 0) & (from_lane < LANES) & (step <= WARP)
    offset = iota((8, LANES), 0) - WARP
    crosses = (lane + offset >= TAIL) != (lane >= TAIL)
    keep = (offset <= WARP) & (same | jnp.logical_not(crosses))
    def terms_of(n, visit):
        here = iota((1, 1, affine.shape[3]), 2) == bands[n][0]
        return jnp.sum(jnp.where(here, affine[visit], 0.0), axis=2, keepdims=True)

    def columns(n, visit):
        a = terms_of(n, visit)
        col_shift = a[1, 0:1] + a[1, 1:2] * (col - (WIDTH - 1) / 2.0) / WIDTH
        cols_out[n * V + visit] = jnp.where(within, lanczos(col_shift - step.astype(F32)), 0.0)

    by_row = []
    for visit in range(V):
        columns(0, visit)
        shifts = []
        for n, (_, top_row) in enumerate(bands):
            a = terms_of(n, visit)
            row = (top_row + lane).astype(F32)
            shifts.append(a[0, 0:1] + a[0, 1:2] * (row - (HEIGHT - 1) / 2.0) / HEIGHT)
        shift = jnp.where(lane < TAIL, shifts[1], shifts[0])
        weights = jnp.where(keep, lanczos(shift - offset.astype(F32)), 0.0)
        by_row.append(jnp.concatenate([weights, jnp.zeros((LANES - 8, LANES), F32)], axis=0).T)

    @pl.when(jnp.logical_not(same))
    def _():
        for visit in range(V):
            columns(1, visit)

    return by_row


def prepare_kernel(
    devices, taps, psf, affine, high_level, step_level, slope, rows_high, rows_low, cols_out
):
    row_weights = lanczos_weights(devices, affine, cols_out)
    bands, same = whereabouts(devices)
    band_lane = iota((1, BAND), 1)
    seg = band_lane // STEP
    lane = iota((1, LANES), 1)
    tap = band_lane - seg * STEP
    onehot = (tap == iota((TAPS, BAND), 0)) & (seg < GROUPS)
    row_taps = dot_exact(taps[:, 0], onehot.astype(F32), ((1,), (0,)))
    eye = (iota((TAPS, STRIP), 0) == iota((TAPS, STRIP), 1)).astype(F32)
    turned_taps = dot_exact(eye, taps[:, 1], ((0,), (1,)))
    def make(n, visit):
        ccd, top_row = bands[n]
        lhs = jnp.concatenate(
            [turned_taps * psf[ccd, c, visit : visit + 1, :] for c in range(3)], axis=0
        )
        kernels = dot_exact(lhs, row_taps, ((1,), (0,)))
        const, by_row, by_col = (kernels[c * STRIP : (c + 1) * STRIP] for c in range(3))
        is_level = seg < 3
        per_strip = 2.0 * STRIP / HEIGHT
        middle_row = (top_row + (MIDDLE * STRIP - WARP)).astype(F32)
        middle_pos = (2.0 * middle_row + 1.0) / HEIGHT - 1.0
        col_move = (iota((STRIP, 1), 0) - HALF).astype(F32) * (2.0 / WIDTH)
        by_row = jnp.where(is_level, by_row, 0.0)
        const = jnp.where(is_level, const + middle_pos * by_row - col_move * by_col, by_col)
        reach = per_strip * (STRIPS - MIDDLE)
        largest = jnp.max(jnp.abs(const) + reach * jnp.abs(by_row), axis=(0, 1), keepdims=True)
        unit = jnp.maximum(largest, 1e-30) * (1.0 / 200.0)
        const = const / unit
        by_row = (by_row * per_strip) / unit
        low_lanes = (lane // STEP) % 3 == 2
        low_band = seg % 3 == 2
        row_part = iota((STRIP, 1), 0).astype(F32) * (1.0 / STRIP)
        for u in range(TAPS):
            at = slice(u * STRIP, (u + 1) * STRIP)
            one = jnp.broadcast_to(const[u : u + 1], (STRIP, BAND))
            x, tail = staircase(one[:, :LANES], 0), staircase(one[:, LANES:], 0)
            y = staircase(jnp.broadcast_to(by_row[u : u + 1, :LANES], (STRIP, LANES)), 0)
            high = tail.astype(BF16).astype(F32)
            slope[n * V + visit, at] = jnp.where(low_band[:, LANES:], tail - high, high).astype(BF16)
            x = x + row_part * y
            high = jnp.where(lane < 3 * STEP, jnp.round(x), x.astype(BF16).astype(F32))
            high_level[n * V + visit, at] = jnp.where(low_lanes, x - high, high)
            high = jnp.round(y)
            step_level[n * V + visit, at] = jnp.where(low_lanes, y - high, high)
        return unit

    def put(visit, at, matrix):
        high = matrix.astype(BF16)
        rows_high[visit, at] = high
        rows_low[visit, at] = (matrix - high.astype(F32)).astype(BF16)

    for visit in range(V):
        weights = row_weights[visit] * make(0, visit)
        put(visit, slice(0, TAIL), staircase(weights[:TAIL], 0))
        put(visit, slice(TAIL, ROWS), staircase(weights[TAIL:ROWS], PAST_STRIPS * STRIP))
        put(visit, slice(ROWS, BLOCK), staircase(weights[ROWS:], 0))

    @pl.when(jnp.logical_not(same))
    def _():
        for visit in range(V):
            weights = row_weights[visit][:TAIL] * make(1, visit)
            put(visit, slice(0, TAIL), staircase(weights, 0))


def small_kernel(body, name, args, shapes):
    vmem = pl.BlockSpec(memory_space=pltpu.VMEM)
    return pl.pallas_call(
        body,
        in_specs=[vmem] * len(args),
        out_specs=[vmem] * len(shapes),
        out_shape=[jax.ShapeDtypeStruct(shape, kind) for shape, kind in shapes],
        compiler_params=pltpu.CompilerParams(vmem_limit_bytes=32 << 20),
        cost_estimate=pl.CostEstimate(flops=1 << 30, bytes_accessed=1 << 20, transcendentals=0),
        name=name,
    )(*args)


def prepare(taps, psf, affine, devices):
    return small_kernel(
        functools.partial(prepare_kernel, devices), "matrices", [taps, psf, affine],
        [
            ((2 * V, TAPS * STRIP, LANES), F32),
            ((2 * V, TAPS * STRIP, LANES), F32),
            ((2 * V, TAPS * STRIP, BAND - LANES), BF16),
            ((V, BLOCK, LANES), BF16),
            ((V, BLOCK, LANES), BF16),
            ((2 * V, 8, WIDTH), F32),
        ],
    )


def sorted_rows(raw, sort):
    col_pos = (2.0 * column_at(iota((1, WIDTH), 1)).astype(F32) + 1.0) / WIDTH - 1.0
    count = raw.shape[0]
    raw_high = raw.astype(BF16)
    raw_low = (raw - raw_high.astype(F32)).astype(BF16)
    both = jnp.dot(
        jnp.concatenate([raw_high, raw_low], axis=0), sort, preferred_element_type=F32
    )
    high, low = both[:count], both[count:]
    tilted = (high + low) * col_pos
    tilted_high = tilted.astype(BF16).astype(F32)
    return high, low, tilted_high, tilted - tilted_high


def match_strip(level, step, slope, source, first, k):
    lane = iota((1, LANES), 1)
    if k != MIDDLE:
        level = level + float(k - MIDDLE) * step
    matrix = jnp.concatenate([level.astype(BF16), slope], axis=1)
    filler = jnp.zeros((BAND - GROUPS * STEP, WIDTH), BF16)
    rows = slice(first, first + STEP)
    columns = jnp.concatenate([source[h, rows] for h in (0, 1, 0, 2, 3, 2)] + [filler], axis=0)
    results = jnp.dot(matrix, columns, preferred_element_type=F32)
    blocks = lane_sum(
        lambda u, v, w: lane_block(results[u * STRIP : (u + 1) * STRIP], w), lane, TAPS, False
    )
    matched = jnp.concatenate(blocks, axis=1)
    high = matched.astype(BF16)
    return high, (matched - high.astype(F32)).astype(BF16)


def upright(line):
    count = line.shape[1]
    square = (count, count)
    return jnp.sum(
        jnp.where(iota(square, 0) == iota(square, 1), jnp.broadcast_to(line, square), 0),
        axis=1, keepdims=True,
    )


def route(patch, owner):
    square = (patch.shape[1], patch.shape[1])
    earlier = (iota(square, 0) < iota(square, 1)) & (upright(patch) == patch)
    rank = jnp.sum(earlier.astype(jnp.int32), axis=0, keepdims=True)
    named = iota((owner.shape[1], patch.shape[1]), 0) == patch
    to = jnp.sum(jnp.where(named, upright(owner), 0), axis=0, keepdims=True)
    return to, rank


def match_kernel(
    patch, slot, owner, weight, high_level, step_level, slope, sort, image,
    places, label, matched_terms, terms,
):
    ((ccd, _), _), _ = whereabouts(label.shape[0])
    to, rank = route(patch[...], owner[...])
    places[...] = to * CAP + rank

    own = jnp.where(iota(weight.shape, 1) == ccd, weight[...].astype(F32), 0.0)
    own = jnp.sum(own, axis=1, keepdims=True)
    each = (V, V * BLKC)
    weights = jnp.sum(
        jnp.where(iota(each, 1) // BLKC == iota(each, 0), own, 0.0), axis=0, keepdims=True
    )
    goes = iota((label.shape[0], V * BLKC), 0) == to
    lane = iota(label.shape, 1)
    lines = jnp.zeros(label.shape, F32)
    for r in range(CAP):
        for n, value in enumerate((weights, slot[...].astype(F32))):
            column = jnp.sum(jnp.where(goes & (rank == r), value, 0.0), axis=1, keepdims=True)
            lines = jnp.where(lane == 2 * r + n, column, lines)
    label[...] = lines

    open_row = FREE_FIRST * STRIP - GOT
    seen = OPEN - STRIP
    terms[:, :, seen:] = jnp.zeros((MATCHED, 4, STRIP, WIDTH), BF16)

    def some_visits(turn):
        visits = [turn * MATCHED + i for i in range(MATCHED)]
        for i, visit in enumerate(visits):
            rows = sorted_rows(image[visit, open_row : open_row + seen], sort[...])
            for h, value in enumerate(rows):
                terms[i, h, :seen] = value.astype(BF16)
        for k in range(FREE_FIRST, STRIPS):
            first = (k - FREE_FIRST) * STRIP
            for i, visit in enumerate(visits):
                at = slice(first, first + STRIP)
                matched_terms[visit, 0, at], matched_terms[visit, 1, at] = match_strip(
                    high_level[visit], step_level[visit], slope[visit], terms.at[i], first, k
                )

    for turn in range(V // MATCHED):
        some_visits(turn)


def warp_kernel(
    owner, places, label, high_level, step_level, slope, rows_high, rows_low, col_weights,
    sort, unsort, image, above, matched_free, out,
    own_terms, past_terms, own_matched, past_matched, both_places, place_of, place_sem,
):
    devices = label.shape[0]
    _, same = whereabouts(devices)
    past_patch = above[V * GOT : V * GOT + 1, : V * BLKC].astype(jnp.int32)
    to, rank = route(past_patch, owner[...])
    both_places[0:1, : V * BLKC] = places[...]
    both_places[1:2, : V * BLKC] = to * CAP + rank
    place_copy = pltpu.make_async_copy(both_places, place_of, place_sem)
    place_copy.start()
    lane = iota((1, LANES), 1)
    out[:, CAP * BLOCK :] = jnp.broadcast_to(
        label[...].reshape(devices, 1, LANES), (devices, LABEL, LANES)
    ).astype(BF16)

    seam = STRIP + STEP
    foreign = iota((seam, 1), 0) < GOT
    both = jnp.where(same, 1.0, 0.0)
    past = jnp.where(same, 0, V)
    own_sees = jnp.where(foreign, both, 1.0)
    past_sees = jnp.where(foreign, 1.0, both)

    def some_visits(turn):
        visits = [turn * WARPED + i for i in range(WARPED)]
        for i, visit in enumerate(visits):
            tail = slice(visit * GOT, (visit + 1) * GOT)
            raw = jnp.concatenate([above[tail], image[visit, : seam - GOT]], axis=0)
            for h, value in enumerate(sorted_rows(raw, sort[...])):
                own_terms[i, h] = (value * own_sees).astype(BF16)
                past_terms[i, h] = (value * past_sees).astype(BF16)
        for i, visit in enumerate(visits):
            own_matched[i, 0], own_matched[i, 1] = match_strip(
                high_level[visit], step_level[visit], slope[visit],
                own_terms.at[i], OWN_FIRST * STRIP, OWN_FIRST,
            )
        for k in range(PAST_STRIPS):
            for i, visit in enumerate(visits):
                at = slice(k * STRIP, (k + 1) * STRIP)
                past_matched[i, 0, at], past_matched[i, 1, at] = match_strip(
                    high_level[past + visit], step_level[past + visit], slope[past + visit],
                    past_terms.at[i], k * STRIP, k,
                )

        warped = []
        for i, visit in enumerate(visits):
            halves = []
            for h in range(HALVES):
                at = slice(h * ROWS, (h + 1) * ROWS)
                high, low = rows_high[visit, at], rows_low[visit, at]
                free = FREE_FIRST * STRIP

                def under(term):
                    if h == 0:
                        parts = [
                            past_matched[i, term],
                            own_matched[i, term],
                            matched_free[visit, term, : WINDOW - free],
                        ]
                    else:
                        parts = [matched_free[visit, term, ROWS - free :]]
                    left = LANES - sum([x.shape[0] for x in parts])
                    return jnp.concatenate(parts + [jnp.zeros((left, WIDTH), BF16)], axis=0)

                first = under(0)
                total = jnp.dot(
                    jnp.concatenate([high, high], axis=1),
                    jnp.concatenate([first, under(1)], axis=0),
                    preferred_element_type=F32,
                )
                halves.append(total + jnp.dot(low, first, preferred_element_type=F32))
            warped.append(jnp.concatenate(halves, axis=0))

        finished = []
        for i, visit in enumerate(visits):
            parts = []
            for rows, weights in (
                (slice(0, TAIL), col_weights[past + visit]),
                (slice(TAIL, BLOCK), col_weights[visit]),
            ):
                some = warped[i][rows]
                blocks = lane_sum(
                    lambda s, v, w: lane_block(weights[s : s + 1], v) * lane_block(some, w),
                    lane, 2 * WARP + 1, True,
                )
                parts.append(jnp.concatenate(blocks, axis=1).astype(BF16))
            result = jnp.dot(
                jnp.concatenate(parts, axis=0), unsort[...], preferred_element_type=F32
            ).astype(BF16)
            finished.append(result)
        return finished

    finished = []
    for turn in range(V // WARPED):
        finished += some_visits(turn)
    place_copy.wait()
    for visit in range(V):
        for j in range(BLKC):
            piece = lane_block(finished[visit], j)
            to = place_of[0, visit * BLKC + j]
            rows = pl.ds(pl.multiple_of(to % CAP * BODY, TAIL), BODY)
            out[to // CAP, rows] = piece[TAIL:]
            to = place_of[1, visit * BLKC + j]
            rows = pl.ds(pl.multiple_of(CAP * BODY + to % CAP * TAIL, TAIL), TAIL)
            out[to // CAP, rows] = piece[:TAIL]


def warp(patch, slot, owner, weight, ready, order, images, above, devices):
    vmem = pl.BlockSpec(memory_space=pltpu.VMEM)
    sort, unsort = order
    *matrices, rows_high, rows_low, col_weights = ready
    owner = owner.reshape(1, -1)
    args = [patch, slot, owner, weight, *matrices, sort, images]
    places, label, matched = pl.pallas_call(
        match_kernel,
        in_specs=[vmem] * len(args),
        out_specs=[vmem, vmem, vmem],
        out_shape=[
            jax.ShapeDtypeStruct((1, V * BLKC), jnp.int32),
            jax.ShapeDtypeStruct((devices, LANES), F32),
            jax.ShapeDtypeStruct((V, 2, (STRIPS - FREE_FIRST) * STRIP, WIDTH), BF16),
        ],
        scratch_shapes=[
            pltpu.VMEM((MATCHED, 4, OPEN, WIDTH), BF16),
        ],
        compiler_params=pltpu.CompilerParams(vmem_limit_bytes=32 << 20),
        cost_estimate=pl.CostEstimate(
            flops=V * 2 * (STRIPS - FREE_FIRST) * TAPS * STRIP * BAND * WIDTH,
            bytes_accessed=V * (BLOCK * WIDTH * 6),
            transcendentals=0,
        ),
        name="match",
    )(*args)
    args = [
        owner, places, label, *matrices, rows_high, rows_low, col_weights,
        sort, unsort, images, above, matched,
    ]
    return pl.pallas_call(
        warp_kernel,
        in_specs=[vmem] * len(args),
        out_specs=vmem,
        scratch_shapes=[
            pltpu.VMEM((WARPED, 4, STRIP + STEP, WIDTH), BF16),
            pltpu.VMEM((WARPED, 4, STRIP + STEP, WIDTH), BF16),
            pltpu.VMEM((WARPED, 2, STRIP, WIDTH), BF16),
            pltpu.VMEM((WARPED, 2, PAST_STRIPS * STRIP, WIDTH), BF16),
            pltpu.VMEM((8, LANES), jnp.int32),
            pltpu.SMEM((8, LANES), jnp.int32),
            pltpu.SemaphoreType.DMA(()),
        ],
        out_shape=jax.ShapeDtypeStruct((devices, CAP * BLOCK + LABEL, BLOCK), BF16),
        compiler_params=pltpu.CompilerParams(vmem_limit_bytes=32 << 20),
        cost_estimate=pl.CostEstimate(
            flops=V * 2 * STRIPS * TAPS * STRIP * BAND * WIDTH,
            bytes_accessed=V * (BLOCK * WIDTH * 6),
            transcendentals=0,
        ),
        name="warp",
    )(*args)


def coadd_kernel(got, out, total, out_sem):
    devices = got.shape[0]
    wide = devices * CAP * STRIP
    labels = got[:, CAP * BLOCK : CAP * BLOCK + LABEL][:, 0]
    lane = iota((1, wide), 1)
    rank = lane // STRIP % CAP
    source = lane // (STRIP * CAP)

    def spread(entry):
        onehot = (iota((LANES, wide), 0) == rank * 2 + entry).astype(F32).astype(BF16)
        every = jnp.dot(labels, onehot, preferred_element_type=F32)
        return jnp.sum(
            jnp.where(iota((devices, wide), 0) == source, every, 0.0), axis=0, keepdims=True
        )

    weights, cells = spread(0), spread(1)
    row = iota((CELLS * STRIP, 1), 0)
    mine = (cells == (row // STRIP).astype(F32)) & (lane % STRIP == row % STRIP)
    matrix = jnp.where(mine, weights, 0.0)
    sums = jnp.sum(matrix, axis=1, keepdims=True)
    inverse = 1.0 / jnp.maximum(sums, 1.0)
    matrix = matrix.astype(BF16)
    taken = {}
    for r in range(CAP):
        column = jnp.broadcast_to(labels[:, 2 * r : 2 * r + 1].astype(F32), (devices, LANES))
        for s in range(devices):
            taken[s, r] = jnp.broadcast_to(column[s : s + 1], (STRIP, LANES)).astype(BF16) > 0

    def tile(s, r, k):
        device, first = s, r * BODY + k * STRIP
        if first - r * BODY >= BODY:
            device, first = (s + 1) % devices, CAP * BODY + r * TAIL
        return jnp.where(taken[s, r], got[device, first : first + STRIP], jnp.zeros((), BF16))

    copies = []
    for pair in range(BLOCK // STRIP // 2):
        columns = jnp.concatenate(
            [
                jnp.concatenate(
                    [tile(s, r, k) for s in range(devices) for r in range(CAP)], axis=0
                )
                for k in (2 * pair, 2 * pair + 1)
            ],
            axis=1,
        )
        result = jnp.dot(matrix, columns, preferred_element_type=F32) * inverse
        for c in range(CELLS):
            part = result[c * STRIP : (c + 1) * STRIP]
            lanes = slice(c % PSIDE * BLOCK, (c % PSIDE + 1) * BLOCK)
            for n in range(2):
                first = (2 * pair + n) * STRIP
                total[c // PSIDE, first : first + STRIP, lanes] = lane_block(part, n)
        size = 2 * STRIP
        for line in range(PSIDE):
            copies.append(
                pltpu.make_async_copy(
                    total.at[line, pl.ds(pair * size, size)],
                    out.at[0, pl.ds(line * BLOCK + pair * size, size)],
                    out_sem.at[pair, line],
                )
            )
            copies[-1].start()
    for copy in copies:
        copy.wait()


def coadd(got):
    return pl.pallas_call(
        coadd_kernel,
        in_specs=[pl.BlockSpec(memory_space=pltpu.VMEM)],
        out_specs=pl.BlockSpec(memory_space=pl.ANY),
        out_shape=jax.ShapeDtypeStruct((1, PSIDE * BLOCK, PSIDE * BLOCK), F32),
        scratch_shapes=[
            pltpu.VMEM((PSIDE, BLOCK, WIDTH), F32),
            pltpu.SemaphoreType.DMA((BLOCK // STRIP // 2, PSIDE)),
        ],
        compiler_params=pltpu.CompilerParams(vmem_limit_bytes=32 << 20),
        name="coadd",
    )(got)


def shards(
    images, basis_taps, psf_coef, affine, visit_weight, block_patch, block_slot, patch_owner
):
    devices = lax.axis_size("ccd")
    patch = block_patch[:, :, 0]
    head = collect(images, patch)
    above = lax.ppermute(head, "ccd", [(i, (i + 1) % devices) for i in range(devices)])
    order = orders()
    ready = prepare(
        basis_taps.transpose(1, 0, 2), psf_coef.transpose(1, 3, 0, 2), affine.transpose(0, 2, 3, 1),
        devices,
    )
    sent = warp(
        patch, block_slot, patch_owner, visit_weight, ready, order, images, above, devices
    )
    got = lax.all_to_all(sent, "ccd", split_axis=0, concat_axis=0, tiled=True)
    return coadd(got)


def solution(mesh):
    placed = (
        P(None, ("group", "ccd"), None),
        P(),
        P(None, "group", None, None),
        P(None, "group", None, None),
        P(None, "group"),
        P(("group", "ccd"), None, None),
        P(("group", "ccd"), None),
        P("group"),
    )
    return jax.shard_map(
        shards,
        mesh=mesh,
        in_specs=placed,
        out_specs=P(("group", "ccd"), None, None),
        check_vma=False,
    )
```

```python
import functools

import jax
import jax.numpy as jnp
from jax import lax
from jax.experimental import pallas as pl
from jax.experimental.pallas import tpu as pltpu
from jax.sharding import PartitionSpec as P

V = 4
BLOCK = 128
BLKC = 4
SPLIT = 4
TAPS = 11
NBASIS = 9
PSIDE = 4
CELLS = PSIDE * PSIDE
CAP = 2

HALF = TAPS // 2
WARP = 3
RIM = HALF + WARP
TAIL = 16
HEIGHT = SPLIT * BLOCK
WIDTH = BLKC * BLOCK
LANES = 128
LANE_BLOCKS = WIDTH // LANES
STRIP = 16
STEP = 32
STRIPS = -(-(BLOCK + 2 * WARP) // STRIP)
MIDDLE = STRIPS // 2
GROUPS = 6
BAND = 256
PAST_STRIPS = 2
OWN_FIRST = 1
FREE_FIRST = 2
HALVES = 2
MATCHED = 4
WARPED = 4
ROWS = BLOCK // HALVES
WINDOW = ROWS + STRIP
BODY = BLOCK - TAIL
GOT = TAIL + RIM
OPEN = (STRIPS - 1) * STRIP + STEP - FREE_FIRST * STRIP
LABEL = 8
F32 = jnp.float32
BF16 = jnp.bfloat16


def sin_pi(t):
    whole = jnp.round(t)
    f = t - whole
    odd = whole - 2.0 * jnp.floor(0.5 * whole)
    f2 = f * f
    out = 0.0
    for c in (
        0.00046630280576761, -0.0073704309457144, 0.0821458866111282,
        -0.599264529320792, 2.55016403987734, -5.16771278004997, 3.14159265358979,
    ):
        out = out * f2 + c
    return f * out * (1.0 - 2.0 * odd)


def lanczos(t):
    zero = t == 0.0
    safe = jnp.where(zero, 1.0, t)
    pt = jnp.pi * safe
    value = 3.0 * sin_pi(safe) * sin_pi(safe / 3.0) / (pt * pt)
    return jnp.where(jnp.abs(t) < 3.0, jnp.where(zero, 1.0, value), 0.0)


def iota(shape, dim):
    return lax.broadcasted_iota(jnp.int32, shape, dim)


def column_at(lane):
    return lane % LANES * LANE_BLOCKS + lane // LANES


def order_kernel(sort, unsort):
    square = (WIDTH, WIDTH)
    one, none = jnp.ones((), F32), jnp.zeros((), F32)
    goes = iota(square, 0) == column_at(iota((1, WIDTH), 1))
    sort[...] = jnp.where(goes, one, none).astype(BF16)
    comes = iota(square, 1) == column_at(iota((WIDTH, 1), 0))
    unsort[...] = jnp.where(comes, one, none).astype(BF16)


def orders():
    return small_kernel(order_kernel, "orders", [], [((WIDTH, WIDTH), BF16)] * 2)


def lane_block(x, v):
    return x[:, v * LANES : (v + 1) * LANES]


def dot_exact(a, b, dims):
    return lax.dot_general(
        a, b, (dims, ((), ())), precision=lax.Precision.HIGHEST, preferred_element_type=F32
    )


def staircase(x, first):
    return jnp.concatenate(
        [
            pltpu.roll(x[g : g + 8], first + g, 1, stride=1, stride_axis=0)
            for g in range(0, x.shape[0], 8)
        ],
        axis=0,
    )


def lane_sum(terms_of, lane, count, weigh):
    blocks = []
    for v in range(LANE_BLOCKS):
        total = None
        half = count // 2
        for q in range(-(-half // LANE_BLOCKS) * -1, (half + LANE_BLOCKS - 1) // LANE_BLOCKS + 1):
            part = None
            for u in range(count):
                if (v + u - half) // LANE_BLOCKS != q:
                    continue
                piece = terms_of(u, v, (v + u - half) % LANE_BLOCKS)
                part = piece if part is None else part + piece
            if part is None:
                continue
            if q:
                part = pltpu.roll(part, -q % LANES, 1)
                if not weigh:
                    part = jnp.where((lane + q >= 0) & (lane + q < LANES), part, 0.0)
            total = part if total is None else total + part
        blocks.append(total)
    return blocks


def whereabouts(devices):
    band = lax.axis_index("ccd")
    past = lax.rem(band + devices - 1, devices)
    quarter = (band + SPLIT // 2) % SPLIT
    own = ((band + SPLIT // 2) // SPLIT, quarter * BLOCK - TAIL)
    before = ((past + SPLIT // 2) // SPLIT, (past + SPLIT // 2) % SPLIT * BLOCK + BODY)
    return (own, before), (quarter > 0) & (band > 0)


def collect_kernel(images, patch, head, numbers, sems):
    copies = [
        pltpu.make_async_copy(
            images.at[v, pl.ds(BLOCK - GOT, GOT)], head.at[pl.ds(v * GOT, GOT)], sems.at[v]
        )
        for v in range(V)
    ]
    names = pltpu.make_async_copy(patch, numbers, sems.at[V])
    names.start()
    for copy in copies:
        copy.start()
    head[V * GOT :] = jnp.zeros((8, WIDTH), F32)
    names.wait()
    head[V * GOT : V * GOT + 1, : V * BLKC] = numbers[...].astype(F32)
    for copy in copies:
        copy.wait()


def collect(images, patch):
    return pl.pallas_call(
        collect_kernel,
        in_specs=[pl.BlockSpec(memory_space=pl.ANY)] * 2,
        out_specs=pl.BlockSpec(memory_space=pltpu.VMEM),
        out_shape=jax.ShapeDtypeStruct((V * GOT + 8, WIDTH), F32),
        scratch_shapes=[pltpu.VMEM(patch.shape, jnp.int32), pltpu.SemaphoreType.DMA((V + 1,))],
        name="collect",
    )(images, patch)


def lanczos_weights(devices, affine, cols_out):
    bands, same = whereabouts(devices)
    lane = iota((1, LANES), 1)
    lanes = iota((8, WIDTH), 1)
    step = iota((8, WIDTH), 0) - WARP
    block = lanes // LANES
    carry = (block + step + LANE_BLOCKS) // LANE_BLOCKS - 1
    from_lane = lanes % LANES - carry
    col = (from_lane * LANE_BLOCKS + block).astype(F32)
    within = (from_lane >= 0) & (from_lane < LANES) & (step <= WARP)
    offset = iota((8, LANES), 0) - WARP
    crosses = (lane + offset >= TAIL) != (lane >= TAIL)
    keep = (offset <= WARP) & (same | jnp.logical_not(crosses))
    def terms_of(n, visit):
        here = iota((1, 1, affine.shape[3]), 2) == bands[n][0]
        return jnp.sum(jnp.where(here, affine[visit], 0.0), axis=2, keepdims=True)

    def columns(n, visit):
        a = terms_of(n, visit)
        col_shift = a[1, 0:1] + a[1, 1:2] * (col - (WIDTH - 1) / 2.0) / WIDTH
        cols_out[n * V + visit] = jnp.where(within, lanczos(col_shift - step.astype(F32)), 0.0)

    by_row = []
    for visit in range(V):
        columns(0, visit)
        shifts = []
        for n, (_, top_row) in enumerate(bands):
            a = terms_of(n, visit)
            row = (top_row + lane).astype(F32)
            shifts.append(a[0, 0:1] + a[0, 1:2] * (row - (HEIGHT - 1) / 2.0) / HEIGHT)
        shift = jnp.where(lane < TAIL, shifts[1], shifts[0])
        weights = jnp.where(keep, lanczos(shift - offset.astype(F32)), 0.0)
        by_row.append(jnp.concatenate([weights, jnp.zeros((LANES - 8, LANES), F32)], axis=0).T)

    @pl.when(jnp.logical_not(same))
    def _():
        for visit in range(V):
            columns(1, visit)

    return by_row


def prepare_kernel(
    devices, taps, psf, affine, high_level, step_level, slope, rows_high, rows_low, cols_out
):
    row_weights = lanczos_weights(devices, affine, cols_out)
    bands, same = whereabouts(devices)
    band_lane = iota((1, BAND), 1)
    seg = band_lane // STEP
    lane = iota((1, LANES), 1)
    tap = band_lane - seg * STEP
    onehot = (tap == iota((TAPS, BAND), 0)) & (seg < GROUPS)
    row_taps = dot_exact(taps[:, 0], onehot.astype(F32), ((1,), (0,)))
    eye = (iota((TAPS, STRIP), 0) == iota((TAPS, STRIP), 1)).astype(F32)
    turned_taps = dot_exact(eye, taps[:, 1], ((0,), (1,)))
    def make(n, visit):
        ccd, top_row = bands[n]
        lhs = jnp.concatenate(
            [turned_taps * psf[ccd, c, visit : visit + 1, :] for c in range(3)], axis=0
        )
        kernels = dot_exact(lhs, row_taps, ((1,), (0,)))
        const, by_row, by_col = (kernels[c * STRIP : (c + 1) * STRIP] for c in range(3))
        is_level = seg < 3
        per_strip = 2.0 * STRIP / HEIGHT
        middle_row = (top_row + (MIDDLE * STRIP - WARP)).astype(F32)
        middle_pos = (2.0 * middle_row + 1.0) / HEIGHT - 1.0
        col_move = (iota((STRIP, 1), 0) - HALF).astype(F32) * (2.0 / WIDTH)
        by_row = jnp.where(is_level, by_row, 0.0)
        const = jnp.where(is_level, const + middle_pos * by_row - col_move * by_col, by_col)
        reach = per_strip * (STRIPS - MIDDLE)
        largest = jnp.max(jnp.abs(const) + reach * jnp.abs(by_row), axis=(0, 1), keepdims=True)
        unit = jnp.maximum(largest, 1e-30) * (1.0 / 200.0)
        const = const / unit
        by_row = (by_row * per_strip) / unit
        low_lanes = (lane // STEP) % 3 == 2
        low_band = seg % 3 == 2
        row_part = iota((STRIP, 1), 0).astype(F32) * (1.0 / STRIP)
        for u in range(TAPS):
            at = slice(u * STRIP, (u + 1) * STRIP)
            one = jnp.broadcast_to(const[u : u + 1], (STRIP, BAND))
            x, tail = staircase(one[:, :LANES], 0), staircase(one[:, LANES:], 0)
            y = staircase(jnp.broadcast_to(by_row[u : u + 1, :LANES], (STRIP, LANES)), 0)
            high = tail.astype(BF16).astype(F32)
            slope[n * V + visit, at] = jnp.where(low_band[:, LANES:], tail - high, high).astype(BF16)
            x = x + row_part * y
            high = jnp.where(lane < 3 * STEP, jnp.round(x), x.astype(BF16).astype(F32))
            high_level[n * V + visit, at] = jnp.where(low_lanes, x - high, high)
            high = jnp.round(y)
            step_level[n * V + visit, at] = jnp.where(low_lanes, y - high, high)
        return unit

    def put(visit, at, matrix):
        high = matrix.astype(BF16)
        rows_high[visit, at] = high
        rows_low[visit, at] = (matrix - high.astype(F32)).astype(BF16)

    for visit in range(V):
        weights = row_weights[visit] * make(0, visit)
        put(visit, slice(0, TAIL), staircase(weights[:TAIL], 0))
        put(visit, slice(TAIL, ROWS), staircase(weights[TAIL:ROWS], PAST_STRIPS * STRIP))
        put(visit, slice(ROWS, BLOCK), staircase(weights[ROWS:], 0))

    @pl.when(jnp.logical_not(same))
    def _():
        for visit in range(V):
            weights = row_weights[visit][:TAIL] * make(1, visit)
            put(visit, slice(0, TAIL), staircase(weights, 0))


def small_kernel(body, name, args, shapes):
    vmem = pl.BlockSpec(memory_space=pltpu.VMEM)
    return pl.pallas_call(
        body,
        in_specs=[vmem] * len(args),
        out_specs=[vmem] * len(shapes),
        out_shape=[jax.ShapeDtypeStruct(shape, kind) for shape, kind in shapes],
        compiler_params=pltpu.CompilerParams(vmem_limit_bytes=32 << 20),
        cost_estimate=pl.CostEstimate(flops=1 << 30, bytes_accessed=1 << 20, transcendentals=0),
        name=name,
    )(*args)


def prepare(taps, psf, affine, devices):
    return small_kernel(
        functools.partial(prepare_kernel, devices), "matrices", [taps, psf, affine],
        [
            ((2 * V, TAPS * STRIP, LANES), F32),
            ((2 * V, TAPS * STRIP, LANES), F32),
            ((2 * V, TAPS * STRIP, BAND - LANES), BF16),
            ((V, BLOCK, LANES), BF16),
            ((V, BLOCK, LANES), BF16),
            ((2 * V, 8, WIDTH), F32),
        ],
    )


def sorted_rows(raw, sort):
    col_pos = (2.0 * column_at(iota((1, WIDTH), 1)).astype(F32) + 1.0) / WIDTH - 1.0
    count = raw.shape[0]
    raw_high = raw.astype(BF16)
    raw_low = (raw - raw_high.astype(F32)).astype(BF16)
    both = jnp.dot(
        jnp.concatenate([raw_high, raw_low], axis=0), sort, preferred_element_type=F32
    )
    high, low = both[:count], both[count:]
    tilted = (high + low) * col_pos
    tilted_high = tilted.astype(BF16).astype(F32)
    return high, low, tilted_high, tilted - tilted_high


def match_strip(level, step, slope, source, first, k):
    lane = iota((1, LANES), 1)
    if k != MIDDLE:
        level = level + float(k - MIDDLE) * step
    matrix = jnp.concatenate([level.astype(BF16), slope], axis=1)
    filler = jnp.zeros((BAND - GROUPS * STEP, WIDTH), BF16)
    rows = slice(first, first + STEP)
    columns = jnp.concatenate([source[h, rows] for h in (0, 1, 0, 2, 3, 2)] + [filler], axis=0)
    results = jnp.dot(matrix, columns, preferred_element_type=F32)
    blocks = lane_sum(
        lambda u, v, w: lane_block(results[u * STRIP : (u + 1) * STRIP], w), lane, TAPS, False
    )
    matched = jnp.concatenate(blocks, axis=1)
    high = matched.astype(BF16)
    return high, (matched - high.astype(F32)).astype(BF16)


def upright(line):
    count = line.shape[1]
    square = (count, count)
    return jnp.sum(
        jnp.where(iota(square, 0) == iota(square, 1), jnp.broadcast_to(line, square), 0),
        axis=1, keepdims=True,
    )


def route(patch, owner):
    square = (patch.shape[1], patch.shape[1])
    earlier = (iota(square, 0) < iota(square, 1)) & (upright(patch) == patch)
    rank = jnp.sum(earlier.astype(jnp.int32), axis=0, keepdims=True)
    named = iota((owner.shape[1], patch.shape[1]), 0) == patch
    to = jnp.sum(jnp.where(named, upright(owner), 0), axis=0, keepdims=True)
    return to, rank


def match_kernel(
    patch, slot, owner, weight, high_level, step_level, slope, sort, image,
    places, label, matched_terms, terms,
):
    ((ccd, _), _), _ = whereabouts(label.shape[0])
    to, rank = route(patch[...], owner[...])
    places[...] = to * CAP + rank

    own = jnp.where(iota(weight.shape, 1) == ccd, weight[...].astype(F32), 0.0)
    own = jnp.sum(own, axis=1, keepdims=True)
    each = (V, V * BLKC)
    weights = jnp.sum(
        jnp.where(iota(each, 1) // BLKC == iota(each, 0), own, 0.0), axis=0, keepdims=True
    )
    goes = iota((label.shape[0], V * BLKC), 0) == to
    lane = iota(label.shape, 1)
    lines = jnp.zeros(label.shape, F32)
    for r in range(CAP):
        for n, value in enumerate((weights, slot[...].astype(F32))):
            column = jnp.sum(jnp.where(goes & (rank == r), value, 0.0), axis=1, keepdims=True)
            lines = jnp.where(lane == 2 * r + n, column, lines)
    label[...] = lines

    open_row = FREE_FIRST * STRIP - GOT
    seen = OPEN - STRIP
    terms[:, :, seen:] = jnp.zeros((MATCHED, 4, STRIP, WIDTH), BF16)

    def some_visits(turn):
        visits = [turn * MATCHED + i for i in range(MATCHED)]
        raw = [image[visit, open_row : open_row + seen] for visit in visits]
        for h, value in enumerate(sorted_rows(jnp.concatenate(raw, axis=0), sort[...])):
            for i in range(MATCHED):
                terms[i, h, :seen] = value[i * seen : (i + 1) * seen].astype(BF16)
        for k in range(FREE_FIRST, STRIPS):
            first = (k - FREE_FIRST) * STRIP
            for i, visit in enumerate(visits):
                at = slice(first, first + STRIP)
                matched_terms[visit, 0, at], matched_terms[visit, 1, at] = match_strip(
                    high_level[visit], step_level[visit], slope[visit], terms.at[i], first, k
                )

    for turn in range(V // MATCHED):
        some_visits(turn)


def warp_kernel(
    owner, places, label, high_level, step_level, slope, rows_high, rows_low, col_weights,
    sort, unsort, image, above, matched_free, out,
    own_terms, past_terms, own_matched, past_matched, both_places, place_of, place_sem,
):
    devices = label.shape[0]
    _, same = whereabouts(devices)
    past_patch = above[V * GOT : V * GOT + 1, : V * BLKC].astype(jnp.int32)
    to, rank = route(past_patch, owner[...])
    both_places[0:1, : V * BLKC] = places[...]
    both_places[1:2, : V * BLKC] = to * CAP + rank
    place_copy = pltpu.make_async_copy(both_places, place_of, place_sem)
    place_copy.start()
    lane = iota((1, LANES), 1)
    out[:, CAP * BLOCK :] = jnp.broadcast_to(
        label[...].reshape(devices, 1, LANES), (devices, LABEL, LANES)
    ).astype(BF16)

    seam = STRIP + STEP
    foreign = iota((seam, 1), 0) < GOT
    both = jnp.where(same, 1.0, 0.0)
    past = jnp.where(same, 0, V)
    own_sees = jnp.where(foreign, both, 1.0)
    past_sees = jnp.where(foreign, 1.0, both)

    def some_visits(turn):
        visits = [turn * WARPED + i for i in range(WARPED)]
        raw = []
        for visit in visits:
            raw += [above[visit * GOT : (visit + 1) * GOT], image[visit, : seam - GOT]]
        for h, value in enumerate(sorted_rows(jnp.concatenate(raw, axis=0), sort[...])):
            for i in range(WARPED):
                rows = value[i * seam : (i + 1) * seam]
                own_terms[i, h] = (rows * own_sees).astype(BF16)
                past_terms[i, h] = (rows * past_sees).astype(BF16)
        for i, visit in enumerate(visits):
            own_matched[i, 0], own_matched[i, 1] = match_strip(
                high_level[visit], step_level[visit], slope[visit],
                own_terms.at[i], OWN_FIRST * STRIP, OWN_FIRST,
            )
        for k in range(PAST_STRIPS):
            for i, visit in enumerate(visits):
                at = slice(k * STRIP, (k + 1) * STRIP)
                past_matched[i, 0, at], past_matched[i, 1, at] = match_strip(
                    high_level[past + visit], step_level[past + visit], slope[past + visit],
                    past_terms.at[i], k * STRIP, k,
                )

        warped = []
        for i, visit in enumerate(visits):
            halves = []
            for h in range(HALVES):
                at = slice(h * ROWS, (h + 1) * ROWS)
                high, low = rows_high[visit, at], rows_low[visit, at]
                free = FREE_FIRST * STRIP

                def under(term):
                    if h == 0:
                        parts = [
                            past_matched[i, term],
                            own_matched[i, term],
                            matched_free[visit, term, : WINDOW - free],
                        ]
                    else:
                        parts = [matched_free[visit, term, ROWS - free :]]
                    left = LANES - sum([x.shape[0] for x in parts])
                    return jnp.concatenate(parts + [jnp.zeros((left, WIDTH), BF16)], axis=0)

                first = under(0)
                total = jnp.dot(
                    jnp.concatenate([high, high], axis=1),
                    jnp.concatenate([first, under(1)], axis=0),
                    preferred_element_type=F32,
                )
                halves.append(total + jnp.dot(low, first, preferred_element_type=F32))
            warped.append(jnp.concatenate(halves, axis=0))

        parts = []
        for i, visit in enumerate(visits):
            for rows, weights in (
                (slice(0, TAIL), col_weights[past + visit]),
                (slice(TAIL, BLOCK), col_weights[visit]),
            ):
                some = warped[i][rows]
                blocks = lane_sum(
                    lambda s, v, w: lane_block(weights[s : s + 1], v) * lane_block(some, w),
                    lane, 2 * WARP + 1, True,
                )
                parts.append(jnp.concatenate(blocks, axis=1).astype(BF16))
        result = jnp.dot(
            jnp.concatenate(parts, axis=0), unsort[...], preferred_element_type=F32
        ).astype(BF16)
        return [result[i * BLOCK : (i + 1) * BLOCK] for i in range(WARPED)]

    finished = []
    for turn in range(V // WARPED):
        finished += some_visits(turn)
    place_copy.wait()
    for visit in range(V):
        for j in range(BLKC):
            piece = lane_block(finished[visit], j)
            to = place_of[0, visit * BLKC + j]
            rows = pl.ds(pl.multiple_of(to % CAP * BODY, TAIL), BODY)
            out[to // CAP, rows] = piece[TAIL:]
            to = place_of[1, visit * BLKC + j]
            rows = pl.ds(pl.multiple_of(CAP * BODY + to % CAP * TAIL, TAIL), TAIL)
            out[to // CAP, rows] = piece[:TAIL]


def warp(patch, slot, owner, weight, ready, order, images, above, devices):
    vmem = pl.BlockSpec(memory_space=pltpu.VMEM)
    sort, unsort = order
    *matrices, rows_high, rows_low, col_weights = ready
    owner = owner.reshape(1, -1)
    args = [patch, slot, owner, weight, *matrices, sort, images]
    places, label, matched = pl.pallas_call(
        match_kernel,
        in_specs=[vmem] * len(args),
        out_specs=[vmem, vmem, vmem],
        out_shape=[
            jax.ShapeDtypeStruct((1, V * BLKC), jnp.int32),
            jax.ShapeDtypeStruct((devices, LANES), F32),
            jax.ShapeDtypeStruct((V, 2, (STRIPS - FREE_FIRST) * STRIP, WIDTH), BF16),
        ],
        scratch_shapes=[
            pltpu.VMEM((MATCHED, 4, OPEN, WIDTH), BF16),
        ],
        compiler_params=pltpu.CompilerParams(vmem_limit_bytes=32 << 20),
        cost_estimate=pl.CostEstimate(
            flops=V * 2 * (STRIPS - FREE_FIRST) * TAPS * STRIP * BAND * WIDTH,
            bytes_accessed=V * (BLOCK * WIDTH * 6),
            transcendentals=0,
        ),
        name="match",
    )(*args)
    args = [
        owner, places, label, *matrices, rows_high, rows_low, col_weights,
        sort, unsort, images, above, matched,
    ]
    return pl.pallas_call(
        warp_kernel,
        in_specs=[vmem] * len(args),
        out_specs=vmem,
        scratch_shapes=[
            pltpu.VMEM((WARPED, 4, STRIP + STEP, WIDTH), BF16),
            pltpu.VMEM((WARPED, 4, STRIP + STEP, WIDTH), BF16),
            pltpu.VMEM((WARPED, 2, STRIP, WIDTH), BF16),
            pltpu.VMEM((WARPED, 2, PAST_STRIPS * STRIP, WIDTH), BF16),
            pltpu.VMEM((8, LANES), jnp.int32),
            pltpu.SMEM((8, LANES), jnp.int32),
            pltpu.SemaphoreType.DMA(()),
        ],
        out_shape=jax.ShapeDtypeStruct((devices, CAP * BLOCK + LABEL, BLOCK), BF16),
        compiler_params=pltpu.CompilerParams(vmem_limit_bytes=32 << 20),
        cost_estimate=pl.CostEstimate(
            flops=V * 2 * STRIPS * TAPS * STRIP * BAND * WIDTH,
            bytes_accessed=V * (BLOCK * WIDTH * 6),
            transcendentals=0,
        ),
        name="warp",
    )(*args)


def coadd_kernel(got, out, total, out_sem):
    devices = got.shape[0]
    wide = devices * CAP * STRIP
    labels = got[:, CAP * BLOCK : CAP * BLOCK + LABEL][:, 0]
    lane = iota((1, wide), 1)
    rank = lane // STRIP % CAP
    source = lane // (STRIP * CAP)

    def spread(entry):
        onehot = (iota((LANES, wide), 0) == rank * 2 + entry).astype(F32).astype(BF16)
        every = jnp.dot(labels, onehot, preferred_element_type=F32)
        return jnp.sum(
            jnp.where(iota((devices, wide), 0) == source, every, 0.0), axis=0, keepdims=True
        )

    weights, cells = spread(0), spread(1)
    row = iota((CELLS * STRIP, 1), 0)
    mine = (cells == (row // STRIP).astype(F32)) & (lane % STRIP == row % STRIP)
    matrix = jnp.where(mine, weights, 0.0)
    sums = jnp.sum(matrix, axis=1, keepdims=True)
    inverse = 1.0 / jnp.maximum(sums, 1.0)
    matrix = matrix.astype(BF16)
    taken = {}
    for r in range(CAP):
        column = jnp.broadcast_to(labels[:, 2 * r : 2 * r + 1].astype(F32), (devices, LANES))
        for s in range(devices):
            taken[s, r] = jnp.broadcast_to(column[s : s + 1], (STRIP, LANES)).astype(BF16) > 0

    def tile(s, r, k):
        device, first = s, r * BODY + k * STRIP
        if first - r * BODY >= BODY:
            device, first = (s + 1) % devices, CAP * BODY + r * TAIL
        return jnp.where(taken[s, r], got[device, first : first + STRIP], jnp.zeros((), BF16))

    copies = []
    for pair in range(BLOCK // STRIP // 2):
        columns = jnp.concatenate(
            [
                jnp.concatenate(
                    [tile(s, r, k) for s in range(devices) for r in range(CAP)], axis=0
                )
                for k in (2 * pair, 2 * pair + 1)
            ],
            axis=1,
        )
        result = jnp.dot(matrix, columns, preferred_element_type=F32) * inverse
        for c in range(CELLS):
            part = result[c * STRIP : (c + 1) * STRIP]
            lanes = slice(c % PSIDE * BLOCK, (c % PSIDE + 1) * BLOCK)
            for n in range(2):
                first = (2 * pair + n) * STRIP
                total[c // PSIDE, first : first + STRIP, lanes] = lane_block(part, n)
        size = 2 * STRIP
        for line in range(PSIDE):
            copies.append(
                pltpu.make_async_copy(
                    total.at[line, pl.ds(pair * size, size)],
                    out.at[0, pl.ds(line * BLOCK + pair * size, size)],
                    out_sem.at[pair, line],
                )
            )
            copies[-1].start()
    for copy in copies:
        copy.wait()


def coadd(got):
    return pl.pallas_call(
        coadd_kernel,
        in_specs=[pl.BlockSpec(memory_space=pltpu.VMEM)],
        out_specs=pl.BlockSpec(memory_space=pl.ANY),
        out_shape=jax.ShapeDtypeStruct((1, PSIDE * BLOCK, PSIDE * BLOCK), F32),
        scratch_shapes=[
            pltpu.VMEM((PSIDE, BLOCK, WIDTH), F32),
            pltpu.SemaphoreType.DMA((BLOCK // STRIP // 2, PSIDE)),
        ],
        compiler_params=pltpu.CompilerParams(vmem_limit_bytes=32 << 20),
        name="coadd",
    )(got)


def shards(
    images, basis_taps, psf_coef, affine, visit_weight, block_patch, block_slot, patch_owner
):
    devices = lax.axis_size("ccd")
    patch = block_patch[:, :, 0]
    head = collect(images, patch)
    above = lax.ppermute(head, "ccd", [(i, (i + 1) % devices) for i in range(devices)])
    order = orders()
    ready = prepare(
        basis_taps.transpose(1, 0, 2), psf_coef.transpose(1, 3, 0, 2), affine.transpose(0, 2, 3, 1),
        devices,
    )
    sent = warp(
        patch, block_slot, patch_owner, visit_weight, ready, order, images, above, devices
    )
    got = lax.all_to_all(sent, "ccd", split_axis=0, concat_axis=0, tiled=True)
    return coadd(got)


def solution(mesh):
    placed = (
        P(None, ("group", "ccd"), None),
        P(),
        P(None, "group", None, None),
        P(None, "group", None, None),
        P(None, "group"),
        P(("group", "ccd"), None, None),
        P(("group", "ccd"), None),
        P("group"),
    )
    return jax.shard_map(
        shards,
        mesh=mesh,
        in_specs=placed,
        out_specs=P(("group", "ccd"), None, None),
        check_vma=False,
    )
```

```python
import functools

import jax
import jax.numpy as jnp
from jax import lax
from jax.experimental import pallas as pl
from jax.experimental.pallas import tpu as pltpu
from jax.sharding import PartitionSpec as P

V = 4
BLOCK = 128
BLKC = 4
SPLIT = 4
TAPS = 11
NBASIS = 9
PSIDE = 4
CELLS = PSIDE * PSIDE
CAP = 2

HALF = TAPS // 2
WARP = 3
RIM = HALF + WARP
TAIL = 16
HEIGHT = SPLIT * BLOCK
WIDTH = BLKC * BLOCK
LANES = 128
LANE_BLOCKS = WIDTH // LANES
STRIP = 16
STEP = 32
STRIPS = -(-(BLOCK + 2 * WARP) // STRIP)
MIDDLE = STRIPS // 2
GROUPS = 6
BAND = 256
PAST_STRIPS = 2
OWN_FIRST = 1
FREE_FIRST = 2
HALVES = 2
MATCHED = 4
WARPED = 4
ROWS = BLOCK // HALVES
WINDOW = ROWS + STRIP
BODY = BLOCK - TAIL
GOT = TAIL + RIM
OPEN = (STRIPS - 1) * STRIP + STEP - FREE_FIRST * STRIP
LABEL = 16
F32 = jnp.float32
BF16 = jnp.bfloat16


def sin_pi(t):
    whole = jnp.round(t)
    f = t - whole
    odd = whole - 2.0 * jnp.floor(0.5 * whole)
    f2 = f * f
    out = 0.0
    for c in (
        0.00046630280576761, -0.0073704309457144, 0.0821458866111282,
        -0.599264529320792, 2.55016403987734, -5.16771278004997, 3.14159265358979,
    ):
        out = out * f2 + c
    return f * out * (1.0 - 2.0 * odd)


def lanczos(t):
    zero = t == 0.0
    safe = jnp.where(zero, 1.0, t)
    pt = jnp.pi * safe
    value = 3.0 * sin_pi(safe) * sin_pi(safe / 3.0) / (pt * pt)
    return jnp.where(jnp.abs(t) < 3.0, jnp.where(zero, 1.0, value), 0.0)


def iota(shape, dim):
    return lax.broadcasted_iota(jnp.int32, shape, dim)


def column_at(lane):
    return lane % LANES * LANE_BLOCKS + lane // LANES


def order_kernel(sort, unsort):
    square = (WIDTH, WIDTH)
    one, none = jnp.ones((), F32), jnp.zeros((), F32)
    goes = iota(square, 0) == column_at(iota((1, WIDTH), 1))
    sort[...] = jnp.where(goes, one, none).astype(BF16)
    comes = iota(square, 1) == column_at(iota((WIDTH, 1), 0))
    unsort[...] = jnp.where(comes, one, none).astype(BF16)


def orders():
    return small_kernel(order_kernel, "orders", [], [((WIDTH, WIDTH), BF16)] * 2)


def lane_block(x, v):
    return x[:, v * LANES : (v + 1) * LANES]


def dot_exact(a, b, dims):
    return lax.dot_general(
        a, b, (dims, ((), ())), precision=lax.Precision.HIGHEST, preferred_element_type=F32
    )


def staircase(x, first):
    return jnp.concatenate(
        [
            pltpu.roll(x[g : g + 8], first + g, 1, stride=1, stride_axis=0)
            for g in range(0, x.shape[0], 8)
        ],
        axis=0,
    )


def lane_sum(terms_of, lane, count, weigh):
    blocks = []
    for v in range(LANE_BLOCKS):
        total = None
        half = count // 2
        for q in range(-(-half // LANE_BLOCKS) * -1, (half + LANE_BLOCKS - 1) // LANE_BLOCKS + 1):
            part = None
            for u in range(count):
                if (v + u - half) // LANE_BLOCKS != q:
                    continue
                piece = terms_of(u, v, (v + u - half) % LANE_BLOCKS)
                part = piece if part is None else part + piece
            if part is None:
                continue
            if q:
                part = pltpu.roll(part, -q % LANES, 1)
                if not weigh:
                    part = jnp.where((lane + q >= 0) & (lane + q < LANES), part, 0.0)
            total = part if total is None else total + part
        blocks.append(total)
    return blocks


def whereabouts(devices):
    band = lax.axis_index("ccd")
    past = lax.rem(band + devices - 1, devices)
    quarter = (band + SPLIT // 2) % SPLIT
    own = ((band + SPLIT // 2) // SPLIT, quarter * BLOCK - TAIL)
    before = ((past + SPLIT // 2) // SPLIT, (past + SPLIT // 2) % SPLIT * BLOCK + BODY)
    return (own, before), (quarter > 0) & (band > 0)


def collect_kernel(images, patch, head, numbers, sems):
    copies = [
        pltpu.make_async_copy(
            images.at[v, pl.ds(BLOCK - GOT, GOT)], head.at[pl.ds(v * GOT, GOT)], sems.at[v]
        )
        for v in range(V)
    ]
    names = pltpu.make_async_copy(patch, numbers, sems.at[V])
    names.start()
    for copy in copies:
        copy.start()
    head[V * GOT :] = jnp.zeros((8, WIDTH), F32)
    names.wait()
    head[V * GOT : V * GOT + 1, : V * BLKC] = numbers[...].astype(F32)
    for copy in copies:
        copy.wait()


def collect(images, patch):
    return pl.pallas_call(
        collect_kernel,
        in_specs=[pl.BlockSpec(memory_space=pl.ANY)] * 2,
        out_specs=pl.BlockSpec(memory_space=pltpu.VMEM),
        out_shape=jax.ShapeDtypeStruct((V * GOT + 8, WIDTH), F32),
        scratch_shapes=[pltpu.VMEM(patch.shape, jnp.int32), pltpu.SemaphoreType.DMA((V + 1,))],
        name="collect",
    )(images, patch)


def lanczos_weights(devices, affine, cols_out):
    bands, same = whereabouts(devices)
    lane = iota((1, LANES), 1)
    lanes = iota((8, WIDTH), 1)
    step = iota((8, WIDTH), 0) - WARP
    block = lanes // LANES
    carry = (block + step + LANE_BLOCKS) // LANE_BLOCKS - 1
    from_lane = lanes % LANES - carry
    col = (from_lane * LANE_BLOCKS + block).astype(F32)
    within = (from_lane >= 0) & (from_lane < LANES) & (step <= WARP)
    offset = iota((8, LANES), 0) - WARP
    crosses = (lane + offset >= TAIL) != (lane >= TAIL)
    keep = (offset <= WARP) & (same | jnp.logical_not(crosses))
    def terms_of(n, visit):
        here = iota((1, 1, affine.shape[3]), 2) == bands[n][0]
        return jnp.sum(jnp.where(here, affine[visit], 0.0), axis=2, keepdims=True)

    def columns(n, visit):
        a = terms_of(n, visit)
        col_shift = a[1, 0:1] + a[1, 1:2] * (col - (WIDTH - 1) / 2.0) / WIDTH
        cols_out[n * V + visit] = jnp.where(within, lanczos(col_shift - step.astype(F32)), 0.0)

    by_row = []
    for visit in range(V):
        columns(0, visit)
        shifts = []
        for n, (_, top_row) in enumerate(bands):
            a = terms_of(n, visit)
            row = (top_row + lane).astype(F32)
            shifts.append(a[0, 0:1] + a[0, 1:2] * (row - (HEIGHT - 1) / 2.0) / HEIGHT)
        shift = jnp.where(lane < TAIL, shifts[1], shifts[0])
        weights = jnp.where(keep, lanczos(shift - offset.astype(F32)), 0.0)
        by_row.append(jnp.concatenate([weights, jnp.zeros((LANES - 8, LANES), F32)], axis=0).T)

    @pl.when(jnp.logical_not(same))
    def _():
        for visit in range(V):
            columns(1, visit)

    return by_row


def prepare_kernel(
    devices, taps, psf, affine, high_level, step_level, slope, rows_high, rows_low, cols_out
):
    row_weights = lanczos_weights(devices, affine, cols_out)
    bands, same = whereabouts(devices)
    band_lane = iota((1, BAND), 1)
    seg = band_lane // STEP
    lane = iota((1, LANES), 1)
    tap = band_lane - seg * STEP
    onehot = (tap == iota((TAPS, BAND), 0)) & (seg < GROUPS)
    row_taps = dot_exact(taps[:, 0], onehot.astype(F32), ((1,), (0,)))
    eye = (iota((TAPS, STRIP), 0) == iota((TAPS, STRIP), 1)).astype(F32)
    turned_taps = dot_exact(eye, taps[:, 1], ((0,), (1,)))
    def make(n, visit):
        ccd, top_row = bands[n]
        lhs = jnp.concatenate(
            [turned_taps * psf[ccd, c, visit : visit + 1, :] for c in range(3)], axis=0
        )
        kernels = dot_exact(lhs, row_taps, ((1,), (0,)))
        const, by_row, by_col = (kernels[c * STRIP : (c + 1) * STRIP] for c in range(3))
        is_level = seg < 3
        per_strip = 2.0 * STRIP / HEIGHT
        middle_row = (top_row + (MIDDLE * STRIP - WARP)).astype(F32)
        middle_pos = (2.0 * middle_row + 1.0) / HEIGHT - 1.0
        col_move = (iota((STRIP, 1), 0) - HALF).astype(F32) * (2.0 / WIDTH)
        by_row = jnp.where(is_level, by_row, 0.0)
        const = jnp.where(is_level, const + middle_pos * by_row - col_move * by_col, by_col)
        reach = per_strip * (STRIPS - MIDDLE)
        largest = jnp.max(jnp.abs(const) + reach * jnp.abs(by_row), axis=(0, 1), keepdims=True)
        unit = jnp.maximum(largest, 1e-30) * (1.0 / 200.0)
        const = const / unit
        by_row = (by_row * per_strip) / unit
        low_lanes = (lane // STEP) % 3 == 2
        low_band = seg % 3 == 2
        row_part = iota((STRIP, 1), 0).astype(F32) * (1.0 / STRIP)
        for u in range(TAPS):
            at = slice(u * STRIP, (u + 1) * STRIP)
            one = jnp.broadcast_to(const[u : u + 1], (STRIP, BAND))
            x, tail = staircase(one[:, :LANES], 0), staircase(one[:, LANES:], 0)
            y = staircase(jnp.broadcast_to(by_row[u : u + 1, :LANES], (STRIP, LANES)), 0)
            high = tail.astype(BF16).astype(F32)
            slope[n * V + visit, at] = jnp.where(low_band[:, LANES:], tail - high, high).astype(BF16)
            x = x + row_part * y
            high = jnp.where(lane < 3 * STEP, jnp.round(x), x.astype(BF16).astype(F32))
            high_level[n * V + visit, at] = jnp.where(low_lanes, x - high, high)
            high = jnp.round(y)
            step_level[n * V + visit, at] = jnp.where(low_lanes, y - high, high)
        return unit

    def put(visit, at, matrix):
        high = matrix.astype(BF16)
        rows_high[visit, at] = high
        rows_low[visit, at] = (matrix - high.astype(F32)).astype(BF16)

    for visit in range(V):
        weights = row_weights[visit] * make(0, visit)
        put(visit, slice(0, TAIL), staircase(weights[:TAIL], 0))
        put(visit, slice(TAIL, ROWS), staircase(weights[TAIL:ROWS], PAST_STRIPS * STRIP))
        put(visit, slice(ROWS, BLOCK), staircase(weights[ROWS:], 0))

    @pl.when(jnp.logical_not(same))
    def _():
        for visit in range(V):
            weights = row_weights[visit][:TAIL] * make(1, visit)
            put(visit, slice(0, TAIL), staircase(weights, 0))


def small_kernel(body, name, args, shapes):
    vmem = pl.BlockSpec(memory_space=pltpu.VMEM)
    return pl.pallas_call(
        body,
        in_specs=[vmem] * len(args),
        out_specs=[vmem] * len(shapes),
        out_shape=[jax.ShapeDtypeStruct(shape, kind) for shape, kind in shapes],
        compiler_params=pltpu.CompilerParams(vmem_limit_bytes=32 << 20),
        cost_estimate=pl.CostEstimate(flops=1 << 30, bytes_accessed=1 << 20, transcendentals=0),
        name=name,
    )(*args)


def prepare(taps, psf, affine, devices):
    return small_kernel(
        functools.partial(prepare_kernel, devices), "matrices", [taps, psf, affine],
        [
            ((2 * V, TAPS * STRIP, LANES), F32),
            ((2 * V, TAPS * STRIP, LANES), F32),
            ((2 * V, TAPS * STRIP, BAND - LANES), BF16),
            ((V, BLOCK, LANES), BF16),
            ((V, BLOCK, LANES), BF16),
            ((2 * V, 8, WIDTH), F32),
        ],
    )


def sorted_rows(raw, sort):
    col_pos = (2.0 * column_at(iota((1, WIDTH), 1)).astype(F32) + 1.0) / WIDTH - 1.0
    count = raw.shape[0]
    raw_high = raw.astype(BF16)
    raw_low = (raw - raw_high.astype(F32)).astype(BF16)
    both = jnp.dot(
        jnp.concatenate([raw_high, raw_low], axis=0), sort, preferred_element_type=F32
    )
    high, low = both[:count], both[count:]
    tilted = (high + low) * col_pos
    tilted_high = tilted.astype(BF16).astype(F32)
    return high, low, tilted_high, tilted - tilted_high


def match_strip(level, step, slope, source, first, k):
    lane = iota((1, LANES), 1)
    if k != MIDDLE:
        level = level + float(k - MIDDLE) * step
    matrix = jnp.concatenate([level.astype(BF16), slope], axis=1)
    filler = jnp.zeros((BAND - GROUPS * STEP, WIDTH), BF16)
    rows = slice(first, first + STEP)
    columns = jnp.concatenate([source[h, rows] for h in (0, 1, 0, 2, 3, 2)] + [filler], axis=0)
    results = jnp.dot(matrix, columns, preferred_element_type=F32)
    blocks = lane_sum(
        lambda u, v, w: lane_block(results[u * STRIP : (u + 1) * STRIP], w), lane, TAPS, False
    )
    matched = jnp.concatenate(blocks, axis=1)
    high = matched.astype(BF16)
    return high, (matched - high.astype(F32)).astype(BF16)


def upright(line):
    count = line.shape[1]
    square = (count, count)
    return jnp.sum(
        jnp.where(iota(square, 0) == iota(square, 1), jnp.broadcast_to(line, square), 0),
        axis=1, keepdims=True,
    )


def route(patch, owner):
    square = (patch.shape[1], patch.shape[1])
    earlier = (iota(square, 0) < iota(square, 1)) & (upright(patch) == patch)
    rank = jnp.sum(earlier.astype(jnp.int32), axis=0, keepdims=True)
    named = iota((owner.shape[1], patch.shape[1]), 0) == patch
    to = jnp.sum(jnp.where(named, upright(owner), 0), axis=0, keepdims=True)
    return to, rank


def match_kernel(
    patch, slot, owner, weight, high_level, step_level, slope, sort, image,
    places, label, matched_terms, terms,
):
    ((ccd, _), _), _ = whereabouts(label.shape[0])
    to, rank = route(patch[...], owner[...])
    places[...] = to * CAP + rank

    own = jnp.where(iota(weight.shape, 1) == ccd, weight[...].astype(F32), 0.0)
    own = jnp.sum(own, axis=1, keepdims=True)
    each = (V, V * BLKC)
    weights = jnp.sum(
        jnp.where(iota(each, 1) // BLKC == iota(each, 0), own, 0.0), axis=0, keepdims=True
    )
    goes = iota((label.shape[0], V * BLKC), 0) == to
    lane = iota(label.shape, 1)
    lines = jnp.zeros(label.shape, F32)
    for r in range(CAP):
        for n, value in enumerate((weights, slot[...].astype(F32))):
            column = jnp.sum(jnp.where(goes & (rank == r), value, 0.0), axis=1, keepdims=True)
            lines = jnp.where(lane == 2 * r + n, column, lines)
    label[...] = lines

    open_row = FREE_FIRST * STRIP - GOT
    seen = OPEN - STRIP
    terms[:, :, seen:] = jnp.zeros((MATCHED, 4, STRIP, WIDTH), BF16)

    def some_visits(turn, _):
        visits = [turn * MATCHED + i for i in range(MATCHED)]
        for i, visit in enumerate(visits):
            rows = sorted_rows(image[visit, open_row : open_row + seen], sort[...])
            for h, value in enumerate(rows):
                terms[i, h, :seen] = value.astype(BF16)
        for k in range(FREE_FIRST, STRIPS):
            first = (k - FREE_FIRST) * STRIP
            for i, visit in enumerate(visits):
                at = slice(first, first + STRIP)
                matched_terms[visit, 0, at], matched_terms[visit, 1, at] = match_strip(
                    high_level[visit], step_level[visit], slope[visit], terms.at[i], first, k
                )
        return 0

    lax.fori_loop(0, V // MATCHED, some_visits, 0)


def warp_kernel(
    owner, places, label, high_level, step_level, slope, rows_high, rows_low, col_weights,
    sort, unsort, image, above, matched_free, out,
    own_terms, past_terms, own_matched, past_matched, both_places, place_of, place_sem,
):
    devices = label.shape[0]
    _, same = whereabouts(devices)
    past_patch = above[V * GOT : V * GOT + 1, : V * BLKC].astype(jnp.int32)
    to, rank = route(past_patch, owner[...])
    both_places[0:1, : V * BLKC] = places[...]
    both_places[1:2, : V * BLKC] = to * CAP + rank
    place_copy = pltpu.make_async_copy(both_places, place_of, place_sem)
    place_copy.start()
    lane = iota((1, LANES), 1)
    out[:, CAP * BLOCK :] = jnp.broadcast_to(
        label[...].reshape(devices, 1, LANES), (devices, LABEL, LANES)
    ).astype(BF16)

    seam = STRIP + STEP
    foreign = iota((seam, 1), 0) < GOT
    both = jnp.where(same, 1.0, 0.0)
    past = jnp.where(same, 0, V)
    own_sees = jnp.where(foreign, both, 1.0)
    past_sees = jnp.where(foreign, 1.0, both)

    def some_visits(turn, _):
        visits = [turn * WARPED + i for i in range(WARPED)]
        for i, visit in enumerate(visits):
            tail = pl.ds(pl.multiple_of(visit * GOT, 8), GOT)
            raw = jnp.concatenate([above[tail], image[visit, : seam - GOT]], axis=0)
            for h, value in enumerate(sorted_rows(raw, sort[...])):
                own_terms[i, h] = (value * own_sees).astype(BF16)
                past_terms[i, h] = (value * past_sees).astype(BF16)
        for i, visit in enumerate(visits):
            own_matched[i, 0], own_matched[i, 1] = match_strip(
                high_level[visit], step_level[visit], slope[visit],
                own_terms.at[i], OWN_FIRST * STRIP, OWN_FIRST,
            )
        for k in range(PAST_STRIPS):
            for i, visit in enumerate(visits):
                at = slice(k * STRIP, (k + 1) * STRIP)
                past_matched[i, 0, at], past_matched[i, 1, at] = match_strip(
                    high_level[past + visit], step_level[past + visit], slope[past + visit],
                    past_terms.at[i], k * STRIP, k,
                )

        warped = []
        for i, visit in enumerate(visits):
            halves = []
            for h in range(HALVES):
                at = slice(h * ROWS, (h + 1) * ROWS)
                high, low = rows_high[visit, at], rows_low[visit, at]
                free = FREE_FIRST * STRIP

                def under(term):
                    if h == 0:
                        parts = [
                            past_matched[i, term],
                            own_matched[i, term],
                            matched_free[visit, term, : WINDOW - free],
                        ]
                    else:
                        parts = [matched_free[visit, term, ROWS - free :]]
                    left = LANES - sum([x.shape[0] for x in parts])
                    return jnp.concatenate(parts + [jnp.zeros((left, WIDTH), BF16)], axis=0)

                first = under(0)
                total = jnp.dot(
                    jnp.concatenate([high, high], axis=1),
                    jnp.concatenate([first, under(1)], axis=0),
                    preferred_element_type=F32,
                )
                halves.append(total + jnp.dot(low, first, preferred_element_type=F32))
            warped.append(jnp.concatenate(halves, axis=0))

        @pl.when(turn == 0)
        def _():
            place_copy.wait()

        for i, visit in enumerate(visits):
            parts = []
            for rows, weights in (
                (slice(0, TAIL), col_weights[past + visit]),
                (slice(TAIL, BLOCK), col_weights[visit]),
            ):
                some = warped[i][rows]
                blocks = lane_sum(
                    lambda s, v, w: lane_block(weights[s : s + 1], v) * lane_block(some, w),
                    lane, 2 * WARP + 1, True,
                )
                parts.append(jnp.concatenate(blocks, axis=1).astype(BF16))
            result = jnp.dot(
                jnp.concatenate(parts, axis=0), unsort[...], preferred_element_type=F32
            ).astype(BF16)
            for j in range(BLKC):
                piece = lane_block(result, j)
                to = place_of[0, visit * BLKC + j]
                rows = pl.ds(pl.multiple_of(to % CAP * BODY, TAIL), BODY)
                out[to // CAP, rows] = piece[TAIL:]
                to = place_of[1, visit * BLKC + j]
                rows = pl.ds(pl.multiple_of(CAP * BODY + to % CAP * TAIL, TAIL), TAIL)
                out[to // CAP, rows] = piece[:TAIL]
        return 0

    lax.fori_loop(0, V // WARPED, some_visits, 0)


def warp(patch, slot, owner, weight, ready, order, images, above, devices):
    vmem = pl.BlockSpec(memory_space=pltpu.VMEM)
    sort, unsort = order
    *matrices, rows_high, rows_low, col_weights = ready
    owner = owner.reshape(1, -1)
    args = [patch, slot, owner, weight, *matrices, sort, images]
    places, label, matched = pl.pallas_call(
        match_kernel,
        in_specs=[vmem] * len(args),
        out_specs=[vmem, vmem, vmem],
        out_shape=[
            jax.ShapeDtypeStruct((1, V * BLKC), jnp.int32),
            jax.ShapeDtypeStruct((devices, LANES), F32),
            jax.ShapeDtypeStruct((V, 2, (STRIPS - FREE_FIRST) * STRIP, WIDTH), BF16),
        ],
        scratch_shapes=[
            pltpu.VMEM((MATCHED, 4, OPEN, WIDTH), BF16),
        ],
        compiler_params=pltpu.CompilerParams(vmem_limit_bytes=32 << 20),
        cost_estimate=pl.CostEstimate(
            flops=V * 2 * (STRIPS - FREE_FIRST) * TAPS * STRIP * BAND * WIDTH,
            bytes_accessed=V * (BLOCK * WIDTH * 6),
            transcendentals=0,
        ),
        name="match",
    )(*args)
    args = [
        owner, places, label, *matrices, rows_high, rows_low, col_weights,
        sort, unsort, images, above, matched,
    ]
    return pl.pallas_call(
        warp_kernel,
        in_specs=[vmem] * len(args),
        out_specs=vmem,
        scratch_shapes=[
            pltpu.VMEM((WARPED, 4, STRIP + STEP, WIDTH), BF16),
            pltpu.VMEM((WARPED, 4, STRIP + STEP, WIDTH), BF16),
            pltpu.VMEM((WARPED, 2, STRIP, WIDTH), BF16),
            pltpu.VMEM((WARPED, 2, PAST_STRIPS * STRIP, WIDTH), BF16),
            pltpu.VMEM((8, LANES), jnp.int32),
            pltpu.SMEM((8, LANES), jnp.int32),
            pltpu.SemaphoreType.DMA(()),
        ],
        out_shape=jax.ShapeDtypeStruct((devices, CAP * BLOCK + LABEL, BLOCK), BF16),
        compiler_params=pltpu.CompilerParams(vmem_limit_bytes=32 << 20),
        cost_estimate=pl.CostEstimate(
            flops=V * 2 * STRIPS * TAPS * STRIP * BAND * WIDTH,
            bytes_accessed=V * (BLOCK * WIDTH * 6),
            transcendentals=0,
        ),
        name="warp",
    )(*args)


def coadd_kernel(got, out, total, out_sem):
    devices = got.shape[0]
    wide = devices * CAP * STRIP
    labels = got[:, CAP * BLOCK : CAP * BLOCK + LABEL][:, 0]
    lane = iota((1, wide), 1)
    rank = lane // STRIP % CAP
    source = lane // (STRIP * CAP)

    def spread(entry):
        onehot = (iota((LANES, wide), 0) == rank * 2 + entry).astype(F32).astype(BF16)
        every = jnp.dot(labels, onehot, preferred_element_type=F32)
        return jnp.sum(
            jnp.where(iota((devices, wide), 0) == source, every, 0.0), axis=0, keepdims=True
        )

    weights, cells = spread(0), spread(1)
    row = iota((CELLS * STRIP, 1), 0)
    mine = (cells == (row // STRIP).astype(F32)) & (lane % STRIP == row % STRIP)
    matrix = jnp.where(mine, weights, 0.0)
    sums = jnp.sum(matrix, axis=1, keepdims=True)
    inverse = 1.0 / jnp.maximum(sums, 1.0)
    matrix = matrix.astype(BF16)
    taken = {}
    for r in range(CAP):
        column = jnp.broadcast_to(labels[:, 2 * r : 2 * r + 1].astype(F32), (devices, LANES))
        for s in range(devices):
            taken[s, r] = jnp.broadcast_to(column[s : s + 1], (STRIP, LANES)).astype(BF16) > 0

    def tile(s, r, k):
        device, first = s, r * BODY + k * STRIP
        if first - r * BODY >= BODY:
            device, first = (s + 1) % devices, CAP * BODY + r * TAIL
        return jnp.where(taken[s, r], got[device, first : first + STRIP], jnp.zeros((), BF16))

    copies = []
    for pair in range(BLOCK // STRIP // 2):
        columns = jnp.concatenate(
            [
                jnp.concatenate(
                    [tile(s, r, k) for s in range(devices) for r in range(CAP)], axis=0
                )
                for k in (2 * pair, 2 * pair + 1)
            ],
            axis=1,
        )
        result = jnp.dot(matrix, columns, preferred_element_type=F32) * inverse
        for c in range(CELLS):
            part = result[c * STRIP : (c + 1) * STRIP]
            lanes = slice(c % PSIDE * BLOCK, (c % PSIDE + 1) * BLOCK)
            for n in range(2):
                first = (2 * pair + n) * STRIP
                total[c // PSIDE, first : first + STRIP, lanes] = lane_block(part, n)
        size = 2 * STRIP
        for line in range(PSIDE):
            copies.append(
                pltpu.make_async_copy(
                    total.at[line, pl.ds(pair * size, size)],
                    out.at[0, pl.ds(line * BLOCK + pair * size, size)],
                    out_sem.at[pair, line],
                )
            )
            copies[-1].start()
    for copy in copies:
        copy.wait()


def coadd(got):
    return pl.pallas_call(
        coadd_kernel,
        in_specs=[pl.BlockSpec(memory_space=pltpu.VMEM)],
        out_specs=pl.BlockSpec(memory_space=pl.ANY),
        out_shape=jax.ShapeDtypeStruct((1, PSIDE * BLOCK, PSIDE * BLOCK), F32),
        scratch_shapes=[
            pltpu.VMEM((PSIDE, BLOCK, WIDTH), F32),
            pltpu.SemaphoreType.DMA((BLOCK // STRIP // 2, PSIDE)),
        ],
        compiler_params=pltpu.CompilerParams(vmem_limit_bytes=32 << 20),
        name="coadd",
    )(got)


def shards(
    images, basis_taps, psf_coef, affine, visit_weight, block_patch, block_slot, patch_owner
):
    devices = lax.axis_size("ccd")
    patch = block_patch[:, :, 0]
    head = collect(images, patch)
    above = lax.ppermute(head, "ccd", [(i, (i + 1) % devices) for i in range(devices)])
    order = orders()
    ready = prepare(
        basis_taps.transpose(1, 0, 2), psf_coef.transpose(1, 3, 0, 2), affine.transpose(0, 2, 3, 1),
        devices,
    )
    sent = warp(
        patch, block_slot, patch_owner, visit_weight, ready, order, images, above, devices
    )
    got = lax.all_to_all(sent, "ccd", split_axis=0, concat_axis=0, tiled=True)
    return coadd(got)


def solution(mesh):
    placed = (
        P(None, ("group", "ccd"), None),
        P(),
        P(None, "group", None, None),
        P(None, "group", None, None),
        P(None, "group"),
        P(("group", "ccd"), None, None),
        P(("group", "ccd"), None),
        P("group"),
    )
    return jax.shard_map(
        shards,
        mesh=mesh,
        in_specs=placed,
        out_specs=P(("group", "ccd"), None, None),
        check_vma=False,
    )
```

```python
import functools

import jax
import jax.numpy as jnp
from jax import lax
from jax.experimental import pallas as pl
from jax.experimental.pallas import tpu as pltpu
from jax.sharding import PartitionSpec as P

V = 4
BLOCK = 128
BLKC = 4
SPLIT = 4
TAPS = 11
NBASIS = 9
PSIDE = 4
CELLS = PSIDE * PSIDE
CAP = 2

HALF = TAPS // 2
WARP = 3
RIM = HALF + WARP
TAIL = 16
HEIGHT = SPLIT * BLOCK
WIDTH = BLKC * BLOCK
LANES = 128
LANE_BLOCKS = WIDTH // LANES
STRIP = 16
STEP = 32
STRIPS = -(-(BLOCK + 2 * WARP) // STRIP)
MIDDLE = STRIPS // 2
GROUPS = 6
BAND = 256
PAST_STRIPS = 2
OWN_FIRST = 1
FREE_FIRST = 2
HALVES = 2
MATCHED = 4
WARPED = 4
ROWS = BLOCK // HALVES
WINDOW = ROWS + STRIP
BODY = BLOCK - TAIL
GOT = TAIL + RIM
OPEN = (STRIPS - 1) * STRIP + STEP - FREE_FIRST * STRIP
LABEL = 16
F32 = jnp.float32
BF16 = jnp.bfloat16


def sin_pi(t):
    whole = jnp.round(t)
    f = t - whole
    odd = whole - 2.0 * jnp.floor(0.5 * whole)
    f2 = f * f
    out = 0.0
    for c in (
        0.00046630280576761, -0.0073704309457144, 0.0821458866111282,
        -0.599264529320792, 2.55016403987734, -5.16771278004997, 3.14159265358979,
    ):
        out = out * f2 + c
    return f * out * (1.0 - 2.0 * odd)


def lanczos(t):
    zero = t == 0.0
    safe = jnp.where(zero, 1.0, t)
    pt = jnp.pi * safe
    value = 3.0 * sin_pi(safe) * sin_pi(safe / 3.0) / (pt * pt)
    return jnp.where(jnp.abs(t) < 3.0, jnp.where(zero, 1.0, value), 0.0)


def iota(shape, dim):
    return lax.broadcasted_iota(jnp.int32, shape, dim)


def column_at(lane):
    return lane % LANES * LANE_BLOCKS + lane // LANES


def order_kernel(sort, unsort):
    square = (WIDTH, WIDTH)
    one, none = jnp.ones((), F32), jnp.zeros((), F32)
    goes = iota(square, 0) == column_at(iota((1, WIDTH), 1))
    sort[...] = jnp.where(goes, one, none).astype(BF16)
    comes = iota(square, 1) == column_at(iota((WIDTH, 1), 0))
    unsort[...] = jnp.where(comes, one, none).astype(BF16)


def orders():
    return small_kernel(order_kernel, "orders", [], [((WIDTH, WIDTH), BF16)] * 2)


def lane_block(x, v):
    return x[:, v * LANES : (v + 1) * LANES]


def dot_exact(a, b, dims):
    return lax.dot_general(
        a, b, (dims, ((), ())), precision=lax.Precision.HIGHEST, preferred_element_type=F32
    )


def staircase(x, first):
    return jnp.concatenate(
        [
            pltpu.roll(x[g : g + 8], first + g, 1, stride=1, stride_axis=0)
            for g in range(0, x.shape[0], 8)
        ],
        axis=0,
    )


def lane_sum(terms_of, lane, count, weigh):
    blocks = []
    for v in range(LANE_BLOCKS):
        total = None
        half = count // 2
        for q in range(-(-half // LANE_BLOCKS) * -1, (half + LANE_BLOCKS - 1) // LANE_BLOCKS + 1):
            part = None
            for u in range(count):
                if (v + u - half) // LANE_BLOCKS != q:
                    continue
                piece = terms_of(u, v, (v + u - half) % LANE_BLOCKS)
                part = piece if part is None else part + piece
            if part is None:
                continue
            if q:
                part = pltpu.roll(part, -q % LANES, 1)
                if not weigh:
                    part = jnp.where((lane + q >= 0) & (lane + q < LANES), part, 0.0)
            total = part if total is None else total + part
        blocks.append(total)
    return blocks


def whereabouts(devices):
    band = lax.axis_index("ccd")
    past = lax.rem(band + devices - 1, devices)
    quarter = (band + SPLIT // 2) % SPLIT
    own = ((band + SPLIT // 2) // SPLIT, quarter * BLOCK - TAIL)
    before = ((past + SPLIT // 2) // SPLIT, (past + SPLIT // 2) % SPLIT * BLOCK + BODY)
    return (own, before), (quarter > 0) & (band > 0)


def lanczos_weights(devices, affine, cols_out):
    bands, same = whereabouts(devices)
    lane = iota((1, LANES), 1)
    lanes = iota((8, WIDTH), 1)
    step = iota((8, WIDTH), 0) - WARP
    block = lanes // LANES
    carry = (block + step + LANE_BLOCKS) // LANE_BLOCKS - 1
    from_lane = lanes % LANES - carry
    col = (from_lane * LANE_BLOCKS + block).astype(F32)
    within = (from_lane >= 0) & (from_lane < LANES) & (step <= WARP)
    offset = iota((8, LANES), 0) - WARP
    crosses = (lane + offset >= TAIL) != (lane >= TAIL)
    keep = (offset <= WARP) & (same | jnp.logical_not(crosses))
    def terms_of(n, visit):
        here = iota((1, 1, affine.shape[3]), 2) == bands[n][0]
        return jnp.sum(jnp.where(here, affine[visit], 0.0), axis=2, keepdims=True)

    def columns(n, visit):
        a = terms_of(n, visit)
        col_shift = a[1, 0:1] + a[1, 1:2] * (col - (WIDTH - 1) / 2.0) / WIDTH
        cols_out[n * V + visit] = jnp.where(within, lanczos(col_shift - step.astype(F32)), 0.0)

    by_row = []
    for visit in range(V):
        columns(0, visit)
        shifts = []
        for n, (_, top_row) in enumerate(bands):
            a = terms_of(n, visit)
            row = (top_row + lane).astype(F32)
            shifts.append(a[0, 0:1] + a[0, 1:2] * (row - (HEIGHT - 1) / 2.0) / HEIGHT)
        shift = jnp.where(lane < TAIL, shifts[1], shifts[0])
        weights = jnp.where(keep, lanczos(shift - offset.astype(F32)), 0.0)
        by_row.append(jnp.concatenate([weights, jnp.zeros((LANES - 8, LANES), F32)], axis=0).T)

    @pl.when(jnp.logical_not(same))
    def _():
        for visit in range(V):
            columns(1, visit)

    return by_row


def prepare_kernel(
    devices, taps, psf, affine, high_level, step_level, slope, rows_high, rows_low, cols_out
):
    row_weights = lanczos_weights(devices, affine, cols_out)
    bands, same = whereabouts(devices)
    band_lane = iota((1, BAND), 1)
    seg = band_lane // STEP
    lane = iota((1, LANES), 1)
    tap = band_lane - seg * STEP
    onehot = (tap == iota((TAPS, BAND), 0)) & (seg < GROUPS)
    row_taps = dot_exact(taps[:, 0], onehot.astype(F32), ((1,), (0,)))
    eye = (iota((TAPS, STRIP), 0) == iota((TAPS, STRIP), 1)).astype(F32)
    turned_taps = dot_exact(eye, taps[:, 1], ((0,), (1,)))
    def make(n, visit):
        ccd, top_row = bands[n]
        lhs = jnp.concatenate(
            [turned_taps * psf[ccd, c, visit : visit + 1, :] for c in range(3)], axis=0
        )
        kernels = dot_exact(lhs, row_taps, ((1,), (0,)))
        const, by_row, by_col = (kernels[c * STRIP : (c + 1) * STRIP] for c in range(3))
        is_level = seg < 3
        per_strip = 2.0 * STRIP / HEIGHT
        middle_row = (top_row + (MIDDLE * STRIP - WARP)).astype(F32)
        middle_pos = (2.0 * middle_row + 1.0) / HEIGHT - 1.0
        col_move = (iota((STRIP, 1), 0) - HALF).astype(F32) * (2.0 / WIDTH)
        by_row = jnp.where(is_level, by_row, 0.0)
        const = jnp.where(is_level, const + middle_pos * by_row - col_move * by_col, by_col)
        reach = per_strip * (STRIPS - MIDDLE)
        largest = jnp.max(jnp.abs(const) + reach * jnp.abs(by_row), axis=(0, 1), keepdims=True)
        unit = jnp.maximum(largest, 1e-30) * (1.0 / 200.0)
        const = const / unit
        by_row = (by_row * per_strip) / unit
        low_lanes = (lane // STEP) % 3 == 2
        low_band = seg % 3 == 2
        row_part = iota((STRIP, 1), 0).astype(F32) * (1.0 / STRIP)
        for u in range(TAPS):
            at = slice(u * STRIP, (u + 1) * STRIP)
            one = jnp.broadcast_to(const[u : u + 1], (STRIP, BAND))
            x, tail = staircase(one[:, :LANES], 0), staircase(one[:, LANES:], 0)
            y = staircase(jnp.broadcast_to(by_row[u : u + 1, :LANES], (STRIP, LANES)), 0)
            high = tail.astype(BF16).astype(F32)
            slope[n * V + visit, at] = jnp.where(low_band[:, LANES:], tail - high, high).astype(BF16)
            x = x + row_part * y
            high = jnp.where(lane < 3 * STEP, jnp.round(x), x.astype(BF16).astype(F32))
            high_level[n * V + visit, at] = jnp.where(low_lanes, x - high, high)
            high = jnp.round(y)
            step_level[n * V + visit, at] = jnp.where(low_lanes, y - high, high)
        return unit

    def put(visit, at, matrix):
        high = matrix.astype(BF16)
        rows_high[visit, at] = high
        rows_low[visit, at] = (matrix - high.astype(F32)).astype(BF16)

    for visit in range(V):
        weights = row_weights[visit] * make(0, visit)
        put(visit, slice(0, TAIL), staircase(weights[:TAIL], 0))
        put(visit, slice(TAIL, ROWS), staircase(weights[TAIL:ROWS], PAST_STRIPS * STRIP))
        put(visit, slice(ROWS, BLOCK), staircase(weights[ROWS:], 0))

    @pl.when(jnp.logical_not(same))
    def _():
        for visit in range(V):
            weights = row_weights[visit][:TAIL] * make(1, visit)
            put(visit, slice(0, TAIL), staircase(weights, 0))


def small_kernel(body, name, args, shapes):
    vmem = pl.BlockSpec(memory_space=pltpu.VMEM)
    return pl.pallas_call(
        body,
        in_specs=[vmem] * len(args),
        out_specs=[vmem] * len(shapes),
        out_shape=[jax.ShapeDtypeStruct(shape, kind) for shape, kind in shapes],
        compiler_params=pltpu.CompilerParams(vmem_limit_bytes=32 << 20),
        cost_estimate=pl.CostEstimate(flops=1 << 30, bytes_accessed=1 << 20, transcendentals=0),
        name=name,
    )(*args)


def prepare(taps, psf, affine, devices):
    return small_kernel(
        functools.partial(prepare_kernel, devices), "matrices", [taps, psf, affine],
        [
            ((2 * V, TAPS * STRIP, LANES), F32),
            ((2 * V, TAPS * STRIP, LANES), F32),
            ((2 * V, TAPS * STRIP, BAND - LANES), BF16),
            ((V, BLOCK, LANES), BF16),
            ((V, BLOCK, LANES), BF16),
            ((2 * V, 8, WIDTH), F32),
        ],
    )


def sorted_rows(raw, sort):
    col_pos = (2.0 * column_at(iota((1, WIDTH), 1)).astype(F32) + 1.0) / WIDTH - 1.0
    count = raw.shape[0]
    raw_high = raw.astype(BF16)
    raw_low = (raw - raw_high.astype(F32)).astype(BF16)
    both = jnp.dot(
        jnp.concatenate([raw_high, raw_low], axis=0), sort, preferred_element_type=F32
    )
    high, low = both[:count], both[count:]
    tilted = (high + low) * col_pos
    tilted_high = tilted.astype(BF16).astype(F32)
    return high, low, tilted_high, tilted - tilted_high


def match_strip(level, step, slope, source, first, k):
    lane = iota((1, LANES), 1)
    if k != MIDDLE:
        level = level + float(k - MIDDLE) * step
    matrix = jnp.concatenate([level.astype(BF16), slope], axis=1)
    filler = jnp.zeros((BAND - GROUPS * STEP, WIDTH), BF16)
    rows = slice(first, first + STEP)
    columns = jnp.concatenate([source[h, rows] for h in (0, 1, 0, 2, 3, 2)] + [filler], axis=0)
    results = jnp.dot(matrix, columns, preferred_element_type=F32)
    blocks = lane_sum(
        lambda u, v, w: lane_block(results[u * STRIP : (u + 1) * STRIP], w), lane, TAPS, False
    )
    matched = jnp.concatenate(blocks, axis=1)
    high = matched.astype(BF16)
    return high, (matched - high.astype(F32)).astype(BF16)


def upright(line):
    count = line.shape[1]
    square = (count, count)
    return jnp.sum(
        jnp.where(iota(square, 0) == iota(square, 1), jnp.broadcast_to(line, square), 0),
        axis=1, keepdims=True,
    )


def route(patch, owner):
    square = (patch.shape[1], patch.shape[1])
    earlier = (iota(square, 0) < iota(square, 1)) & (upright(patch) == patch)
    rank = jnp.sum(earlier.astype(jnp.int32), axis=0, keepdims=True)
    named = iota((owner.shape[1], patch.shape[1]), 0) == patch
    to = jnp.sum(jnp.where(named, upright(owner), 0), axis=0, keepdims=True)
    return to, rank


def match_kernel(
    patch, slot, owner, weight, high_level, step_level, slope, sort, image,
    places, label, matched_terms, terms,
):
    ((ccd, _), _), _ = whereabouts(label.shape[0])
    to, rank = route(patch[...], owner[...])
    places[...] = to * CAP + rank

    own = jnp.where(iota(weight.shape, 1) == ccd, weight[...].astype(F32), 0.0)
    own = jnp.sum(own, axis=1, keepdims=True)
    each = (V, V * BLKC)
    weights = jnp.sum(
        jnp.where(iota(each, 1) // BLKC == iota(each, 0), own, 0.0), axis=0, keepdims=True
    )
    goes = iota((label.shape[0], V * BLKC), 0) == to
    lane = iota(label.shape, 1)
    lines = jnp.zeros(label.shape, F32)
    for r in range(CAP):
        for n, value in enumerate((weights, slot[...].astype(F32))):
            column = jnp.sum(jnp.where(goes & (rank == r), value, 0.0), axis=1, keepdims=True)
            lines = jnp.where(lane == 2 * r + n, column, lines)
    label[...] = lines

    open_row = FREE_FIRST * STRIP - GOT
    seen = OPEN - STRIP
    terms[:, :, seen:] = jnp.zeros((MATCHED, 4, STRIP, WIDTH), BF16)

    def some_visits(turn, _):
        visits = [turn * MATCHED + i for i in range(MATCHED)]
        for i, visit in enumerate(visits):
            rows = sorted_rows(image[visit, open_row : open_row + seen], sort[...])
            for h, value in enumerate(rows):
                terms[i, h, :seen] = value.astype(BF16)
        for k in range(FREE_FIRST, STRIPS):
            first = (k - FREE_FIRST) * STRIP
            for i, visit in enumerate(visits):
                at = slice(first, first + STRIP)
                matched_terms[visit, 0, at], matched_terms[visit, 1, at] = match_strip(
                    high_level[visit], step_level[visit], slope[visit], terms.at[i], first, k
                )
        return 0

    lax.fori_loop(0, V // MATCHED, some_visits, 0)


def warp_kernel(
    owner, places, label, high_level, step_level, slope, rows_high, rows_low, col_weights,
    sort, unsort, image, above, matched_free, out,
    own_terms, past_terms, own_matched, past_matched, both_places, place_of, place_sem,
):
    devices = label.shape[0]
    _, same = whereabouts(devices)
    past_patch = above[V * GOT : V * GOT + 1, : V * BLKC].astype(jnp.int32)
    to, rank = route(past_patch, owner[...])
    both_places[0:1, : V * BLKC] = places[...]
    both_places[1:2, : V * BLKC] = to * CAP + rank
    place_copy = pltpu.make_async_copy(both_places, place_of, place_sem)
    place_copy.start()
    lane = iota((1, LANES), 1)
    out[:, CAP * BLOCK :] = jnp.broadcast_to(
        label[...].reshape(devices, 1, LANES), (devices, LABEL, LANES)
    ).astype(BF16)

    seam = STRIP + STEP
    foreign = iota((seam, 1), 0) < GOT
    both = jnp.where(same, 1.0, 0.0)
    past = jnp.where(same, 0, V)
    own_sees = jnp.where(foreign, both, 1.0)
    past_sees = jnp.where(foreign, 1.0, both)

    def some_visits(turn, _):
        visits = [turn * WARPED + i for i in range(WARPED)]
        for i, visit in enumerate(visits):
            tail = pl.ds(pl.multiple_of(visit * GOT, 8), GOT)
            raw = jnp.concatenate([above[tail], image[visit, : seam - GOT]], axis=0)
            for h, value in enumerate(sorted_rows(raw, sort[...])):
                own_terms[i, h] = (value * own_sees).astype(BF16)
                past_terms[i, h] = (value * past_sees).astype(BF16)
        for i, visit in enumerate(visits):
            own_matched[i, 0], own_matched[i, 1] = match_strip(
                high_level[visit], step_level[visit], slope[visit],
                own_terms.at[i], OWN_FIRST * STRIP, OWN_FIRST,
            )
        for k in range(PAST_STRIPS):
            for i, visit in enumerate(visits):
                at = slice(k * STRIP, (k + 1) * STRIP)
                past_matched[i, 0, at], past_matched[i, 1, at] = match_strip(
                    high_level[past + visit], step_level[past + visit], slope[past + visit],
                    past_terms.at[i], k * STRIP, k,
                )

        warped = []
        for i, visit in enumerate(visits):
            halves = []
            for h in range(HALVES):
                at = slice(h * ROWS, (h + 1) * ROWS)
                high, low = rows_high[visit, at], rows_low[visit, at]
                free = FREE_FIRST * STRIP

                def under(term):
                    if h == 0:
                        parts = [
                            past_matched[i, term],
                            own_matched[i, term],
                            matched_free[visit, term, : WINDOW - free],
                        ]
                    else:
                        parts = [matched_free[visit, term, ROWS - free :]]
                    left = LANES - sum([x.shape[0] for x in parts])
                    return jnp.concatenate(parts + [jnp.zeros((left, WIDTH), BF16)], axis=0)

                first = under(0)
                total = jnp.dot(
                    jnp.concatenate([high, high], axis=1),
                    jnp.concatenate([first, under(1)], axis=0),
                    preferred_element_type=F32,
                )
                halves.append(total + jnp.dot(low, first, preferred_element_type=F32))
            warped.append(jnp.concatenate(halves, axis=0))

        @pl.when(turn == 0)
        def _():
            place_copy.wait()

        for i, visit in enumerate(visits):
            parts = []
            for rows, weights in (
                (slice(0, TAIL), col_weights[past + visit]),
                (slice(TAIL, BLOCK), col_weights[visit]),
            ):
                some = warped[i][rows]
                blocks = lane_sum(
                    lambda s, v, w: lane_block(weights[s : s + 1], v) * lane_block(some, w),
                    lane, 2 * WARP + 1, True,
                )
                parts.append(jnp.concatenate(blocks, axis=1).astype(BF16))
            result = jnp.dot(
                jnp.concatenate(parts, axis=0), unsort[...], preferred_element_type=F32
            ).astype(BF16)
            for j in range(BLKC):
                piece = lane_block(result, j)
                to = place_of[0, visit * BLKC + j]
                rows = pl.ds(pl.multiple_of(to % CAP * BODY, TAIL), BODY)
                out[to // CAP, rows] = piece[TAIL:]
                to = place_of[1, visit * BLKC + j]
                rows = pl.ds(pl.multiple_of(CAP * BODY + to % CAP * TAIL, TAIL), TAIL)
                out[to // CAP, rows] = piece[:TAIL]
        return 0

    lax.fori_loop(0, V // WARPED, some_visits, 0)


def warp(patch, slot, owner, weight, ready, order, images, above, devices):
    vmem = pl.BlockSpec(memory_space=pltpu.VMEM)
    sort, unsort = order
    *matrices, rows_high, rows_low, col_weights = ready
    owner = owner.reshape(1, -1)
    args = [patch, slot, owner, weight, *matrices, sort, images]
    places, label, matched = pl.pallas_call(
        match_kernel,
        in_specs=[vmem] * len(args),
        out_specs=[vmem, vmem, vmem],
        out_shape=[
            jax.ShapeDtypeStruct((1, V * BLKC), jnp.int32),
            jax.ShapeDtypeStruct((devices, LANES), F32),
            jax.ShapeDtypeStruct((V, 2, (STRIPS - FREE_FIRST) * STRIP, WIDTH), BF16),
        ],
        scratch_shapes=[
            pltpu.VMEM((MATCHED, 4, OPEN, WIDTH), BF16),
        ],
        compiler_params=pltpu.CompilerParams(vmem_limit_bytes=32 << 20),
        cost_estimate=pl.CostEstimate(
            flops=V * 2 * (STRIPS - FREE_FIRST) * TAPS * STRIP * BAND * WIDTH,
            bytes_accessed=V * (BLOCK * WIDTH * 6),
            transcendentals=0,
        ),
        name="match",
    )(*args)
    args = [
        owner, places, label, *matrices, rows_high, rows_low, col_weights,
        sort, unsort, images, above, matched,
    ]
    return pl.pallas_call(
        warp_kernel,
        in_specs=[vmem] * len(args),
        out_specs=vmem,
        scratch_shapes=[
            pltpu.VMEM((WARPED, 4, STRIP + STEP, WIDTH), BF16),
            pltpu.VMEM((WARPED, 4, STRIP + STEP, WIDTH), BF16),
            pltpu.VMEM((WARPED, 2, STRIP, WIDTH), BF16),
            pltpu.VMEM((WARPED, 2, PAST_STRIPS * STRIP, WIDTH), BF16),
            pltpu.VMEM((8, LANES), jnp.int32),
            pltpu.SMEM((8, LANES), jnp.int32),
            pltpu.SemaphoreType.DMA(()),
        ],
        out_shape=jax.ShapeDtypeStruct((devices, CAP * BLOCK + LABEL, BLOCK), BF16),
        compiler_params=pltpu.CompilerParams(vmem_limit_bytes=32 << 20),
        cost_estimate=pl.CostEstimate(
            flops=V * 2 * STRIPS * TAPS * STRIP * BAND * WIDTH,
            bytes_accessed=V * (BLOCK * WIDTH * 6),
            transcendentals=0,
        ),
        name="warp",
    )(*args)


def coadd_kernel(got, out, total, out_sem):
    devices = got.shape[0]
    wide = devices * CAP * STRIP
    labels = got[:, CAP * BLOCK : CAP * BLOCK + LABEL][:, 0]
    lane = iota((1, wide), 1)
    rank = lane // STRIP % CAP
    source = lane // (STRIP * CAP)

    def spread(entry):
        onehot = (iota((LANES, wide), 0) == rank * 2 + entry).astype(F32).astype(BF16)
        every = jnp.dot(labels, onehot, preferred_element_type=F32)
        return jnp.sum(
            jnp.where(iota((devices, wide), 0) == source, every, 0.0), axis=0, keepdims=True
        )

    weights, cells = spread(0), spread(1)
    row = iota((CELLS * STRIP, 1), 0)
    mine = (cells == (row // STRIP).astype(F32)) & (lane % STRIP == row % STRIP)
    matrix = jnp.where(mine, weights, 0.0)
    sums = jnp.sum(matrix, axis=1, keepdims=True)
    inverse = 1.0 / jnp.maximum(sums, 1.0)
    matrix = matrix.astype(BF16)
    taken = {}
    for r in range(CAP):
        column = jnp.broadcast_to(labels[:, 2 * r : 2 * r + 1].astype(F32), (devices, LANES))
        for s in range(devices):
            taken[s, r] = jnp.broadcast_to(column[s : s + 1], (STRIP, LANES)).astype(BF16) > 0

    def tile(s, r, k):
        device, first = s, r * BODY + k * STRIP
        if first - r * BODY >= BODY:
            device, first = (s + 1) % devices, CAP * BODY + r * TAIL
        return jnp.where(taken[s, r], got[device, first : first + STRIP], jnp.zeros((), BF16))

    copies = []
    for pair in range(BLOCK // STRIP // 2):
        columns = jnp.concatenate(
            [
                jnp.concatenate(
                    [tile(s, r, k) for s in range(devices) for r in range(CAP)], axis=0
                )
                for k in (2 * pair, 2 * pair + 1)
            ],
            axis=1,
        )
        result = jnp.dot(matrix, columns, preferred_element_type=F32) * inverse
        for c in range(CELLS):
            part = result[c * STRIP : (c + 1) * STRIP]
            lanes = slice(c % PSIDE * BLOCK, (c % PSIDE + 1) * BLOCK)
            for n in range(2):
                first = (2 * pair + n) * STRIP
                total[c // PSIDE, first : first + STRIP, lanes] = lane_block(part, n)
        size = 2 * STRIP
        for line in range(PSIDE):
            copies.append(
                pltpu.make_async_copy(
                    total.at[line, pl.ds(pair * size, size)],
                    out.at[0, pl.ds(line * BLOCK + pair * size, size)],
                    out_sem.at[pair, line],
                )
            )
            copies[-1].start()
    for copy in copies:
        copy.wait()


def coadd(got):
    return pl.pallas_call(
        coadd_kernel,
        in_specs=[pl.BlockSpec(memory_space=pltpu.VMEM)],
        out_specs=pl.BlockSpec(memory_space=pl.ANY),
        out_shape=jax.ShapeDtypeStruct((1, PSIDE * BLOCK, PSIDE * BLOCK), F32),
        scratch_shapes=[
            pltpu.VMEM((PSIDE, BLOCK, WIDTH), F32),
            pltpu.SemaphoreType.DMA((BLOCK // STRIP // 2, PSIDE)),
        ],
        compiler_params=pltpu.CompilerParams(vmem_limit_bytes=32 << 20),
        name="coadd",
    )(got)


def shards(
    images, basis_taps, psf_coef, affine, visit_weight, block_patch, block_slot, patch_owner
):
    devices = lax.axis_size("ccd")
    patch = block_patch[:, :, 0]
    rows = V * GOT
    names = lax.pad(
        patch, jnp.zeros((), jnp.int32), ((rows, 7, 0), (0, WIDTH - V * BLKC, 0))
    )
    rims = images[:, BLOCK - GOT :].reshape(rows, WIDTH)
    head = lax.pad(rims, jnp.zeros((), F32), ((0, 8, 0), (0, 0, 0))) + names.astype(F32)
    above = lax.ppermute(head, "ccd", [(i, (i + 1) % devices) for i in range(devices)])
    order = orders()
    ready = prepare(
        basis_taps.transpose(1, 0, 2), psf_coef.transpose(1, 3, 0, 2), affine.transpose(0, 2, 3, 1),
        devices,
    )
    sent = warp(
        patch, block_slot, patch_owner, visit_weight, ready, order, images, above, devices
    )
    got = lax.all_to_all(sent, "ccd", split_axis=0, concat_axis=0, tiled=True)
    return coadd(got)


def solution(mesh):
    placed = (
        P(None, ("group", "ccd"), None),
        P(),
        P(None, "group", None, None),
        P(None, "group", None, None),
        P(None, "group"),
        P(("group", "ccd"), None, None),
        P(("group", "ccd"), None),
        P("group"),
    )
    return jax.shard_map(
        shards,
        mesh=mesh,
        in_specs=placed,
        out_specs=P(("group", "ccd"), None, None),
        check_vma=False,
    )
```

```python
import functools
import itertools

import jax
import jax.numpy as jnp
from jax import lax
from jax.experimental import pallas as pl
from jax.experimental.pallas import tpu as pltpu
from jax.sharding import PartitionSpec as P

V = 4
BLOCK = 128
BLKC = 4
SPLIT = 4
TAPS = 11
NBASIS = 9
PSIDE = 4
CELLS = PSIDE * PSIDE
CAP = 2

HALF = TAPS // 2
WARP = 3
RIM = HALF + WARP
TAIL = 16
HEIGHT = SPLIT * BLOCK
WIDTH = BLKC * BLOCK
LANES = 128
LANE_BLOCKS = WIDTH // LANES
STRIP = 16
STEP = 32
STRIPS = -(-(BLOCK + 2 * WARP) // STRIP)
MIDDLE = STRIPS // 2
GROUPS = 6
BAND = 256
PAST_STRIPS = 2
OWN_FIRST = 1
FREE_FIRST = 2
HALVES = 2
MATCHED = 4
WARPED = 4
ROWS = BLOCK // HALVES
WINDOW = ROWS + STRIP
BODY = BLOCK - TAIL
GOT = TAIL + RIM
OPEN = (STRIPS - 1) * STRIP + STEP - FREE_FIRST * STRIP
LABEL = 16
F32 = jnp.float32
BF16 = jnp.bfloat16


def sin_pi(t):
    whole = jnp.round(t)
    f = t - whole
    odd = whole - 2.0 * jnp.floor(0.5 * whole)
    f2 = f * f
    out = 0.0
    for c in (
        0.00046630280576761, -0.0073704309457144, 0.0821458866111282,
        -0.599264529320792, 2.55016403987734, -5.16771278004997, 3.14159265358979,
    ):
        out = out * f2 + c
    return f * out * (1.0 - 2.0 * odd)


def lanczos(t):
    zero = t == 0.0
    safe = jnp.where(zero, 1.0, t)
    pt = jnp.pi * safe
    value = 3.0 * sin_pi(safe) * sin_pi(safe / 3.0) / (pt * pt)
    return jnp.where(jnp.abs(t) < 3.0, jnp.where(zero, 1.0, value), 0.0)


def iota(shape, dim):
    return lax.broadcasted_iota(jnp.int32, shape, dim)


def column_at(lane):
    return lane % LANES * LANE_BLOCKS + lane // LANES


def order_kernel(sort, unsort):
    square = (WIDTH, WIDTH)
    one, none = jnp.ones((), F32), jnp.zeros((), F32)
    goes = iota(square, 0) == column_at(iota((1, WIDTH), 1))
    sort[...] = jnp.where(goes, one, none).astype(BF16)
    comes = iota(square, 1) == column_at(iota((WIDTH, 1), 0))
    unsort[...] = jnp.where(comes, one, none).astype(BF16)


def orders():
    return small_kernel(order_kernel, "orders", [], [((WIDTH, WIDTH), BF16)] * 2)


def lane_block(x, v):
    return x[:, v * LANES : (v + 1) * LANES]


def dot_exact(a, b, dims):
    return lax.dot_general(
        a, b, (dims, ((), ())), precision=lax.Precision.HIGHEST, preferred_element_type=F32
    )


def staircase(x, first):
    return jnp.concatenate(
        [
            pltpu.roll(x[g : g + 8], first + g, 1, stride=1, stride_axis=0)
            for g in range(0, x.shape[0], 8)
        ],
        axis=0,
    )


def lane_sum(terms_of, lane, count, weigh):
    blocks = []
    for v in range(LANE_BLOCKS):
        total = None
        half = count // 2
        for q in range(-(-half // LANE_BLOCKS) * -1, (half + LANE_BLOCKS - 1) // LANE_BLOCKS + 1):
            part = None
            for u in range(count):
                if (v + u - half) // LANE_BLOCKS != q:
                    continue
                piece = terms_of(u, v, (v + u - half) % LANE_BLOCKS)
                part = piece if part is None else part + piece
            if part is None:
                continue
            if q:
                part = pltpu.roll(part, -q % LANES, 1)
                if not weigh:
                    part = jnp.where((lane + q >= 0) & (lane + q < LANES), part, 0.0)
            total = part if total is None else total + part
        blocks.append(total)
    return blocks


def whereabouts(devices):
    band = lax.axis_index("ccd")
    past = lax.rem(band + devices - 1, devices)
    quarter = (band + SPLIT // 2) % SPLIT
    own = ((band + SPLIT // 2) // SPLIT, quarter * BLOCK - TAIL)
    before = ((past + SPLIT // 2) // SPLIT, (past + SPLIT // 2) % SPLIT * BLOCK + BODY)
    return (own, before), (quarter > 0) & (band > 0)


def collect_kernel(images, patch, owner, head, numbers, owners, sems):
    copies = [
        pltpu.make_async_copy(
            images.at[v, pl.ds(BLOCK - GOT, GOT)], head.at[pl.ds(v * GOT, GOT)], sems.at[v]
        )
        for v in range(V)
    ]
    names = pltpu.make_async_copy(patch, numbers, sems.at[V])
    names.start()
    named = pltpu.make_async_copy(owner, owners, sems.at[V + 1])
    named.start()
    for copy in copies:
        copy.start()
    head[V * GOT :] = jnp.zeros((8, WIDTH), F32)
    names.wait()
    named.wait()
    to, rank = route(numbers[...], owners[...])
    head[V * GOT : V * GOT + 1, : V * BLKC] = (to * CAP + rank).astype(F32)
    for copy in copies:
        copy.wait()


def collect(images, patch, owner):
    return pl.pallas_call(
        collect_kernel,
        in_specs=[pl.BlockSpec(memory_space=pl.ANY)] * 3,
        out_specs=pl.BlockSpec(memory_space=pltpu.VMEM),
        out_shape=jax.ShapeDtypeStruct((V * GOT + 8, WIDTH), F32),
        scratch_shapes=[
            pltpu.VMEM(patch.shape, jnp.int32),
            pltpu.VMEM(owner.shape, jnp.int32),
            pltpu.SemaphoreType.DMA((V + 2,)),
        ],
        name="collect",
    )(images, patch, owner)


def lanczos_weights(devices, affine, cols_out):
    bands, same = whereabouts(devices)
    lane = iota((1, LANES), 1)
    lanes = iota((8, WIDTH), 1)
    step = iota((8, WIDTH), 0) - WARP
    block = lanes // LANES
    carry = (block + step + LANE_BLOCKS) // LANE_BLOCKS - 1
    from_lane = lanes % LANES - carry
    col = (from_lane * LANE_BLOCKS + block).astype(F32)
    within = (from_lane >= 0) & (from_lane < LANES) & (step <= WARP)
    offset = iota((8, LANES), 0) - WARP
    crosses = (lane + offset >= TAIL) != (lane >= TAIL)
    keep = (offset <= WARP) & (same | jnp.logical_not(crosses))
    by_row = []
    for visit in range(V):
        shifts = []
        for n, (ccd, top_row) in enumerate(bands):
            a = jnp.sum(
                jnp.where(iota((1, 1, affine.shape[3]), 2) == ccd, affine[visit], 0.0),
                axis=2, keepdims=True,
            )
            row = (top_row + lane).astype(F32)
            shifts.append(a[0, 0:1] + a[0, 1:2] * (row - (HEIGHT - 1) / 2.0) / HEIGHT)
            col_shift = a[1, 0:1] + a[1, 1:2] * (col - (WIDTH - 1) / 2.0) / WIDTH
            cols_out[n * V + visit] = jnp.where(within, lanczos(col_shift - step.astype(F32)), 0.0)
        shift = jnp.where(lane < TAIL, shifts[1], shifts[0])
        weights = jnp.where(keep, lanczos(shift - offset.astype(F32)), 0.0)
        by_row.append(jnp.concatenate([weights, jnp.zeros((LANES - 8, LANES), F32)], axis=0).T)
    return by_row


def prepare_kernel(
    devices, taps, psf, affine, high_level, step_level, slope, rows_high, rows_low, cols_out
):
    row_weights = lanczos_weights(devices, affine, cols_out)
    bands, _ = whereabouts(devices)
    band_lane = iota((1, BAND), 1)
    seg = band_lane // STEP
    lane = iota((1, LANES), 1)
    tap = band_lane - seg * STEP
    onehot = (tap == iota((TAPS, BAND), 0)) & (seg < GROUPS)
    row_taps = dot_exact(taps[:, 0], onehot.astype(F32), ((1,), (0,)))
    eye = (iota((TAPS, STRIP), 0) == iota((TAPS, STRIP), 1)).astype(F32)
    turned_taps = dot_exact(eye, taps[:, 1], ((0,), (1,)))
    units = []
    for n, visit in itertools.product(range(2), range(V)):
        ccd, top_row = bands[n]
        lhs = jnp.concatenate(
            [turned_taps * psf[ccd, c, visit : visit + 1, :] for c in range(3)], axis=0
        )
        kernels = dot_exact(lhs, row_taps, ((1,), (0,)))
        const, by_row, by_col = (kernels[c * STRIP : (c + 1) * STRIP] for c in range(3))
        is_level = seg < 3
        per_strip = 2.0 * STRIP / HEIGHT
        middle_row = (top_row + (MIDDLE * STRIP - WARP)).astype(F32)
        middle_pos = (2.0 * middle_row + 1.0) / HEIGHT - 1.0
        col_move = (iota((STRIP, 1), 0) - HALF).astype(F32) * (2.0 / WIDTH)
        by_row = jnp.where(is_level, by_row, 0.0)
        const = jnp.where(is_level, const + middle_pos * by_row - col_move * by_col, by_col)
        reach = per_strip * (STRIPS - MIDDLE)
        largest = jnp.max(jnp.abs(const) + reach * jnp.abs(by_row), axis=(0, 1), keepdims=True)
        unit = jnp.maximum(largest, 1e-30) * (1.0 / 200.0)
        units.append(unit)
        const = const / unit
        by_row = (by_row * per_strip) / unit
        low_lanes = (lane // STEP) % 3 == 2
        low_band = seg % 3 == 2
        row_part = iota((STRIP, 1), 0).astype(F32) * (1.0 / STRIP)
        for u in range(TAPS):
            at = slice(u * STRIP, (u + 1) * STRIP)
            one = jnp.broadcast_to(const[u : u + 1], (STRIP, BAND))
            x, tail = staircase(one[:, :LANES], 0), staircase(one[:, LANES:], 0)
            y = staircase(jnp.broadcast_to(by_row[u : u + 1, :LANES], (STRIP, LANES)), 0)
            high = tail.astype(BF16).astype(F32)
            slope[n * V + visit, at] = jnp.where(low_band[:, LANES:], tail - high, high).astype(BF16)
            x = x + row_part * y
            high = jnp.where(lane < 3 * STEP, jnp.round(x), x.astype(BF16).astype(F32))
            high_level[n * V + visit, at] = jnp.where(low_lanes, x - high, high)
            high = jnp.round(y)
            step_level[n * V + visit, at] = jnp.where(low_lanes, y - high, high)

    for visit in range(V):
        weights = row_weights[visit]
        matrix = jnp.concatenate(
            [
                staircase(weights[:TAIL] * units[V + visit], 0),
                staircase(weights[TAIL:ROWS] * units[visit], PAST_STRIPS * STRIP),
                staircase(weights[ROWS:] * units[visit], 0),
            ],
            axis=0,
        )
        high = matrix.astype(BF16)
        rows_high[visit] = high
        rows_low[visit] = (matrix - high.astype(F32)).astype(BF16)


def small_kernel(body, name, args, shapes):
    vmem = pl.BlockSpec(memory_space=pltpu.VMEM)
    return pl.pallas_call(
        body,
        in_specs=[vmem] * len(args),
        out_specs=[vmem] * len(shapes),
        out_shape=[jax.ShapeDtypeStruct(shape, kind) for shape, kind in shapes],
        compiler_params=pltpu.CompilerParams(vmem_limit_bytes=32 << 20),
        cost_estimate=pl.CostEstimate(flops=1 << 30, bytes_accessed=1 << 20, transcendentals=0),
        name=name,
    )(*args)


def prepare(taps, psf, affine, devices):
    return small_kernel(
        functools.partial(prepare_kernel, devices), "matrices", [taps, psf, affine],
        [
            ((2 * V, TAPS * STRIP, LANES), F32),
            ((2 * V, TAPS * STRIP, LANES), F32),
            ((2 * V, TAPS * STRIP, BAND - LANES), BF16),
            ((V, BLOCK, LANES), BF16),
            ((V, BLOCK, LANES), BF16),
            ((2 * V, 8, WIDTH), F32),
        ],
    )


def sorted_rows(raw, sort):
    col_pos = (2.0 * column_at(iota((1, WIDTH), 1)).astype(F32) + 1.0) / WIDTH - 1.0
    count = raw.shape[0]
    raw_high = raw.astype(BF16)
    raw_low = (raw - raw_high.astype(F32)).astype(BF16)
    both = jnp.dot(
        jnp.concatenate([raw_high, raw_low], axis=0), sort, preferred_element_type=F32
    )
    high, low = both[:count], both[count:]
    tilted = (high + low) * col_pos
    tilted_high = tilted.astype(BF16).astype(F32)
    return high, low, tilted_high, tilted - tilted_high


def match_strip(level, step, slope, source, first, k):
    lane = iota((1, LANES), 1)
    if k != MIDDLE:
        level = level + float(k - MIDDLE) * step
    matrix = jnp.concatenate([level.astype(BF16), slope], axis=1)
    filler = jnp.zeros((BAND - GROUPS * STEP, WIDTH), BF16)
    rows = slice(first, first + STEP)
    columns = jnp.concatenate([source[h, rows] for h in (0, 1, 0, 2, 3, 2)] + [filler], axis=0)
    results = jnp.dot(matrix, columns, preferred_element_type=F32)
    blocks = lane_sum(
        lambda u, v, w: lane_block(results[u * STRIP : (u + 1) * STRIP], w), lane, TAPS, False
    )
    matched = jnp.concatenate(blocks, axis=1)
    high = matched.astype(BF16)
    return high, (matched - high.astype(F32)).astype(BF16)


def upright(line):
    count = line.shape[1]
    square = (count, count)
    return jnp.sum(
        jnp.where(iota(square, 0) == iota(square, 1), jnp.broadcast_to(line, square), 0),
        axis=1, keepdims=True,
    )


def route(patch, owner):
    square = (patch.shape[1], patch.shape[1])
    earlier = (iota(square, 0) < iota(square, 1)) & (upright(patch) == patch)
    rank = jnp.sum(earlier.astype(jnp.int32), axis=0, keepdims=True)
    named = iota((owner.shape[1], patch.shape[1]), 0) == patch
    to = jnp.sum(jnp.where(named, upright(owner), 0), axis=0, keepdims=True)
    return to, rank


def match_kernel(
    patch, slot, owner, weight, high_level, step_level, slope, sort, image,
    places, label, matched_terms, terms,
):
    ((ccd, _), _), _ = whereabouts(label.shape[0])
    to, rank = route(patch[...], owner[...])
    places[...] = to * CAP + rank

    own = jnp.where(iota(weight.shape, 1) == ccd, weight[...].astype(F32), 0.0)
    own = jnp.sum(own, axis=1, keepdims=True)
    each = (V, V * BLKC)
    weights = jnp.sum(
        jnp.where(iota(each, 1) // BLKC == iota(each, 0), own, 0.0), axis=0, keepdims=True
    )
    goes = iota((label.shape[0], V * BLKC), 0) == to
    lane = iota(label.shape, 1)
    lines = jnp.zeros(label.shape, F32)
    for r in range(CAP):
        for n, value in enumerate((weights, slot[...].astype(F32))):
            column = jnp.sum(jnp.where(goes & (rank == r), value, 0.0), axis=1, keepdims=True)
            lines = jnp.where(lane == 2 * r + n, column, lines)
    label[...] = lines

    open_row = FREE_FIRST * STRIP - GOT
    seen = OPEN - STRIP
    terms[:, :, seen:] = jnp.zeros((MATCHED, 4, STRIP, WIDTH), BF16)

    def some_visits(turn, _):
        visits = [turn * MATCHED + i for i in range(MATCHED)]
        for i, visit in enumerate(visits):
            rows = sorted_rows(image[visit, open_row : open_row + seen], sort[...])
            for h, value in enumerate(rows):
                terms[i, h, :seen] = value.astype(BF16)
        for k in range(FREE_FIRST, STRIPS):
            first = (k - FREE_FIRST) * STRIP
            for i, visit in enumerate(visits):
                at = slice(first, first + STRIP)
                matched_terms[visit, 0, at], matched_terms[visit, 1, at] = match_strip(
                    high_level[visit], step_level[visit], slope[visit], terms.at[i], first, k
                )
        return 0

    lax.fori_loop(0, V // MATCHED, some_visits, 0)


def warp_kernel(
    owner, places, label, high_level, step_level, slope, rows_high, rows_low, col_weights,
    sort, unsort, image, above, matched_free, out,
    own_terms, past_terms, own_matched, past_matched, both_places, place_of, past_place, place_sem,
):
    devices = label.shape[0]
    _, same = whereabouts(devices)
    both_places[0:1, : V * BLKC] = places[...]
    place_copy = pltpu.make_async_copy(both_places, place_of, place_sem.at[0])
    place_copy.start()
    past_copy = pltpu.make_async_copy(
        above.at[pl.ds(V * GOT, 8), pl.ds(0, LANES)], past_place, place_sem.at[1]
    )
    past_copy.start()
    lane = iota((1, LANES), 1)
    out[:, CAP * BLOCK :] = jnp.broadcast_to(
        label[...].reshape(devices, 1, LANES), (devices, LABEL, LANES)
    ).astype(BF16)

    seam = STRIP + STEP
    foreign = iota((seam, 1), 0) < GOT
    both = jnp.where(same, 1.0, 0.0)
    own_sees = jnp.where(foreign, both, 1.0)
    past_sees = jnp.where(foreign, 1.0, both)

    def some_visits(turn, _):
        visits = [turn * WARPED + i for i in range(WARPED)]
        for i, visit in enumerate(visits):
            tail = pl.ds(pl.multiple_of(visit * GOT, 8), GOT)
            raw = jnp.concatenate([above[tail], image[visit, : seam - GOT]], axis=0)
            for h, value in enumerate(sorted_rows(raw, sort[...])):
                own_terms[i, h] = (value * own_sees).astype(BF16)
                past_terms[i, h] = (value * past_sees).astype(BF16)
        for i, visit in enumerate(visits):
            own_matched[i, 0], own_matched[i, 1] = match_strip(
                high_level[visit], step_level[visit], slope[visit],
                own_terms.at[i], OWN_FIRST * STRIP, OWN_FIRST,
            )
        for k in range(PAST_STRIPS):
            for i, visit in enumerate(visits):
                at = slice(k * STRIP, (k + 1) * STRIP)
                past_matched[i, 0, at], past_matched[i, 1, at] = match_strip(
                    high_level[V + visit], step_level[V + visit], slope[V + visit],
                    past_terms.at[i], k * STRIP, k,
                )

        warped = []
        for i, visit in enumerate(visits):
            halves = []
            for h in range(HALVES):
                at = slice(h * ROWS, (h + 1) * ROWS)
                high, low = rows_high[visit, at], rows_low[visit, at]
                free = FREE_FIRST * STRIP

                def under(term):
                    if h == 0:
                        parts = [
                            past_matched[i, term],
                            own_matched[i, term],
                            matched_free[visit, term, : WINDOW - free],
                        ]
                    else:
                        parts = [matched_free[visit, term, ROWS - free :]]
                    left = LANES - sum([x.shape[0] for x in parts])
                    return jnp.concatenate(parts + [jnp.zeros((left, WIDTH), BF16)], axis=0)

                first = under(0)
                total = jnp.dot(
                    jnp.concatenate([high, high], axis=1),
                    jnp.concatenate([first, under(1)], axis=0),
                    preferred_element_type=F32,
                )
                halves.append(total + jnp.dot(low, first, preferred_element_type=F32))
            warped.append(jnp.concatenate(halves, axis=0))

        @pl.when(turn == 0)
        def _():
            place_copy.wait()
            past_copy.wait()

        for i, visit in enumerate(visits):
            parts = []
            for rows, weights in (
                (slice(0, TAIL), col_weights[V + visit]),
                (slice(TAIL, BLOCK), col_weights[visit]),
            ):
                some = warped[i][rows]
                blocks = lane_sum(
                    lambda s, v, w: lane_block(weights[s : s + 1], v) * lane_block(some, w),
                    lane, 2 * WARP + 1, True,
                )
                parts.append(jnp.concatenate(blocks, axis=1).astype(BF16))
            result = jnp.dot(
                jnp.concatenate(parts, axis=0), unsort[...], preferred_element_type=F32
            ).astype(BF16)
            for j in range(BLKC):
                piece = lane_block(result, j)
                to = place_of[0, visit * BLKC + j]
                rows = pl.ds(pl.multiple_of(to % CAP * BODY, TAIL), BODY)
                out[to // CAP, rows] = piece[TAIL:]
                to = past_place[0, visit * BLKC + j].astype(jnp.int32)
                rows = pl.ds(pl.multiple_of(CAP * BODY + to % CAP * TAIL, TAIL), TAIL)
                out[to // CAP, rows] = piece[:TAIL]
        return 0

    lax.fori_loop(0, V // WARPED, some_visits, 0)


def warp(patch, slot, owner, weight, ready, order, images, above, devices):
    vmem = pl.BlockSpec(memory_space=pltpu.VMEM)
    sort, unsort = order
    *matrices, rows_high, rows_low, col_weights = ready
    owner = owner.reshape(1, -1)
    args = [patch, slot, owner, weight, *matrices, sort, images]
    places, label, matched = pl.pallas_call(
        match_kernel,
        in_specs=[vmem] * len(args),
        out_specs=[vmem, vmem, vmem],
        out_shape=[
            jax.ShapeDtypeStruct((1, V * BLKC), jnp.int32),
            jax.ShapeDtypeStruct((devices, LANES), F32),
            jax.ShapeDtypeStruct((V, 2, (STRIPS - FREE_FIRST) * STRIP, WIDTH), BF16),
        ],
        scratch_shapes=[
            pltpu.VMEM((MATCHED, 4, OPEN, WIDTH), BF16),
        ],
        compiler_params=pltpu.CompilerParams(vmem_limit_bytes=32 << 20),
        cost_estimate=pl.CostEstimate(
            flops=V * 2 * (STRIPS - FREE_FIRST) * TAPS * STRIP * BAND * WIDTH,
            bytes_accessed=V * (BLOCK * WIDTH * 6),
            transcendentals=0,
        ),
        name="match",
    )(*args)
    args = [
        owner, places, label, *matrices, rows_high, rows_low, col_weights,
        sort, unsort, images, above, matched,
    ]
    return pl.pallas_call(
        warp_kernel,
        in_specs=[vmem] * len(args),
        out_specs=vmem,
        scratch_shapes=[
            pltpu.VMEM((WARPED, 4, STRIP + STEP, WIDTH), BF16),
            pltpu.VMEM((WARPED, 4, STRIP + STEP, WIDTH), BF16),
            pltpu.VMEM((WARPED, 2, STRIP, WIDTH), BF16),
            pltpu.VMEM((WARPED, 2, PAST_STRIPS * STRIP, WIDTH), BF16),
            pltpu.VMEM((8, LANES), jnp.int32),
            pltpu.SMEM((8, LANES), jnp.int32),
            pltpu.SMEM((8, LANES), F32),
            pltpu.SemaphoreType.DMA((2,)),
        ],
        out_shape=jax.ShapeDtypeStruct((devices, CAP * BLOCK + LABEL, BLOCK), BF16),
        compiler_params=pltpu.CompilerParams(vmem_limit_bytes=32 << 20),
        cost_estimate=pl.CostEstimate(
            flops=V * 2 * STRIPS * TAPS * STRIP * BAND * WIDTH,
            bytes_accessed=V * (BLOCK * WIDTH * 6),
            transcendentals=0,
        ),
        name="warp",
    )(*args)


def coadd_kernel(got, out, total, out_sem):
    devices = got.shape[0]
    wide = devices * CAP * STRIP
    labels = got[:, CAP * BLOCK : CAP * BLOCK + LABEL][:, 0]
    lane = iota((1, wide), 1)
    rank = lane // STRIP % CAP
    source = lane // (STRIP * CAP)

    def spread(entry):
        onehot = (iota((LANES, wide), 0) == rank * 2 + entry).astype(F32).astype(BF16)
        every = jnp.dot(labels, onehot, preferred_element_type=F32)
        return jnp.sum(
            jnp.where(iota((devices, wide), 0) == source, every, 0.0), axis=0, keepdims=True
        )

    weights, cells = spread(0), spread(1)
    row = iota((CELLS * STRIP, 1), 0)
    mine = (cells == (row // STRIP).astype(F32)) & (lane % STRIP == row % STRIP)
    matrix = jnp.where(mine, weights, 0.0)
    sums = jnp.sum(matrix, axis=1, keepdims=True)
    inverse = 1.0 / jnp.maximum(sums, 1.0)
    matrix = matrix.astype(BF16)
    taken = {}
    for r in range(CAP):
        column = jnp.broadcast_to(labels[:, 2 * r : 2 * r + 1].astype(F32), (devices, LANES))
        for s in range(devices):
            taken[s, r] = jnp.broadcast_to(column[s : s + 1], (STRIP, LANES)).astype(BF16) > 0

    def tile(s, r, k):
        device, first = s, r * BODY + k * STRIP
        if first - r * BODY >= BODY:
            device, first = (s + 1) % devices, CAP * BODY + r * TAIL
        return jnp.where(taken[s, r], got[device, first : first + STRIP], jnp.zeros((), BF16))

    copies = []
    for pair in range(BLOCK // STRIP // 2):
        columns = jnp.concatenate(
            [
                jnp.concatenate(
                    [tile(s, r, k) for s in range(devices) for r in range(CAP)], axis=0
                )
                for k in (2 * pair, 2 * pair + 1)
            ],
            axis=1,
        )
        result = jnp.dot(matrix, columns, preferred_element_type=F32) * inverse
        for c in range(CELLS):
            part = result[c * STRIP : (c + 1) * STRIP]
            lanes = slice(c % PSIDE * BLOCK, (c % PSIDE + 1) * BLOCK)
            for n in range(2):
                first = (2 * pair + n) * STRIP
                total[c // PSIDE, first : first + STRIP, lanes] = lane_block(part, n)
        size = 2 * STRIP
        for line in range(PSIDE):
            copies.append(
                pltpu.make_async_copy(
                    total.at[line, pl.ds(pair * size, size)],
                    out.at[0, pl.ds(line * BLOCK + pair * size, size)],
                    out_sem.at[pair, line],
                )
            )
            copies[-1].start()
    for copy in copies:
        copy.wait()


def coadd(got):
    return pl.pallas_call(
        coadd_kernel,
        in_specs=[pl.BlockSpec(memory_space=pltpu.VMEM)],
        out_specs=pl.BlockSpec(memory_space=pl.ANY),
        out_shape=jax.ShapeDtypeStruct((1, PSIDE * BLOCK, PSIDE * BLOCK), F32),
        scratch_shapes=[
            pltpu.VMEM((PSIDE, BLOCK, WIDTH), F32),
            pltpu.SemaphoreType.DMA((BLOCK // STRIP // 2, PSIDE)),
        ],
        compiler_params=pltpu.CompilerParams(vmem_limit_bytes=32 << 20),
        name="coadd",
    )(got)


def shards(
    images, basis_taps, psf_coef, affine, visit_weight, block_patch, block_slot, patch_owner
):
    devices = lax.axis_size("ccd")
    patch = block_patch[:, :, 0]
    head = collect(images, patch, patch_owner.reshape(1, -1))
    above = lax.ppermute(head, "ccd", [(i, (i + 1) % devices) for i in range(devices)])
    order = orders()
    ready = prepare(
        basis_taps.transpose(1, 0, 2), psf_coef.transpose(1, 3, 0, 2), affine.transpose(0, 2, 3, 1),
        devices,
    )
    sent = warp(
        patch, block_slot, patch_owner, visit_weight, ready, order, images, above, devices
    )
    got = lax.all_to_all(sent, "ccd", split_axis=0, concat_axis=0, tiled=True)
    return coadd(got)


def solution(mesh):
    placed = (
        P(None, ("group", "ccd"), None),
        P(),
        P(None, "group", None, None),
        P(None, "group", None, None),
        P(None, "group"),
        P(("group", "ccd"), None, None),
        P(("group", "ccd"), None),
        P("group"),
    )
    return jax.shard_map(
        shards,
        mesh=mesh,
        in_specs=placed,
        out_specs=P(("group", "ccd"), None, None),
        check_vma=False,
    )
```

```python
import functools
import itertools

import jax
import jax.numpy as jnp
from jax import lax
from jax.experimental import pallas as pl
from jax.experimental.pallas import tpu as pltpu
from jax.sharding import PartitionSpec as P

V = 4
BLOCK = 128
BLKC = 4
SPLIT = 4
TAPS = 11
NBASIS = 9
PSIDE = 4
CELLS = PSIDE * PSIDE
CAP = 2

HALF = TAPS // 2
WARP = 3
RIM = HALF + WARP
TAIL = 16
HEIGHT = SPLIT * BLOCK
WIDTH = BLKC * BLOCK
LANES = 128
LANE_BLOCKS = WIDTH // LANES
STRIP = 16
STEP = 32
STRIPS = -(-(BLOCK + 2 * WARP) // STRIP)
MIDDLE = STRIPS // 2
GROUPS = 6
BAND = 256
PAST_STRIPS = 2
OWN_FIRST = 1
FREE_FIRST = 2
HALVES = 2
MATCHED = 4
WARPED = 4
ROWS = BLOCK // HALVES
WINDOW = ROWS + STRIP
BODY = BLOCK - TAIL
GOT = TAIL + RIM
OPEN = (STRIPS - 1) * STRIP + STEP - FREE_FIRST * STRIP
LABEL = 16
F32 = jnp.float32
BF16 = jnp.bfloat16


def sin_pi(t):
    whole = jnp.round(t)
    f = t - whole
    odd = whole - 2.0 * jnp.floor(0.5 * whole)
    f2 = f * f
    out = 0.0
    for c in (
        0.00046630280576761, -0.0073704309457144, 0.0821458866111282,
        -0.599264529320792, 2.55016403987734, -5.16771278004997, 3.14159265358979,
    ):
        out = out * f2 + c
    return f * out * (1.0 - 2.0 * odd)


def lanczos(t):
    zero = t == 0.0
    safe = jnp.where(zero, 1.0, t)
    pt = jnp.pi * safe
    value = 3.0 * sin_pi(safe) * sin_pi(safe / 3.0) / (pt * pt)
    return jnp.where(jnp.abs(t) < 3.0, jnp.where(zero, 1.0, value), 0.0)


def iota(shape, dim):
    return lax.broadcasted_iota(jnp.int32, shape, dim)


def column_at(lane):
    return lane % LANES * LANE_BLOCKS + lane // LANES


def order_kernel(sort, unsort):
    square = (WIDTH, WIDTH)
    one, none = jnp.ones((), F32), jnp.zeros((), F32)
    goes = iota(square, 0) == column_at(iota((1, WIDTH), 1))
    sort[...] = jnp.where(goes, one, none).astype(BF16)
    comes = iota(square, 1) == column_at(iota((WIDTH, 1), 0))
    unsort[...] = jnp.where(comes, one, none).astype(BF16)


def orders():
    return small_kernel(order_kernel, "orders", [], [((WIDTH, WIDTH), BF16)] * 2)


def lane_block(x, v):
    return x[:, v * LANES : (v + 1) * LANES]


def dot_exact(a, b, dims):
    return lax.dot_general(
        a, b, (dims, ((), ())), precision=lax.Precision.HIGHEST, preferred_element_type=F32
    )


def staircase(x, first):
    return jnp.concatenate(
        [
            pltpu.roll(x[g : g + 8], first + g, 1, stride=1, stride_axis=0)
            for g in range(0, x.shape[0], 8)
        ],
        axis=0,
    )


def lane_sum(terms_of, lane, count, weigh):
    blocks = []
    for v in range(LANE_BLOCKS):
        total = None
        half = count // 2
        for q in range(-(-half // LANE_BLOCKS) * -1, (half + LANE_BLOCKS - 1) // LANE_BLOCKS + 1):
            part = None
            for u in range(count):
                if (v + u - half) // LANE_BLOCKS != q:
                    continue
                piece = terms_of(u, v, (v + u - half) % LANE_BLOCKS)
                part = piece if part is None else part + piece
            if part is None:
                continue
            if q:
                part = pltpu.roll(part, -q % LANES, 1)
                if not weigh:
                    part = jnp.where((lane + q >= 0) & (lane + q < LANES), part, 0.0)
            total = part if total is None else total + part
        blocks.append(total)
    return blocks


def whereabouts(devices):
    band = lax.axis_index("ccd")
    past = lax.rem(band + devices - 1, devices)
    quarter = (band + SPLIT // 2) % SPLIT
    own = ((band + SPLIT // 2) // SPLIT, quarter * BLOCK - TAIL)
    before = ((past + SPLIT // 2) // SPLIT, (past + SPLIT // 2) % SPLIT * BLOCK + BODY)
    return (own, before), (quarter > 0) & (band > 0)


def collect_kernel(images, patch, head, numbers, sems):
    copies = [
        pltpu.make_async_copy(
            images.at[v, pl.ds(BLOCK - GOT, GOT)], head.at[pl.ds(v * GOT, GOT)], sems.at[v]
        )
        for v in range(V)
    ]
    names = pltpu.make_async_copy(patch, numbers, sems.at[V])
    names.start()
    for copy in copies:
        copy.start()
    head[V * GOT :] = jnp.zeros((8, WIDTH), F32)
    names.wait()
    head[V * GOT : V * GOT + 1, : V * BLKC] = numbers[...].astype(F32)
    for copy in copies:
        copy.wait()


def collect(images, patch):
    return pl.pallas_call(
        collect_kernel,
        in_specs=[pl.BlockSpec(memory_space=pl.ANY)] * 2,
        out_specs=pl.BlockSpec(memory_space=pltpu.VMEM),
        out_shape=jax.ShapeDtypeStruct((V * GOT + 8, WIDTH), F32),
        scratch_shapes=[pltpu.VMEM(patch.shape, jnp.int32), pltpu.SemaphoreType.DMA((V + 1,))],
        name="collect",
    )(images, patch)


def lanczos_weights(devices, affine, cols_out):
    bands, same = whereabouts(devices)
    lane = iota((1, LANES), 1)
    lanes = iota((8, WIDTH), 1)
    step = iota((8, WIDTH), 0) - WARP
    block = lanes // LANES
    carry = (block + step + LANE_BLOCKS) // LANE_BLOCKS - 1
    from_lane = lanes % LANES - carry
    col = (from_lane * LANE_BLOCKS + block).astype(F32)
    within = (from_lane >= 0) & (from_lane < LANES) & (step <= WARP)
    offset = iota((8, LANES), 0) - WARP
    crosses = (lane + offset >= TAIL) != (lane >= TAIL)
    keep = (offset <= WARP) & (same | jnp.logical_not(crosses))
    by_row = []
    for visit in range(V):
        shifts = []
        for n, (ccd, top_row) in enumerate(bands):
            a = jnp.sum(
                jnp.where(iota((1, 1, affine.shape[3]), 2) == ccd, affine[visit], 0.0),
                axis=2, keepdims=True,
            )
            row = (top_row + lane).astype(F32)
            shifts.append(a[0, 0:1] + a[0, 1:2] * (row - (HEIGHT - 1) / 2.0) / HEIGHT)
            col_shift = a[1, 0:1] + a[1, 1:2] * (col - (WIDTH - 1) / 2.0) / WIDTH
            cols_out[n * V + visit] = jnp.where(within, lanczos(col_shift - step.astype(F32)), 0.0)
        shift = jnp.where(lane < TAIL, shifts[1], shifts[0])
        weights = jnp.where(keep, lanczos(shift - offset.astype(F32)), 0.0)
        by_row.append(jnp.concatenate([weights, jnp.zeros((LANES - 8, LANES), F32)], axis=0).T)
    return by_row


def prepare_kernel(
    devices, taps, psf, affine, high_level, step_level, slope, rows_high, rows_low, cols_out
):
    row_weights = lanczos_weights(devices, affine, cols_out)
    bands, _ = whereabouts(devices)
    band_lane = iota((1, BAND), 1)
    seg = band_lane // STEP
    lane = iota((1, LANES), 1)
    tap = band_lane - seg * STEP
    onehot = (tap == iota((TAPS, BAND), 0)) & (seg < GROUPS)
    row_taps = dot_exact(taps[:, 0], onehot.astype(F32), ((1,), (0,)))
    eye = (iota((TAPS, STRIP), 0) == iota((TAPS, STRIP), 1)).astype(F32)
    turned_taps = dot_exact(eye, taps[:, 1], ((0,), (1,)))
    units = []
    for n, visit in itertools.product(range(2), range(V)):
        ccd, top_row = bands[n]
        lhs = jnp.concatenate(
            [turned_taps * psf[ccd, c, visit : visit + 1, :] for c in range(3)], axis=0
        )
        kernels = dot_exact(lhs, row_taps, ((1,), (0,)))
        const, by_row, by_col = (kernels[c * STRIP : (c + 1) * STRIP] for c in range(3))
        is_level = seg < 3
        per_strip = 2.0 * STRIP / HEIGHT
        middle_row = (top_row + (MIDDLE * STRIP - WARP)).astype(F32)
        middle_pos = (2.0 * middle_row + 1.0) / HEIGHT - 1.0
        col_move = (iota((STRIP, 1), 0) - HALF).astype(F32) * (2.0 / WIDTH)
        by_row = jnp.where(is_level, by_row, 0.0)
        const = jnp.where(is_level, const + middle_pos * by_row - col_move * by_col, by_col)
        reach = per_strip * (STRIPS - MIDDLE)
        largest = jnp.max(jnp.abs(const) + reach * jnp.abs(by_row), axis=(0, 1), keepdims=True)
        unit = jnp.maximum(largest, 1e-30) * (1.0 / 200.0)
        units.append(unit)
        const = const / unit
        by_row = (by_row * per_strip) / unit
        low_lanes = (lane // STEP) % 3 == 2
        low_band = seg % 3 == 2
        row_part = iota((STRIP, 1), 0).astype(F32) * (1.0 / STRIP)
        for u in range(TAPS):
            at = slice(u * STRIP, (u + 1) * STRIP)
            one = jnp.broadcast_to(const[u : u + 1], (STRIP, BAND))
            x, tail = staircase(one[:, :LANES], 0), staircase(one[:, LANES:], 0)
            y = staircase(jnp.broadcast_to(by_row[u : u + 1, :LANES], (STRIP, LANES)), 0)
            high = tail.astype(BF16).astype(F32)
            slope[n * V + visit, at] = jnp.where(low_band[:, LANES:], tail - high, high).astype(BF16)
            x = x + row_part * y
            high = jnp.where(lane < 3 * STEP, jnp.round(x), x.astype(BF16).astype(F32))
            high_level[n * V + visit, at] = jnp.where(low_lanes, x - high, high)
            high = jnp.round(y)
            step_level[n * V + visit, at] = jnp.where(low_lanes, y - high, high)

    for visit in range(V):
        weights = row_weights[visit]
        matrix = jnp.concatenate(
            [
                staircase(weights[:TAIL] * units[V + visit], 0),
                staircase(weights[TAIL:ROWS] * units[visit], PAST_STRIPS * STRIP),
                staircase(weights[ROWS:] * units[visit], 0),
            ],
            axis=0,
        )
        high = matrix.astype(BF16)
        rows_high[visit] = high
        rows_low[visit] = (matrix - high.astype(F32)).astype(BF16)


def small_kernel(body, name, args, shapes):
    vmem = pl.BlockSpec(memory_space=pltpu.VMEM)
    return pl.pallas_call(
        body,
        in_specs=[vmem] * len(args),
        out_specs=[vmem] * len(shapes),
        out_shape=[jax.ShapeDtypeStruct(shape, kind) for shape, kind in shapes],
        compiler_params=pltpu.CompilerParams(vmem_limit_bytes=32 << 20),
        cost_estimate=pl.CostEstimate(flops=1 << 30, bytes_accessed=1 << 20, transcendentals=0),
        name=name,
    )(*args)


def prepare(taps, psf, affine, devices):
    return small_kernel(
        functools.partial(prepare_kernel, devices), "matrices", [taps, psf, affine],
        [
            ((2 * V, TAPS * STRIP, LANES), F32),
            ((2 * V, TAPS * STRIP, LANES), F32),
            ((2 * V, TAPS * STRIP, BAND - LANES), BF16),
            ((V, BLOCK, LANES), BF16),
            ((V, BLOCK, LANES), BF16),
            ((2 * V, 8, WIDTH), F32),
        ],
    )


def sorted_rows(raw, sort):
    col_pos = (2.0 * column_at(iota((1, WIDTH), 1)).astype(F32) + 1.0) / WIDTH - 1.0
    count = raw.shape[0]
    raw_high = raw.astype(BF16)
    raw_low = (raw - raw_high.astype(F32)).astype(BF16)
    both = jnp.dot(
        jnp.concatenate([raw_high, raw_low], axis=0), sort, preferred_element_type=F32
    )
    high, low = both[:count], both[count:]
    tilted = (high + low) * col_pos
    tilted_high = tilted.astype(BF16).astype(F32)
    return high, low, tilted_high, tilted - tilted_high


def match_strip(level, step, slope, source, first, k):
    lane = iota((1, LANES), 1)
    if k != MIDDLE:
        level = level + float(k - MIDDLE) * step
    matrix = jnp.concatenate([level.astype(BF16), slope], axis=1)
    filler = jnp.zeros((BAND - GROUPS * STEP, WIDTH), BF16)
    rows = slice(first, first + STEP)
    columns = jnp.concatenate([source[h, rows] for h in (0, 1, 0, 2, 3, 2)] + [filler], axis=0)
    results = jnp.dot(matrix, columns, preferred_element_type=F32)
    blocks = lane_sum(
        lambda u, v, w: lane_block(results[u * STRIP : (u + 1) * STRIP], w), lane, TAPS, False
    )
    matched = jnp.concatenate(blocks, axis=1)
    high = matched.astype(BF16)
    return high, (matched - high.astype(F32)).astype(BF16)


def upright(line):
    count = line.shape[1]
    square = (count, count)
    return jnp.sum(
        jnp.where(iota(square, 0) == iota(square, 1), jnp.broadcast_to(line, square), 0),
        axis=1, keepdims=True,
    )


def route(patch, owner):
    square = (patch.shape[1], patch.shape[1])
    earlier = (iota(square, 0) < iota(square, 1)) & (upright(patch) == patch)
    rank = jnp.sum(earlier.astype(jnp.int32), axis=0, keepdims=True)
    named = iota((owner.shape[1], patch.shape[1]), 0) == patch
    to = jnp.sum(jnp.where(named, upright(owner), 0), axis=0, keepdims=True)
    return to, rank


def match_kernel(
    patch, slot, owner, weight, high_level, step_level, slope, sort, image,
    places, label, matched_terms, terms,
):
    ((ccd, _), _), _ = whereabouts(label.shape[0])
    to, rank = route(patch[...], owner[...])
    places[...] = to * CAP + rank

    own = jnp.where(iota(weight.shape, 1) == ccd, weight[...].astype(F32), 0.0)
    own = jnp.sum(own, axis=1, keepdims=True)
    each = (V, V * BLKC)
    weights = jnp.sum(
        jnp.where(iota(each, 1) // BLKC == iota(each, 0), own, 0.0), axis=0, keepdims=True
    )
    goes = iota((label.shape[0], V * BLKC), 0) == to
    lane = iota(label.shape, 1)
    lines = jnp.zeros(label.shape, F32)
    for r in range(CAP):
        for n, value in enumerate((weights, slot[...].astype(F32))):
            column = jnp.sum(jnp.where(goes & (rank == r), value, 0.0), axis=1, keepdims=True)
            lines = jnp.where(lane == 2 * r + n, column, lines)
    label[...] = lines

    open_row = FREE_FIRST * STRIP - GOT
    seen = OPEN - STRIP
    terms[:, :, seen:] = jnp.zeros((MATCHED, 4, STRIP, WIDTH), BF16)

    def some_visits(turn, _):
        visits = [turn * MATCHED + i for i in range(MATCHED)]
        for i, visit in enumerate(visits):
            rows = sorted_rows(image[visit, open_row : open_row + seen], sort[...])
            for h, value in enumerate(rows):
                terms[i, h, :seen] = value.astype(BF16)
        for k in range(FREE_FIRST, STRIPS):
            first = (k - FREE_FIRST) * STRIP
            for i, visit in enumerate(visits):
                at = slice(first, first + STRIP)
                matched_terms[visit, 0, at], matched_terms[visit, 1, at] = match_strip(
                    high_level[visit], step_level[visit], slope[visit], terms.at[i], first, k
                )
        return 0

    lax.fori_loop(0, V // MATCHED, some_visits, 0)


def warp_kernel(
    owner, places, label, high_level, step_level, slope, rows_high, rows_low, col_weights,
    sort, unsort, image, above, matched_free, out,
    own_terms, past_terms, own_matched, past_matched, both_places, place_of, place_sem,
):
    devices = label.shape[0]
    _, same = whereabouts(devices)
    past_patch = above[V * GOT : V * GOT + 1, : V * BLKC].astype(jnp.int32)
    to, rank = route(past_patch, owner[...])
    both_places[0:1, : V * BLKC] = places[...]
    both_places[1:2, : V * BLKC] = to * CAP + rank
    place_copy = pltpu.make_async_copy(both_places, place_of, place_sem)
    place_copy.start()
    lane = iota((1, LANES), 1)
    out[:, CAP * BLOCK :] = jnp.broadcast_to(
        label[...].reshape(devices, 1, LANES), (devices, LABEL, LANES)
    ).astype(BF16)

    seam = STRIP + STEP
    foreign = iota((seam, 1), 0) < GOT
    both = jnp.where(same, 1.0, 0.0)
    own_sees = jnp.where(foreign, both, 1.0)
    past_sees = jnp.where(foreign, 1.0, both)

    def some_visits(turn, _):
        visits = [turn * WARPED + i for i in range(WARPED)]
        for i, visit in enumerate(visits):
            tail = pl.ds(pl.multiple_of(visit * GOT, 8), GOT)
            raw = jnp.concatenate([above[tail], image[visit, : seam - GOT]], axis=0)
            for h, value in enumerate(sorted_rows(raw, sort[...])):
                own_terms[i, h] = (value * own_sees).astype(BF16)
                past_terms[i, h] = (value * past_sees).astype(BF16)
        for i, visit in enumerate(visits):
            own_matched[i, 0], own_matched[i, 1] = match_strip(
                high_level[visit], step_level[visit], slope[visit],
                own_terms.at[i], OWN_FIRST * STRIP, OWN_FIRST,
            )
        for k in range(PAST_STRIPS):
            for i, visit in enumerate(visits):
                at = slice(k * STRIP, (k + 1) * STRIP)
                past_matched[i, 0, at], past_matched[i, 1, at] = match_strip(
                    high_level[V + visit], step_level[V + visit], slope[V + visit],
                    past_terms.at[i], k * STRIP, k,
                )

        warped = []
        for i, visit in enumerate(visits):
            halves = []
            for h in range(HALVES):
                at = slice(h * ROWS, (h + 1) * ROWS)
                high, low = rows_high[visit, at], rows_low[visit, at]
                free = FREE_FIRST * STRIP

                def under(term):
                    if h == 0:
                        parts = [
                            past_matched[i, term],
                            own_matched[i, term],
                            matched_free[visit, term, : WINDOW - free],
                        ]
                    else:
                        parts = [matched_free[visit, term, ROWS - free :]]
                    left = LANES - sum([x.shape[0] for x in parts])
                    return jnp.concatenate(parts + [jnp.zeros((left, WIDTH), BF16)], axis=0)

                first = under(0)
                total = jnp.dot(
                    jnp.concatenate([high, high], axis=1),
                    jnp.concatenate([first, under(1)], axis=0),
                    preferred_element_type=F32,
                )
                halves.append(total + jnp.dot(low, first, preferred_element_type=F32))
            warped.append(jnp.concatenate(halves, axis=0))

        @pl.when(turn == 0)
        def _():
            place_copy.wait()

        for i, visit in enumerate(visits):
            parts = []
            for rows, weights in (
                (slice(0, TAIL), col_weights[V + visit]),
                (slice(TAIL, BLOCK), col_weights[visit]),
            ):
                some = warped[i][rows]
                blocks = lane_sum(
                    lambda s, v, w: lane_block(weights[s : s + 1], v) * lane_block(some, w),
                    lane, 2 * WARP + 1, True,
                )
                parts.append(jnp.concatenate(blocks, axis=1).astype(BF16))
            result = jnp.dot(
                jnp.concatenate(parts, axis=0), unsort[...], preferred_element_type=F32
            ).astype(BF16)
            for j in range(BLKC):
                piece = lane_block(result, j)
                to = place_of[0, visit * BLKC + j]
                rows = pl.ds(pl.multiple_of(to % CAP * BODY, TAIL), BODY)
                out[to // CAP, rows] = piece[TAIL:]
                to = place_of[1, visit * BLKC + j]
                rows = pl.ds(pl.multiple_of(CAP * BODY + to % CAP * TAIL, TAIL), TAIL)
                out[to // CAP, rows] = piece[:TAIL]
        return 0

    lax.fori_loop(0, V // WARPED, some_visits, 0)


def warp(patch, slot, owner, weight, ready, order, images, above, devices):
    vmem = pl.BlockSpec(memory_space=pltpu.VMEM)
    sort, unsort = order
    *matrices, rows_high, rows_low, col_weights = ready
    owner = owner.reshape(1, -1)
    args = [patch, slot, owner, weight, *matrices, sort, images]
    places, label, matched = pl.pallas_call(
        match_kernel,
        in_specs=[vmem] * len(args),
        out_specs=[vmem, vmem, vmem],
        out_shape=[
            jax.ShapeDtypeStruct((1, V * BLKC), jnp.int32),
            jax.ShapeDtypeStruct((devices, LANES), F32),
            jax.ShapeDtypeStruct((V, 2, (STRIPS - FREE_FIRST) * STRIP, WIDTH), BF16),
        ],
        scratch_shapes=[
            pltpu.VMEM((MATCHED, 4, OPEN, WIDTH), BF16),
        ],
        compiler_params=pltpu.CompilerParams(vmem_limit_bytes=32 << 20),
        cost_estimate=pl.CostEstimate(
            flops=V * 2 * (STRIPS - FREE_FIRST) * TAPS * STRIP * BAND * WIDTH,
            bytes_accessed=V * (BLOCK * WIDTH * 6),
            transcendentals=0,
        ),
        name="match",
    )(*args)
    args = [
        owner, places, label, *matrices, rows_high, rows_low, col_weights,
        sort, unsort, images, above, matched,
    ]
    return pl.pallas_call(
        warp_kernel,
        in_specs=[vmem] * len(args),
        out_specs=vmem,
        scratch_shapes=[
            pltpu.VMEM((WARPED, 4, STRIP + STEP, WIDTH), BF16),
            pltpu.VMEM((WARPED, 4, STRIP + STEP, WIDTH), BF16),
            pltpu.VMEM((WARPED, 2, STRIP, WIDTH), BF16),
            pltpu.VMEM((WARPED, 2, PAST_STRIPS * STRIP, WIDTH), BF16),
            pltpu.VMEM((8, LANES), jnp.int32),
            pltpu.SMEM((8, LANES), jnp.int32),
            pltpu.SemaphoreType.DMA(()),
        ],
        out_shape=jax.ShapeDtypeStruct((devices, CAP * BLOCK + LABEL, BLOCK), BF16),
        compiler_params=pltpu.CompilerParams(vmem_limit_bytes=32 << 20),
        cost_estimate=pl.CostEstimate(
            flops=V * 2 * STRIPS * TAPS * STRIP * BAND * WIDTH,
            bytes_accessed=V * (BLOCK * WIDTH * 6),
            transcendentals=0,
        ),
        name="warp",
    )(*args)


def coadd_kernel(got, out, total, out_sem):
    devices = got.shape[0]
    wide = devices * CAP * STRIP
    labels = got[:, CAP * BLOCK : CAP * BLOCK + LABEL][:, 0]
    lane = iota((1, wide), 1)
    rank = lane // STRIP % CAP
    source = lane // (STRIP * CAP)

    def spread(entry):
        onehot = (iota((LANES, wide), 0) == rank * 2 + entry).astype(F32).astype(BF16)
        every = jnp.dot(labels, onehot, preferred_element_type=F32)
        return jnp.sum(
            jnp.where(iota((devices, wide), 0) == source, every, 0.0), axis=0, keepdims=True
        )

    weights, cells = spread(0), spread(1)
    row = iota((CELLS * STRIP, 1), 0)
    mine = (cells == (row // STRIP).astype(F32)) & (lane % STRIP == row % STRIP)
    matrix = jnp.where(mine, weights, 0.0)
    sums = jnp.sum(matrix, axis=1, keepdims=True)
    inverse = 1.0 / jnp.maximum(sums, 1.0)
    matrix = matrix.astype(BF16)
    taken = {}
    for r in range(CAP):
        column = jnp.broadcast_to(labels[:, 2 * r : 2 * r + 1].astype(F32), (devices, LANES))
        for s in range(devices):
            taken[s, r] = jnp.broadcast_to(column[s : s + 1], (STRIP, LANES)).astype(BF16) > 0

    def tile(s, r, k):
        device, first = s, r * BODY + k * STRIP
        if first - r * BODY >= BODY:
            device, first = (s + 1) % devices, CAP * BODY + r * TAIL
        return jnp.where(taken[s, r], got[device, first : first + STRIP], jnp.zeros((), BF16))

    copies = []
    for pair in range(BLOCK // STRIP // 4):
        columns = jnp.concatenate(
            [
                jnp.concatenate(
                    [tile(s, r, k) for s in range(devices) for r in range(CAP)], axis=0
                )
                for k in range(4 * pair, 4 * pair + 4)
            ],
            axis=1,
        )
        result = jnp.dot(matrix, columns, preferred_element_type=F32) * inverse
        for c in range(CELLS):
            part = result[c * STRIP : (c + 1) * STRIP]
            lanes = slice(c % PSIDE * BLOCK, (c % PSIDE + 1) * BLOCK)
            for n in range(4):
                first = (4 * pair + n) * STRIP
                total[c // PSIDE, first : first + STRIP, lanes] = lane_block(part, n)
        size = 4 * STRIP
        for line in range(PSIDE):
            copies.append(
                pltpu.make_async_copy(
                    total.at[line, pl.ds(pair * size, size)],
                    out.at[0, pl.ds(line * BLOCK + pair * size, size)],
                    out_sem.at[pair, line],
                )
            )
            copies[-1].start()
    for copy in copies:
        copy.wait()


def coadd(got):
    return pl.pallas_call(
        coadd_kernel,
        in_specs=[pl.BlockSpec(memory_space=pltpu.VMEM)],
        out_specs=pl.BlockSpec(memory_space=pl.ANY),
        out_shape=jax.ShapeDtypeStruct((1, PSIDE * BLOCK, PSIDE * BLOCK), F32),
        scratch_shapes=[
            pltpu.VMEM((PSIDE, BLOCK, WIDTH), F32),
            pltpu.SemaphoreType.DMA((BLOCK // STRIP // 4, PSIDE)),
        ],
        compiler_params=pltpu.CompilerParams(vmem_limit_bytes=32 << 20),
        name="coadd",
    )(got)


def shards(
    images, basis_taps, psf_coef, affine, visit_weight, block_patch, block_slot, patch_owner
):
    devices = lax.axis_size("ccd")
    patch = block_patch[:, :, 0]
    head = collect(images, patch)
    above = lax.ppermute(head, "ccd", [(i, (i + 1) % devices) for i in range(devices)])
    order = orders()
    ready = prepare(
        basis_taps.transpose(1, 0, 2), psf_coef.transpose(1, 3, 0, 2), affine.transpose(0, 2, 3, 1),
        devices,
    )
    sent = warp(
        patch, block_slot, patch_owner, visit_weight, ready, order, images, above, devices
    )
    got = lax.all_to_all(sent, "ccd", split_axis=0, concat_axis=0, tiled=True)
    return coadd(got)


def solution(mesh):
    placed = (
        P(None, ("group", "ccd"), None),
        P(),
        P(None, "group", None, None),
        P(None, "group", None, None),
        P(None, "group"),
        P(("group", "ccd"), None, None),
        P(("group", "ccd"), None),
        P("group"),
    )
    return jax.shard_map(
        shards,
        mesh=mesh,
        in_specs=placed,
        out_specs=P(("group", "ccd"), None, None),
        check_vma=False,
    )
```
